32 devices in a mesh: dp: 4 (over y, x), seq: 8 (over z, core).
Axes of the slice: x: 2, y: 2, z: 4, core: 2. Of those that a mesh axis runs over, the one named last changes fastest.
Arguments:
- tokens: bfloat16 [4, 1024, 1024], P('dp', 'seq'), may hold values from -6 to 6
- cotangent: bfloat16 [4, 1024, 1024], P('dp', 'seq'), may hold values from -6 to 6
- doc_starts: int32 [4, 4], P('dp'), may hold values from 0 to 1023, as said below
- in_weight: bfloat16 [1024, 4096], replicated, may hold values from -0.1875 to 0.1875
- conv_weight: bfloat16 [2048, 4], replicated, may hold values from -3 to 3
- conv_bias: bfloat16 [2048], replicated, may hold values from -3 to 3
- xproj_weight: bfloat16 [2048, 96], replicated, may hold values from -0.125 to 0.125
- dt_weight: bfloat16 [64, 2048], replicated, may hold values from -0.75 to 0.75
- dt_bias: bfloat16 [2048], replicated, may hold values from -3.6875 to -2.296875
- a_log: float32 [2048, 16], replicated
- skip_scale: bfloat16 [2048], replicated, may hold values from 0.5 to 1.5
- out_weight: bfloat16 [2048, 1024], replicated, may hold values from -0.125 to 0.125
- norm_gain: bfloat16 [1024], replicated, may hold values from 0.5 to 1.5
Outputs:
- mixed: bfloat16 [4, 1024, 1024], P('dp', 'seq')
- tokens_grad: bfloat16 [4, 1024, 1024], P('dp', 'seq')
- in_weight_grad: float32 [1024, 4096], P(None, ('dp', 'seq'))
- conv_weight_grad: float32 [2048, 4], replicated
- conv_bias_grad: float32 [2048], replicated
- xproj_weight_grad: float32 [2048, 96], replicated
- dt_weight_grad: float32 [64, 2048], replicated
- dt_bias_grad: float32 [2048], replicated
- a_log_grad: float32 [2048, 16], replicated
- skip_scale_grad: float32 [2048], replicated
- out_weight_grad: float32 [2048, 1024], P(None, ('dp', 'seq'))
- norm_gain_grad: float32 [1024], replicated
The draws below stay inside these ranges and needn't reach their ends.
Inputs may be any that keep to these rules, and one draw needn't show every extreme that they name: `doc_starts`: the first entry of each row is 0 and the entries of a row increase strictly.
All inputs are finite; a program needn't handle non-finite values.
Results may differ from the reference program's by a relative error of at most 0.012.
Values may be sent and summed in bfloat16 or wider, within the bound.
No kernel may reach another device: no remote copies, remote signals or barrier semaphores. Data moves between devices by JAX's collectives and lax.ppermute only.
A program may use at most 320 MiB of HBM per device.

```python
import math
import jax
import jax.numpy as jnp
from jax import lax

D = 1024
E = 2048
NST = 16
KCONV = 4
DTR = 64
R_DEV = 1
L_DEV = 128
DOCS = 4
ROWS = 4
LEN = 1024


def draw_doc_starts(key, part):
    key = jax.random.fold_in(key, 5)
    row_keys = jax.random.split(key, 2 * ROWS + 1)

    def spread_row(row_key):
        return jax.random.permutation(row_key, LEN - 1)[:DOCS - 1] + 1

    def late_row(row_key):
        picked = jax.random.permutation(row_key, L_DEV - 2)[:DOCS - 2] + LEN - L_DEV + 1
        return jnp.concatenate([picked, jnp.full((1,), LEN - 1, jnp.int32)])
    spread = jax.vmap(spread_row)(row_keys[:ROWS])
    late_starts = jax.vmap(late_row)(row_keys[ROWS:2 * ROWS])
    chosen = jax.random.randint(row_keys[2 * ROWS], (ROWS // R_DEV,), 0, R_DEV)
    long_rows = jnp.arange(ROWS) % R_DEV == jnp.repeat(chosen, R_DEV)
    sorted_rest = jnp.sort(jnp.where(long_rows[:, None], late_starts, spread), axis=1)
    return jnp.concatenate([jnp.zeros((ROWS, 1), jnp.int32), sorted_rest.astype(jnp.int32)], axis=1)


def draw_a_log(key, part):
    key = jax.random.fold_in(key, 9)
    pick_key, slow_key, fast_key = jax.random.split(key, 3)
    slow_share = 0.5
    slow_pick = jax.random.uniform(pick_key, (E, NST)) < slow_share
    slow_log = jax.random.uniform(slow_key, (E, NST), minval=jnp.log(4.0 / LEN), maxval=jnp.log(40.0 / LEN))
    fast_log = jax.random.uniform(fast_key, (E, NST), minval=jnp.log(0.5), maxval=jnp.log(4.0))
    return jnp.where(slow_pick, slow_log, fast_log).astype(jnp.float32)


def level_of(rng, shape, shards, least, largest):
    loudness = 1.0
    for dim, blocks in shards:
        heights = jax.random.uniform(jax.random.fold_in(jax.random.fold_in(rng, 6), dim), (blocks,), jnp.float32, least / len(shards), largest / len(shards))
        loudness = loudness * jnp.repeat(jnp.exp(heights), shape[dim] // blocks).reshape((-1,) + (1,) * (len(shape) - 1 - dim))
    return loudness


def centred(own_key, extent, deviation, bound, shards=(), kind=jnp.bfloat16):
    loudness = level_of(own_key, extent, shards, -0.22, 0.18) if shards else 1.0
    drawn = jax.random.normal(own_key, extent, jnp.float32) * deviation * loudness
    return jnp.minimum(jnp.maximum(drawn, -bound), bound).astype(kind)


def setup_inputs(seed: int = 0) -> dict:
    key_of = jax.random.split(jax.random.key(seed), 14)
    return {
        "tokens": centred(key_of[0], (ROWS, LEN, D), 1.0, 6.0, ((0, 4), (1, 8))),
        "cotangent": centred(key_of[1], (ROWS, LEN, D), 1.0, 6.0, ((0, 4), (1, 8))),
        "doc_starts": draw_doc_starts(jax.random.fold_in(key_of[13], 71), 0),
        "in_weight": centred(key_of[3], (D, 2 * E), D ** -0.5, 0.1875),
        "conv_weight": centred(key_of[4], (E, KCONV), KCONV ** -0.5, 3.0),
        "conv_bias": centred(key_of[5], (E,), 0.5, 3.0),
        "xproj_weight": centred(key_of[6], (E, DTR + 2 * NST), E ** -0.5, 0.125),
        "dt_weight": centred(key_of[7], (DTR, E), DTR ** -0.5, 0.75),
        "dt_bias": jnp.clip(jax.random.uniform(key_of[8], (E,), jnp.float32, -3.6875, -2.296875), -3.6875, -2.296875).astype(jnp.bfloat16),
        "a_log": draw_a_log(jax.random.fold_in(key_of[13], 71), 0),
        "skip_scale": jnp.clip(jax.random.uniform(key_of[10], (E,), jnp.float32, 0.5, 1.5), 0.5, 1.5).astype(jnp.bfloat16),
        "out_weight": centred(key_of[11], (E, D), E ** -0.5, 0.125),
        "norm_gain": jnp.clip(1.0 + 0.1 * jax.random.normal(key_of[12], (D,), jnp.float32), 0.5, 1.5).astype(jnp.bfloat16),
    }


epsilon = 1e-05
highest = lax.Precision.HIGHEST

@jax.custom_vjp
def low(v):
    return lax.optimization_barrier(v.astype(jnp.bfloat16)).astype(jnp.float32)

@jax.custom_vjp
def low_back(v):
    return v

def low_keep(v):
    return (low(v), None)

def low_pass(kept, grad):
    return (grad,)

def back_keep(v):
    return (v, None)

def back_low(kept, grad):
    return (low(grad),)
low.defvjp(low_keep, low_pass)
low_back.defvjp(back_keep, back_low)

def doc_layout(starts_row):
    places = jnp.arange(LEN, dtype=jnp.int32)
    hits = starts_row[:, None] <= places[None, :]
    doc_begin = lax.optimization_barrier(jnp.max(jnp.where(hits, starts_row[:, None], 0), axis=0))
    doc_reset = jnp.any(starts_row[:, None] == places[None, :], axis=0)
    return (places, doc_begin, doc_reset)

def scan_block(carry_pair, pieces):
    hidden_state, decay_rates = carry_pair
    step_blk, inner_blk, in_blk, out_blk, keep_blk = pieces

    def advance(current, column_item):
        step_now, inner_now, in_now, out_now, keep_now = column_item
        current = jnp.exp(step_now[:, None] * decay_rates) * keep_now * current + (step_now * inner_now)[:, None] * in_now[None, :]
        return (current, lax.optimization_barrier(jnp.sum(current * out_now[None, :], axis=1)))
    hidden_state, outputs = lax.scan(advance, hidden_state, (step_blk, inner_blk, in_blk, out_blk, keep_blk))
    return ((hidden_state, decay_rates), outputs)

def layer_row(row_vals, in_weight, conv_weight, conv_bias, xproj_weight, dt_weight, dt_bias, a_log, skip_scale, out_weight, norm_gain, places, doc_begin, persist):
    inv_rms = lax.rsqrt(lax.optimization_barrier(jnp.mean(row_vals * row_vals, axis=-1, keepdims=True)) + epsilon)
    normed = low(row_vals * inv_rms * norm_gain)
    joined = low_back(jnp.dot(normed, in_weight, precision=highest))
    conv_in = low(joined[:, :E])
    gate_in = joined[:, E:]
    padded = jnp.concatenate([jnp.zeros((KCONV - 1, E), row_vals.dtype), conv_in], axis=0)
    pre_conv = conv_bias + jnp.zeros_like(conv_in)
    for offset in range(KCONV):
        usable = (doc_begin <= places - offset).astype(row_vals.dtype)
        pre_conv = pre_conv + conv_weight[:, KCONV - 1 - offset] * padded[KCONV - 1 - offset:KCONV - 1 - offset + LEN] * usable[:, None]
    inner_act = low(jax.nn.silu(pre_conv))
    projected = low_back(jnp.dot(inner_act, xproj_weight, precision=highest))
    dt_low = low(projected[:, :DTR])
    input_map = projected[:, DTR:DTR + NST]
    output_map = projected[:, DTR + NST:]
    time_step = jax.nn.softplus(low_back(jnp.dot(dt_low, dt_weight, precision=highest)) + dt_bias)
    decay_rates = -jnp.exp(a_log)
    span_size = math.gcd(LEN, 64)
    span_count = LEN // span_size
    pieces = tuple((piece.reshape((span_count, span_size) + piece.shape[1:]) for piece in (time_step, inner_act, input_map, output_map, persist)))
    initial = jnp.zeros((E, NST), row_vals.dtype)
    final_carry, scan_core = lax.scan(jax.checkpoint(scan_block), (initial, decay_rates), pieces)
    scanned = scan_core.reshape(LEN, E) + skip_scale * inner_act
    gated_out = low(scanned * jax.nn.silu(gate_in))
    return row_vals + jnp.dot(gated_out, out_weight, precision=highest)

def reference(tokens, cotangent, doc_starts, in_weight, conv_weight, conv_bias, xproj_weight, dt_weight, dt_bias, a_log, skip_scale, out_weight, norm_gain):
    weights = tuple((piece.astype(jnp.float32) for piece in (in_weight, conv_weight, conv_bias, xproj_weight, dt_weight, dt_bias, a_log, skip_scale, out_weight, norm_gain)))

    def row_pass(totals, column_item):
        tokens_row, cot_row, starts_row = column_item
        places, doc_begin, doc_reset = doc_layout(starts_row)
        persist = 1.0 - doc_reset.astype(jnp.float32)

        def forward(row_vals, *params):
            return layer_row(row_vals, *params, places, doc_begin, persist)
        mixed_row, pull_back = jax.vjp(forward, tokens_row.astype(jnp.float32), *weights)
        gradients = pull_back(cot_row.astype(jnp.float32))
        totals = tuple((running + addition for running, addition in zip(totals, gradients[1:])))
        return (totals, (mixed_row.astype(jnp.bfloat16), gradients[0].astype(jnp.bfloat16)))
    zero_totals = tuple((jnp.zeros_like(weight_arr) for weight_arr in weights))
    totals, (mixed, tokens_grad) = lax.scan(row_pass, zero_totals, (tokens, cotangent, doc_starts))
    return (mixed, tokens_grad, totals[0], totals[1], totals[2], totals[3], totals[4], totals[5], totals[6], totals[7], totals[8], totals[9])
```

```python
import functools

import jax
import jax.numpy as jnp
from jax import lax
from jax.experimental import pallas as pl
from jax.experimental.pallas import tpu as pltpu
from jax.sharding import PartitionSpec as P

epsilon = 1e-05
LANES = 128
SUBS = 8
FAR = 1e36
LEAST_RATE = 1e-33
LN2 = 0.6931471805599453
bf16, f32 = jnp.bfloat16, jnp.float32


def spread_maps(maps_ref, table_ref, steps, width):
    def lap(t, _):
        v = maps_ref[pl.ds(pl.multiple_of(t * SUBS, SUBS), SUBS), :]
        for n in range(width):
            table_ref[t, n] = jnp.broadcast_to(v[:, n : n + 1], (SUBS, LANES))
        return 0
    lax.fori_loop(0, steps, lap, 0)


def sub_scan(decay, value, forward):
    row = lax.broadcasted_iota(jnp.int32, decay.shape, 0)
    if not forward:
        row = SUBS - 1 - row
    def moved(x, by, fill):
        return jnp.where(row < by, fill, pltpu.roll(x, by if forward else SUBS - by, 0))
    by = 1
    while by < SUBS:
        d, v = moved(decay, by, 1.0), moved(value, by, 0.0)
        value = decay * v + value
        decay = decay * d
        by *= 2
    return decay, value, moved(decay, 1, 1.0), moved(value, 1, 0.0)


def ends_kernel(states, dtm_ref, dtx_ref, gs_ref, maps_ref, rates_ref,
                s_ref, f_ref, dx_ref, ex_ref, db_ref, fx_ref, table):
    steps = dtm_ref.shape[0] // SUBS
    @pl.when(pl.program_id(0) == 0)
    def _():
        spread_maps(maps_ref, table, steps, 2 * states)
    half = states // 2
    for tile in range(dtm_ref.shape[1] // LANES):
        at = pl.ds(tile * LANES, LANES)
        for first in range(0, states, half):
            rates = [jnp.broadcast_to(rates_ref[pl.ds(first + k, 1), at], (SUBS, LANES)) for k in range(half)]
            def lap(t, carry):
                h, f, p = carry
                rows = pl.ds(pl.multiple_of(t * SUBS, SUBS), SUBS)
                d, u, g = dtm_ref[rows, at], dtx_ref[rows, at], gs_ref[rows, at]
                hn, fn, pn = [], [], []
                for k in range(half):
                    a = jnp.exp2(d * rates[k])
                    hn.append(a * h[k] + u * table[t, first + k])
                    q = p[k] * a
                    pn.append(q)
                    fn.append(f[k] + q * (g * table[t, states + first + k]))
                return tuple(hn), tuple(fn), tuple(pn)
            zero = jnp.zeros((SUBS, LANES), jnp.float32)
            one = jnp.ones((SUBS, LANES), jnp.float32)
            h, f, p = lax.fori_loop(0, steps, lap, ((zero,) * half, (zero,) * half, (one,) * half), unroll=4)
            for k in range(half):
                n = first + k
                _, e_in, d_ex, e_ex = sub_scan(p[k], h[k], True)
                _, f_in, b_ex, f_ex = sub_scan(p[k], f[k], False)
                s_ref[pl.ds(n, 1), at] = e_in[SUBS - 1 :, :]
                f_ref[pl.ds(n, 1), at] = f_in[:1, :]
                dx_ref[n, :, at] = d_ex
                ex_ref[n, :, at] = e_ex
                db_ref[n, :, at] = b_ex
                fx_ref[n, :, at] = f_ex


def scan_ends(dtm, dtx, gs, maps, rates, block):
    length, width = dtm.shape
    states = rates.shape[0]
    f32 = jnp.float32
    wide = pl.BlockSpec((length, block), lambda i: (0, i))
    thin = pl.BlockSpec((states, block), lambda i: (0, i))
    deep = pl.BlockSpec((states, SUBS, block), lambda i: (0, 0, i))
    return pl.pallas_call(
        functools.partial(ends_kernel, states),
        grid=(width // block,),
        in_specs=[wide, wide, wide, pl.BlockSpec(maps.shape, lambda i: (0, 0)), thin],
        out_specs=[thin, thin] + [deep] * 4,
        out_shape=[jax.ShapeDtypeStruct((states, width), f32)] * 2 + [jax.ShapeDtypeStruct((states, SUBS, width), f32)] * 4,
        scratch_shapes=[pltpu.VMEM((length // SUBS, 2 * states, SUBS, LANES), f32)],
        compiler_params=pltpu.CompilerParams(vmem_limit_bytes=48 << 20),
        name="scan_ends",
    )(dtm, dtx, gs, maps, rates)


def core_kernel(states, dtm_ref, dt_ref, x_ref, gs_ref, maps_ref, rates_ref, entry_ref, arrive_ref,
                dx_ref, ex_ref, db_ref, fx_ref,
                y_ref, s1_ref, s2_ref, rate_ref, mapg_ref, table, acc, hs, decays):
    steps = dtm_ref.shape[0] // SUBS
    step_id = pl.program_id(0)
    f32 = jnp.float32
    @pl.when(step_id == 0)
    def _():
        spread_maps(maps_ref, table, steps, 2 * states)
        acc[...] = jnp.zeros_like(acc)
    half = states // 2
    zero = jnp.zeros((SUBS, LANES), f32)
    for tile in range(dtm_ref.shape[1] // LANES):
        at = pl.ds(tile * LANES, LANES)
        def wide(ref, n):
            return jnp.broadcast_to(ref[pl.ds(n, 1), at], (SUBS, LANES))
        rates = [wide(rates_ref, n) for n in range(states)]
        start = []
        for n in range(states):
            h0 = dx_ref[n, :, at] * wide(entry_ref, n) + ex_ref[n, :, at]
            hs[0, n] = h0
            start.append(h0)
        def lap(t, h):
            rows = pl.ds(pl.multiple_of(t * SUBS, SUBS), SUBS)
            d = dtm_ref[rows, at]
            u = dt_ref[rows, at] * x_ref[rows, at]
            new, y = [], [zero, zero]
            for n in range(states):
                a = jnp.exp2(d * rates[n])
                decays[t, n] = a
                now = a * h[n] + u * table[t, n]
                hs[t + 1, n] = now
                y[n % 2] = y[n % 2] + now * table[t, states + n]
                new.append(now)
            y_ref[rows, at] = y[0] + y[1]
            return tuple(new)
        lax.fori_loop(0, steps, lap, tuple(start), unroll=4)
        for first in range(0, states, half):
            some = rates[first : first + half]
            def back(i, carry):
                f, r = carry
                t = steps - 1 - i
                rows = pl.ds(pl.multiple_of(t * SUBS, SUBS), SUBS)
                dt, g = dt_ref[rows, at], gs_ref[rows, at]
                u = dt * x_ref[rows, at]
                fn, rn, s1, s2 = [], [], zero, zero
                for k in range(half):
                    n = first + k
                    adj = g * table[t, states + n] + f[k]
                    acc[t, n] += adj * u
                    acc[t, states + n] += g * hs[t + 1, n]
                    s1 = s1 + adj * table[t, n]
                    flow = decays[t, n] * adj
                    fn.append(flow)
                    flow = flow * hs[t, n]
                    s2 = s2 + flow * some[k]
                    rn.append(r[k] + flow * dt)
                if first == 0:
                    s1_ref[rows, at] = s1
                    s2_ref[rows, at] = s2
                else:
                    s1_ref[rows, at] += s1
                    s2_ref[rows, at] += s2
                return tuple(fn), tuple(rn)
            f0 = tuple(db_ref[first + k, :, at] * wide(arrive_ref, first + k) + fx_ref[first + k, :, at] for k in range(half))
            _, r = lax.fori_loop(0, steps, back, (f0, (zero,) * half), unroll=4)
            for k in range(half):
                rate_ref[pl.ds(first + k, 1), at] = jnp.sum(r[k], axis=0, keepdims=True)
    @pl.when(step_id == pl.num_programs(0) - 1)
    def _():
        lane = lax.broadcasted_iota(jnp.int32, (SUBS, LANES), 1)
        def lap(t, _):
            out = zero
            for n in range(2 * states):
                out = jnp.where(lane == n, jnp.sum(acc[t, n], axis=1, keepdims=True), out)
            mapg_ref[pl.ds(pl.multiple_of(t * SUBS, SUBS), SUBS), :] = out
            return 0
        lax.fori_loop(0, steps, lap, 0)


def scan_core(dtm, dt, x, gs, maps, rates, entry, arrive, deep4, block):
    length, width = dtm.shape
    states = rates.shape[0]
    steps = length // SUBS
    f32 = jnp.float32
    wide = pl.BlockSpec((length, block), lambda i: (0, i))
    thin = pl.BlockSpec((states, block), lambda i: (0, i))
    deep = pl.BlockSpec((states, SUBS, block), lambda i: (0, 0, i))
    full = pl.BlockSpec(maps.shape, lambda i: (0, 0))
    big = jax.ShapeDtypeStruct((length, width), f32)
    return pl.pallas_call(
        functools.partial(core_kernel, states),
        grid=(width // block,),
        in_specs=[wide] * 4 + [full] + [thin] * 3 + [deep] * 4,
        out_specs=[wide] * 3 + [thin, full],
        out_shape=[big] * 3 + [jax.ShapeDtypeStruct((states, width), f32), jax.ShapeDtypeStruct(maps.shape, f32)],
        scratch_shapes=[
            pltpu.VMEM((steps, 2 * states, SUBS, LANES), f32),
            pltpu.VMEM((steps, 2 * states, SUBS, LANES), f32),
            pltpu.VMEM((steps + 1, states, SUBS, LANES), f32),
            pltpu.VMEM((steps, states, SUBS, LANES), f32),
        ],
        compiler_params=pltpu.CompilerParams(vmem_limit_bytes=56 << 20),
        name="scan_core",
    )(dtm, dt, x, gs, maps, rates, entry, arrive, *deep4)


class Group:
    def __init__(self, axis, size, stride):
        self.axis, self.size, self.stride = axis, size, stride
        self.direct = size <= 4
        self.place = (lax.axis_index(axis) // stride) % size

    def lists(self):
        n = lax.axis_size(self.axis)
        span = self.stride * self.size
        return [
            [base + low + self.stride * k for k in range(self.size)]
            for base in range(0, n, span)
            for low in range(self.stride)
        ]

    def swap(self, x, k):
        n = lax.axis_size(self.axis)
        return lax.ppermute(x, self.axis, [(i, i ^ (k * self.stride)) for i in range(n)])

    def exchange(self, blocks):
        if not self.direct:
            got = lax.all_to_all(blocks, self.axis, 0, 0, axis_index_groups=self.lists(), tiled=True)
            return [got[k] for k in range(self.size)]
        pick = lambda k: lax.dynamic_index_in_dim(blocks, self.place ^ k, 0, keepdims=False)
        return [pick(0)] + [self.swap(pick(k), k) for k in range(1, self.size)]

    def gather(self, x):
        if not self.direct:
            got = lax.all_gather(x, self.axis, axis_index_groups=self.lists())
            return [got[k] for k in range(self.size)]
        return [x] + [self.swap(x, k) for k in range(1, self.size)]

    def in_order(self, parts):
        if not self.direct:
            return jnp.stack(parts)
        stacked = jnp.stack(parts)
        return jnp.stack(
            [lax.dynamic_index_in_dim(stacked, self.place ^ q, 0, keepdims=False) for q in range(self.size)]
        )


def total(parts):
    return functools.reduce(lambda a, b: a + b, [part.astype(f32) for part in parts])


def silu_slope(values):
    sigma = jax.nn.sigmoid(values)
    return sigma * (1.0 + values * (1.0 - sigma))


def pack(state, flow, span):
    high = span.astype(bf16)
    rest = span - high.astype(f32)
    middle = rest.astype(bf16)
    low = (rest - middle.astype(f32)).astype(bf16)
    return jnp.concatenate([state.astype(bf16), flow.astype(bf16), high, middle, low], axis=0)


def unpack(packed, states):
    wide = packed.astype(f32)
    span = wide[2 * states : 2 * states + 1] + wide[2 * states + 1 : 2 * states + 2] + wide[2 * states + 2 :]
    return wide[:states], wide[states : 2 * states], span


def carried(state, flow, span, rates, core, outer):
    states = state.shape[0]
    mine = pack(state, flow, span)
    pair = core.in_order(core.gather(mine))
    (s0, f0, d0), (s1, f1, d1) = unpack(pair[0], states), unpack(pair[1], states)
    whole0, whole1 = jnp.exp2(rates * d0), jnp.exp2(rates * d1)
    chips = outer.in_order(outer.gather(pack(whole1 * s0 + s1, f0 + whole0 * f1, d0 + d1)))
    entry, arrive = jnp.zeros_like(state), jnp.zeros_like(flow)
    for q in range(outer.size):
        s, f, d = unpack(chips[q], states)
        entry = jnp.where(q < outer.place, jnp.exp2(rates * d) * entry + s, entry)
        r = outer.size - 1 - q
        s, f, d = unpack(chips[r], states)
        arrive = jnp.where(r > outer.place, jnp.exp2(rates * d) * arrive + f, arrive)
    entry = jnp.where(core.place == 1, whole0 * entry + s0, entry)
    arrive = jnp.where(core.place == 0, whole1 * arrive + f1, arrive)
    return entry, arrive


def matmul(a, b):
    return jnp.dot(a, b, preferred_element_type=f32)


def body(
    tokens,
    cotangent,
    doc_starts,
    in_weight,
    conv_weight,
    conv_bias,
    xproj_weight,
    dt_weight,
    dt_bias,
    a_log,
    skip_scale,
    out_weight,
    norm_gain,
):
    length, model = tokens.shape[1:]
    inner_width, states = a_log.shape
    low_rank = dt_weight.shape[0]
    tap_count = conv_weight.shape[1]
    rim = tap_count - 1
    steps = length // SUBS
    dp_size, seq_size = lax.axis_size("dp"), lax.axis_size("seq")
    core, outer = Group("seq", 2, 1), Group("seq", seq_size // 2, 2)
    rows_group = Group("dp", dp_size, 1)
    row_at = lax.axis_index("dp")

    def mixed_order(x):
        return x.reshape(SUBS, steps, -1).swapaxes(0, 1).reshape(length, -1)

    def plain_order(x):
        return x.reshape(steps, SUBS, -1).swapaxes(0, 1).reshape(length, -1)

    base = lax.axis_index("seq") * length
    order = jnp.arange(length, dtype=jnp.int32)
    places = (base + (order % SUBS) * steps + order // SUBS)[:, None]
    doc_begin = jnp.max(jnp.where(doc_starts <= places, doc_starts, 0), axis=1, keepdims=True)
    reset = jnp.any(doc_starts == places, axis=1, keepdims=True)

    tok_row = tokens[0]
    left = lax.ppermute(tok_row[length - rim :], "seq", [(i, i + 1) for i in range(seq_size - 1)])
    tok_all = jnp.concatenate([mixed_order(tok_row), left, jnp.zeros((SUBS - rim, model), bf16)], axis=0)
    all_f = tok_all.astype(f32)
    inv_all = lax.rsqrt(jnp.mean(all_f * all_f, axis=-1, keepdims=True) + epsilon)
    scaled_all = all_f * inv_all
    normed_all = (scaled_all * norm_gain.astype(f32)).astype(bf16)
    normed = normed_all[:length]
    cot = mixed_order(cotangent[0])

    conv_all = matmul(normed_all, in_weight[:, :inner_width]).astype(bf16)
    gate_in = matmul(normed, in_weight[:, inner_width:])
    conv_in = conv_all[:length]
    tail_blocks = conv_in[length - rim * SUBS :].reshape(rim, SUBS, inner_width)
    head = jnp.concatenate([conv_all[length : length + rim][:, None], tail_blocks[:, : SUBS - 1]], axis=1)
    extended = jnp.concatenate([head.reshape(rim * SUBS, inner_width), conv_in], axis=0).astype(f32)
    conv_f = conv_weight.astype(f32)
    pre_conv = jnp.zeros((length, inner_width), f32) + conv_bias.astype(f32)
    masks, windows = [], []
    for offset in range(tap_count):
        masks.append((doc_begin <= places - offset).astype(f32))
        windows.append(extended[(rim - offset) * SUBS : (rim - offset) * SUBS + length])
        pre_conv = pre_conv + conv_f[:, tap_count - 1 - offset] * windows[offset] * masks[offset]
    inner_act = jax.nn.silu(pre_conv).astype(bf16)
    inner_f = inner_act.astype(f32)
    projected = matmul(inner_act, xproj_weight)
    dt_low = projected[:, :low_rank].astype(bf16)
    maps = jnp.pad(projected[:, low_rank:], ((0, 0), (0, LANES - 2 * states)))
    dt_raw = matmul(dt_low, dt_weight) + dt_bias.astype(f32)
    time_step = jax.nn.softplus(dt_raw)
    masked_step = jnp.where(reset, FAR, time_step)
    decay_rates = -jnp.exp(a_log).T
    rates = jnp.minimum(decay_rates, -LEAST_RATE) / LN2
    skip_f = skip_scale.astype(f32)
    g_gated = lax.dot_general(cot, out_weight, (((1,), (1,)), ((), ())), preferred_element_type=f32)
    gate_act = jax.nn.silu(gate_in)
    g_scanned = g_gated * gate_act

    block = min(512, inner_width)
    state_end, flow_end, *deep = scan_ends(masked_step, time_step * inner_f, g_scanned, maps, rates, block)
    span = jnp.sum(masked_step, axis=0, keepdims=True)
    entry, arrive = carried(state_end, flow_end, span, rates, core, outer)
    scan_out, adjoint_in, flow_rates, rate_part, map_grads = scan_core(
        masked_step, time_step, inner_f, g_scanned, maps, rates, entry, arrive, deep, block
    )
    scanned = scan_out + skip_f * inner_f
    gated_out = (scanned * gate_act).astype(bf16)
    mixed = (all_f[:length] + matmul(gated_out, out_weight)).astype(bf16)
    g_gate_in = g_gated * scanned * silu_slope(gate_in)

    step_grad = adjoint_in * inner_f + LN2 * flow_rates
    inner_scan_grad = adjoint_in * time_step + g_scanned * skip_f
    a_log_part = decay_rates * rate_part
    skip_part = jnp.sum(g_scanned * inner_f, axis=0)
    raw_grad = step_grad * jax.nn.sigmoid(dt_raw)
    dt_bias_part = jnp.sum(raw_grad, axis=0)
    raw_low = raw_grad.astype(bf16)
    dt_weight_part = matmul(dt_low.T, raw_low)
    low_grad = lax.dot_general(raw_low, dt_weight, (((1,), (1,)), ((), ())), preferred_element_type=f32)
    proj_grad = jnp.concatenate([low_grad, map_grads[:, : 2 * states]], axis=-1).astype(bf16)
    xproj_part = matmul(proj_grad.T, inner_act)
    inner_grad = inner_scan_grad + lax.dot_general(
        proj_grad, xproj_weight, (((1,), (1,)), ((), ())), preferred_element_type=f32
    )
    pre_grad = inner_grad * silu_slope(pre_conv)
    conv_bias_part = jnp.sum(pre_grad, axis=0)
    ext_grad = jnp.zeros(extended.shape, f32)
    taps = []
    for offset in range(tap_count):
        masked = pre_grad * masks[offset]
        taps.append(jnp.sum(masked * windows[offset], axis=0))
        ext_grad = ext_grad + jnp.pad(
            conv_f[:, tap_count - 1 - offset] * masked,
            (((rim - offset) * SUBS, offset * SUBS), (0, 0)),
        )
    head_grad = ext_grad[: rim * SUBS].reshape(rim, SUBS, inner_width)
    rim_grad = head_grad[:, 0]
    moved = jnp.pad(head_grad[:, 1:], ((0, 0), (0, 1), (0, 0))).reshape(rim * SUBS, inner_width)
    near_grad = ext_grad[rim * SUBS :] + jnp.pad(moved, ((length - rim * SUBS, 0), (0, 0)))
    rim_back = lax.ppermute(rim_grad, "seq", [(i, i - 1) for i in range(1, seq_size)])
    far_grad = jnp.pad(rim_back[:, None], ((0, 0), (SUBS - 1, 0), (0, 0))).reshape(rim * SUBS, inner_width)
    conv_grad = near_grad + jnp.pad(far_grad, ((length - rim * SUBS, 0), (0, 0)))

    width = in_weight.shape[1] // (dp_size * seq_size)
    half_rows = dp_size // 2

    def by_chip(x):
        rows = x.shape[0]
        blocks = x.reshape(rows, half_rows, outer.size, 2, width)
        return blocks.transpose(2, 0, 3, 1, 4).reshape(outer.size, rows, 2 * half_rows * width)

    normed_parts = outer.gather(normed_all)
    cot_parts = outer.gather(cot)
    sent = jnp.concatenate([near_grad, rim_grad, jnp.zeros((SUBS - rim, inner_width), f32)], axis=0).astype(bf16)
    conv_got = outer.exchange(by_chip(sent))
    gate_got = outer.exchange(by_chip(g_gate_in.astype(bf16)))
    out_got = outer.exchange(gated_out.reshape(length, outer.size, -1).swapaxes(0, 1))

    def summed(lefts, rights):
        return functools.reduce(
            lambda a, b: a + b,
            [
                lax.dot_general(a, b, (((0,), (0,)), ((), ())), preferred_element_type=f32)
                for a, b in zip(lefts, rights, strict=True)
            ],
        )

    conv_sum = summed(normed_parts, conv_got).reshape(model, 2, half_rows, width)
    gate_sum = summed([part[:length] for part in normed_parts], gate_got).reshape(model, 2, half_rows, width)
    in_sum = jnp.concatenate([conv_sum, gate_sum], axis=2).transpose(1, 2, 0, 3)
    in_core = total(core.exchange(in_sum.astype(bf16)))
    in_share = total(rows_group.exchange(in_core.astype(bf16)))

    out_sum = summed(out_got, cot_parts)
    thin = model // (dp_size * seq_size)
    out_sum = out_sum.reshape(-1, dp_size, outer.size, 2, thin).transpose(3, 1, 2, 0, 4)
    out_core = total(core.exchange(out_sum.astype(bf16)))
    out_row = total(rows_group.exchange(out_core.astype(bf16)))
    out_share = outer.in_order(outer.exchange(out_row.astype(bf16))).reshape(inner_width, thin).astype(f32)

    joined_grad = jnp.concatenate([conv_grad, g_gate_in], axis=-1).astype(bf16)
    normed_grad = lax.dot_general(joined_grad, in_weight, (((1,), (1,)), ((), ())), preferred_element_type=f32)
    scaled = scaled_all[:length]
    gain_part = jnp.sum(normed_grad * scaled, axis=0)
    hat_grad = normed_grad * norm_gain.astype(f32)
    tokens_grad = (
        cot.astype(f32)
        + inv_all[:length] * (hat_grad - scaled * jnp.mean(hat_grad * scaled, axis=-1, keepdims=True))
    ).astype(bf16)

    small = jnp.concatenate(
        [
            xproj_part,
            dt_weight_part,
            a_log_part,
            jnp.stack(taps[::-1], axis=0),
            dt_bias_part[None],
            skip_part[None],
            conv_bias_part[None],
            jnp.pad(gain_part, (0, inner_width - model))[None],
        ],
        axis=0,
    )
    rows = small.shape[0]
    small = small.reshape(rows, 2, dp_size, -1).transpose(1, 2, 0, 3)
    small = total(core.exchange(small.astype(bf16)))
    small = total(rows_group.exchange(small.astype(bf16)))
    small = total(list(outer.in_order(outer.gather(small.astype(bf16)))))
    small = rows_group.in_order(rows_group.gather(small))
    small = core.in_order(core.gather(small))
    small = small.transpose(2, 0, 1, 3).reshape(rows, inner_width)
    edges = [0, low_rank + 2 * states, low_rank, states, tap_count, 1, 1, 1, 1]
    cuts = [sum(edges[: k + 1]) for k in range(len(edges))]
    parts = [small[a:b] for a, b in zip(cuts[:-1], cuts[1:], strict=True)]
    return (
        plain_order(mixed)[None],
        plain_order(tokens_grad)[None],
        in_share,
        parts[3].T,
        parts[6][0],
        parts[0].T,
        parts[1],
        parts[4][0],
        parts[2].T,
        parts[5][0],
        out_share,
        parts[7][0, :model],
    )


def solution(mesh):
    whole = (P(),) * 10
    row = P("dp", "seq", None)
    columns = P(None, ("dp", "seq"))
    return jax.shard_map(
        body,
        mesh=mesh,
        in_specs=(row, row, P("dp", None)) + whole,
        out_specs=(row, row, columns) + (P(),) * 7 + (columns, P()),
        check_vma=False,
    )
```

```python
import functools

import jax
import jax.numpy as jnp
from jax import lax
from jax.experimental import pallas as pl
from jax.experimental.pallas import tpu as pltpu
from jax.sharding import PartitionSpec as P

epsilon = 1e-05
LANES = 128
SUBS = 8
FAR = 1e36
LEAST_RATE = 1e-33
LN2 = 0.6931471805599453
EDGE = 16
bf16, f32 = jnp.bfloat16, jnp.float32


def nt(a, b):
    return lax.dot_general(a, b, (((1,), (1,)), ((), ())), preferred_element_type=f32)


def tn(a, b):
    return lax.dot_general(a, b, (((0,), (0,)), ((), ())), preferred_element_type=f32)


def nn(a, b):
    return jnp.dot(a, b, preferred_element_type=f32)


def softplus(v):
    return jnp.maximum(v, 0.0) + jnp.log1p(jnp.exp(-jnp.abs(v)))


def tile_at(start):
    return pl.ds(pl.multiple_of(start, LANES), LANES)


def step_rows(t):
    return pl.ds(pl.multiple_of(t * SUBS, SUBS), SUBS)


def tap_masks(info_ref, docs, taps, length):
    row = lax.broadcasted_iota(jnp.int32, (length, LANES), 0)
    place = info_ref[0] + (row % SUBS) * (length // SUBS) + row // SUBS
    begin = jnp.zeros_like(place)
    reset = jnp.zeros((length, LANES), f32)
    for k in range(docs):
        start = info_ref[1 + k]
        begin = jnp.maximum(begin, jnp.where(place >= start, start, 0))
        reset = jnp.where(place == start, 1.0, reset)
    return [reset] + [jnp.where(begin <= place - j, 1.0, 0.0) for j in range(1, taps)]


def spread_maps(maps_ref, table_ref, steps, first, width):
    def lap(t, _):
        v = maps_ref[step_rows(t), :]
        for n in range(width):
            table_ref[t, n] = jnp.broadcast_to(v[:, first + n : first + n + 1], (SUBS, LANES))
        return 0

    lax.fori_loop(0, steps, lap, 0)


def sub_scan(decay, value, forward):
    row = lax.broadcasted_iota(jnp.int32, decay.shape, 0)
    if not forward:
        row = SUBS - 1 - row

    def moved(x, by, fill):
        return jnp.where(row < by, fill, pltpu.roll(x, by if forward else SUBS - by, 0))

    by = 1
    while by < SUBS:
        d, v = moved(decay, by, 1.0), moved(value, by, 0.0)
        value = decay * v + value
        decay = decay * d
        by *= 2
    return value, moved(decay, 1, 1.0), moved(value, 1, 0.0)


def conv_windows(ext, taps, length):
    return [ext[(taps - 1 - j) * SUBS : (taps - 1 - j) * SUBS + length] for j in range(taps)]


def conv_sum(windows, masks, vec_ref, at, taps):
    out = vec_ref[pl.ds(taps, 1), at] + vec_ref[pl.ds(taps - 1, 1), at] * windows[0]
    for j in range(1, taps):
        out = out + vec_ref[pl.ds(taps - 1 - j, 1), at] * windows[j] * masks[j]
    return out


def front_kernel(
    states, rank, taps, docs, lap1, lap2,
    info_ref, tok_ref, cot_ref, gain_ref, vec_ref, rates_ref, dtw_ref, wc_ref, wg_ref, wo_ref, wx_ref,
    ext_ref, inner_ref, gate_ref, ggated_ref, proj_ref, pack_ref, dx_ref, ex_ref, db_ref, fx_ref,
    normed, masks, inner_s, gs_s, table, dtm_s, u_s, ends,
):
    i = pl.program_id(0)
    length = cot_ref.shape[0]
    steps = length // SUBS
    rim = taps - 1
    block1, block2 = wc_ref.shape[1], pack_ref.shape[1]

    @pl.when(i == 0)
    def _():
        x = tok_ref[...].astype(f32)
        inv = lax.rsqrt(jnp.mean(x * x, axis=-1, keepdims=True) + epsilon)
        normed[...] = (x * inv * gain_ref[...]).astype(bf16)
        for k, mask in enumerate(tap_masks(info_ref, docs, taps, length)):
            masks[k] = mask
        proj_ref[...] = jnp.zeros_like(proj_ref)

    @pl.when(i < lap1)
    def _():
        own = normed[pl.ds(0, length), :]
        conv = nn(normed[...], wc_ref[...]).astype(bf16)
        gate = nn(own, wg_ref[...])
        ggated = nt(cot_ref[...], wo_ref[...])
        gate_ref[...] = gate
        ggated_ref[...] = ggated
        gs_s[:, pl.ds(pl.multiple_of(i * block1, LANES), block1)] = ggated * gate * jax.nn.sigmoid(gate)
        row = lax.broadcasted_iota(jnp.int32, (SUBS, LANES), 0)
        mask = [masks[k] for k in range(taps)]
        for tile in range(block1 // LANES):
            near = pl.ds(tile * LANES, LANES)
            far = tile_at(i * block1 + tile * LANES)
            part = conv[:, tile * LANES : (tile + 1) * LANES].astype(f32)
            pieces = []
            for b in range(rim):
                first = length - (rim - b) * SUBS
                moved = pltpu.roll(part[first : first + SUBS], 1, 0)
                pieces.append(jnp.where(row == 0, part[length + b : length + b + 1], moved))
            ext = jnp.concatenate(pieces + [part[:length]], axis=0)
            ext_ref[:, near] = jnp.concatenate(
                [jnp.zeros((2 * EDGE - rim * SUBS, LANES), f32), ext], axis=0
            ).astype(bf16)
            pre = conv_sum(conv_windows(ext, taps, length), mask, vec_ref, far, taps)
            act = (pre * jax.nn.sigmoid(pre)).astype(bf16)
            inner_ref[:, near] = act
            inner_s[:, far] = act.astype(f32)
        width = rank + 2 * states
        proj_ref[:, :width] += nn(inner_ref[...], wx_ref[...])

    @pl.when(i == lap1)
    def _():
        spread_maps(proj_ref, table, steps, rank, 2 * states)

    @pl.when(i >= lap1)
    def _():
        j = i - lap1
        wide = pl.ds(pl.multiple_of(j * block2, LANES), block2)
        low = proj_ref[:, :rank].astype(bf16)
        dt = softplus(nn(low, dtw_ref[:, wide]) + vec_ref[pl.ds(taps + 1, 1), wide])
        u_s[...] = dt * inner_s[:, wide]
        for tile in range(block2 // LANES):
            near = pl.ds(tile * LANES, LANES)
            dtm = jnp.where(masks[0] > 0.0, FAR, dt[:, tile * LANES : (tile + 1) * LANES])
            dtm_s[:, near] = dtm
            span = jnp.sum(dtm, axis=0, keepdims=True)
            high = span.astype(bf16).astype(f32)
            middle = (span - high).astype(bf16).astype(f32)
            ends[pl.ds(2 * states, 1), near] = high
            ends[pl.ds(2 * states + 1, 1), near] = middle
            ends[pl.ds(2 * states + 2, 1), near] = span - high - middle
        half = states // 2
        zero = jnp.zeros((SUBS, LANES), f32)
        one = jnp.ones((SUBS, LANES), f32)
        for tile in range(block2 // LANES):
            near = pl.ds(tile * LANES, LANES)
            far = tile_at(j * block2 + tile * LANES)
            for first in range(0, states, half):
                rates = [jnp.broadcast_to(rates_ref[pl.ds(first + k, 1), far], (SUBS, LANES)) for k in range(half)]

                def lap(t, carry):
                    h, f, p = carry
                    rows = step_rows(t)
                    d, u, g = dtm_s[rows, near], u_s[rows, near], gs_s[rows, far]
                    hn, fn, pn = [], [], []
                    for k in range(half):
                        a = jnp.exp2(d * rates[k])
                        hn.append(a * h[k] + u * table[t, first + k])
                        q = p[k] * a
                        pn.append(q)
                        fn.append(f[k] + q * (g * table[t, states + first + k]))
                    return tuple(hn), tuple(fn), tuple(pn)

                h, f, p = lax.fori_loop(
                    0, steps, lap, ((zero,) * half, (zero,) * half, (one,) * half), unroll=4
                )
                for k in range(half):
                    n = first + k
                    e_in, d_ex, e_ex = sub_scan(p[k], h[k], True)
                    f_in, b_ex, f_ex = sub_scan(p[k], f[k], False)
                    ends[pl.ds(n, 1), near] = e_in[SUBS - 1 :, :]
                    ends[pl.ds(states + n, 1), near] = f_in[:1, :]
                    dx_ref[n, :, near] = d_ex
                    ex_ref[n, :, near] = e_ex
                    db_ref[n, :, near] = b_ex
                    fx_ref[n, :, near] = f_ex
        pack_ref[...] = ends[...].astype(bf16)


def front(info, tok, cot, gain, vec, rates, dtw, in_weight, out_weight, xproj, taps, docs):
    length, model = cot.shape
    states, width = rates.shape
    rank = dtw.shape[0]
    block1, block2 = min(256, width), min(512, width)
    lap1, lap2 = width // block1, width // block2
    first = lambda i: jnp.minimum(i, lap1 - 1)
    second = lambda i: jnp.maximum(i - lap1, 0)
    full = lambda x: pl.BlockSpec(x.shape, lambda i: (0,) * x.ndim)
    wide1 = pl.BlockSpec((length, block1), lambda i: (0, first(i)))
    deep = pl.BlockSpec((states, SUBS, block2), lambda i: (0, 0, second(i)))
    pack_rows = 2 * states + EDGE
    big = lambda dtype: jax.ShapeDtypeStruct((length, width), dtype)
    return pl.pallas_call(
        functools.partial(front_kernel, states, rank, taps, docs, lap1, lap2),
        grid=(lap1 + lap2,),
        in_specs=[pl.BlockSpec(memory_space=pltpu.SMEM), full(tok), full(cot), full(gain), full(vec), full(rates), full(dtw)]
        + [
            pl.BlockSpec((model, block1), lambda i: (0, first(i))),
            pl.BlockSpec((model, block1), lambda i: (0, lap1 + first(i))),
            pl.BlockSpec((block1, model), lambda i: (first(i), 0)),
            pl.BlockSpec((block1, xproj.shape[1]), lambda i: (first(i), 0)),
        ],
        out_specs=[
            pl.BlockSpec((2 * EDGE + length, block1), lambda i: (0, first(i))),
            wide1, wide1, wide1,
            pl.BlockSpec((length, LANES), lambda i: (0, 0)),
            pl.BlockSpec((pack_rows, block2), lambda i: (0, second(i))),
            deep, deep, deep, deep,
        ],
        out_shape=[
            jax.ShapeDtypeStruct((2 * EDGE + length, width), bf16),
            big(bf16), big(f32), big(f32),
            jax.ShapeDtypeStruct((length, LANES), f32),
            jax.ShapeDtypeStruct((pack_rows, width), bf16),
        ] + [jax.ShapeDtypeStruct((states, SUBS, width), f32)] * 4,
        scratch_shapes=[
            pltpu.VMEM(tok.shape, bf16),
            pltpu.VMEM((taps, length, LANES), f32),
            pltpu.VMEM((length, width), f32),
            pltpu.VMEM((length, width), f32),
            pltpu.VMEM((length // SUBS, 2 * states, SUBS, LANES), f32),
            pltpu.VMEM((length, block2), f32),
            pltpu.VMEM((length, block2), f32),
            pltpu.VMEM((pack_rows, block2), f32),
        ],
        compiler_params=pltpu.CompilerParams(vmem_limit_bytes=48 << 20),
        cost_estimate=pl.CostEstimate(flops=0, bytes_accessed=72000000, transcendentals=0),
        name="front",
    )(info, tok, cot, gain, vec, rates, dtw, in_weight, in_weight, out_weight, xproj)


def chip_spot(tile, chips, tiles):
    if chips == 1:
        return 0, tile
    half, chip, core = tile // (2 * chips), (tile // 2) % chips, tile % 2
    return chip, core * (tiles // (2 * chips)) + half


def forward_kernel(
    states, rank, taps, docs, chips, laps,
    info_ref, proj_ref, dtw_ref, vec_ref, rates_ref, entry_ref, inner_ref, gate_ref, ggated_ref, dx_ref, ex_ref,
    gated_ref, ggate_ref, *rest,
):
    blocks, (table, masks, dtm_s, u_s, y_s, held) = rest[: chips], rest[chips:]
    length = inner_ref.shape[0]
    tiles = laps * inner_ref.shape[1] // LANES
    steps = length // SUBS
    zero = jnp.zeros((SUBS, LANES), f32)

    @pl.when(pl.program_id(0) == 0)
    def _():
        spread_maps(proj_ref, table, steps, rank, 2 * states)
        masks[0] = tap_masks(info_ref, docs, 1, length)[0]

    low = proj_ref[:, :rank].astype(bf16)
    dt_all = softplus(nn(low, dtw_ref[...]) + vec_ref[pl.ds(taps + 1, 1), :])
    for tile in range(inner_ref.shape[1] // LANES):
        at = pl.ds(tile * LANES, LANES)
        dt = dt_all[:, tile * LANES : (tile + 1) * LANES]
        x = inner_ref[:, at].astype(f32)
        dtm_s[...] = jnp.where(masks[0] > 0.0, FAR, dt)
        u_s[...] = dt * x

        def wide(ref, n):
            return jnp.broadcast_to(ref[pl.ds(n, 1), at], (SUBS, LANES))

        rates = [wide(rates_ref, n) for n in range(states)]
        start = tuple(dx_ref[n, :, at] * wide(entry_ref, n) + ex_ref[n, :, at] for n in range(states))

        def lap(t, h):
            rows = step_rows(t)
            d, u = dtm_s[rows, :], u_s[rows, :]
            new, y = [], [zero, zero]
            for n in range(states):
                now = jnp.exp2(d * rates[n]) * h[n] + u * table[t, n]
                y[n % 2] = y[n % 2] + now * table[t, states + n]
                new.append(now)
            y_s[rows, :] = y[0] + y[1]
            return tuple(new)

        lax.fori_loop(0, steps, lap, start, unroll=4)
        scanned = y_s[...] + vec_ref[pl.ds(taps + 2, 1), at] * x
        gate = gate_ref[:, at]
        sig = jax.nn.sigmoid(gate)
        gated_ref[:, at] = (scanned * gate * sig).astype(bf16)
        ggate = (ggated_ref[:, at] * scanned * (sig * (1.0 + gate * (1.0 - sig)))).astype(bf16)
        ggate_ref[:, at] = ggate
        chip, spot = chip_spot(pl.program_id(0) * (inner_ref.shape[1] // LANES) + tile, chips, tiles)
        held[chip, :, tile_at(spot * LANES)] = ggate

    @pl.when(pl.program_id(0) == laps - 1)
    def _():
        for n in range(chips):
            blocks[n][...] = held[info_ref[1 + docs] ^ n] if chips > 1 else held[0]


def forward(info, proj, dtw, vec, rates, entry, inner, gate, ggated, dx, ex, taps, docs, chips):
    length, width = inner.shape
    states = rates.shape[0]
    rank = dtw.shape[0]
    block = min(512, width)
    wide = pl.BlockSpec((length, block), lambda i: (0, i))
    deep = pl.BlockSpec((states, SUBS, block), lambda i: (0, 0, i))
    thin = lambda x: pl.BlockSpec((x.shape[0], block), lambda i: (0, i))
    return pl.pallas_call(
        functools.partial(forward_kernel, states, rank, taps, docs, chips, width // block),
        grid=(width // block,),
        in_specs=[pl.BlockSpec(memory_space=pltpu.SMEM), pl.BlockSpec(proj.shape, lambda i: (0, 0))]
        + [thin(dtw), thin(vec), thin(rates), thin(entry), wide, wide, wide, deep, deep],
        out_specs=[wide, wide] + [pl.BlockSpec((length, width // chips), lambda i: (0, 0))] * chips,
        out_shape=[jax.ShapeDtypeStruct((length, width), bf16)] * 2
        + [jax.ShapeDtypeStruct((length, width // chips), bf16)] * chips,
        scratch_shapes=[
            pltpu.VMEM((length // SUBS, 2 * states, SUBS, LANES), f32),
            pltpu.VMEM((1, length, LANES), f32),
        ] + [pltpu.VMEM((length, LANES), f32)] * 3 + [pltpu.VMEM((chips, length, width // chips), bf16)],
        compiler_params=pltpu.CompilerParams(vmem_limit_bytes=48 << 20),
        cost_estimate=pl.CostEstimate(flops=0, bytes_accessed=32400000, transcendentals=0),
        name="forward",
    )(info, proj, dtw, vec, rates, entry, inner, gate, ggated, dx, ex)


def backward_kernel(
    states, rank, taps, docs, laps, chips,
    info_ref, proj_ref, tok_ref, gain_ref, dtw_ref, vec_ref, rates_ref, entry_ref, arrive_ref,
    inner_ref, gate_ref, ggated_ref, dx_ref, ex_ref, db_ref, fx_ref, gated_ref, ggate_ref, wo_ref, wg_ref,
    ext_ref, wc_ref, wx_ref,
    mine_ref, theirs_ref, ngrad_ref, mixed_ref, *rest,
):
    blocks = rest[:chips]
    (table, acc, hs, decays, masks, dtm_s, dt_s, u_s, gs_s, s1_s, s2_s,
    isg, inner_s, raw_s, sent_s, low_acc, pg, mixed_acc, ngrad, small, held) = rest[chips:]
    i = pl.program_id(0)
    length, block = inner_ref.shape
    model = tok_ref.shape[1]
    steps = length // SUBS
    rim = taps - 1
    maps = rank + 2 * states
    row_dtw = maps
    row_rate = row_dtw + rank
    row_taps = row_rate + states
    row_dtb, row_skip, row_cb, row_gain = (row_taps + taps + k for k in range(4))
    zero = jnp.zeros((SUBS, LANES), f32)
    half = states // 2

    @pl.when(i == 0)
    def _():
        spread_maps(proj_ref, table, steps, rank, 2 * states)
        for k, mask in enumerate(tap_masks(info_ref, docs, taps, length)):
            masks[k] = mask
        acc[...] = jnp.zeros_like(acc)
        low_acc[...] = jnp.zeros_like(low_acc)
        mixed_acc[...] = jnp.zeros_like(mixed_acc)
        ngrad[...] = jnp.zeros_like(ngrad)
        small[pl.ds(small.shape[0] - EDGE, EDGE), :] = jnp.zeros((EDGE, small.shape[1]), f32)

    @pl.when(i < laps)
    def _():
        mixed_acc[...] += nn(gated_ref[...], wo_ref[...])
        ngrad[pl.ds(0, length), :] += nt(ggate_ref[...], wg_ref[...])
        wide_far = pl.ds(pl.multiple_of(i * block, LANES), block)
        low = proj_ref[:, :rank].astype(bf16)
        raw_all = nn(low, dtw_ref[...]) + vec_ref[pl.ds(taps + 1, 1), wide_far]
        for tile in range(block // LANES):
            at = pl.ds(tile * LANES, LANES)
            far = tile_at(i * block + tile * LANES)
            raw = raw_all[:, tile * LANES : (tile + 1) * LANES]
            dt = softplus(raw)
            x = inner_ref[:, at].astype(f32)
            inner_s[:, far] = inner_ref[:, at]
            gate = gate_ref[:, at]
            gs = ggated_ref[:, at] * gate * jax.nn.sigmoid(gate)
            dtm_s[...] = jnp.where(masks[0] > 0.0, FAR, dt)
            dt_s[...] = dt
            u_s[...] = dt * x
            gs_s[...] = gs

            def wide(ref, n):
                return jnp.broadcast_to(ref[pl.ds(n, 1), at], (SUBS, LANES))

            rates = [wide(rates_ref, n) for n in range(states)]
            start = []
            for n in range(states):
                h0 = dx_ref[n, :, at] * wide(entry_ref, n) + ex_ref[n, :, at]
                hs[0, n] = h0
                start.append(h0)

            def lap(t, h):
                rows = step_rows(t)
                d, u = dtm_s[rows, :], u_s[rows, :]
                new = []
                for n in range(states):
                    a = jnp.exp2(d * rates[n])
                    decays[t, n] = a
                    now = a * h[n] + u * table[t, n]
                    hs[t + 1, n] = now
                    new.append(now)
                return tuple(new)

            lax.fori_loop(0, steps, lap, tuple(start), unroll=4)
            for first in range(0, states, half):
                some = rates[first : first + half]

                def back(k, carry):
                    f, r = carry
                    t = steps - 1 - k
                    rows = step_rows(t)
                    dtt, g, u = dt_s[rows, :], gs_s[rows, :], u_s[rows, :]
                    fn, rn, s1, s2 = [], [], zero, zero
                    for k in range(half):
                        n = first + k
                        adj = g * table[t, states + n] + f[k]
                        acc[t, n] += adj * u
                        acc[t, states + n] += g * hs[t + 1, n]
                        s1 = s1 + adj * table[t, n]
                        flow = decays[t, n] * adj
                        fn.append(flow)
                        flow = flow * hs[t, n]
                        s2 = s2 + flow * some[k]
                        rn.append(r[k] + flow * dtt)
                    if first == 0:
                        s1_s[rows, :] = s1
                        s2_s[rows, :] = s2
                    else:
                        s1_s[rows, :] += s1
                        s2_s[rows, :] += s2
                    return tuple(fn), tuple(rn)

                f0 = tuple(
                    db_ref[first + k, :, at] * wide(arrive_ref, first + k) + fx_ref[first + k, :, at]
                    for k in range(half)
                )
                _, r = lax.fori_loop(0, steps, back, (f0, (zero,) * half), unroll=4)
                for k in range(half):
                    small[pl.ds(row_rate + first + k, 1), far] = jnp.sum(r[k], axis=0, keepdims=True)
            s1 = s1_s[...]
            step_grad = s1 * x + LN2 * s2_s[...]
            isg[:, far] = s1 * dt + gs * vec_ref[pl.ds(taps + 2, 1), far]
            raw_grad = step_grad * jax.nn.sigmoid(raw)
            raw_s[:, at] = raw_grad.astype(bf16)
            small[pl.ds(row_dtb, 1), far] = jnp.sum(raw_grad, axis=0, keepdims=True)
            small[pl.ds(row_skip, 1), far] = jnp.sum(gs * x, axis=0, keepdims=True)
        small[pl.ds(row_dtw, rank), wide_far] = tn(low, raw_s[...])
        low_acc[:, :rank] += nt(raw_s[...], dtw_ref[...])

    @pl.when(i == laps - 1)
    def _():
        lane = lax.broadcasted_iota(jnp.int32, (SUBS, LANES), 1)

        def lap(t, _):
            out = low_acc[step_rows(t), :]
            for n in range(2 * states):
                out = jnp.where(lane == rank + n, jnp.sum(acc[t, n], axis=1, keepdims=True), out)
            low_acc[step_rows(t), :] = out
            return 0

        lax.fori_loop(0, steps, lap, 0)
        pg[...] = low_acc[...].astype(bf16)

    @pl.when(i >= laps)
    def _():
        j = i - laps
        wide_far = pl.ds(pl.multiple_of(j * block, LANES), block)
        small[pl.ds(0, maps), wide_far] = tn(pg[...], inner_s[:, wide_far])[:maps]
        inner_grad = isg[:, wide_far] + nt(pg[:, :maps], wx_ref[...])
        mask = [masks[k] for k in range(taps)]
        row = lax.broadcasted_iota(jnp.int32, (SUBS, LANES), 0)
        for tile in range(block // LANES):
            at = pl.ds(tile * LANES, LANES)
            far = tile_at(j * block + tile * LANES)
            ext = ext_ref[:, at].astype(f32)[2 * EDGE - rim * SUBS :]
            windows = conv_windows(ext, taps, length)
            pre = conv_sum(windows, mask, vec_ref, far, taps)
            sig = jax.nn.sigmoid(pre)
            grad = inner_grad[:, tile * LANES : (tile + 1) * LANES] * (sig * (1.0 + pre * (1.0 - sig)))
            small[pl.ds(row_cb, 1), far] = jnp.sum(grad, axis=0, keepdims=True)
            small[pl.ds(row_taps + rim, 1), far] = jnp.sum(grad * windows[0], axis=0, keepdims=True)
            near = [grad[step * SUBS : (step + 1) * SUBS] * vec_ref[pl.ds(rim, 1), far] for step in range(steps)]
            head = [zero] * rim
            for k in range(1, taps):
                masked = grad * mask[k]
                small[pl.ds(row_taps + rim - k, 1), far] = jnp.sum(masked * windows[k], axis=0, keepdims=True)
                masked = masked * vec_ref[pl.ds(rim - k, 1), far]
                for step in range(steps):
                    piece = masked[step * SUBS : (step + 1) * SUBS]
                    if step >= k:
                        near[step - k] = near[step - k] + piece
                    else:
                        head[rim + step - k] = head[rim + step - k] + piece
            edge = zero
            for b in range(rim):
                moved = jnp.where(row == SUBS - 1, 0.0, pltpu.roll(head[b], SUBS - 1, 0))
                near[steps - rim + b] = near[steps - rim + b] + moved
                edge = jnp.where(row == b, jnp.broadcast_to(head[b][:1], (SUBS, LANES)), edge)
            sent = jnp.concatenate(near + [edge] + [zero] * (EDGE // SUBS - 1), axis=0).astype(bf16)
            sent_s[:, at] = sent
            chip, spot = chip_spot(j * (block // LANES) + tile, chips, laps * block // LANES)
            held[chip, :, tile_at(spot * LANES)] = sent
        ngrad[...] += nt(sent_s[...], wc_ref[...])

    @pl.when(i == 2 * laps - 1)
    def _():
        x = tok_ref[...].astype(f32)
        inv = lax.rsqrt(jnp.mean(x * x, axis=-1, keepdims=True) + epsilon)
        grad = ngrad[...]
        ngrad_ref[...] = grad
        small[pl.ds(row_gain, 1), pl.ds(0, model)] = jnp.sum(grad * x * inv, axis=0, keepdims=True)
        for n in range(chips):
            blocks[n][...] = held[info_ref[1 + docs] ^ n] if chips > 1 else held[0]
        count, chunk = mine_ref.shape[0], mine_ref.shape[2]
        for c in range(2):
            @pl.when(info_ref[2 + docs] == c)
            def _():
                for n in range(count):
                    at, other = (c * count + n) * chunk, ((1 - c) * count + n) * chunk
                    mine_ref[n] = small[:, at : at + chunk]
                    theirs_ref[n] = small[:, other : other + chunk].astype(bf16)
        mixed_ref[...] = turned((x[:length] + mixed_acc[...]).astype(bf16), True)


def turned(x, plain):
    length = x.shape[0]
    steps = length // SUBS
    a = lax.broadcasted_iota(jnp.int32, (length, length), 1 - plain)
    b = lax.broadcasted_iota(jnp.int32, (length, length), plain + 0)
    turn = jnp.where(b == (a % steps) * SUBS + a // steps, 1.0, 0.0).astype(bf16)
    return nn(turn, x).astype(bf16)


def backward(info, proj, tok, gain, dtw, vec, rates, entry, arrive, inner, gate, ggated, deep4, gated, ggate,
             in_weight, out_weight, ext, xproj, taps, docs, chips, chunks):
    length, width = inner.shape
    model = tok.shape[1]
    states = rates.shape[0]
    rank = dtw.shape[0]
    block = min(512, width)
    laps = width // block
    steps = length // SUBS
    first = lambda i: jnp.minimum(i, laps - 1)
    second = lambda i: jnp.maximum(i - laps, 0)
    full = lambda x: pl.BlockSpec(x.shape, lambda i: (0,) * x.ndim)
    wide = pl.BlockSpec((length, block), lambda i: (0, first(i)))
    deep = pl.BlockSpec((states, SUBS, block), lambda i: (0, 0, first(i)))
    thin = lambda x: pl.BlockSpec((x.shape[0], block), lambda i: (0, first(i)))
    rows = 2 * rank + 3 * states + taps + 4
    rows = -(-rows // EDGE) * EDGE
    return pl.pallas_call(
        functools.partial(backward_kernel, states, rank, taps, docs, laps, chips),
        grid=(2 * laps,),
        in_specs=[pl.BlockSpec(memory_space=pltpu.SMEM), full(proj), full(tok), full(gain), thin(dtw), full(vec)]
        + [thin(rates), thin(entry), thin(arrive), wide, wide, wide, deep, deep, deep, deep, wide, wide]
        + [
            pl.BlockSpec((block, model), lambda i: (first(i), 0)),
            pl.BlockSpec((model, block), lambda i: (0, laps + first(i))),
            pl.BlockSpec((ext.shape[0], block), lambda i: (0, second(i))),
            pl.BlockSpec((model, block), lambda i: (0, second(i))),
            pl.BlockSpec((block, xproj.shape[1]), lambda i: (second(i), 0)),
        ],
        out_specs=[
            pl.BlockSpec((chunks, rows, width // (2 * chunks)), lambda i: (0, 0, 0)),
            pl.BlockSpec((chunks, rows, width // (2 * chunks)), lambda i: (0, 0, 0)),
            pl.BlockSpec((length + EDGE, model), lambda i: (0, 0)),
            pl.BlockSpec((length, model), lambda i: (0, 0)),
        ] + [pl.BlockSpec((length + EDGE, width // chips), lambda i: (0, 0))] * chips,
        out_shape=[
            jax.ShapeDtypeStruct((chunks, rows, width // (2 * chunks)), f32),
            jax.ShapeDtypeStruct((chunks, rows, width // (2 * chunks)), bf16),
            jax.ShapeDtypeStruct((length + EDGE, model), f32),
            jax.ShapeDtypeStruct((length, model), bf16),
        ] + [jax.ShapeDtypeStruct((length + EDGE, width // chips), bf16)] * chips,
        scratch_shapes=[
            pltpu.VMEM((steps, 2 * states, SUBS, LANES), f32),
            pltpu.VMEM((steps, 2 * states, SUBS, LANES), f32),
            pltpu.VMEM((steps + 1, states, SUBS, LANES), f32),
            pltpu.VMEM((steps, states, SUBS, LANES), f32),
            pltpu.VMEM((taps, length, LANES), f32),
        ] + [pltpu.VMEM((length, LANES), f32)] * 6
        + [
            pltpu.VMEM((length, width), f32),
            pltpu.VMEM((length, width), bf16),
            pltpu.VMEM((length, block), bf16),
            pltpu.VMEM((length + EDGE, block), bf16),
            pltpu.VMEM((length, LANES), f32),
            pltpu.VMEM((length, LANES), bf16),
            pltpu.VMEM((length, model), f32),
            pltpu.VMEM((length + EDGE, model), f32),
            pltpu.VMEM((rows, width), f32),
            pltpu.VMEM((chips, length + EDGE, width // chips), bf16),
        ],
        compiler_params=pltpu.CompilerParams(vmem_limit_bytes=56 << 20),
        cost_estimate=pl.CostEstimate(flops=0, bytes_accessed=100800000, transcendentals=0),
        name="backward",
    )(info, proj, tok, gain, dtw, vec, rates, entry, arrive, inner, gate, ggated, *deep4, gated, ggate,
      out_weight, in_weight, ext, in_weight, xproj)


def finish_kernel(rim, ngrad_ref, back_ref, tok_ref, cot_ref, gain_ref, out_ref):
    length = cot_ref.shape[0]
    x = tok_ref[pl.ds(0, length), :].astype(f32)
    inv = lax.rsqrt(jnp.mean(x * x, axis=-1, keepdims=True) + epsilon)
    scaled = x * inv
    row = lax.broadcasted_iota(jnp.int32, (SUBS, x.shape[1]), 0)
    pieces = [ngrad_ref[pl.ds(0, length - rim * SUBS), :]]
    for b in range(rim):
        late = jnp.where(row == SUBS - 1, back_ref[pl.ds(b, 1), :], 0.0)
        pieces.append(ngrad_ref[pl.ds(length - (rim - b) * SUBS, SUBS), :] + late)
    hat = jnp.concatenate(pieces, axis=0) * gain_ref[...]
    grad = cot_ref[...].astype(f32) + inv * (hat - scaled * jnp.mean(hat * scaled, axis=-1, keepdims=True))
    out_ref[...] = turned(grad.astype(bf16), True)


def finish(ngrad, back, tok, cot, gain, rim):
    return pl.pallas_call(
        functools.partial(finish_kernel, rim),
        out_shape=jax.ShapeDtypeStruct(cot.shape, bf16),
        compiler_params=pltpu.CompilerParams(vmem_limit_bytes=32 << 20),
        cost_estimate=pl.CostEstimate(flops=0, bytes_accessed=7200000, transcendentals=0),
        name="finish",
    )(ngrad, back, tok, cot, gain)


SMEM_SPEC = pl.BlockSpec(memory_space=pltpu.SMEM)


def plain_call(kernel, name, out_shape, args, us, scratch=()):
    full = lambda x: pl.BlockSpec(x.shape, lambda: (0,) * len(x.shape))
    return pl.pallas_call(
        kernel,
        in_specs=[SMEM_SPEC] + [full(x) for x in args[1:]],
        out_specs=[full(x) for x in out_shape],
        out_shape=out_shape,
        scratch_shapes=list(scratch),
        compiler_params=pltpu.CompilerParams(vmem_limit_bytes=40 << 20),
        cost_estimate=pl.CostEstimate(flops=0, bytes_accessed=int(us * 3.6e6), transcendentals=0),
        name=name,
    )(*args)


def prepare_kernel(rim, size, info_ref, tok_ref, left_ref, cot_ref, tok_out, cot_out, *parts):
    length = tok_ref.shape[0]
    tok_out[pl.ds(0, length), :] = turned(tok_ref[...], False)
    left = left_ref[...].astype(f32)
    tok_out[pl.ds(length, EDGE), :] = jnp.concatenate(
        [left, jnp.zeros((EDGE - rim, left.shape[1]), f32)], axis=0
    ).astype(bf16)
    cot = turned(cot_ref[...], False)
    cot_out[...] = cot
    thin = cot.shape[1] // size
    for q in range(size):
        for k in range(size):
            @pl.when((info_ref[0] ^ k) == q)
            def _():
                parts[k][...] = cot[:, q * thin : (q + 1) * thin]


def pair_kernel(states, info_ref, mine_ref, other_ref, rates_ref, out_ref):
    first = info_ref[0] == 0
    mine, other, rates = mine_ref[...].astype(f32), other_ref[...].astype(f32), rates_ref[...]
    near, far = jnp.where(first, mine, other), jnp.where(first, other, mine)

    def span(x):
        return x[2 * states : 2 * states + 1] + x[2 * states + 1 : 2 * states + 2] + x[2 * states + 2 : 2 * states + 3]

    d0, d1 = span(near), span(far)
    out_ref[pl.ds(0, states), :] = (jnp.exp2(rates * d1) * near[:states] + far[:states]).astype(bf16)
    flow = near[states : 2 * states] + jnp.exp2(rates * d0) * far[states : 2 * states]
    out_ref[pl.ds(states, states), :] = flow.astype(bf16)
    d = d0 + d1
    high = d.astype(bf16).astype(f32)
    middle = (d - high).astype(bf16).astype(f32)
    row = lax.broadcasted_iota(jnp.int32, (EDGE, d.shape[1]), 0)
    rest = jnp.where(row == 0, high, jnp.where(row == 1, middle, jnp.where(row == 2, d - high - middle, 0.0)))
    out_ref[pl.ds(2 * states, EDGE), :] = rest.astype(bf16)


def enter_kernel(states, count, info_ref, mine_ref, other_ref, rates_ref, *rest):
    chips, (entry_ref, arrive_ref, held) = rest[:count], rest[count:]
    core, place, turn = info_ref[0], info_ref[1], info_ref[2]
    rates = rates_ref[...]
    for k in range(count):
        held[(place & turn) ^ k] = chips[k][...].astype(f32)

    def split(x):
        span = x[2 * states : 2 * states + 1] + x[2 * states + 1 : 2 * states + 2] + x[2 * states + 2 : 2 * states + 3]
        return x[:states], x[states : 2 * states], jnp.exp2(rates * span)

    def lap(k, carry):
        entry, arrive = carry
        s, _, whole = split(held[k])
        entry = jnp.where(k < place, whole * entry + s, entry)
        back = count - 1 - k
        _, f, whole = split(held[back])
        arrive = jnp.where(back > place, whole * arrive + f, arrive)
        return entry, arrive

    entry, arrive = lax.fori_loop(0, count, lap, (jnp.zeros_like(rates), jnp.zeros_like(rates)))
    s, f, whole = split(other_ref[...].astype(f32))
    entry_ref[...] = jnp.where(core == 1, whole * entry + s, entry)
    arrive_ref[...] = jnp.where(core == 0, whole * arrive + f, arrive)


def enter(where, mine, other, rates, chips):
    states, width = rates.shape
    block = min(512, width)
    thin = lambda x: pl.BlockSpec((x.shape[0], block), lambda i: (0, i))
    return pl.pallas_call(
        functools.partial(enter_kernel, states, len(chips)),
        grid=(width // block,),
        in_specs=[SMEM_SPEC] + [thin(x) for x in (mine, other, rates, *chips)],
        out_specs=[thin(rates)] * 2,
        out_shape=[jax.ShapeDtypeStruct(rates.shape, f32)] * 2,
        scratch_shapes=[pltpu.VMEM((len(chips), mine.shape[0], block), f32)],
        compiler_params=pltpu.CompilerParams(vmem_limit_bytes=40 << 20),
        cost_estimate=pl.CostEstimate(flops=0, bytes_accessed=7000000, transcendentals=0),
        name="enter",
    )(where, mine, other, rates, *chips)


def split_cores(info_ref, x, mine_ref, theirs_ref):
    half = x.shape[1] // 2
    for c in range(2):
        @pl.when(info_ref[0] == c)
        def _():
            mine_ref[...] = x[:, c * half : (c + 1) * half]
            theirs_ref[...] = x[:, (1 - c) * half : (2 - c) * half].astype(bf16)


def gate_kernel(count, info_ref, gain_ref, *rest):
    toks, gots, (turned_ref, mine_ref, theirs_ref) = rest[:count], rest[count : 2 * count], rest[2 * count :]
    length = gots[0].shape[0]
    edges = []
    for k in range(count):
        x = toks[k][...].astype(f32)
        inv = lax.rsqrt(jnp.mean(x * x, axis=-1, keepdims=True) + epsilon)
        normed = x * inv * gain_ref[...]
        turned_ref[:, k * length : (k + 1) * length] = normed[:length].T.astype(bf16)
        edges.append(normed[length:])
    pad = jnp.zeros((length - count * EDGE, edges[0].shape[1]), f32)
    turned_ref[:, count * length :] = jnp.concatenate(edges + [pad], axis=0).T.astype(bf16)
    got = jnp.concatenate([got[...] for got in gots], axis=0)
    split_cores(info_ref, nn(turned_ref[:, : count * length], got), mine_ref, theirs_ref)


def conv_kernel(count, info_ref, turned_ref, *rest):
    gots, (mine_ref, theirs_ref) = rest[:count], rest[count:]
    length = gots[0].shape[0] - EDGE
    wide = gots[0].shape[1]
    pad = jnp.zeros((length - count * EDGE, wide), bf16)
    got = jnp.concatenate([got[:length, :] for got in gots] + [got[length:, :] for got in gots] + [pad], axis=0)
    split_cores(info_ref, nn(turned_ref[...], got), mine_ref, theirs_ref)


def out_kernel(count, chips, thin, info_ref, *rest):
    cots, gateds, (mine_ref, theirs_ref) = rest[:count], rest[count : 2 * count], rest[2 * count :]
    left = jnp.concatenate([cot[...].astype(f32).T for cot in cots], axis=1).astype(bf16)
    out = nn(left, jnp.concatenate([gated[...] for gated in gateds], axis=0))
    for c in range(2):
        @pl.when(info_ref[0] == c)
        def _():
            for q in range(chips):
                at = 2 * q * thin
                mine_ref[pl.ds(q * thin, thin), :] = out[at + c * thin : at + (c + 1) * thin]
                theirs_ref[pl.ds(q * thin, thin), :] = out[at + (1 - c) * thin : at + (2 - c) * thin].astype(bf16)


def in_merge_kernel(info_ref, conv_mine, conv_got, gate_mine, gate_got, own_ref, *rest):
    size = len(rest)
    parts, held = rest[: size - 1], rest[size - 1]
    width = own_ref.shape[1]
    half = held.shape[0] // 2
    for mine, got, first in ((conv_mine, conv_got, 0), (gate_mine, gate_got, half)):
        for k in range(half):
            at = pl.ds(k * width, width)
            held[first + k] = mine[:, at] + got[:, at].astype(f32)
    own_ref[...] = held[info_ref[1]]
    for k, part in enumerate(parts):
        part[...] = held[info_ref[1] ^ (k + 1)].astype(bf16)


def out_merge_kernel(chips, info_ref, mine_ref, got_ref, own_ref, *rest):
    parts, held = rest[:-1], rest[-1]
    thin = own_ref.shape[0]
    for q in range(chips):
        at = pl.ds(q * thin, thin)
        held[q] = mine_ref[at, :] + got_ref[at, :].astype(f32)
    own_ref[...] = held[info_ref[2]]
    for k, part in enumerate(parts):
        part[...] = held[info_ref[2] ^ (k + 1)].astype(bf16)


def small_merge_kernel(info_ref, mine_ref, got_ref, own_ref, *parts):
    size = mine_ref.shape[0]
    for k in range(size):
        at = info_ref[1] ^ k
        total = mine_ref[at] + got_ref[at].astype(f32)
        if k == 0:
            own_ref[...] = total
        else:
            parts[k - 1][...] = total.astype(bf16)


def small_sum_kernel(info_ref, *refs):
    parts, out_ref, held = refs[:-2], refs[-2], refs[-1]
    for k, part in enumerate(parts):
        held[info_ref[2] ^ k] = part[...].astype(f32)
    total = held[0]
    for k in range(1, len(parts)):
        total = total + held[k]
    out_ref[...] = total.astype(bf16)


def unpack_kernel(edges, info_ref, rates_ref, mine_ref, other_ref, *outs):
    size = mine_ref.shape[0]
    chunk = mine_ref.shape[2]
    for c, part in ((info_ref[0], mine_ref), (1 - info_ref[0], other_ref)):
        for k in range(size):
            at = pl.ds(pl.multiple_of((c * size + (info_ref[1] ^ k)) * chunk, LANES), chunk)
            block = part[k].astype(f32)
            for n, out in enumerate(outs):
                piece = block[edges[n] : edges[n + 1]]
                out[:, at] = piece * rates_ref[:, at] if n == 2 else piece


class Group:
    def __init__(self, axis, size, stride):
        self.axis, self.size, self.stride = axis, size, stride
        self.direct = size <= 4
        self.place = (lax.axis_index(axis) // stride) % size

    def lists(self):
        n = lax.axis_size(self.axis)
        span = self.stride * self.size
        return [
            [base + low + self.stride * k for k in range(self.size)]
            for base in range(0, n, span)
            for low in range(self.stride)
        ]

    def swap(self, x, k):
        n = lax.axis_size(self.axis)
        return lax.ppermute(x, self.axis, [(i, i ^ (k * self.stride)) for i in range(n)])

    def exchange(self, blocks):
        if not self.direct:
            got = lax.all_to_all(blocks, self.axis, 0, 0, axis_index_groups=self.lists(), tiled=True)
            return [got[k] for k in range(self.size)]
        pick = lambda k: lax.dynamic_index_in_dim(blocks, self.place ^ k, 0, keepdims=False)
        return [pick(0)] + [self.swap(pick(k), k) for k in range(1, self.size)]

    def trade(self, blocks):
        if not self.direct:
            return self.exchange(jnp.stack(blocks))
        return [blocks[0]] + [self.swap(blocks[k], k) for k in range(1, self.size)]

    def gather(self, x):
        if not self.direct:
            got = lax.all_gather(x, self.axis, axis_index_groups=self.lists())
            return [got[k] for k in range(self.size)]
        return [x] + [self.swap(x, k) for k in range(1, self.size)]

    def sender(self, k):
        return self.place ^ k if self.direct else k

    def in_order(self, parts):
        if not self.direct:
            return jnp.stack(parts)
        stacked = jnp.stack(parts)
        return jnp.stack(
            [lax.dynamic_index_in_dim(stacked, self.place ^ q, 0, keepdims=False) for q in range(self.size)]
        )


def total(parts):
    return functools.reduce(lambda a, b: a + b, [part.astype(f32) for part in parts])


def body(
    tokens,
    cotangent,
    doc_starts,
    in_weight,
    conv_weight,
    conv_bias,
    xproj_weight,
    dt_weight,
    dt_bias,
    a_log,
    skip_scale,
    out_weight,
    norm_gain,
):
    length, model = tokens.shape[1:]
    inner_width, states = a_log.shape
    low_rank = dt_weight.shape[0]
    taps = conv_weight.shape[1]
    docs = doc_starts.shape[1]
    rim = taps - 1
    dp_size, seq_size = lax.axis_size("dp"), lax.axis_size("seq")
    core, outer = Group("seq", 2, 1), Group("seq", seq_size // 2, 2)
    rows_group = Group("dp", dp_size, 1)
    width = in_weight.shape[1] // (dp_size * seq_size)
    half_rows = dp_size // 2
    thin = model // (dp_size * seq_size)
    tiled = outer.direct and width % LANES == 0 and thin % EDGE == 0
    chips = outer.size if tiled else 1
    shape = jax.ShapeDtypeStruct

    base = lax.axis_index("seq") * length
    as_int = lambda *v: jnp.stack([jnp.asarray(x, jnp.int32) for x in v])
    info = jnp.concatenate([as_int(base), doc_starts[0], as_int(outer.place, core.place)])
    where = as_int(core.place, rows_group.place, outer.place)
    gain = norm_gain.astype(f32)[None]
    vec = jnp.concatenate(
        [conv_weight.T, conv_bias[None], dt_bias[None], skip_scale[None], jnp.zeros((1, inner_width), bf16)], axis=0
    ).astype(f32)
    decay_rates = -jnp.exp(a_log).T
    rates = jnp.minimum(decay_rates, -LEAST_RATE) / LN2

    left = lax.ppermute(tokens[0, length - rim :], "seq", [(i, i + 1) for i in range(seq_size - 1)])
    slim = shape((length, model // dp_size), bf16)
    tok, cot, *cot_blocks = plain_call(
        functools.partial(prepare_kernel, rim, dp_size),
        "prepare",
        [shape((length + EDGE, model), bf16), shape((length, model), bf16)] + [slim] * dp_size,
        (as_int(rows_group.place), tokens[0], left, cotangent[0]),
        2,
    )
    tok_parts = outer.gather(tok)
    cot_got = rows_group.trade(cot_blocks)

    ext, inner, gate, ggated, proj, mine, *deep = front(
        info, tok, cot, gain, vec, rates, dt_weight, in_weight, out_weight, xproj_weight, taps, docs
    )
    mine, tok_parts, cot_got = lax.optimization_barrier((mine, tok_parts, cot_got))
    other = core.swap(mine, 1)
    (chip,) = plain_call(
        functools.partial(pair_kernel, states), "pair", [shape(mine.shape, bf16)], (where, mine, other, rates), 2
    )
    spot = as_int(core.place, outer.place, -1 if outer.direct else 0)
    entry, arrive = enter(spot, mine, other, rates, outer.gather(chip))
    gated, ggate, *gate_blocks = forward(
        info, proj, dt_weight, vec, rates, entry, inner, gate, ggated, deep[0], deep[1], taps, docs, chips
    )

    def by_chip(blocks):
        if tiled:
            return outer.trade(blocks)
        (x,) = blocks
        blocks = x.reshape(x.shape[0], half_rows, outer.size, 2, width)
        return outer.exchange(blocks.transpose(2, 0, 3, 1, 4).reshape(outer.size, x.shape[0], -1))

    gate_got = by_chip(gate_blocks)
    gated_parts = rows_group.gather(gated)

    small_mine, small_theirs, ngrad, mixed, *sent = backward(
        info, proj, tok, gain, dt_weight, vec, rates, entry, arrive, inner, gate, ggated, deep, gated, ggate,
        in_weight, out_weight, ext, xproj_weight, taps, docs, chips, dp_size,
    )
    sent, small_theirs, gate_got, gated_parts = lax.optimization_barrier((sent, small_theirs, gate_got, gated_parts))
    conv_got = by_chip(sent)
    rows = small_mine.shape[1]
    chunk = shape((rows, inner_width // (2 * dp_size)), bf16)
    small_own, *small_blocks = plain_call(
        small_merge_kernel,
        "small_merge",
        [shape(chunk.shape, f32)] + [chunk] * (dp_size - 1),
        (where, small_mine, core.swap(small_theirs, 1)),
        1.5,
    )
    small = total(rows_group.trade([small_own] + small_blocks)).astype(bf16)
    if outer.direct:
        (small,) = plain_call(
            small_sum_kernel,
            "small_sum",
            [chunk],
            (where, *outer.gather(small)),
            1,
            [pltpu.VMEM((outer.size,) + chunk.shape, f32)],
        )
    else:
        small = total(outer.gather(small)).astype(bf16)
    small = jnp.stack(rows_group.gather(small))
    sizes = [low_rank + 2 * states, low_rank, states, taps, 1, 1, 1, 1]
    edges = [sum(sizes[:k]) for k in range(len(sizes) + 1)]
    parts = plain_call(
        functools.partial(unpack_kernel, edges),
        "unpack",
        [shape((size, inner_width), f32) for size in sizes],
        (where, decay_rates, small, core.swap(small, 1)),
        2,
    )

    back = lax.ppermute(ngrad[length:], "seq", [(i, i - 1) for i in range(1, seq_size)])
    tokens_grad = finish(ngrad, back, tok, cot, gain, rim)

    if tiled:
        halves = [shape((model, half_rows * width), f32), shape((model, half_rows * width), bf16)]
        turned_over, gate_mine, gate_theirs = plain_call(
            functools.partial(gate_kernel, chips),
            "gate_columns",
            [shape((model, (chips + 1) * length), bf16)] + halves,
            (where, gain, *tok_parts, *gate_got),
            4,
        )
        gate_other = core.swap(gate_theirs, 1)
        conv_mine, conv_theirs = plain_call(
            functools.partial(conv_kernel, chips), "conv_columns", halves, (where, turned_over, *conv_got), 3
        )
        slab = (model, width)
        in_own, *in_blocks = plain_call(
            in_merge_kernel,
            "in_merge",
            [shape(slab, f32)] + [shape(slab, bf16)] * (dp_size - 1),
            (where, conv_mine, core.swap(conv_theirs, 1), gate_mine, gate_other),
            2,
            [pltpu.VMEM((dp_size,) + slab, f32)],
        )
        in_share = total(rows_group.trade([in_own] + in_blocks))
        thick = (chips * thin, inner_width)
        out_mine, out_theirs = plain_call(
            functools.partial(out_kernel, dp_size, chips, thin),
            "out_columns",
            [shape(thick, f32), shape(thick, bf16)],
            (where, *cot_got, *gated_parts),
            4,
        )
        slab = (thin, inner_width)
        out_own, *out_blocks = plain_call(
            functools.partial(out_merge_kernel, chips),
            "out_merge",
            [shape(slab, f32)] + [shape(slab, bf16)] * (chips - 1),
            (where, out_mine, core.swap(out_theirs, 1)),
            2,
            [pltpu.VMEM((chips,) + slab, f32)],
        )
        out_share = total(outer.trade([out_own] + out_blocks))
    else:

        def normalised(x):
            wide = x.astype(f32)
            inv = lax.rsqrt(jnp.mean(wide * wide, axis=-1, keepdims=True) + epsilon)
            return (wide * inv * gain).astype(bf16)

        def summed(lefts, rights):
            return functools.reduce(lambda a, b: a + b, [tn(a, b) for a, b in zip(lefts, rights, strict=True)])

        def halved(x):
            return x.astype(bf16).reshape(model, 2, -1).swapaxes(0, 1)

        normed_parts = [normalised(part) for part in tok_parts]
        gate_core = total(core.exchange(halved(summed([part[:length] for part in normed_parts], gate_got))))
        conv_core = total(core.exchange(halved(summed(normed_parts, conv_got))))
        in_core = jnp.concatenate([conv_core, gate_core], axis=1).astype(bf16)
        in_share = total(rows_group.exchange(in_core.reshape(model, dp_size, width).swapaxes(0, 1)))
        out_sum = summed(cot_got, gated_parts).astype(bf16)
        out_core = total(core.exchange(out_sum.reshape(outer.size, 2, thin, inner_width).swapaxes(0, 1)))
        out_share = total(outer.exchange(out_core.astype(bf16)))

    return (
        mixed[None],
        tokens_grad[None],
        in_share,
        parts[3].T,
        parts[6][0],
        parts[0].T,
        parts[1],
        parts[4][0],
        parts[2].T,
        parts[5][0],
        out_share.T,
        parts[7][0, :model],
    )


def solution(mesh):
    whole = (P(),) * 10
    row = P("dp", "seq", None)
    columns = P(None, ("dp", "seq"))
    return jax.shard_map(
        body,
        mesh=mesh,
        in_specs=(row, row, P("dp", None)) + whole,
        out_specs=(row, row, columns) + (P(),) * 7 + (columns, P()),
        check_vma=False,
    )
```

```python
import functools

import jax
import jax.numpy as jnp
from jax import lax
from jax.experimental import pallas as pl
from jax.experimental.pallas import tpu as pltpu
from jax.sharding import PartitionSpec as P

epsilon = 1e-05
LANES = 128
SUBS = 8
FAR = 1e36
LEAST_RATE = 1e-33
LN2 = 0.6931471805599453
EDGE = 16
UNROLL = 8
bf16, f32 = jnp.bfloat16, jnp.float32
SMEM_SPEC = pl.BlockSpec(memory_space=pltpu.SMEM)


def nt(a, b):
    return lax.dot_general(a, b, (((1,), (1,)), ((), ())), preferred_element_type=f32)


def tn(a, b):
    return lax.dot_general(a, b, (((0,), (0,)), ((), ())), preferred_element_type=f32)


def nn(a, b):
    return jnp.dot(a, b, preferred_element_type=f32)


def plain_call(kernel, name, out_shape, args, us, scratch=(), limit=12):
    full = lambda x: pl.BlockSpec(x.shape, lambda: (0,) * len(x.shape))
    return pl.pallas_call(
        kernel,
        in_specs=[SMEM_SPEC] + [full(x) for x in args[1:]],
        out_specs=[full(x) for x in out_shape],
        out_shape=out_shape,
        scratch_shapes=list(scratch),
        compiler_params=pltpu.CompilerParams(vmem_limit_bytes=limit << 20),
        cost_estimate=pl.CostEstimate(flops=0, bytes_accessed=int(us * 3.6e6), transcendentals=0),
        name=name,
    )(*args)


def softplus(v):
    return jnp.maximum(v, 0.0) + jnp.log1p(jnp.exp(-jnp.abs(v)))


def tile_at(start, size=LANES):
    return pl.ds(pl.multiple_of(start, LANES), size)


def step_rows(t):
    return pl.ds(pl.multiple_of(t * SUBS, SUBS), SUBS)


def tap_masks(info_ref, docs, taps, length):
    row = lax.broadcasted_iota(jnp.int32, (length, LANES), 0)
    place = info_ref[0] + (row % SUBS) * (length // SUBS) + row // SUBS
    begin = jnp.zeros_like(place)
    reset = jnp.zeros((length, LANES), f32)
    for k in range(docs):
        start = info_ref[1 + k]
        begin = jnp.maximum(begin, jnp.where(place >= start, start, 0))
        reset = jnp.where(place == start, 1.0, reset)
    return [reset] + [jnp.where(begin <= place - j, 1.0, 0.0) for j in range(1, taps)]


def turned(x, plain):
    length = x.shape[0]
    steps = length // SUBS
    a = lax.broadcasted_iota(jnp.int32, (length, length), 1 - plain)
    b = lax.broadcasted_iota(jnp.int32, (length, length), plain + 0)
    turn = jnp.where(b == (a % steps) * SUBS + a // steps, 1.0, 0.0).astype(bf16)
    return nn(turn, x).astype(bf16)


def spread(maps, table_ref, first, width):
    high = maps.astype(bf16)
    rest = maps - high.astype(f32)
    middle = rest.astype(bf16)
    low = (rest - middle.astype(f32)).astype(bf16)
    row = lax.broadcasted_iota(jnp.int32, (LANES, width * LANES), 0)
    lane = lax.broadcasted_iota(jnp.int32, (LANES, width * LANES), 1)
    ones = jnp.where(row == first + lane // LANES, 1.0, 0.0).astype(bf16)
    table_ref[...] = nn(high, ones) + nn(middle, ones) + nn(low, ones)


def sub_scan(decay, value, forward):
    row = lax.broadcasted_iota(jnp.int32, decay.shape, 0)
    if not forward:
        row = SUBS - 1 - row

    def moved(x, by, fill):
        return jnp.where(row < by, fill, pltpu.roll(x, by if forward else SUBS - by, 0))

    by = 1
    while by < SUBS:
        d, v = moved(decay, by, 1.0), moved(value, by, 0.0)
        value = decay * v + value
        decay = decay * d
        by *= 2
    return value, moved(decay, 1, 1.0), moved(value, 1, 0.0)


def conv_windows(ext, taps, length):
    return [ext[(taps - 1 - j) * SUBS : (taps - 1 - j) * SUBS + length] for j in range(taps)]


def conv_sum(windows, masks, vec_ref, at, taps):
    out = vec_ref[pl.ds(taps, 1), at] + vec_ref[pl.ds(taps - 1, 1), at] * windows[0]
    for j in range(1, taps):
        out = out + vec_ref[pl.ds(taps - 1 - j, 1), at] * windows[j] * masks[j]
    return out


def normalise(x, gain):
    wide = x.astype(f32)
    inv = lax.rsqrt(jnp.mean(wide * wide, axis=-1, keepdims=True) + epsilon)
    return (wide * inv * gain).astype(bf16)


def front_kernel(
    states, rank, taps, docs, rows_size,
    info_ref, tok_ref, left_ref, cot_ref, gain_ref, vec_ref, rates_ref, dtw_ref, win_ref, wo_ref, wx_ref,
    tok_out, cot_out, ext_ref, inner_ref, gate_ref, ggated_ref, gs_ref, dt_ref, proj_ref, table, pack_ref,
    dx_ref, ex_ref, db_ref, fx_ref, *rest,
):
    blocks, (normed, masks, dtm_s, u_s, ends) = rest[:rows_size], rest[rows_size:]
    length, model = cot_ref.shape
    width = rates_ref.shape[1]
    steps = length // SUBS
    rim = taps - 1
    maps = rank + 2 * states

    tok_out[pl.ds(0, length), :] = turned(tok_ref[...], False)
    left = left_ref[...].astype(f32)
    tok_out[pl.ds(length, EDGE), :] = jnp.concatenate([left, jnp.zeros((EDGE - rim, model), f32)], axis=0).astype(bf16)
    cot = turned(cot_ref[...], False)
    cot_out[...] = cot
    thin = model // rows_size
    for k in range(rows_size):
        blocks[k][:, :model] = tok_out[pl.ds(0, length), :]
        for q in range(rows_size):

            @pl.when((info_ref[3 + docs] ^ k) == q)
            def _():
                blocks[k][:, model:] = cot[:, q * thin : (q + 1) * thin]

    normed[...] = normalise(tok_out[...], gain_ref[...])
    for k, mask in enumerate(tap_masks(info_ref, docs, taps, length)):
        masks[k] = mask
    proj_ref[...] = jnp.zeros_like(proj_ref)
    block = min(512, width)

    def project(j, _):
        wide = tile_at(j * block, block)
        conv = nn(normed[...], win_ref[:, wide]).astype(bf16)
        gate = nn(normed[pl.ds(0, length), :], win_ref[:, tile_at(width + j * block, block)])
        ggated = nt(cot_out[...], wo_ref[wide, :])
        gate_ref[:, wide] = gate
        ggated_ref[:, wide] = ggated
        gs_ref[:, wide] = ggated * gate * jax.nn.sigmoid(gate)
        row = lax.broadcasted_iota(jnp.int32, (SUBS, LANES), 0)
        mask = [masks[k] for k in range(taps)]
        for tile in range(block // LANES):
            far = tile_at(j * block + tile * LANES)
            part = conv[:, tile * LANES : (tile + 1) * LANES].astype(f32)
            pieces = []
            for b in range(rim):
                first = length - (rim - b) * SUBS
                moved = pltpu.roll(part[first : first + SUBS], 1, 0)
                pieces.append(jnp.where(row == 0, part[length + b : length + b + 1], moved))
            ext = jnp.concatenate(pieces + [part[:length]], axis=0)
            pad = jnp.zeros((2 * EDGE - rim * SUBS, LANES), f32)
            ext_ref[:, far] = jnp.concatenate([pad, ext], axis=0).astype(bf16)
            pre = conv_sum(conv_windows(ext, taps, length), mask, vec_ref, far, taps)
            inner_ref[:, far] = (pre * jax.nn.sigmoid(pre)).astype(bf16)
        proj_ref[:, :maps] += nt(inner_ref[:, wide], wx_ref[:, wide])
        return 0

    lax.fori_loop(0, width // block, project, 0)
    spread(proj_ref[...], table, rank, 2 * states)
    ends[...] = jnp.zeros_like(ends)
    half = states // 2
    zero = jnp.zeros((SUBS, LANES), f32)
    one = jnp.ones((SUBS, LANES), f32)
    low = proj_ref[:, :rank].astype(bf16)

    def scan(tile, _):
        at = tile_at(tile * LANES)
        dt = softplus(nn(low, dtw_ref[:, at]) + vec_ref[pl.ds(taps + 1, 1), at])
        dt_ref[:, at] = dt
        u_s[...] = dt * inner_ref[:, at].astype(f32)
        dtm = jnp.where(masks[0] > 0.0, FAR, dt)
        dtm_s[...] = dtm
        span = jnp.sum(dtm, axis=0, keepdims=True)
        high = span.astype(bf16).astype(f32)
        middle = (span - high).astype(bf16).astype(f32)
        ends[pl.ds(2 * states, 1), at] = high
        ends[pl.ds(2 * states + 1, 1), at] = middle
        ends[pl.ds(2 * states + 2, 1), at] = span - high - middle
        for first in range(0, states, half):
            rates = [jnp.broadcast_to(rates_ref[pl.ds(first + k, 1), at], (SUBS, LANES)) for k in range(half)]

            def lap(t, carry):
                h, f, p = carry
                rows = step_rows(t)
                d, u, g = dtm_s[rows, :], u_s[rows, :], gs_ref[rows, at]
                hn, fn, pn = [], [], []
                for k in range(half):
                    n = first + k
                    a = jnp.exp2(d * rates[k])
                    hn.append(a * h[k] + u * table[rows, n * LANES : (n + 1) * LANES])
                    q = p[k] * a
                    pn.append(q)
                    n += states
                    fn.append(f[k] + q * (g * table[rows, n * LANES : (n + 1) * LANES]))
                return tuple(hn), tuple(fn), tuple(pn)

            start = ((zero,) * half, (zero,) * half, (one,) * half)
            h, f, p = lax.fori_loop(0, steps, lap, start, unroll=UNROLL)
            for k in range(half):
                n = first + k
                e_in, d_ex, e_ex = sub_scan(p[k], h[k], True)
                f_in, b_ex, f_ex = sub_scan(p[k], f[k], False)
                ends[pl.ds(n, 1), at] = e_in[SUBS - 1 :, :]
                ends[pl.ds(states + n, 1), at] = f_in[:1, :]
                dx_ref[n, :, at] = d_ex
                ex_ref[n, :, at] = e_ex
                db_ref[n, :, at] = b_ex
                fx_ref[n, :, at] = f_ex
        return 0

    lax.fori_loop(0, width // LANES, scan, 0)
    pack_ref[...] = ends[...].astype(bf16)


def front(info, tok, left, cot, gain, vec, rates, dtw, in_weight, out_weight, wx, taps, docs, rows_size):
    length, model = cot.shape
    states, width = rates.shape
    rank = dtw.shape[0]
    pack_rows = 2 * states + EDGE
    shape = jax.ShapeDtypeStruct
    big = lambda dtype: shape((length, width), dtype)
    out = [
        shape((length + EDGE, model), bf16), shape((length, model), bf16), shape((length + 2 * EDGE, width), bf16),
        big(bf16), big(f32), big(f32), big(f32), big(f32),
        shape((length, LANES), f32), shape((length, 2 * states * LANES), f32), shape((pack_rows, width), bf16),
    ] + [shape((states, SUBS, width), f32)] * 4 + [shape((length, model + model // rows_size), bf16)] * rows_size
    scratch = [
        pltpu.VMEM((length + EDGE, model), bf16),
        pltpu.VMEM((taps, length, LANES), f32),
        pltpu.VMEM((length, LANES), f32),
        pltpu.VMEM((length, LANES), f32),
        pltpu.VMEM((pack_rows, width), f32),
    ]
    return plain_call(
        functools.partial(front_kernel, states, rank, taps, docs, rows_size), "front", out,
        (info, tok, left, cot, gain, vec, rates, dtw, in_weight, out_weight, wx), 18, scratch, 10,
    )


def halves_of(near, far):
    lane = lax.broadcasted_iota(jnp.int32, near.shape, 1)
    half = LANES // 2
    low = jnp.where(lane < half, near, pltpu.roll(far, half, 1))
    high = jnp.where(lane < half, pltpu.roll(near, half, 1), far)
    return low.astype(bf16), high.astype(bf16)


def forward_kernel(
    states, taps, docs, slices,
    info_ref, vec_ref, rates_ref, entry_ref, table, dt_ref, inner_ref, gate_ref, ggated_ref, dx_ref, ex_ref,
    gated_ref, ggate_ref, *rest,
):
    blocks, (reset, dtm_s, u_s, y_s, held) = rest[:slices], rest[slices:]
    length, width = inner_ref.shape
    tiles, steps = width // LANES, length // SUBS
    zero = jnp.zeros((SUBS, LANES), f32)
    reset[...] = tap_masks(info_ref, docs, 1, length)[0]

    def scan(tile, _):
        at = tile_at(tile * LANES)
        dt = dt_ref[:, at]
        x = inner_ref[:, at].astype(f32)
        dtm_s[...] = jnp.where(reset[...] > 0.0, FAR, dt)
        u_s[...] = dt * x

        def wide(ref, n):
            return jnp.broadcast_to(ref[pl.ds(n, 1), at], (SUBS, LANES))

        rates = [wide(rates_ref, n) for n in range(states)]
        start = tuple(dx_ref[n, :, at] * wide(entry_ref, n) + ex_ref[n, :, at] for n in range(states))

        def lap(t, h):
            rows = step_rows(t)
            d, u = dtm_s[rows, :], u_s[rows, :]
            new, y = [], [zero, zero]
            for n in range(states):
                now = jnp.exp2(d * rates[n]) * h[n] + u * table[rows, n * LANES : (n + 1) * LANES]
                y[n % 2] = y[n % 2] + now * table[rows, (states + n) * LANES : (states + n + 1) * LANES]
                new.append(now)
            y_s[rows, :] = y[0] + y[1]
            return tuple(new)

        lax.fori_loop(0, steps, lap, start, unroll=UNROLL)
        scanned = y_s[...] + vec_ref[pl.ds(taps + 2, 1), at] * x
        gate = gate_ref[:, at]
        sig = jax.nn.sigmoid(gate)
        gated_ref[:, at] = (scanned * gate * sig).astype(bf16)
        ggate = (ggated_ref[:, at] * scanned * (sig * (1.0 + gate * (1.0 - sig)))).astype(bf16)
        ggate_ref[:, at] = ggate
        return 0

    lax.fori_loop(0, tiles, scan, 0)
    if not slices:
        return
    for pair in range(tiles // 2):
        side, spot = pair // (tiles // 4), pair % (tiles // 4)
        near, far = (ggate_ref[:, (2 * pair + n) * LANES : (2 * pair + n + 1) * LANES].astype(f32) for n in range(2))
        at = pl.ds(spot * LANES, LANES)
        held[side, :, at], held[side + 2, :, at] = halves_of(near, far)
    for n in range(slices):
        blocks[n][:, :width] = gated_ref[...]
        blocks[n][:, width:] = held[info_ref[3 + docs] ^ n]


def forward(info, vec, rates, entry, table, dt, inner, gate, ggated, dx, ex, taps, docs, slices):
    length, width = inner.shape
    states = rates.shape[0]
    shape = jax.ShapeDtypeStruct
    return plain_call(
        functools.partial(forward_kernel, states, taps, docs, slices),
        "forward",
        [shape((length, width), bf16)] * 2 + [shape((length, width + width // max(slices, 1)), bf16)] * slices,
        (info, vec, rates, entry, table, dt, inner, gate, ggated, dx, ex),
        8,
        [pltpu.VMEM((length, LANES), f32)] * 4 + [pltpu.VMEM((max(slices, 1), length, width // max(slices, 1)), bf16)],
        8,
    )


def backward_kernel(
    states, rank, taps, docs, slices,
    info_ref, proj_ref, tok_ref, gain_ref, dtw_ref, vec_ref, rates_ref, entry_ref, arrive_ref, table,
    dt_ref, inner_ref, gs_ref, dx_ref, ex_ref, db_ref, fx_ref, ggate_ref, ext_ref, win_ref, wx_ref,
    mine_ref, theirs_ref, ngrad, *rest,
):
    blocks = rest[: max(slices, 1)]
    (acc, hs, decays, masks, dtm_s, u_s, s1_s, s2_s, isg, raw_s, sent_s, low_acc, pg, small, held) = rest[max(slices, 1) :]
    length, width = inner_ref.shape
    model = tok_ref.shape[1]
    steps, tiles = length // SUBS, width // LANES
    rim = taps - 1
    maps = rank + 2 * states
    row_dtw = maps
    row_rate = row_dtw + rank
    row_taps = row_rate + states
    row_dtb, row_skip, row_cb, row_gain = (row_taps + taps + k for k in range(4))
    zero = jnp.zeros((SUBS, LANES), f32)
    half = states // 2
    block = min(512, width)

    for k, mask in enumerate(tap_masks(info_ref, docs, taps, length)):
        masks[k] = mask
    low_acc[...] = jnp.zeros_like(low_acc)
    small[pl.ds(small.shape[0] - EDGE, EDGE), :] = jnp.zeros((EDGE, width), f32)
    low = proj_ref[:, :rank].astype(bf16)

    def clear(t, _):
        acc[step_rows(t), :] = jnp.zeros((SUBS, acc.shape[1]), f32)
        return 0

    lax.fori_loop(0, steps, clear, 0)

    def scan(tile, _):
        at = tile_at(tile * LANES)
        dt = dt_ref[:, at]
        x = inner_ref[:, at].astype(f32)
        dtm_s[...] = jnp.where(masks[0] > 0.0, FAR, dt)
        u_s[...] = dt * x

        def wide(ref, n):
            return jnp.broadcast_to(ref[pl.ds(n, 1), at], (SUBS, LANES))

        rates = [wide(rates_ref, n) for n in range(states)]
        start = []
        for n in range(states):
            h0 = dx_ref[n, :, at] * wide(entry_ref, n) + ex_ref[n, :, at]
            hs[0, n] = h0
            start.append(h0)

        def lap(t, h):
            rows = step_rows(t)
            d, u = dtm_s[rows, :], u_s[rows, :]
            new = []
            for n in range(states):
                a = jnp.exp2(d * rates[n])
                decays[t, n] = a
                now = a * h[n] + u * table[rows, n * LANES : (n + 1) * LANES]
                hs[t + 1, n] = now
                new.append(now)
            return tuple(new)

        lax.fori_loop(0, steps, lap, tuple(start), unroll=UNROLL)
        for first in range(0, states, half):
            some = rates[first : first + half]

            def back(k, carry):
                f, r = carry
                t = steps - 1 - k
                rows = step_rows(t)
                dtt, g, u = dt_ref[rows, at], gs_ref[rows, at], u_s[rows, :]
                fn, rn, s1, s2 = [], [], zero, zero
                for k in range(half):
                    n = first + k
                    into, out = (slice(m * LANES, (m + 1) * LANES) for m in (n, states + n))
                    adj = g * table[rows, out] + f[k]
                    acc[rows, into] += adj * u
                    acc[rows, out] += g * hs[t + 1, n]
                    s1 = s1 + adj * table[rows, into]
                    flow = decays[t, n] * adj
                    fn.append(flow)
                    flow = flow * hs[t, n]
                    s2 = s2 + flow * some[k]
                    rn.append(r[k] + flow * dtt)
                if first == 0:
                    s1_s[rows, :] = s1
                    s2_s[rows, :] = s2
                else:
                    s1_s[rows, :] += s1
                    s2_s[rows, :] += s2
                return tuple(fn), tuple(rn)

            f0 = tuple(
                db_ref[first + k, :, at] * wide(arrive_ref, first + k) + fx_ref[first + k, :, at] for k in range(half)
            )
            _, r = lax.fori_loop(0, steps, back, (f0, (zero,) * half), unroll=UNROLL)
            for k in range(half):
                small[pl.ds(row_rate + first + k, 1), at] = jnp.sum(r[k], axis=0, keepdims=True)
        s1, gs = s1_s[...], gs_ref[:, at]
        step_grad = s1 * x + LN2 * s2_s[...]
        isg[:, at] = s1 * dt + gs * vec_ref[pl.ds(taps + 2, 1), at]
        raw = nn(low, dtw_ref[:, at]) + vec_ref[pl.ds(taps + 1, 1), at]
        raw_grad = step_grad * jax.nn.sigmoid(raw)
        raw_s[:, at] = raw_grad.astype(bf16)
        small[pl.ds(row_dtb, 1), at] = jnp.sum(raw_grad, axis=0, keepdims=True)
        small[pl.ds(row_skip, 1), at] = jnp.sum(gs * x, axis=0, keepdims=True)
        return 0

    lax.fori_loop(0, tiles, scan, 0)

    def low_part(j, _):
        wide = tile_at(j * block, block)
        small[pl.ds(row_dtw, rank), wide] = tn(low, raw_s[:, wide])
        low_acc[:, :rank] += nt(raw_s[:, wide], dtw_ref[:, wide])
        return 0

    lax.fori_loop(0, width // block, low_part, 0)
    lane = lax.broadcasted_iota(jnp.int32, (SUBS, LANES), 1)

    def gather_maps(t, _):
        rows = step_rows(t)
        out = low_acc[rows, :]
        for n in range(2 * states):
            part = jnp.sum(acc[rows, n * LANES : (n + 1) * LANES], axis=1, keepdims=True)
            out = jnp.where(lane == rank + n, part, out)
        low_acc[rows, :] = out
        return 0

    lax.fori_loop(0, steps, gather_maps, 0)
    pg[...] = low_acc[...].astype(bf16)
    ngrad[...] = jnp.zeros_like(ngrad)

    def close(j, _):
        wide = tile_at(j * block, block)
        ngrad[pl.ds(0, length), :] += nt(ggate_ref[:, wide], win_ref[:, tile_at(width + j * block, block)])
        small[pl.ds(0, maps), wide] = tn(pg[...], inner_ref[:, wide])[:maps]
        inner_grad = isg[:, wide] + nn(pg[:, :maps], wx_ref[:, wide])
        mask = [masks[k] for k in range(taps)]
        row = lax.broadcasted_iota(jnp.int32, (SUBS, LANES), 0)
        for tile in range(block // LANES):
            far = tile_at(j * block + tile * LANES)
            ext = ext_ref[:, far].astype(f32)[2 * EDGE - rim * SUBS :]
            windows = conv_windows(ext, taps, length)
            pre = conv_sum(windows, mask, vec_ref, far, taps)
            sig = jax.nn.sigmoid(pre)
            grad = inner_grad[:, tile * LANES : (tile + 1) * LANES] * (sig * (1.0 + pre * (1.0 - sig)))
            small[pl.ds(row_cb, 1), far] = jnp.sum(grad, axis=0, keepdims=True)
            small[pl.ds(row_taps + rim, 1), far] = jnp.sum(grad * windows[0], axis=0, keepdims=True)
            near = [grad[step * SUBS : (step + 1) * SUBS] * vec_ref[pl.ds(rim, 1), far] for step in range(steps)]
            head = [zero] * rim
            for k in range(1, taps):
                masked = grad * mask[k]
                small[pl.ds(row_taps + rim - k, 1), far] = jnp.sum(masked * windows[k], axis=0, keepdims=True)
                masked = masked * vec_ref[pl.ds(rim - k, 1), far]
                for step in range(steps):
                    piece = masked[step * SUBS : (step + 1) * SUBS]
                    if step >= k:
                        near[step - k] = near[step - k] + piece
                    else:
                        head[rim + step - k] = head[rim + step - k] + piece
            edge = zero
            for b in range(rim):
                moved = jnp.where(row == SUBS - 1, 0.0, pltpu.roll(head[b], SUBS - 1, 0))
                near[steps - rim + b] = near[steps - rim + b] + moved
                edge = jnp.where(row == b, jnp.broadcast_to(head[b][:1], (SUBS, LANES)), edge)
            sent = jnp.concatenate(near + [edge, zero], axis=0)
            sent_s[:, tile * LANES : (tile + 1) * LANES] = sent.astype(bf16)
            if not slices:
                blocks[0][:, far] = sent.astype(bf16)
            elif tile % 2 == 1:
                pair = j * (block // LANES // 2) + tile // 2
                side, spot = pair // (tiles // 4), tile_at(pair % (tiles // 4) * LANES)
                held[side, :, spot], held[side + 2, :, spot] = halves_of(last, sent)
            last = sent
        ngrad[...] += nt(sent_s[...], win_ref[:, wide])
        return 0

    lax.fori_loop(0, width // block, close, 0)
    x = tok_ref[...].astype(f32)
    inv = lax.rsqrt(jnp.mean(x * x, axis=-1, keepdims=True) + epsilon)
    small[pl.ds(row_gain, 1), pl.ds(0, model)] = jnp.sum(ngrad[...] * (x * inv), axis=0, keepdims=True)
    if slices:
        part = width // slices
        row = lax.broadcasted_iota(jnp.int32, (EDGE, part), 0)
        extra = jnp.zeros((EDGE, part), f32)
        normed = x[length:] * inv[length:] * gain_ref[...]
        count = model // part
        for b in range(rim):
            for c in range(count):
                piece = jnp.broadcast_to(normed[b : b + 1, c * part : (c + 1) * part], (EDGE, part))
                extra = jnp.where(row == rim + b * count + c, piece, extra)
        edge_rows = pl.ds(length, EDGE)
        for n in range(slices):
            held[n, edge_rows, :] = (held[n, edge_rows, :].astype(f32) + extra).astype(bf16)
        for n in range(slices):
            blocks[n][...] = held[info_ref[3 + docs] ^ n]
    count, chunk = mine_ref.shape[0], mine_ref.shape[2]
    for c in range(2):

        @pl.when(info_ref[2 + docs] == c)
        def _():
            for n in range(count):
                at, other = (c * count + n) * chunk, ((1 - c) * count + n) * chunk
                mine_ref[n] = small[:, at : at + chunk]
                theirs_ref[n] = small[:, other : other + chunk].astype(bf16)


def backward(info, proj, tok, gain, dtw, vec, rates, entry, arrive, table, dt, inner, gs, deep4, ggate, ext,
             in_weight, wx, taps, docs, slices, chunks):
    length, width = inner.shape
    model = tok.shape[1]
    states = rates.shape[0]
    rank = dtw.shape[0]
    block = min(512, width)
    steps = length // SUBS
    rows = 2 * rank + 3 * states + taps + 4
    rows = -(-rows // EDGE) * EDGE
    shape = jax.ShapeDtypeStruct
    chunk = (chunks, rows, width // (2 * chunks))
    parts = max(slices, 1)
    return plain_call(
        functools.partial(backward_kernel, states, rank, taps, docs, slices),
        "backward",
        [shape(chunk, f32), shape(chunk, bf16), shape((length + EDGE, model), f32)]
        + [shape((length + EDGE, width // parts), bf16)] * parts,
        (info, proj, tok, gain, dtw, vec, rates, entry, arrive, table, dt, inner, gs, *deep4, ggate, ext, in_weight, wx),
        24,
        [
            pltpu.VMEM((length, 2 * states * LANES), f32),
            pltpu.VMEM((steps + 1, states, SUBS, LANES), f32),
            pltpu.VMEM((steps, states, SUBS, LANES), f32),
            pltpu.VMEM((taps, length, LANES), f32),
        ]
        + [pltpu.VMEM((length, LANES), f32)] * 4
        + [
            pltpu.VMEM((length, width), f32),
            pltpu.VMEM((length, width), bf16),
            pltpu.VMEM((length + EDGE, block), bf16),
            pltpu.VMEM((length, LANES), f32),
            pltpu.VMEM((length, LANES), bf16),
            pltpu.VMEM((rows, width), f32),
            pltpu.VMEM((parts, length + EDGE, width // parts), bf16),
        ],
        14,
    )


def finish_kernel(rim, info_ref, ngrad_ref, back_ref, tok_ref, cot_ref, gain_ref, gated_ref, wo_ref, grad_ref, mixed_ref):
    length = cot_ref.shape[0]
    x = tok_ref[pl.ds(0, length), :].astype(f32)
    mixed_ref[...] = turned((x + nn(gated_ref[...], wo_ref[...])).astype(bf16), True)
    inv = lax.rsqrt(jnp.mean(x * x, axis=-1, keepdims=True) + epsilon)
    scaled = x * inv
    row = lax.broadcasted_iota(jnp.int32, (SUBS, x.shape[1]), 0)
    pieces = [ngrad_ref[pl.ds(0, length - rim * SUBS), :]]
    for b in range(rim):
        late = jnp.where(row == SUBS - 1, back_ref[pl.ds(b, 1), :], 0.0)
        pieces.append(ngrad_ref[pl.ds(length - (rim - b) * SUBS, SUBS), :] + late)
    hat = jnp.concatenate(pieces, axis=0) * gain_ref[...]
    grad = cot_ref[...].astype(f32) + inv * (hat - scaled * jnp.mean(hat * scaled, axis=-1, keepdims=True))
    grad_ref[...] = turned(grad.astype(bf16), True)


def span_of(x, states):
    return x[2 * states : 2 * states + 1] + x[2 * states + 1 : 2 * states + 2] + x[2 * states + 2 : 2 * states + 3]


def span_rows(d):
    high = d.astype(bf16).astype(f32)
    middle = (d - high).astype(bf16).astype(f32)
    row = lax.broadcasted_iota(jnp.int32, (EDGE, d.shape[1]), 0)
    return jnp.where(row == 0, high, jnp.where(row == 1, middle, jnp.where(row == 2, d - high - middle, 0.0)))


def pair_parts(info_ref, mine, other, rates, states):
    first = info_ref[0] == 0
    near, far = jnp.where(first, mine, other), jnp.where(first, other, mine)
    d0, d1 = span_of(near, states), span_of(far, states)
    state = jnp.exp2(rates * d1) * near[:states] + far[:states]
    flow = near[states : 2 * states] + jnp.exp2(rates * d0) * far[states : 2 * states]
    return state, flow, span_rows(d0 + d1)


def pair_kernel(states, info_ref, mine_ref, other_ref, rates_ref, out_ref):
    state, flow, spans = pair_parts(
        info_ref, mine_ref[...].astype(f32), other_ref[...].astype(f32), rates_ref[...], states
    )
    out_ref[...] = jnp.concatenate([state, flow, spans], axis=0).astype(bf16)


def pair_half_kernel(states, info_ref, mine_ref, other_ref, rates_ref, *outs):
    half = rates_ref.shape[1] // 2
    at = tile_at(info_ref[0] * half, half)
    state, flow, spans = pair_parts(
        info_ref, mine_ref[:, at].astype(f32), other_ref[:, at].astype(f32), rates_ref[:, at], states
    )
    place = info_ref[2]
    for k, out in enumerate(outs):
        up = (place ^ (k + 1)) > place
        out[...] = jnp.concatenate([jnp.where(up, state, flow), spans], axis=0).astype(bf16)


def enter_half_kernel(states, count, info_ref, rates_ref, *rest):
    gots, (out_ref, held) = rest[: count - 1], rest[count - 1 :]
    half = rates_ref.shape[1] // 2
    rates = rates_ref[:, tile_at(info_ref[0] * half, half)]
    place = info_ref[2]
    for k, got in enumerate(gots):
        held[place ^ (k + 1)] = got[...].astype(f32)
    held[place] = jnp.zeros_like(held[0])
    entry, arrive = jnp.zeros_like(rates), jnp.zeros_like(rates)
    for k in range(count):
        x = held[k]
        whole = jnp.exp2(rates * (x[states : states + 1] + x[states + 1 : states + 2] + x[states + 2 : states + 3]))
        entry = jnp.where(k < place, whole * entry + x[:states], entry)
    for k in reversed(range(count)):
        x = held[k]
        whole = jnp.exp2(rates * (x[states : states + 1] + x[states + 1 : states + 2] + x[states + 2 : states + 3]))
        arrive = jnp.where(k > place, whole * arrive + x[:states], arrive)
    out_ref[...] = jnp.concatenate([entry, arrive], axis=0)


def enter_both_kernel(states, info_ref, other_ref, rates_ref, here_ref, there_ref, entry_ref, arrive_ref):
    core = info_ref[0]
    half = rates_ref.shape[1] // 2
    for part, side in ((here_ref, core), (there_ref, 1 - core)):
        at = tile_at(side * half, half)
        other = other_ref[:, at].astype(f32)
        whole = jnp.exp2(rates_ref[:, at] * span_of(other, states))
        entry, arrive = part[pl.ds(0, states), :], part[pl.ds(states, states), :]
        entry_ref[:, at] = jnp.where(core == 1, whole * entry + other[:states], entry)
        arrive_ref[:, at] = jnp.where(core == 0, whole * arrive + other[states : 2 * states], arrive)


def enter_kernel(states, count, info_ref, other_ref, rates_ref, chips_ref, entry_ref, arrive_ref):
    core, place = info_ref[0], info_ref[2]
    rates = rates_ref[...]

    def split(x):
        return x[:states], x[states : 2 * states], jnp.exp2(rates * span_of(x, states))

    def lap(k, carry):
        entry, arrive = carry
        s, _, whole = split(chips_ref[k].astype(f32))
        entry = jnp.where(k < place, whole * entry + s, entry)
        back = count - 1 - k
        _, f, whole = split(chips_ref[back].astype(f32))
        arrive = jnp.where(back > place, whole * arrive + f, arrive)
        return entry, arrive

    entry, arrive = lax.fori_loop(0, count, lap, (jnp.zeros_like(rates), jnp.zeros_like(rates)))
    s, f, whole = split(other_ref[...].astype(f32))
    entry_ref[...] = jnp.where(core == 1, whole * entry + s, entry)
    arrive_ref[...] = jnp.where(core == 0, whole * arrive + f, arrive)


def gate_out_kernel(size, chips, thin, info_ref, gain_ref, *rest):
    early, late, (normed_ref, mine_ref, theirs_ref) = rest[:size], rest[size : 2 * size], rest[2 * size :]
    model = gain_ref.shape[1]
    length = early[0].shape[0]
    width = late[0].shape[1] * size // (size + 1)
    for k in range(size):
        normed_ref[pl.ds(k * length, length), :] = normalise(early[k][:, :model], gain_ref[...])
    gate = tn(jnp.concatenate([x[:, width:] for x in late], axis=0), normed_ref[...])
    left = jnp.concatenate([x[:, model:] for x in early], axis=0)
    out = tn(left, jnp.concatenate([x[:, :width] for x in late], axis=0))
    half = LANES // 2
    for c in range(2):

        @pl.when(info_ref[0] == c)
        def _():
            for q in range(chips):
                for ref, side in ((mine_ref, c), (theirs_ref, 1 - c)):
                    at = q * LANES + side * half
                    ref[q, pl.ds(0, half), :] = gate[at : at + half].astype(ref.dtype)
                    at = (2 * q + side) * thin
                    for n in range(width // model):
                        piece = out[at : at + thin, n * model : (n + 1) * model]
                        ref[q, pl.ds(half + n * thin, thin), :] = piece.astype(ref.dtype)


def conv_kernel(size, chips, rim, info_ref, normed_ref, *rest):
    gots, (mine_ref, theirs_ref) = rest[:size], rest[size:]
    length, wide = gots[0].shape[0] - EDGE, gots[0].shape[1]
    model = normed_ref.shape[1]
    pieces = model // wide
    got = jnp.concatenate([got[pl.ds(0, length), :] for got in gots], axis=0)
    lefts, rights = [], []
    for k in range(size):
        edge = gots[k][pl.ds(length, EDGE), :].astype(f32)
        row = lax.broadcasted_iota(jnp.int32, (SUBS, model), 0)
        left = jnp.zeros((SUBS, model), f32)
        for b in range(rim):
            at = rim + b * pieces
            one = jnp.concatenate([edge[at + c : at + c + 1] for c in range(pieces)], axis=1)
            left = jnp.where(row == b, jnp.broadcast_to(one, left.shape), left)
        lefts.append(left)
        right = edge[:SUBS]
        rights.append(jnp.where(lax.broadcasted_iota(jnp.int32, right.shape, 0) < rim, right, 0.0))
    left, right = (jnp.concatenate(x, axis=0).astype(bf16) for x in (lefts, rights))
    conv = tn(got, normed_ref[...]) + tn(right, left)
    half = LANES // 2
    for c in range(2):

        @pl.when(info_ref[0] == c)
        def _():
            for q in range(chips):
                at = q * LANES
                mine_ref[q] = conv[at + c * half : at + (c + 1) * half]
                theirs_ref[q] = conv[at + (1 - c) * half : at + (2 - c) * half].astype(bf16)


def halve_kernel(which, bit, info_ref, mine_ref, got_ref, keep_ref, send_ref):
    place = (info_ref[which] >> bit) & 1
    for n in range(mine_ref.shape[0] // 2):
        stay, leave = 2 * n + place, 2 * n + 1 - place
        keep_ref[n] = mine_ref[stay] + got_ref[stay].astype(f32)
        send_ref[n] = (mine_ref[leave] + got_ref[leave].astype(f32)).astype(bf16)


def go_last_kernel(thin, info_ref, mine_ref, got_ref, gate_ref, out_ref):
    half, model = gate_ref.shape
    both = mine_ref[0] + got_ref[0].astype(f32)
    gate_ref[...] = both[:half]
    for n in range(out_ref.shape[1] // model):
        out_ref[:, n * model : (n + 1) * model] = both[half + n * thin : half + (n + 1) * thin]


def cross_kernel(info_ref, mine_ref, got_ref, gate_ref, keep_ref, send_ref):
    conv = mine_ref[0] + got_ref[0].astype(f32)
    first = info_ref[1] < 2
    keep_ref[...] = jnp.where(first, conv, gate_ref[...])
    send_ref[...] = jnp.where(first, gate_ref[...], conv).astype(bf16)


def in_last_kernel(info_ref, keep_ref, got_ref, out_ref):
    keep, got = keep_ref[...], got_ref[...].astype(f32)
    first = info_ref[1] < 2
    both = jnp.concatenate([jnp.where(first, keep, got), jnp.where(first, got, keep)], axis=0)
    out_ref[...] = both.T


def add_kernel(info_ref, mine_ref, got_ref, out_ref):
    mine = mine_ref[...].reshape(out_ref.shape).astype(bf16).astype(f32)
    out_ref[...] = (mine + got_ref[...].reshape(out_ref.shape).astype(f32)).astype(bf16)


def join_kernel(which, bit, info_ref, mine_ref, got_ref, out_ref):
    place = (info_ref[which] >> bit) & 1
    for n in range(mine_ref.shape[0]):
        out_ref[2 * n + place] = mine_ref[n]
        out_ref[2 * n + 1 - place] = got_ref[n]


def unpack_kernel(edges, info_ref, rates_ref, mine_ref, other_ref, *outs):
    size, chunk = mine_ref.shape[0], mine_ref.shape[2]
    for c, part in ((info_ref[0], mine_ref), (1 - info_ref[0], other_ref)):
        for k in range(size):
            at = tile_at((c * size + k) * chunk, chunk)
            block = part[k].astype(f32)
            for n, out in enumerate(outs):
                piece = block[edges[n] : edges[n + 1]]
                out[:, at] = piece * rates_ref[:, at] if n == 2 else piece


class Group:
    def __init__(self, axis, size, stride):
        self.axis, self.size, self.stride = axis, size, stride
        self.direct = size <= 4
        self.place = (lax.axis_index(axis) // stride) % size

    def lists(self):
        n = lax.axis_size(self.axis)
        span = self.stride * self.size
        return [
            [base + low + self.stride * k for k in range(self.size)]
            for base in range(0, n, span)
            for low in range(self.stride)
        ]

    def swap(self, x, k):
        n = lax.axis_size(self.axis)
        return lax.ppermute(x, self.axis, [(i, i ^ (k * self.stride)) for i in range(n)])

    def exchange(self, blocks):
        if not self.direct:
            got = lax.all_to_all(blocks, self.axis, 0, 0, axis_index_groups=self.lists(), tiled=True)
            return [got[k] for k in range(self.size)]
        pick = lambda k: lax.dynamic_index_in_dim(blocks, self.place ^ k, 0, keepdims=False)
        return [pick(0)] + [self.swap(pick(k), k) for k in range(1, self.size)]

    def trade(self, blocks):
        if not self.direct:
            return self.exchange(jnp.stack(blocks))
        return [blocks[0]] + [self.swap(blocks[k], k) for k in range(1, self.size)]

    def gather(self, x):
        if not self.direct:
            got = lax.all_gather(x, self.axis, axis_index_groups=self.lists())
            return [got[k] for k in range(self.size)]
        return [x] + [self.swap(x, k) for k in range(1, self.size)]

    def sender(self, k):
        return self.place ^ k if self.direct else k

    def in_order(self, parts):
        if not self.direct:
            return jnp.stack(parts)
        stacked = jnp.stack(parts)
        return jnp.stack(
            [lax.dynamic_index_in_dim(stacked, self.place ^ q, 0, keepdims=False) for q in range(self.size)]
        )


def total(parts):
    return functools.reduce(lambda a, b: a + b, [part.astype(f32) for part in parts])


def body(
    tokens,
    cotangent,
    doc_starts,
    in_weight,
    conv_weight,
    conv_bias,
    xproj_weight,
    dt_weight,
    dt_bias,
    a_log,
    skip_scale,
    out_weight,
    norm_gain,
):
    length, model = tokens.shape[1:]
    inner_width, states = a_log.shape
    low_rank = dt_weight.shape[0]
    taps = conv_weight.shape[1]
    docs = doc_starts.shape[1]
    rim = taps - 1
    dp_size, seq_size = lax.axis_size("dp"), lax.axis_size("seq")
    core, outer = Group("seq", 2, 1), Group("seq", seq_size // 2, 2)
    rows_group = Group("dp", dp_size, 1)
    width = in_weight.shape[1] // (dp_size * seq_size)
    half_rows = dp_size // 2
    thin = model // (dp_size * seq_size)
    part = inner_width // dp_size
    tiled = outer.size == 4 and dp_size == 4 and width == LANES and thin % EDGE == 0
    tiled = tiled and model % part == 0 and rim * (1 + model // part) <= EDGE
    chips, slices = outer.size, dp_size if tiled else 0
    shape = jax.ShapeDtypeStruct

    base = lax.axis_index("seq") * length
    as_int = lambda *v: jnp.stack([jnp.asarray(x, jnp.int32) for x in v])
    info = jnp.concatenate([as_int(base), doc_starts[0], as_int(outer.place, core.place, rows_group.place)])
    where = as_int(core.place, rows_group.place, outer.place)
    gain = norm_gain.astype(f32)[None]
    vec = jnp.concatenate(
        [conv_weight.T, conv_bias[None], dt_bias[None], skip_scale[None], jnp.zeros((1, inner_width), bf16)], axis=0
    ).astype(f32)
    decay_rates = -jnp.exp(a_log).T
    rates = jnp.minimum(decay_rates, -LEAST_RATE) / LN2

    left = lax.ppermute(tokens[0, length - rim :], "seq", [(i, i + 1) for i in range(seq_size - 1)])
    wx = xproj_weight.T
    tok, cot, ext, inner, gate, ggated, gs, dt, proj, table, mine, dx, ex, db, fx, *early = front(
        info, tokens[0], left, cotangent[0], gain, vec, rates, dt_weight, in_weight, out_weight, wx, taps, docs, dp_size
    )
    other = core.swap(mine, 1)
    half = shape((states + EDGE, inner_width // 2), bf16)
    entering = [shape(rates.shape, f32)] * 2
    if tiled:
        to_chips = plain_call(
            functools.partial(pair_half_kernel, states), "pair", [half] * (chips - 1), (where, mine, other, rates), 2
        )
        gots = [outer.swap(x, k + 1) for k, x in enumerate(to_chips)]
        (here,) = plain_call(
            functools.partial(enter_half_kernel, states, chips),
            "enter_half",
            [shape((2 * states, inner_width // 2), f32)],
            (where, rates, *gots),
            1,
            [pltpu.VMEM((chips, states + EDGE, inner_width // 2), f32)],
        )
        entry, arrive = plain_call(
            functools.partial(enter_both_kernel, states), "enter", entering, (where, other, rates, here, core.swap(here, 1)), 1
        )
    else:
        (chip,) = plain_call(
            functools.partial(pair_kernel, states), "pair", [shape(mine.shape, bf16)], (where, mine, other, rates), 2
        )
        got = outer.in_order(outer.gather(chip))
        entry, arrive = plain_call(
            functools.partial(enter_kernel, states, outer.size), "enter", entering, (where, other, rates, got), 2
        )
    early = rows_group.trade(early)
    if tiled:
        entry, early = lax.optimization_barrier((entry, early))
    gated, ggate, *late = forward(info, vec, rates, entry, table, dt, inner, gate, ggated, dx, ex, taps, docs, slices)
    late = rows_group.trade(late) if tiled else rows_group.gather(gated)
    small_mine, small_theirs, ngrad, *sent = backward(
        info, proj, tok, gain, dt_weight, vec, rates, entry, arrive, table, dt, inner, gs, (dx, ex, db, fx), ggate, ext,
        in_weight, wx, taps, docs, slices, dp_size,
    )
    sent, small_theirs, late = lax.optimization_barrier((sent, small_theirs, late))
    rows, chunk = small_mine.shape[1:]

    def call(kernel, name, outs, args, us=1, scratch=()):
        return plain_call(kernel, name, [shape(*x) for x in outs], (where, *args), us, scratch)

    def halve(group, bit, which, mine, got, name):
        count, *rest = mine.shape
        outs = [((count // 2, *rest), f32), ((count // 2, *rest), bf16)]
        keep, send = call(functools.partial(halve_kernel, which, bit), name, outs, (mine, got))
        return keep, group.swap(send, 1 << bit)

    conv_got = rows_group.trade(sent) if tiled else None
    small_got = core.swap(small_theirs, 1)
    small, got = halve(rows_group, 0, 1, small_mine, small_got, "small_row0")
    small, got = halve(rows_group, 1, 1, small, got, "small_row1")
    one = ((1, rows, chunk), bf16)
    (small,) = call(add_kernel, "small_add", [one], (small, got))
    if tiled:
        (small,) = call(add_kernel, "small_chip0", [one], (small, outer.swap(small, 1)))
        (small,) = call(add_kernel, "small_chip1", [one], (small, outer.swap(small, 2)))
    else:
        small = total(outer.gather(small)).astype(bf16)
    join = lambda bit, x, got, name: call(
        functools.partial(join_kernel, 1, bit), name, [((2 * x.shape[0], rows, chunk), bf16)], (x, got)
    )[0]
    small = join(1, small, rows_group.swap(small, 2), "small_join1")
    small = join(0, small, rows_group.swap(small, 1), "small_join0")
    sizes = [low_rank + 2 * states, low_rank, states, taps, 1, 1, 1, 1]
    edges = [sum(sizes[:k]) for k in range(len(sizes) + 1)]
    parts = call(
        functools.partial(unpack_kernel, edges),
        "unpack",
        [((size, inner_width), f32) for size in sizes],
        (decay_rates, small, core.swap(small, 1)),
        2,
    )

    back = lax.ppermute(ngrad[length:], "seq", [(i, i - 1) for i in range(1, seq_size)])
    tokens_grad, mixed = plain_call(
        functools.partial(finish_kernel, rim),
        "finish",
        [shape((length, model), bf16)] * 2,
        (where, ngrad, back, tok, cot, gain, gated, out_weight),
        3,
    )

    if tiled:
        block = (chips, LANES, model)
        normed, go_mine, go_theirs = call(
            functools.partial(gate_out_kernel, dp_size, chips, thin),
            "gate_out_columns",
            [((dp_size * length, model), bf16), (block, f32), (block, bf16)],
            (gain, *early, *late),
            5,
        )
        go, got = halve(outer, 0, 2, go_mine, core.swap(go_theirs, 1), "go_chip0")
        go, got = halve(outer, 1, 2, go, got, "go_chip1")
        half = LANES // 2
        gate_slice, out_share = call(
            functools.partial(go_last_kernel, thin),
            "go_last",
            [((half, model), f32), ((thin, inner_width), f32)],
            (go, got),
        )
        block = (chips, half, model)
        conv_mine, conv_theirs = call(
            functools.partial(conv_kernel, dp_size, chips, rim),
            "conv_columns",
            [(block, f32), (block, bf16)],
            (normed, *conv_got),
            3,
        )
        conv, got = halve(outer, 0, 2, conv_mine, core.swap(conv_theirs, 1), "conv_chip0")
        conv, got = halve(outer, 1, 2, conv, got, "conv_chip1")
        keep, send = call(cross_kernel, "cross", [((half, model), f32), ((half, model), bf16)], (conv, got, gate_slice))
        (in_share,) = call(in_last_kernel, "in_last", [((model, width), f32)], (keep, rows_group.swap(send, 2)))
    else:

        def normalised(x):
            wide = x.astype(f32)
            inv = lax.rsqrt(jnp.mean(wide * wide, axis=-1, keepdims=True) + epsilon)
            return (wide * inv * gain).astype(bf16)

        def summed(lefts, rights):
            return functools.reduce(lambda a, b: a + b, [tn(a, b) for a, b in zip(lefts, rights, strict=True)])

        def halved(x):
            return x.astype(bf16).reshape(model, 2, -1).swapaxes(0, 1)

        def by_chip(x):
            blocks = x.reshape(x.shape[0], half_rows, outer.size, 2, width)
            return outer.exchange(blocks.transpose(2, 0, 3, 1, 4).reshape(outer.size, x.shape[0], -1))

        normed_parts = [normalised(x) for x in outer.gather(tok)]
        gate_core = total(core.exchange(halved(summed([x[:length] for x in normed_parts], by_chip(ggate)))))
        conv_core = total(core.exchange(halved(summed(normed_parts, by_chip(sent[0])))))
        in_core = jnp.concatenate([conv_core, gate_core], axis=1).astype(bf16)
        in_share = total(rows_group.exchange(in_core.reshape(model, dp_size, width).swapaxes(0, 1)))
        out_sum = summed([x[:, model:] for x in early], late).astype(bf16)
        out_core = total(core.exchange(out_sum.reshape(outer.size, 2, thin, inner_width).swapaxes(0, 1)))
        out_share = total(outer.exchange(out_core.astype(bf16)))

    return (
        mixed[None],
        tokens_grad[None],
        in_share,
        parts[3].T,
        parts[6][0],
        parts[0].T,
        parts[1],
        parts[4][0],
        parts[2].T,
        parts[5][0],
        out_share.T,
        parts[7][0, :model],
    )


def solution(mesh):
    whole = (P(),) * 10
    row = P("dp", "seq", None)
    columns = P(None, ("dp", "seq"))
    return jax.shard_map(
        body,
        mesh=mesh,
        in_specs=(row, row, P("dp", None)) + whole,
        out_specs=(row, row, columns) + (P(),) * 7 + (columns, P()),
        check_vma=False,
    )
```

```python
import functools

import jax
import jax.numpy as jnp
from jax import lax
from jax.experimental import pallas as pl
from jax.experimental.pallas import tpu as pltpu
from jax.sharding import PartitionSpec as P

epsilon = 1e-05
LANES = 128
SUBS = 8
FAR = 1e36
LEAST_RATE = 1e-33
LN2 = 0.6931471805599453
EDGE = 16
UNROLL = 8
bf16, f32 = jnp.bfloat16, jnp.float32


def nt(a, b):
    return lax.dot_general(a, b, (((1,), (1,)), ((), ())), preferred_element_type=f32)


def tn(a, b):
    return lax.dot_general(a, b, (((0,), (0,)), ((), ())), preferred_element_type=f32)


def nn(a, b):
    return jnp.dot(a, b, preferred_element_type=f32)


ANY_SPEC = pl.BlockSpec(memory_space=pltpu.HBM)


class Here:
    def __getitem__(self, which):
        if which == 1:
            return lax.axis_index("dp")
        seq = lax.axis_index("seq")
        return seq % 2 if which == 0 else seq // 2


def plain_call(kernel, name, out_shape, args, us, scratch=(), limit=12, specs=None):
    specs = specs or []
    full = lambda x: pl.BlockSpec(x.shape, lambda: (0,) * len(x.shape))
    stay = lambda n, x: pltpu.with_memory_space_constraint(x, pltpu.HBM) if specs[n : n + 1] == [ANY_SPEC] else x
    args = [stay(n, x) for n, x in enumerate(args)]
    return pl.pallas_call(
        lambda *refs: kernel(Here(), *refs),
        in_specs=list(specs) + [full(x) for x in args[len(specs) :]],
        out_specs=[full(x) for x in out_shape],
        out_shape=out_shape,
        scratch_shapes=list(scratch),
        compiler_params=pltpu.CompilerParams(vmem_limit_bytes=limit << 20),
        cost_estimate=pl.CostEstimate(flops=int(us * 1e6), bytes_accessed=0, transcendentals=0),
        name=name,
    )(*args)


def softplus(v):
    return jnp.maximum(v, 0.0) + jnp.log1p(jnp.exp(-jnp.abs(v)))


def tile_at(start, size=LANES):
    return pl.ds(pl.multiple_of(start, LANES), size)


def step_rows(t):
    return pl.ds(pl.multiple_of(t * SUBS, SUBS), SUBS)


def tap_masks(starts_ref, taps, length):
    row = lax.broadcasted_iota(jnp.int32, (length, LANES), 0)
    place = lax.axis_index("seq") * length + (row % SUBS) * (length // SUBS) + row // SUBS
    begin = jnp.zeros_like(place)
    reset = jnp.zeros((length, LANES), f32)
    for k in range(starts_ref.shape[1]):
        start = starts_ref[0, k]
        begin = jnp.maximum(begin, jnp.where(place >= start, start, 0))
        reset = jnp.where(place == start, 1.0, reset)
    return [reset] + [jnp.where(begin <= place - j, 1.0, 0.0) for j in range(1, taps)]


def turned(x, plain):
    length = x.shape[0]
    steps = length // SUBS
    a = lax.broadcasted_iota(jnp.int32, (length, length), 1 - plain)
    b = lax.broadcasted_iota(jnp.int32, (length, length), plain + 0)
    turn = jnp.where(b == (a % steps) * SUBS + a // steps, 1.0, 0.0).astype(bf16)
    return nn(turn, x).astype(bf16)


def spread(maps, table_ref, first, width):
    high = maps.astype(bf16)
    rest = maps - high.astype(f32)
    middle = rest.astype(bf16)
    low = (rest - middle.astype(f32)).astype(bf16)
    row = lax.broadcasted_iota(jnp.int32, (LANES, width * LANES), 0)
    lane = lax.broadcasted_iota(jnp.int32, (LANES, width * LANES), 1)
    ones = jnp.where(row == first + lane // LANES, 1.0, 0.0).astype(bf16)
    table_ref[...] = nn(high, ones) + nn(middle, ones) + nn(low, ones)


def sub_scan(decay, value, forward):
    row = lax.broadcasted_iota(jnp.int32, decay.shape, 0)
    if not forward:
        row = SUBS - 1 - row

    def moved(x, by, fill):
        return jnp.where(row < by, fill, pltpu.roll(x, by if forward else SUBS - by, 0))

    by = 1
    while by < SUBS:
        d, v = moved(decay, by, 1.0), moved(value, by, 0.0)
        value = decay * v + value
        decay = decay * d
        by *= 2
    return value, moved(decay, 1, 1.0), moved(value, 1, 0.0)


def conv_windows(ext, taps, length):
    return [ext[(taps - 1 - j) * SUBS : (taps - 1 - j) * SUBS + length] for j in range(taps)]


def conv_sum(windows, masks, vec_ref, at, taps):
    out = vec_ref[pl.ds(taps, 1), at] + vec_ref[pl.ds(taps - 1, 1), at] * windows[0]
    for j in range(1, taps):
        out = out + vec_ref[pl.ds(taps - 1 - j, 1), at] * windows[j] * masks[j]
    return out


def normalise(x, gain):
    wide = x.astype(f32)
    inv = lax.rsqrt(jnp.mean(wide * wide, axis=-1, keepdims=True) + epsilon)
    return (wide * inv * gain).astype(bf16)


def front_kernel(
    states, rank, taps, rows_size,
    here, starts_hbm, tok_hbm, cot_hbm, gain_hbm, convw_hbm, convb_hbm, dtb_hbm, skip_hbm, alog_hbm, dtw_hbm, wx_hbm,
    win_hbm, wo_hbm, left_ref,
    tok_out, cot_out, ext_ref, inner_ref, gate_ref, ggated_ref, gs_ref, dt_ref, proj_ref, table, pack_ref,
    dx_ref, ex_ref, db_ref, fx_ref, vec_ref, rates_ref, gain_ref, masks, *rest,
):
    blocks = rest[:rows_size]
    (normed, dtm_s, u_s, ends, starts_ref, tok_ref, cot_ref, gain_s, convw_s, convb_s, dtb_s, skip_s, alog_s, dtw_ref, wx_ref,
     win_ref, wo_ref, sems, wide_sems) = rest[rows_size:]
    length, model = cot_ref.shape
    width = rates_ref.shape[1]
    steps = length // SUBS
    rim = taps - 1
    maps = rank + 2 * states
    block = min(512, width)
    pairs = (
        (tok_hbm.at[0], tok_ref), (gain_hbm, gain_s), (cot_hbm.at[0], cot_ref), (convw_hbm, convw_s),
        (convb_hbm, convb_s), (dtb_hbm, dtb_s), (skip_hbm, skip_s), (alog_hbm, alog_s), (wx_hbm, wx_ref),
        (dtw_hbm, dtw_ref), (starts_hbm, starts_ref),
    )
    loads = [pltpu.make_async_copy(a, b, sems.at[n]) for n, (a, b) in enumerate(pairs)]

    def weights(j):
        conv = tile_at(j * block, block)
        gate = tile_at(width + j * block, block)
        return [
            pltpu.make_async_copy(win_hbm.at[:, conv], win_ref.at[:, conv], wide_sems.at[0, j]),
            pltpu.make_async_copy(win_hbm.at[:, gate], win_ref.at[:, gate], wide_sems.at[1, j]),
            pltpu.make_async_copy(wo_hbm.at[conv, :], wo_ref.at[conv, :], wide_sems.at[2, j]),
        ]

    for load in loads:
        load.start()
    for j in range(width // block):
        for load in weights(j):
            load.start()
    for load in loads[:2]:
        load.wait()
    gain_ref[...] = gain_s[...].astype(f32).reshape(1, model)
    tok_out[pl.ds(0, length), :] = turned(tok_ref[...], False)
    left = left_ref[...].astype(f32)
    tok_out[pl.ds(length, EDGE), :] = jnp.concatenate([left, jnp.zeros((EDGE - rim, model), f32)], axis=0).astype(bf16)
    for load in loads[2:]:
        load.wait()
    vec_ref[pl.ds(0, taps), :] = convw_s[...].astype(f32)
    for n, ref in enumerate((convb_s, dtb_s, skip_s)):
        vec_ref[pl.ds(taps + n, 1), :] = ref[...].astype(f32).reshape(1, width)
    rates_ref[...] = jnp.minimum(-jnp.exp(alog_s[...]), -LEAST_RATE) * (1.0 / LN2)
    cot = turned(cot_ref[...], False)
    cot_out[...] = cot
    thin = model // rows_size
    for k in range(rows_size):
        blocks[k][:, :model] = tok_out[pl.ds(0, length), :]
        for q in range(rows_size):

            @pl.when((here[1] ^ k) == q)
            def _():
                blocks[k][:, model:] = cot[:, q * thin : (q + 1) * thin]

    normed[...] = normalise(tok_out[...], gain_ref[...])
    for k, mask in enumerate(tap_masks(starts_ref, taps, length)):
        masks[k] = mask
    proj_ref[...] = jnp.zeros_like(proj_ref)

    def project(j, _):
        wide = tile_at(j * block, block)
        for load in weights(j):
            load.wait()
        conv = nn(normed[...], win_ref[:, wide]).astype(bf16)
        gate = nn(normed[pl.ds(0, length), :], win_ref[:, tile_at(width + j * block, block)])
        ggated = nt(cot_out[...], wo_ref[wide, :])
        gate_ref[:, wide] = gate
        ggated_ref[:, wide] = ggated
        gs_ref[:, wide] = ggated * gate * jax.nn.sigmoid(gate)
        row = lax.broadcasted_iota(jnp.int32, (SUBS, LANES), 0)
        mask = [masks[k] for k in range(taps)]
        for tile in range(block // LANES):
            far = tile_at(j * block + tile * LANES)
            part = conv[:, tile * LANES : (tile + 1) * LANES].astype(f32)
            pieces = []
            for b in range(rim):
                first = length - (rim - b) * SUBS
                moved = pltpu.roll(part[first : first + SUBS], 1, 0)
                pieces.append(jnp.where(row == 0, part[length + b : length + b + 1], moved))
            ext = jnp.concatenate(pieces + [part[:length]], axis=0)
            pad = jnp.zeros((2 * EDGE - rim * SUBS, LANES), f32)
            ext_ref[:, far] = jnp.concatenate([pad, ext], axis=0).astype(bf16)
            pre = conv_sum(conv_windows(ext, taps, length), mask, vec_ref, far, taps)
            inner_ref[:, far] = (pre * jax.nn.sigmoid(pre)).astype(bf16)
        proj_ref[:, :maps] += nt(inner_ref[:, wide], wx_ref[:, wide])
        return 0

    lax.fori_loop(0, width // block, project, 0)
    spread(proj_ref[...], table, rank, 2 * states)
    ends[...] = jnp.zeros_like(ends)
    half = states // 2
    zero = jnp.zeros((SUBS, LANES), f32)
    one = jnp.ones((SUBS, LANES), f32)
    low = proj_ref[:, :rank].astype(bf16)

    def scan(tile, _):
        at = tile_at(tile * LANES)
        dt = softplus(nn(low, dtw_ref[:, at]) + vec_ref[pl.ds(taps + 1, 1), at])
        dt_ref[:, at] = dt
        u_s[...] = dt * inner_ref[:, at].astype(f32)
        dtm = jnp.where(masks[0] > 0.0, FAR, dt)
        dtm_s[...] = dtm
        span = jnp.sum(dtm, axis=0, keepdims=True)
        high = span.astype(bf16).astype(f32)
        middle = (span - high).astype(bf16).astype(f32)
        ends[pl.ds(2 * states, 1), at] = high
        ends[pl.ds(2 * states + 1, 1), at] = middle
        ends[pl.ds(2 * states + 2, 1), at] = span - high - middle
        for first in range(0, states, half):
            rates = [jnp.broadcast_to(rates_ref[pl.ds(first + k, 1), at], (SUBS, LANES)) for k in range(half)]

            def lap(t, carry):
                h, f, p = carry
                rows = step_rows(t)
                d, u, g = dtm_s[rows, :], u_s[rows, :], gs_ref[rows, at]
                hn, fn, pn = [], [], []
                for k in range(half):
                    n = first + k
                    a = jnp.exp2(d * rates[k])
                    hn.append(a * h[k] + u * table[rows, n * LANES : (n + 1) * LANES])
                    q = p[k] * a
                    pn.append(q)
                    n += states
                    fn.append(f[k] + q * (g * table[rows, n * LANES : (n + 1) * LANES]))
                return tuple(hn), tuple(fn), tuple(pn)

            start = ((zero,) * half, (zero,) * half, (one,) * half)
            h, f, p = lax.fori_loop(0, steps, lap, start, unroll=UNROLL)
            for k in range(half):
                n = first + k
                e_in, d_ex, e_ex = sub_scan(p[k], h[k], True)
                f_in, b_ex, f_ex = sub_scan(p[k], f[k], False)
                ends[pl.ds(n, 1), at] = e_in[SUBS - 1 :, :]
                ends[pl.ds(states + n, 1), at] = f_in[:1, :]
                dx_ref[n, :, at] = d_ex
                ex_ref[n, :, at] = e_ex
                db_ref[n, :, at] = b_ex
                fx_ref[n, :, at] = f_ex
        return 0

    lax.fori_loop(0, width // LANES, scan, 0)
    pack_ref[...] = ends[...].astype(bf16)


def front(starts, tok, cot, gain, convw, convb, dtb, skip, alog, dtw, wx, in_weight, out_weight, left, rows_size):
    length, model = cot.shape[1:]
    states, width = alog.shape
    rank, taps = dtw.shape[0], convw.shape[0]
    pack_rows = 2 * states + EDGE
    shape = jax.ShapeDtypeStruct
    big = lambda dtype: shape((length, width), dtype)
    out = [
        shape((length + EDGE, model), bf16), shape((length, model), bf16), shape((length + 2 * EDGE, width), bf16),
        big(bf16), big(f32), big(f32), big(f32), big(f32),
        shape((length, LANES), f32), shape((length, 2 * states * LANES), f32), shape((pack_rows, width), bf16),
    ] + [shape((states, SUBS, width), f32)] * 4 + [
        shape((taps + 4, width), f32), shape((states, width), f32), shape((1, model), f32),
        shape((taps, length, LANES), f32),
    ] + [shape((length, model + model // rows_size), bf16)] * rows_size
    args = (starts, tok, cot, gain, convw, convb, dtb, skip, alog, dtw, wx, in_weight, out_weight, left)
    scratch = [
        pltpu.VMEM((length + EDGE, model), bf16),
        pltpu.VMEM((length, LANES), f32),
        pltpu.VMEM((length, LANES), f32),
        pltpu.VMEM((pack_rows, width), f32),
        pltpu.SMEM(starts.shape, jnp.int32),
        pltpu.VMEM((length, model), bf16),
        pltpu.VMEM((length, model), bf16),
    ] + [pltpu.VMEM(x.shape, x.dtype) for x in args[3:13]]
    scratch += [pltpu.SemaphoreType.DMA((11,)), pltpu.SemaphoreType.DMA((3, width // min(512, width)))]
    return plain_call(
        functools.partial(front_kernel, states, rank, taps, rows_size), "front", out,
        args, 20, scratch, 24, [ANY_SPEC] * 13,
    )


def halves_of(near, far):
    lane = lax.broadcasted_iota(jnp.int32, near.shape, 1)
    half = LANES // 2
    low = jnp.where(lane < half, near, pltpu.roll(far, half, 1))
    high = jnp.where(lane < half, pltpu.roll(near, half, 1), far)
    return low.astype(bf16), high.astype(bf16)


def forward_kernel(
    states, taps, slices,
    here, masks, vec_ref, rates_ref, entry_ref, table, dt_ref, inner_ref, gate_ref, ggated_ref, dx_ref, ex_ref,
    gated_ref, ggate_ref, *rest,
):
    blocks, (dtm_s, u_s, y_s, held) = rest[:slices], rest[slices:]
    length, width = inner_ref.shape
    tiles, steps = width // LANES, length // SUBS
    zero = jnp.zeros((SUBS, LANES), f32)

    def scan(tile, _):
        at = tile_at(tile * LANES)
        dt = dt_ref[:, at]
        x = inner_ref[:, at].astype(f32)
        dtm_s[...] = jnp.where(masks[0] > 0.0, FAR, dt)
        u_s[...] = dt * x

        def wide(ref, n):
            return jnp.broadcast_to(ref[pl.ds(n, 1), at], (SUBS, LANES))

        rates = [wide(rates_ref, n) for n in range(states)]
        start = tuple(dx_ref[n, :, at] * wide(entry_ref, n) + ex_ref[n, :, at] for n in range(states))

        def lap(t, h):
            rows = step_rows(t)
            d, u = dtm_s[rows, :], u_s[rows, :]
            new, y = [], [zero, zero]
            for n in range(states):
                now = jnp.exp2(d * rates[n]) * h[n] + u * table[rows, n * LANES : (n + 1) * LANES]
                y[n % 2] = y[n % 2] + now * table[rows, (states + n) * LANES : (states + n + 1) * LANES]
                new.append(now)
            y_s[rows, :] = y[0] + y[1]
            return tuple(new)

        lax.fori_loop(0, steps, lap, start, unroll=UNROLL)
        scanned = y_s[...] + vec_ref[pl.ds(taps + 2, 1), at] * x
        gate = gate_ref[:, at]
        sig = jax.nn.sigmoid(gate)
        gated_ref[:, at] = (scanned * gate * sig).astype(bf16)
        ggate = (ggated_ref[:, at] * scanned * (sig * (1.0 + gate * (1.0 - sig)))).astype(bf16)
        ggate_ref[:, at] = ggate
        return 0

    lax.fori_loop(0, tiles, scan, 0)
    if not slices:
        return
    for pair in range(tiles // 2):
        side, spot = pair // (tiles // 4), pair % (tiles // 4)
        near, far = (ggate_ref[:, (2 * pair + n) * LANES : (2 * pair + n + 1) * LANES].astype(f32) for n in range(2))
        at = pl.ds(spot * LANES, LANES)
        held[side, :, at], held[side + 2, :, at] = halves_of(near, far)
    for n in range(slices):
        blocks[n][:, :width] = gated_ref[...]
        blocks[n][:, width:] = held[here[1] ^ n]


def forward(masks, vec, rates, entry, table, dt, inner, gate, ggated, dx, ex, taps, slices):
    length, width = inner.shape
    states = rates.shape[0]
    shape = jax.ShapeDtypeStruct
    return plain_call(
        functools.partial(forward_kernel, states, taps, slices),
        "forward",
        [shape((length, width), bf16)] * 2 + [shape((length, width + width // max(slices, 1)), bf16)] * slices,
        (masks, vec, rates, entry, table, dt, inner, gate, ggated, dx, ex),
        8,
        [pltpu.VMEM((length, LANES), f32)] * 3 + [pltpu.VMEM((max(slices, 1), length, width // max(slices, 1)), bf16)],
        8,
    )


def backward_kernel(
    states, rank, taps, slices,
    here, win_hbm, dtw_hbm, wx_hbm, masks, proj_ref, tok_ref, gain_ref, vec_ref, rates_ref, entry_ref, arrive_ref,
    table, dt_ref, inner_ref, gs_ref, dx_ref, ex_ref, db_ref, fx_ref, ggate_ref, ext_ref,
    ngrad, *rest,
):
    blocks, rest = rest[: max(slices, 1)], rest[max(slices, 1) :]
    (acc, hs, decays, dtm_s, u_s, s1_s, s2_s, isg, raw_s, sent_s, low_acc, pg, small, held, win_ref, dtw_ref, wx_ref, sems) = rest[-18:]
    length, width = inner_ref.shape
    model = tok_ref.shape[1]
    steps, tiles = length // SUBS, width // LANES
    rim = taps - 1
    maps = rank + 2 * states
    row_dtw = maps
    row_rate = row_dtw + rank
    row_taps = row_rate + states
    row_dtb, row_skip, row_cb, row_gain = (row_taps + taps + k for k in range(4))
    zero = jnp.zeros((SUBS, LANES), f32)
    half = states // 2
    block = min(512, width)
    pairs = ((dtw_hbm, dtw_ref), (wx_hbm, wx_ref), (win_hbm, win_ref))
    loads = [pltpu.make_async_copy(a, b, sems.at[n]) for n, (a, b) in enumerate(pairs)]
    for load in loads:
        load.start()
    low_acc[...] = jnp.zeros_like(low_acc)
    small[pl.ds(small.shape[0] - EDGE, EDGE), :] = jnp.zeros((EDGE, width), f32)
    low = proj_ref[:, :rank].astype(bf16)

    def clear(t, _):
        acc[step_rows(t), :] = jnp.zeros((SUBS, acc.shape[1]), f32)
        return 0

    lax.fori_loop(0, steps, clear, 0)
    loads[0].wait()

    def scan(tile, _):
        at = tile_at(tile * LANES)
        dt = dt_ref[:, at]
        x = inner_ref[:, at].astype(f32)
        dtm_s[...] = jnp.where(masks[0] > 0.0, FAR, dt)
        u_s[...] = dt * x

        def wide(ref, n):
            return jnp.broadcast_to(ref[pl.ds(n, 1), at], (SUBS, LANES))

        rates = [wide(rates_ref, n) for n in range(states)]
        start = []
        for n in range(states):
            h0 = dx_ref[n, :, at] * wide(entry_ref, n) + ex_ref[n, :, at]
            hs[0, n] = h0
            start.append(h0)

        def lap(t, h):
            rows = step_rows(t)
            d, u = dtm_s[rows, :], u_s[rows, :]
            new = []
            for n in range(states):
                a = jnp.exp2(d * rates[n])
                decays[t, n] = a
                now = a * h[n] + u * table[rows, n * LANES : (n + 1) * LANES]
                hs[t + 1, n] = now
                new.append(now)
            return tuple(new)

        lax.fori_loop(0, steps, lap, tuple(start), unroll=UNROLL)
        for first in range(0, states, half):
            some = rates[first : first + half]

            def back(k, carry):
                f, r = carry
                t = steps - 1 - k
                rows = step_rows(t)
                dtt, g, u = dt_ref[rows, at], gs_ref[rows, at], u_s[rows, :]
                fn, rn, s1, s2 = [], [], zero, zero
                for k in range(half):
                    n = first + k
                    into, out = (slice(m * LANES, (m + 1) * LANES) for m in (n, states + n))
                    adj = g * table[rows, out] + f[k]
                    acc[rows, into] += adj * u
                    acc[rows, out] += g * hs[t + 1, n]
                    s1 = s1 + adj * table[rows, into]
                    flow = decays[t, n] * adj
                    fn.append(flow)
                    flow = flow * hs[t, n]
                    s2 = s2 + flow * some[k]
                    rn.append(r[k] + flow * dtt)
                if first == 0:
                    s1_s[rows, :] = s1
                    s2_s[rows, :] = s2
                else:
                    s1_s[rows, :] += s1
                    s2_s[rows, :] += s2
                return tuple(fn), tuple(rn)

            f0 = tuple(
                db_ref[first + k, :, at] * wide(arrive_ref, first + k) + fx_ref[first + k, :, at] for k in range(half)
            )
            _, r = lax.fori_loop(0, steps, back, (f0, (zero,) * half), unroll=UNROLL)
            for k in range(half):
                small[pl.ds(row_rate + first + k, 1), at] = jnp.sum(r[k], axis=0, keepdims=True)
        s1, gs = s1_s[...], gs_ref[:, at]
        step_grad = s1 * x + LN2 * s2_s[...]
        isg[:, at] = s1 * dt + gs * vec_ref[pl.ds(taps + 2, 1), at]
        raw = nn(low, dtw_ref[:, at]) + vec_ref[pl.ds(taps + 1, 1), at]
        raw_grad = step_grad * jax.nn.sigmoid(raw)
        raw_s[:, at] = raw_grad.astype(bf16)
        small[pl.ds(row_dtb, 1), at] = jnp.sum(raw_grad, axis=0, keepdims=True)
        small[pl.ds(row_skip, 1), at] = jnp.sum(gs * x, axis=0, keepdims=True)
        return 0

    lax.fori_loop(0, tiles, scan, 0)

    def low_part(j, _):
        wide = tile_at(j * block, block)
        small[pl.ds(row_dtw, rank), wide] = tn(low, raw_s[:, wide])
        low_acc[:, :rank] += nt(raw_s[:, wide], dtw_ref[:, wide])
        return 0

    lax.fori_loop(0, width // block, low_part, 0)
    lane = lax.broadcasted_iota(jnp.int32, (SUBS, LANES), 1)

    def gather_maps(t, _):
        rows = step_rows(t)
        out = low_acc[rows, :]
        for n in range(2 * states):
            part = jnp.sum(acc[rows, n * LANES : (n + 1) * LANES], axis=1, keepdims=True)
            out = jnp.where(lane == rank + n, part, out)
        low_acc[rows, :] = out
        return 0

    lax.fori_loop(0, steps, gather_maps, 0)
    pg[...] = low_acc[...].astype(bf16)
    for load in loads[1:]:
        load.wait()
    ngrad[...] = jnp.zeros_like(ngrad)

    def close(j, _):
        wide = tile_at(j * block, block)
        ngrad[pl.ds(0, length), :] += nt(ggate_ref[:, wide], win_ref[:, tile_at(width + j * block, block)])
        small[pl.ds(0, maps), wide] = tn(pg[...], inner_ref[:, wide])[:maps]
        inner_grad = isg[:, wide] + nn(pg[:, :maps], wx_ref[:, wide])
        mask = [masks[k] for k in range(taps)]
        row = lax.broadcasted_iota(jnp.int32, (SUBS, LANES), 0)
        for tile in range(block // LANES):
            far = tile_at(j * block + tile * LANES)
            ext = ext_ref[:, far].astype(f32)[2 * EDGE - rim * SUBS :]
            windows = conv_windows(ext, taps, length)
            pre = conv_sum(windows, mask, vec_ref, far, taps)
            sig = jax.nn.sigmoid(pre)
            grad = inner_grad[:, tile * LANES : (tile + 1) * LANES] * (sig * (1.0 + pre * (1.0 - sig)))
            small[pl.ds(row_cb, 1), far] = jnp.sum(grad, axis=0, keepdims=True)
            small[pl.ds(row_taps + rim, 1), far] = jnp.sum(grad * windows[0], axis=0, keepdims=True)
            near = [grad[step * SUBS : (step + 1) * SUBS] * vec_ref[pl.ds(rim, 1), far] for step in range(steps)]
            head = [zero] * rim
            for k in range(1, taps):
                masked = grad * mask[k]
                small[pl.ds(row_taps + rim - k, 1), far] = jnp.sum(masked * windows[k], axis=0, keepdims=True)
                masked = masked * vec_ref[pl.ds(rim - k, 1), far]
                for step in range(steps):
                    piece = masked[step * SUBS : (step + 1) * SUBS]
                    if step >= k:
                        near[step - k] = near[step - k] + piece
                    else:
                        head[rim + step - k] = head[rim + step - k] + piece
            edge = zero
            for b in range(rim):
                moved = jnp.where(row == SUBS - 1, 0.0, pltpu.roll(head[b], SUBS - 1, 0))
                near[steps - rim + b] = near[steps - rim + b] + moved
                edge = jnp.where(row == b, jnp.broadcast_to(head[b][:1], (SUBS, LANES)), edge)
            sent = jnp.concatenate(near + [edge, zero], axis=0)
            sent_s[:, tile * LANES : (tile + 1) * LANES] = sent.astype(bf16)
            if not slices:
                blocks[0][:, far] = sent.astype(bf16)
            elif tile % 2 == 1:
                pair = j * (block // LANES // 2) + tile // 2
                side, spot = pair // (tiles // 4), tile_at(pair % (tiles // 4) * LANES)
                held[side, :, spot], held[side + 2, :, spot] = halves_of(last, sent)
            last = sent
        ngrad[...] += nt(sent_s[...], win_ref[:, wide])
        return 0

    lax.fori_loop(0, width // block, close, 0)
    x = tok_ref[...].astype(f32)
    inv = lax.rsqrt(jnp.mean(x * x, axis=-1, keepdims=True) + epsilon)
    small[pl.ds(row_gain, 1), pl.ds(0, model)] = jnp.sum(ngrad[...] * (x * inv), axis=0, keepdims=True)
    if slices:
        part = width // slices
        row = lax.broadcasted_iota(jnp.int32, (EDGE, part), 0)
        extra = jnp.zeros((EDGE, part), f32)
        normed = x[length:] * inv[length:] * gain_ref[...]
        count = model // part
        for b in range(rim):
            for c in range(count):
                piece = jnp.broadcast_to(normed[b : b + 1, c * part : (c + 1) * part], (EDGE, part))
                extra = jnp.where(row == rim + b * count + c, piece, extra)
        edge_rows = pl.ds(length, EDGE)
        for n in range(slices):
            held[n, edge_rows, :] = (held[n, edge_rows, :].astype(f32) + extra).astype(bf16)
        for n in range(slices):
            blocks[n][...] = held[here[1] ^ n]
    mine_ref, theirs_ref = rest[:2]
    chunk = mine_ref.shape[2]
    for c in range(2):

        @pl.when(here[0] == c)
        def _():
            for n in range(mine_ref.shape[0]):
                at, other = (2 * n + c) * chunk, (2 * n + 1 - c) * chunk
                mine_ref[n] = small[:, at : at + chunk]
                theirs_ref[n] = small[:, other : other + chunk].astype(bf16)


def backward(masks, in_weight, dtw, wx, proj, tok, gain, vec, rates, entry, arrive, table, dt, inner, gs, deep4,
             ggate, ext, taps, slices, chunks):
    length, width = inner.shape
    model = tok.shape[1]
    states = rates.shape[0]
    rank = dtw.shape[0]
    block = min(512, width)
    steps = length // SUBS
    rows = 2 * rank + 3 * states + taps + 4
    rows = -(-rows // EDGE) * EDGE
    shape = jax.ShapeDtypeStruct
    parts = max(slices, 1)
    chunk = (chunks, rows, width // (2 * chunks))
    return plain_call(
        functools.partial(backward_kernel, states, rank, taps, slices),
        "backward",
        [shape((length + EDGE, model), f32)]
        + [shape((length + EDGE, width // parts), bf16)] * parts
        + [shape(chunk, f32), shape(chunk, bf16)],
        (in_weight, dtw, wx, masks, proj, tok, gain, vec, rates, entry, arrive, table, dt, inner, gs, *deep4, ggate, ext),
        24,
        [
            pltpu.VMEM((length, 2 * states * LANES), f32),
            pltpu.VMEM((steps + 1, states, SUBS, LANES), f32),
            pltpu.VMEM((steps, states, SUBS, LANES), f32),
        ]
        + [pltpu.VMEM((length, LANES), f32)] * 4
        + [
            pltpu.VMEM((length, width), f32),
            pltpu.VMEM((length, width), bf16),
            pltpu.VMEM((length + EDGE, block), bf16),
            pltpu.VMEM((length, LANES), f32),
            pltpu.VMEM((length, LANES), bf16),
            pltpu.VMEM((rows, width), f32),
            pltpu.VMEM((parts, length + EDGE, width // parts), bf16),
        ]
        + [pltpu.VMEM(x.shape, x.dtype) for x in (in_weight, dtw, wx)]
        + [pltpu.SemaphoreType.DMA((3,))],
        24,
        [ANY_SPEC] * 3,
    )


def finish_kernel(rim, here, ngrad_ref, back_ref, tok_ref, cot_ref, gain_ref, gated_ref, wo_ref, grad_ref, mixed_ref):
    length = cot_ref.shape[0]
    x = tok_ref[pl.ds(0, length), :].astype(f32)
    mixed_ref[...] = turned((x + nn(gated_ref[...], wo_ref[...])).astype(bf16), True)
    inv = lax.rsqrt(jnp.mean(x * x, axis=-1, keepdims=True) + epsilon)
    scaled = x * inv
    row = lax.broadcasted_iota(jnp.int32, (SUBS, x.shape[1]), 0)
    pieces = [ngrad_ref[pl.ds(0, length - rim * SUBS), :]]
    for b in range(rim):
        late = jnp.where(row == SUBS - 1, back_ref[pl.ds(b, 1), :], 0.0)
        pieces.append(ngrad_ref[pl.ds(length - (rim - b) * SUBS, SUBS), :] + late)
    hat = jnp.concatenate(pieces, axis=0) * gain_ref[...]
    grad = cot_ref[...].astype(f32) + inv * (hat - scaled * jnp.mean(hat * scaled, axis=-1, keepdims=True))
    grad_ref[...] = turned(grad.astype(bf16), True)


def span_of(x, states):
    return x[2 * states : 2 * states + 1] + x[2 * states + 1 : 2 * states + 2] + x[2 * states + 2 : 2 * states + 3]


def span_rows(d):
    high = d.astype(bf16).astype(f32)
    middle = (d - high).astype(bf16).astype(f32)
    row = lax.broadcasted_iota(jnp.int32, (EDGE, d.shape[1]), 0)
    return jnp.where(row == 0, high, jnp.where(row == 1, middle, jnp.where(row == 2, d - high - middle, 0.0)))


def pair_parts(here, mine, other, rates, states):
    first = here[0] == 0
    near, far = jnp.where(first, mine, other), jnp.where(first, other, mine)
    d0, d1 = span_of(near, states), span_of(far, states)
    state = jnp.exp2(rates * d1) * near[:states] + far[:states]
    flow = near[states : 2 * states] + jnp.exp2(rates * d0) * far[states : 2 * states]
    return state, flow, span_rows(d0 + d1)


def pair_kernel(states, here, mine_ref, other_ref, rates_ref, out_ref):
    state, flow, spans = pair_parts(
        here, mine_ref[...].astype(f32), other_ref[...].astype(f32), rates_ref[...], states
    )
    out_ref[...] = jnp.concatenate([state, flow, spans], axis=0).astype(bf16)


def pair_half_kernel(states, here, mine_ref, other_ref, rates_ref, out_ref):
    half = rates_ref.shape[1] // 2
    at = tile_at(here[0] * half, half)
    parts = pair_parts(here, mine_ref[:, at].astype(f32), other_ref[:, at].astype(f32), rates_ref[:, at], states)
    out_ref[...] = jnp.concatenate(parts, axis=0).astype(bf16)


def quad_kernel(states, here, mine_ref, got_ref, rates_ref, near_ref, out_ref):
    half = rates_ref.shape[1] // 2
    rates = rates_ref[:, tile_at(here[0] * half, half)]
    mine, got = mine_ref[...].astype(f32), got_ref[...].astype(f32)
    first = here[2] % 2 == 0
    low, high = jnp.where(first, mine, got), jnp.where(first, got, mine)
    d0, d1 = span_of(low, states), span_of(high, states)
    w0, w1 = jnp.exp2(rates * d0), jnp.exp2(rates * d1)
    near_ref[pl.ds(0, states), :] = jnp.where(first, 0.0, low[:states])
    near_ref[pl.ds(states, states), :] = jnp.where(first, high[states : 2 * states], 0.0)
    near_ref[pl.ds(2 * states, states), :] = jnp.where(first, 1.0, w0)
    near_ref[pl.ds(3 * states, states), :] = jnp.where(first, w1, 1.0)
    state = w1 * low[:states] + high[:states]
    flow = low[states : 2 * states] + w0 * high[states : 2 * states]
    out_ref[...] = jnp.where(here[2] < 2, state, flow).astype(bf16)


def enter_half_kernel(states, here, near_ref, got_ref, out_ref):
    got = got_ref[...].astype(f32)
    low = here[2] < 2
    entry = near_ref[pl.ds(0, states), :] + jnp.where(low, 0.0, near_ref[pl.ds(2 * states, states), :] * got)
    arrive = near_ref[pl.ds(states, states), :] + jnp.where(low, near_ref[pl.ds(3 * states, states), :] * got, 0.0)
    out_ref[...] = jnp.concatenate([entry, arrive], axis=0)


def enter_both_kernel(states, here, other_ref, rates_ref, here_ref, there_ref, entry_ref, arrive_ref):
    core = here[0]
    half = rates_ref.shape[1] // 2
    for part, side in ((here_ref, core), (there_ref, 1 - core)):
        at = tile_at(side * half, half)
        other = other_ref[:, at].astype(f32)
        whole = jnp.exp2(rates_ref[:, at] * span_of(other, states))
        entry, arrive = part[pl.ds(0, states), :], part[pl.ds(states, states), :]
        entry_ref[:, at] = jnp.where(core == 1, whole * entry + other[:states], entry)
        arrive_ref[:, at] = jnp.where(core == 0, whole * arrive + other[states : 2 * states], arrive)


def enter_kernel(states, count, here, other_ref, rates_ref, chips_ref, entry_ref, arrive_ref):
    core, place = here[0], here[2]
    rates = rates_ref[...]

    def split(x):
        return x[:states], x[states : 2 * states], jnp.exp2(rates * span_of(x, states))

    def lap(k, carry):
        entry, arrive = carry
        s, _, whole = split(chips_ref[k].astype(f32))
        entry = jnp.where(k < place, whole * entry + s, entry)
        back = count - 1 - k
        _, f, whole = split(chips_ref[back].astype(f32))
        arrive = jnp.where(back > place, whole * arrive + f, arrive)
        return entry, arrive

    entry, arrive = lax.fori_loop(0, count, lap, (jnp.zeros_like(rates), jnp.zeros_like(rates)))
    s, f, whole = split(other_ref[...].astype(f32))
    entry_ref[...] = jnp.where(core == 1, whole * entry + s, entry)
    arrive_ref[...] = jnp.where(core == 0, whole * arrive + f, arrive)


def early_kernel(here, gain_ref, *rest):
    early, (normed_ref, left_ref) = rest[:-2], rest[-2:]
    length, model = early[0].shape[0], gain_ref.shape[1]
    for k, x in enumerate(early):
        at = pl.ds(k * length, length)
        normed_ref[at, :] = normalise(x[:, :model], gain_ref[...])
        left_ref[at, :] = x[:, model:]


def gate_out_kernel(size, chips, thin, here, normed_ref, left_ref, *rest):
    late, mine_ref, theirs = rest[:size], rest[size], rest[size + 1 :]
    model = normed_ref.shape[1]
    width = late[0].shape[1] * size // (size + 1)
    gate = tn(jnp.concatenate([x[:, width:] for x in late], axis=0), normed_ref[...])
    out = tn(left_ref[...], jnp.concatenate([x[:, :width] for x in late], axis=0))
    half = LANES // 2
    for c in range(2):

        @pl.when(here[0] == c)
        def _():
            for q in range(chips):
                for ref, side in ((mine_ref.at[q], c), (theirs[q], 1 - c)):
                    at = q * LANES + side * half
                    ref[pl.ds(0, half), :] = gate[at : at + half].astype(ref.dtype)
                    at = (2 * q + side) * thin
                    for n in range(width // model):
                        piece = out[at : at + thin, n * model : (n + 1) * model]
                        ref[pl.ds(half + n * thin, thin), :] = piece.astype(ref.dtype)


def flat(x, pieces):
    rows = x.shape[0] // pieces
    return jnp.concatenate([x[n * rows : (n + 1) * rows] for n in range(pieces)], axis=1)


def tall(x, pieces):
    lanes = x.shape[1] // pieces
    return jnp.concatenate([x[:, n * lanes : (n + 1) * lanes] for n in range(pieces)], axis=0)


def conv_kernel(length, chips, rim, here, normed_ref, *rest):
    gots, (mine_ref, theirs_ref) = rest[:-2], rest[-2:]
    wide = gots[0].shape[1]
    model = normed_ref.shape[1]
    pieces = model // wide
    got = jnp.concatenate([got[pl.ds(0, length), :] for got in gots], axis=0)
    lefts, rights = [], []
    for k in range(len(gots)):
        edge = gots[k][pl.ds(length, EDGE), :].astype(f32)
        row = lax.broadcasted_iota(jnp.int32, (SUBS, model), 0)
        left = jnp.zeros((SUBS, model), f32)
        for b in range(rim):
            at = rim + b * pieces
            one = jnp.concatenate([edge[at + c : at + c + 1] for c in range(pieces)], axis=1)
            left = jnp.where(row == b, jnp.broadcast_to(one, left.shape), left)
        lefts.append(left)
        right = edge[:SUBS]
        rights.append(jnp.where(lax.broadcasted_iota(jnp.int32, right.shape, 0) < rim, right, 0.0))
    left, right = (jnp.concatenate(x, axis=0).astype(bf16) for x in (lefts, rights))
    conv = tn(got, normed_ref[...]) + tn(right, left)
    half = LANES // 2
    for c in range(2):

        @pl.when(here[0] == c)
        def _():
            for q in range(chips):
                at = q * LANES
                mine_ref[q] = conv[at + c * half : at + (c + 1) * half]
                theirs_ref[pl.ds(q * half, half), :] = conv[at + (1 - c) * half : at + (2 - c) * half].astype(bf16)


def mix0_kernel(here, mine_ref, got_ref, small_ref, small_got, keep_ref, small_out, send_ref):
    place = here[2] & 1
    half, count = mine_ref.shape[1], mine_ref.shape[0] // 2
    at = lambda n: pl.ds(pl.multiple_of(n * half, half), half)
    for n in range(count):
        stay, leave = 2 * n + place, 2 * n + 1 - place
        keep_ref[n] = mine_ref[stay] + got_ref[at(stay), :].astype(f32)
        send_ref[at(n), :] = (mine_ref[leave] + got_ref[at(leave), :].astype(f32)).astype(bf16)
    small = small_ref[0] + small_got[0].astype(f32)
    small = flat(small, mine_ref.shape[2] // small.shape[1]).astype(bf16)
    small_out[...] = small
    send_ref[pl.ds(count * half, small.shape[0]), :] = small


def mix1_kernel(here, mine_ref, got_ref, small_ref, keep_ref, small_out, send_ref):
    place = (here[2] >> 1) & 1
    half = mine_ref.shape[1]
    at = lambda n: pl.ds(pl.multiple_of(n * half, half), half)
    keep_ref[...] = mine_ref[place] + got_ref[at(place), :].astype(f32)
    send_ref[pl.ds(0, half), :] = (mine_ref[1 - place] + got_ref[at(1 - place), :].astype(f32)).astype(bf16)
    rows = small_ref.shape[0]
    small = (small_ref[...].astype(f32) + got_ref[pl.ds(2 * half, rows), :].astype(f32)).astype(bf16)
    small_out[...] = small
    send_ref[pl.ds(half, rows), :] = small


def halve_kernel(which, bit, here, mine_ref, *rest):
    gots, (keep_ref, send_ref) = rest[:-2], rest[-2:]
    place = (here[which] >> bit) & 1
    each = mine_ref.shape[0] // len(gots)
    for n in range(mine_ref.shape[0]):
        got = gots[n // each]
        total = mine_ref[n] + (got[n % each] if len(got.shape) == 3 else got[...]).astype(f32)
        for side in range(2):

            @pl.when(place == side)
            def _():
                if n % 2 == side:
                    keep_ref[n // 2] = total
                else:
                    send_ref[n // 2] = total.astype(bf16)


def cross_kernel(here, mine_ref, got_ref, small_ref, gate_ref, keep_ref, small_out, send_ref):
    half = mine_ref.shape[0]
    conv = mine_ref[...] + got_ref[pl.ds(0, half), :].astype(f32)
    first = here[1] < 2
    keep_ref[...] = jnp.where(first, conv, gate_ref[...])
    send_ref[pl.ds(0, half), :] = jnp.where(first, gate_ref[...], conv).astype(bf16)
    rows = small_ref.shape[0]
    small = (small_ref[...].astype(f32) + got_ref[pl.ds(half, rows), :].astype(f32)).astype(bf16)
    small_out[...] = small
    send_ref[pl.ds(half, rows), :] = small


def go_last_kernel(thin, here, mine_ref, got_ref, gate_ref, out_ref):
    half, model = gate_ref.shape
    both = mine_ref[0] + got_ref[0].astype(f32)
    gate_ref[...] = both[:half]
    for n in range(out_ref.shape[1] // model):
        out_ref[:, n * model : (n + 1) * model] = both[half + n * thin : half + (n + 1) * thin]


def in_last_kernel(here, keep_ref, got_ref, out_ref):
    half = keep_ref.shape[0]
    keep, got = keep_ref[...], got_ref[pl.ds(0, half), :].astype(f32)
    first = here[1] < 2
    both = jnp.concatenate([jnp.where(first, keep, got), jnp.where(first, got, keep)], axis=0)
    out_ref[...] = both.T


def join_kernel(here, *refs):
    parts, out_ref = refs[:-1], refs[-1]
    rows = out_ref.shape[1]
    for k, part in enumerate(parts):
        out_ref[here[1] ^ k] = part[pl.ds(part.shape[0] - rows, rows), :]


def unpack_kernel(edges, here, rates_ref, mine_ref, other_ref, *outs):
    size = mine_ref.shape[0]
    chunk = rates_ref.shape[1] // (2 * size)
    pieces = mine_ref.shape[2] // chunk
    for c, part in ((here[0], mine_ref), (1 - here[0], other_ref)):
        for k in range(size):
            at = tile_at((2 * k + c) * chunk, chunk)
            block = tall(part[k].astype(f32), pieces)
            for n, out in enumerate(outs):
                piece = block[edges[n] : edges[n + 1]]
                out[:, at] = piece * rates_ref[:, at] if n == 2 else piece


class Group:
    def __init__(self, axis, size, stride):
        self.axis, self.size, self.stride = axis, size, stride
        self.direct = size <= 4
        self.place = (lax.axis_index(axis) // stride) % size

    def lists(self):
        n = lax.axis_size(self.axis)
        span = self.stride * self.size
        return [
            [base + low + self.stride * k for k in range(self.size)]
            for base in range(0, n, span)
            for low in range(self.stride)
        ]

    def swap(self, x, k):
        n = lax.axis_size(self.axis)
        return lax.ppermute(x, self.axis, [(i, i ^ (k * self.stride)) for i in range(n)])

    def exchange(self, blocks):
        if not self.direct:
            got = lax.all_to_all(blocks, self.axis, 0, 0, axis_index_groups=self.lists(), tiled=True)
            return [got[k] for k in range(self.size)]
        pick = lambda k: lax.dynamic_index_in_dim(blocks, self.place ^ k, 0, keepdims=False)
        return [pick(0)] + [self.swap(pick(k), k) for k in range(1, self.size)]

    def trade(self, blocks):
        if not self.direct:
            return self.exchange(jnp.stack(blocks))
        return [blocks[0]] + [self.swap(blocks[k], k) for k in range(1, self.size)]

    def gather(self, x):
        if not self.direct:
            got = lax.all_gather(x, self.axis, axis_index_groups=self.lists())
            return [got[k] for k in range(self.size)]
        return [x] + [self.swap(x, k) for k in range(1, self.size)]

    def sender(self, k):
        return self.place ^ k if self.direct else k

    def in_order(self, parts):
        if not self.direct:
            return jnp.stack(parts)
        stacked = jnp.stack(parts)
        return jnp.stack(
            [lax.dynamic_index_in_dim(stacked, self.place ^ q, 0, keepdims=False) for q in range(self.size)]
        )


def total(parts):
    return functools.reduce(lambda a, b: a + b, [part.astype(f32) for part in parts])


def body(
    tokens,
    cotangent,
    doc_starts,
    in_weight,
    conv_weight,
    conv_bias,
    xproj_weight,
    dt_weight,
    dt_bias,
    a_log,
    skip_scale,
    out_weight,
    norm_gain,
):
    length, model = tokens.shape[1:]
    inner_width, states = a_log.shape
    low_rank = dt_weight.shape[0]
    taps = conv_weight.shape[1]
    rim = taps - 1
    dp_size, seq_size = lax.axis_size("dp"), lax.axis_size("seq")
    core, outer = Group("seq", 2, 1), Group("seq", seq_size // 2, 2)
    rows_group = Group("dp", dp_size, 1)
    width = in_weight.shape[1] // (dp_size * seq_size)
    half_rows = dp_size // 2
    thin = model // (dp_size * seq_size)
    part = inner_width // dp_size
    tiled = outer.size == 4 and dp_size == 4 and width == LANES and thin % EDGE == 0
    tiled = tiled and model % part == 0 and rim * (1 + model // part) <= EDGE
    chips, slices = outer.size, dp_size if tiled else 0
    shape = jax.ShapeDtypeStruct

    wx = xproj_weight.T
    decay_rates = -jnp.exp(a_log).T

    left = lax.ppermute(tokens[0, length - rim :], "seq", [(i, i + 1) for i in range(seq_size - 1)])
    tok, cot, ext, inner, gate, ggated, gs, dt, proj, table, mine, dx, ex, db, fx, vec, rates, gain, masks, *early = front(
        doc_starts, tokens, cotangent, norm_gain, conv_weight.T, conv_bias, dt_bias, skip_scale, a_log.T, dt_weight, wx,
        in_weight, out_weight, left, dp_size,
    )
    early = rows_group.trade(early)
    other = core.swap(mine, 1)
    entering = [shape(rates.shape, f32)] * 2
    if tiled:
        half = inner_width // 2
        (mine_half,) = plain_call(
            functools.partial(pair_half_kernel, states),
            "pair",
            [shape((2 * states + EDGE, half), bf16)],
            (mine, other, rates),
            1,
        )
        near, far = plain_call(
            functools.partial(quad_kernel, states),
            "quad",
            [shape((4 * states, half), f32), shape((states, half), bf16)],
            (mine_half, outer.swap(mine_half, 1), rates),
            1,
        )
        (here,) = plain_call(
            functools.partial(enter_half_kernel, states),
            "enter_half",
            [shape((2 * states, half), f32)],
            (near, outer.swap(far, 2)),
            1,
        )
        entry, arrive = plain_call(
            functools.partial(enter_both_kernel, states), "enter", entering, (other, rates, here, core.swap(here, 1)), 1
        )
    else:
        (chip,) = plain_call(
            functools.partial(pair_kernel, states), "pair", [shape(mine.shape, bf16)], (mine, other, rates), 2
        )
        got = outer.in_order(outer.gather(chip))
        entry, arrive = plain_call(
            functools.partial(enter_kernel, states, outer.size), "enter", entering, (other, rates, got), 2
        )
    entry, early = lax.optimization_barrier((entry, early))
    gated, ggate, *late = forward(masks, vec, rates, entry, table, dt, inner, gate, ggated, dx, ex, taps, slices)
    late = rows_group.trade(late) if tiled else rows_group.gather(gated)
    if tiled:
        early, _ = lax.optimization_barrier((early, ggate))
        normed, left_cols = plain_call(
            early_kernel,
            "early",
            [shape((dp_size * length, model), bf16), shape((dp_size * length, model // dp_size), bf16)],
            (gain, *early),
            1,
        )
        arrive, _ = lax.optimization_barrier((arrive, normed))
    ngrad, *sent, small, small_theirs = backward(
        masks, in_weight, dt_weight, wx, proj, tok, gain, vec, rates, entry, arrive, table, dt, inner, gs,
        (dx, ex, db, fx), ggate, ext, taps, slices, dp_size,
    )
    rows, chunk = small.shape[1:]
    turn = [ngrad]

    def call(kernel, name, outs, args, us=1):
        args, _ = lax.optimization_barrier((tuple(args), turn[0]))
        got = plain_call(kernel, name, [shape(*x) for x in outs], args, us)
        turn[0] = got[0]
        return got

    def halve(group, bit, which, mine, got, name):
        count, *rest = mine.shape
        outs = [((count // 2, *rest), f32), ((count // 2, *rest), bf16)]
        keep, send = call(functools.partial(halve_kernel, which, bit), name, outs, (mine, *got))
        return keep, [group.swap(send, 1 << bit)]

    half = LANES // 2
    lines = rows * chunk // model
    part = ((lines, model), bf16)
    back = lax.ppermute(ngrad[length:], "seq", [(i, i - 1) for i in range(1, seq_size)])

    def finished():
        return call(
            functools.partial(finish_kernel, rim),
            "finish",
            [((length, model), bf16)] * 2,
            (ngrad, back, tok, cot, gain, gated, out_weight),
        )

    if tiled:
        small_got = [core.swap(small_theirs, 1)]
        conv_got = rows_group.trade(sent)
        small, small_got = halve(rows_group, 0, 1, small, small_got, "small_row0")
        go, *theirs = call(
            functools.partial(gate_out_kernel, dp_size, chips, thin),
            "gate_out_columns",
            [((chips, LANES, model), f32)] + [((LANES, model), bf16)] * chips,
            (normed, left_cols, *late),
        )
        go_got = [core.swap(x, 1) for x in theirs]
        go, go_got = halve(outer, 0, 2, go, go_got, "go_chip0")
        small, small_got = halve(rows_group, 1, 1, small, small_got, "small_row1")
        go, go_got = halve(outer, 1, 2, go, go_got, "go_chip1")
        outs = [((chips, half, model), f32), ((chips * half, model), bf16)]
        conv, theirs = call(functools.partial(conv_kernel, length, chips, rim), "conv_columns", outs, (normed, *conv_got))
        got = core.swap(theirs, 1)
        outs = [((chips // 2, half, model), f32), part, ((chips // 2 * half + lines, model), bf16)]
        conv, small, send = call(mix0_kernel, "mix0", outs, (conv, got, small, *small_got))
        got = outer.swap(send, 1)
        outs = [((half, model), f32), ((thin, inner_width), f32)]
        gate_slice, out_share = call(functools.partial(go_last_kernel, thin), "go_last", outs, (go, *go_got))
        outs = [((half, model), f32), part, ((half + lines, model), bf16)]
        conv, small, send = call(mix1_kernel, "mix1", outs, (conv, got, small))
        got = outer.swap(send, 2)
        tokens_grad, mixed = finished()
        outs = [((half, model), f32), part, ((half + lines, model), bf16)]
        keep, small, send = call(cross_kernel, "cross", outs, (conv, got, small, gate_slice))
        in_got = rows_group.swap(send, 2)
        smalls = [small, rows_group.swap(small, 1), in_got, rows_group.swap(small, 3)]
        (small,) = call(join_kernel, "join", [((dp_size, lines, model), bf16)], smalls)
        small_other = core.swap(small, 1)
        (in_share,) = call(in_last_kernel, "in_last", [((model, width), f32)], (keep, in_got))
    else:
        tokens_grad, mixed = finished()
        small = small + core.swap(small_theirs, 1).astype(f32)
        small = total(rows_group.exchange(small.astype(bf16)))
        small = total(outer.gather(small.astype(bf16))).astype(bf16)
        small = small.reshape(rows // lines, lines, -1).swapaxes(0, 1).reshape(lines, model)
        small = rows_group.in_order(rows_group.gather(small))
        small_other = core.swap(small, 1)
    sizes = [low_rank + 2 * states, low_rank, states, taps, 1, 1, 1, 1]
    edges = [sum(sizes[:k]) for k in range(len(sizes) + 1)]
    parts = call(
        functools.partial(unpack_kernel, edges),
        "unpack",
        [((size, inner_width), f32) for size in sizes],
        (decay_rates, small, small_other),
    )
    if not tiled:

        def normalised(x):
            wide = x.astype(f32)
            inv = lax.rsqrt(jnp.mean(wide * wide, axis=-1, keepdims=True) + epsilon)
            return (wide * inv * gain).astype(bf16)

        def summed(lefts, rights):
            return functools.reduce(lambda a, b: a + b, [tn(a, b) for a, b in zip(lefts, rights, strict=True)])

        def halved(x):
            return x.astype(bf16).reshape(model, 2, -1).swapaxes(0, 1)

        def by_chip(x):
            blocks = x.reshape(x.shape[0], half_rows, outer.size, 2, width)
            return outer.exchange(blocks.transpose(2, 0, 3, 1, 4).reshape(outer.size, x.shape[0], -1))

        normed_parts = [normalised(x) for x in outer.gather(tok)]
        gate_core = total(core.exchange(halved(summed([x[:length] for x in normed_parts], by_chip(ggate)))))
        conv_core = total(core.exchange(halved(summed(normed_parts, by_chip(sent[0])))))
        in_core = jnp.concatenate([conv_core, gate_core], axis=1).astype(bf16)
        in_share = total(rows_group.exchange(in_core.reshape(model, dp_size, width).swapaxes(0, 1)))
        out_sum = summed([x[:, model:] for x in early], late).astype(bf16)
        out_core = total(core.exchange(out_sum.reshape(outer.size, 2, thin, inner_width).swapaxes(0, 1)))
        out_share = total(outer.exchange(out_core.astype(bf16)))

    return (
        mixed[None],
        tokens_grad[None],
        in_share,
        parts[3].T,
        parts[6][0],
        parts[0].T,
        parts[1],
        parts[4][0],
        parts[2].T,
        parts[5][0],
        out_share.T,
        parts[7][0, :model],
    )


def solution(mesh):
    whole = (P(),) * 10
    row = P("dp", "seq", None)
    columns = P(None, ("dp", "seq"))
    return jax.shard_map(
        body,
        mesh=mesh,
        in_specs=(row, row, P("dp", None)) + whole,
        out_specs=(row, row, columns) + (P(),) * 7 + (columns, P()),
        check_vma=False,
    )
```

```python
import functools

import jax
import jax.numpy as jnp
from jax import lax
from jax.experimental import pallas as pl
from jax.experimental.pallas import tpu as pltpu
from jax.sharding import PartitionSpec as P

epsilon = 1e-05
LANES = 128
SUBS = 8
FAR = 1e36
LEAST_RATE = 1e-33
LN2 = 0.6931471805599453
EDGE = 16
UNROLL = 16
bf16, f32 = jnp.bfloat16, jnp.float32


def nt(a, b):
    return lax.dot_general(a, b, (((1,), (1,)), ((), ())), preferred_element_type=f32)


def tn(a, b):
    return lax.dot_general(a, b, (((0,), (0,)), ((), ())), preferred_element_type=f32)


def nn(a, b):
    return jnp.dot(a, b, preferred_element_type=f32)


ANY_SPEC = pl.BlockSpec(memory_space=pltpu.HBM)


class Here:
    def __getitem__(self, which):
        if which == 1:
            return lax.axis_index("dp")
        seq = lax.axis_index("seq")
        return seq % 2 if which == 0 else seq // 2


def plain_call(kernel, name, out_shape, args, us, scratch=(), limit=12, specs=None):
    specs = specs or []
    full = lambda x: pl.BlockSpec(x.shape, lambda: (0,) * len(x.shape))
    stay = lambda n, x: pltpu.with_memory_space_constraint(x, pltpu.HBM) if specs[n : n + 1] == [ANY_SPEC] else x
    args = [stay(n, x) for n, x in enumerate(args)]
    return pl.pallas_call(
        lambda *refs: kernel(Here(), *refs),
        in_specs=list(specs) + [full(x) for x in args[len(specs) :]],
        out_specs=[full(x) for x in out_shape],
        out_shape=out_shape,
        scratch_shapes=list(scratch),
        compiler_params=pltpu.CompilerParams(vmem_limit_bytes=limit << 20),
        cost_estimate=pl.CostEstimate(flops=int(us * 1.1e9), bytes_accessed=0, transcendentals=0),
        name=name,
    )(*args)


def softplus(v):
    return jnp.maximum(v, 0.0) + jnp.log1p(jnp.exp(-jnp.abs(v)))


def tile_at(start, size=LANES):
    return pl.ds(pl.multiple_of(start, LANES), size)


def step_rows(t):
    return pl.ds(pl.multiple_of(t * SUBS, SUBS), SUBS)


def tap_masks(starts_ref, taps, length):
    row = lax.broadcasted_iota(jnp.int32, (length, LANES), 0)
    place = lax.axis_index("seq") * length + (row % SUBS) * (length // SUBS) + row // SUBS
    begin = jnp.zeros_like(place)
    reset = jnp.zeros((length, LANES), f32)
    for k in range(starts_ref.shape[1]):
        start = starts_ref[0, k]
        begin = jnp.maximum(begin, jnp.where(place >= start, start, 0))
        reset = jnp.where(place == start, 1.0, reset)
    return [reset] + [jnp.where(begin <= place - j, 1.0, 0.0) for j in range(1, taps)]


def turned(x, plain):
    length = x.shape[0]
    steps = length // SUBS
    a = lax.broadcasted_iota(jnp.int32, (length, length), 1 - plain)
    b = lax.broadcasted_iota(jnp.int32, (length, length), plain + 0)
    turn = jnp.where(b == (a % steps) * SUBS + a // steps, 1.0, 0.0).astype(bf16)
    return nn(turn, x).astype(bf16)


def spread(maps, table_ref, first, width):
    high = maps.astype(bf16)
    rest = maps - high.astype(f32)
    middle = rest.astype(bf16)
    low = (rest - middle.astype(f32)).astype(bf16)
    row = lax.broadcasted_iota(jnp.int32, (LANES, width * LANES), 0)
    lane = lax.broadcasted_iota(jnp.int32, (LANES, width * LANES), 1)
    ones = jnp.where(row == first + lane // LANES, 1.0, 0.0).astype(bf16)
    table_ref[...] = nn(high, ones) + nn(middle, ones) + nn(low, ones)


def sub_scan(decay, value, forward):
    row = lax.broadcasted_iota(jnp.int32, decay.shape, 0)
    if not forward:
        row = SUBS - 1 - row

    def moved(x, by, fill):
        return jnp.where(row < by, fill, pltpu.roll(x, by if forward else SUBS - by, 0))

    by = 1
    while by < SUBS:
        d, v = moved(decay, by, 1.0), moved(value, by, 0.0)
        value = decay * v + value
        decay = decay * d
        by *= 2
    return value, moved(decay, 1, 1.0), moved(value, 1, 0.0)


def conv_windows(ext, taps, length):
    return [ext[(taps - 1 - j) * SUBS : (taps - 1 - j) * SUBS + length] for j in range(taps)]


def conv_sum(windows, masks, vec_ref, at, taps):
    out = vec_ref[pl.ds(taps, 1), at] + vec_ref[pl.ds(taps - 1, 1), at] * windows[0]
    for j in range(1, taps):
        out = out + vec_ref[pl.ds(taps - 1 - j, 1), at] * windows[j] * masks[j]
    return out


def normalise(x, gain):
    wide = x.astype(f32)
    inv = lax.rsqrt(jnp.mean(wide * wide, axis=-1, keepdims=True) + epsilon)
    return (wide * inv * gain).astype(bf16)


def front_kernel(
    states, rank, taps,
    here, starts_hbm, tok_hbm, cot_hbm, gain_hbm, convw_hbm, convb_hbm, dtb_hbm, skip_hbm, alog_hbm, dtw_hbm, wx_hbm,
    win_hbm, wo_hbm, left_ref,
    tok_out, cot_out, ext_ref, inner_ref, gate_ref, ggated_ref, gs_ref, dt_ref, proj_ref, table, pack_ref,
    dx_ref, ex_ref, db_ref, fx_ref, vec_ref, rates_ref, gain_ref, masks, *rest,
):
    (normed, dtm_s, u_s, ends, starts_ref, tok_ref, cot_ref, gain_s, convw_s, convb_s, dtb_s, skip_s, alog_s, dtw_ref, wx_ref,
     win_ref, wo_ref, sems, wide_sems) = rest
    length, model = cot_ref.shape
    width = rates_ref.shape[1]
    steps = length // SUBS
    rim = taps - 1
    maps = rank + 2 * states
    block = min(512, width)
    pairs = (
        (tok_hbm.at[0], tok_ref), (gain_hbm, gain_s), (cot_hbm.at[0], cot_ref), (convw_hbm, convw_s),
        (convb_hbm, convb_s), (dtb_hbm, dtb_s), (skip_hbm, skip_s), (alog_hbm, alog_s), (wx_hbm, wx_ref),
        (dtw_hbm, dtw_ref), (starts_hbm, starts_ref),
    )
    loads = [pltpu.make_async_copy(a, b, sems.at[n]) for n, (a, b) in enumerate(pairs)]

    def weights(j):
        conv = tile_at(j * block, block)
        gate = tile_at(width + j * block, block)
        return [
            pltpu.make_async_copy(win_hbm.at[:, conv], win_ref.at[:, conv], wide_sems.at[0, j]),
            pltpu.make_async_copy(win_hbm.at[:, gate], win_ref.at[:, gate], wide_sems.at[1, j]),
            pltpu.make_async_copy(wo_hbm.at[conv, :], wo_ref.at[conv, :], wide_sems.at[2, j]),
        ]

    for load in loads:
        load.start()
    for j in range(min(2, width // block)):
        for load in weights(j):
            load.start()
    for load in loads[:2]:
        load.wait()
    gain_ref[...] = gain_s[...].astype(f32).reshape(1, model)
    tok_out[pl.ds(0, length), :] = turned(tok_ref[...], False)
    left = left_ref[...].astype(f32)
    tok_out[pl.ds(length, EDGE), :] = jnp.concatenate([left, jnp.zeros((EDGE - rim, model), f32)], axis=0).astype(bf16)
    for load in loads[2:]:
        load.wait()
    vec_ref[pl.ds(0, taps), :] = convw_s[...].astype(f32)
    for n, ref in enumerate((convb_s, dtb_s, skip_s)):
        vec_ref[pl.ds(taps + n, 1), :] = ref[...].astype(f32).reshape(1, width)
    rates_ref[...] = jnp.minimum(-jnp.exp(alog_s[...]), -LEAST_RATE) * (1.0 / LN2)
    cot = turned(cot_ref[...], False)
    cot_out[...] = cot
    normed[...] = normalise(tok_out[...], gain_ref[...])
    for k, mask in enumerate(tap_masks(starts_ref, taps, length)):
        masks[k] = mask
    proj_ref[...] = jnp.zeros_like(proj_ref)

    def project(j, _):
        wide = tile_at(j * block, block)
        for load in weights(j):
            load.wait()

        @pl.when(j + 2 < width // block)
        def _():
            for load in weights(j + 2):
                load.start()

        conv = nn(normed[...], win_ref[:, wide]).astype(bf16)
        gate = nn(normed[pl.ds(0, length), :], win_ref[:, tile_at(width + j * block, block)])
        ggated = nt(cot_out[...], wo_ref[wide, :])
        gate_ref[:, wide] = gate
        ggated_ref[:, wide] = ggated
        gs_ref[:, wide] = ggated * gate * jax.nn.sigmoid(gate)
        row = lax.broadcasted_iota(jnp.int32, (SUBS, LANES), 0)
        mask = [masks[k] for k in range(taps)]
        for tile in range(block // LANES):
            far = tile_at(j * block + tile * LANES)
            part = conv[:, tile * LANES : (tile + 1) * LANES].astype(f32)
            pieces = []
            for b in range(rim):
                first = length - (rim - b) * SUBS
                moved = pltpu.roll(part[first : first + SUBS], 1, 0)
                pieces.append(jnp.where(row == 0, part[length + b : length + b + 1], moved))
            ext = jnp.concatenate(pieces + [part[:length]], axis=0)
            pad = jnp.zeros((2 * EDGE - rim * SUBS, LANES), f32)
            ext_ref[:, far] = jnp.concatenate([pad, ext], axis=0).astype(bf16)
            pre = conv_sum(conv_windows(ext, taps, length), mask, vec_ref, far, taps)
            inner_ref[:, far] = (pre * jax.nn.sigmoid(pre)).astype(bf16)
        proj_ref[:, :maps] += nt(inner_ref[:, wide], wx_ref[:, wide])
        return 0

    lax.fori_loop(0, width // block, project, 0)
    spread(proj_ref[...], table, rank, 2 * states)
    ends[...] = jnp.zeros_like(ends)
    half = states // 2
    zero = jnp.zeros((SUBS, LANES), f32)
    one = jnp.ones((SUBS, LANES), f32)
    low = proj_ref[:, :rank].astype(bf16)

    def scan(tile, _):
        at = tile_at(tile * LANES)
        dt = softplus(nn(low, dtw_ref[:, at]) + vec_ref[pl.ds(taps + 1, 1), at])
        dt_ref[:, at] = dt
        u_s[...] = dt * inner_ref[:, at].astype(f32)
        dtm = jnp.where(masks[0] > 0.0, FAR, dt)
        dtm_s[...] = dtm
        span = jnp.sum(dtm, axis=0, keepdims=True)
        high = span.astype(bf16).astype(f32)
        middle = (span - high).astype(bf16).astype(f32)
        ends[pl.ds(2 * states, 1), at] = high
        ends[pl.ds(2 * states + 1, 1), at] = middle
        ends[pl.ds(2 * states + 2, 1), at] = span - high - middle
        for first in range(0, states, half):
            rates = [jnp.broadcast_to(rates_ref[pl.ds(first + k, 1), at], (SUBS, LANES)) for k in range(half)]

            def lap(t, carry):
                h, f, p = carry
                rows = step_rows(t)
                d, u, g = dtm_s[rows, :], u_s[rows, :], gs_ref[rows, at]
                hn, fn, pn = [], [], []
                for k in range(half):
                    n = first + k
                    a = jnp.exp2(d * rates[k])
                    hn.append(a * h[k] + u * table[rows, n * LANES : (n + 1) * LANES])
                    q = p[k] * a
                    pn.append(q)
                    n += states
                    fn.append(f[k] + q * (g * table[rows, n * LANES : (n + 1) * LANES]))
                return tuple(hn), tuple(fn), tuple(pn)

            start = ((zero,) * half, (zero,) * half, (one,) * half)
            h, f, p = lax.fori_loop(0, steps, lap, start, unroll=UNROLL)
            for k in range(half):
                n = first + k
                e_in, d_ex, e_ex = sub_scan(p[k], h[k], True)
                f_in, b_ex, f_ex = sub_scan(p[k], f[k], False)
                ends[pl.ds(n, 1), at] = e_in[SUBS - 1 :, :]
                ends[pl.ds(states + n, 1), at] = f_in[:1, :]
                dx_ref[n, :, at] = d_ex
                ex_ref[n, :, at] = e_ex
                db_ref[n, :, at] = b_ex
                fx_ref[n, :, at] = f_ex
        return 0

    lax.fori_loop(0, width // LANES, scan, 0)
    pack_ref[...] = ends[...].astype(bf16)


def front(starts, tok, cot, gain, convw, convb, dtb, skip, alog, dtw, wx, in_weight, out_weight, left):
    length, model = cot.shape[1:]
    states, width = alog.shape
    rank, taps = dtw.shape[0], convw.shape[0]
    pack_rows = 2 * states + EDGE
    shape = jax.ShapeDtypeStruct
    big = lambda dtype: shape((length, width), dtype)
    out = [
        shape((length + EDGE, model), bf16), shape((length, model), bf16), shape((length + 2 * EDGE, width), bf16),
        big(bf16), big(f32), big(f32), big(f32), big(f32),
        shape((length, LANES), f32), shape((length, 2 * states * LANES), f32), shape((pack_rows, width), bf16),
    ] + [shape((states, SUBS, width), f32)] * 4 + [
        shape((taps + 4, width), f32), shape((states, width), f32), shape((1, model), f32),
        shape((taps, length, LANES), f32),
    ]
    args = (starts, tok, cot, gain, convw, convb, dtb, skip, alog, dtw, wx, in_weight, out_weight, left)
    scratch = [
        pltpu.VMEM((length + EDGE, model), bf16),
        pltpu.VMEM((length, LANES), f32),
        pltpu.VMEM((length, LANES), f32),
        pltpu.VMEM((pack_rows, width), f32),
        pltpu.SMEM(starts.shape, jnp.int32),
        pltpu.VMEM((length, model), bf16),
        pltpu.VMEM((length, model), bf16),
    ] + [pltpu.VMEM(x.shape, x.dtype) for x in args[3:13]]
    scratch += [pltpu.SemaphoreType.DMA((11,)), pltpu.SemaphoreType.DMA((3, width // min(512, width)))]
    return plain_call(
        functools.partial(front_kernel, states, rank, taps), "front", out,
        args, 20, scratch, 24, [ANY_SPEC] * 13,
    )


def chip_spot(tile, chips, tiles):
    half, chip, core = tile // (2 * chips), (tile // 2) % chips, tile % 2
    return chip, core * (tiles // (2 * chips)) + half


def forward_kernel(
    states, taps, chips, rows_size,
    here, masks, cot_ref, vec_ref, rates_ref, entry_ref, table, dt_ref, inner_ref, gate_ref, ggated_ref, dx_ref, ex_ref,
    gated_ref, ggate_ref, *rest,
):
    lines, blocks, (dtm_s, u_s, y_s, held) = rest[:rows_size], rest[rows_size:-4], rest[-4:]
    length, width = inner_ref.shape
    tiles, steps = width // LANES, length // SUBS
    zero = jnp.zeros((SUBS, LANES), f32)

    def scan(tile, _):
        at = tile_at(tile * LANES)
        dt = dt_ref[:, at]
        x = inner_ref[:, at].astype(f32)
        dtm_s[...] = jnp.where(masks[0] > 0.0, FAR, dt)
        u_s[...] = dt * x

        def wide(ref, n):
            return jnp.broadcast_to(ref[pl.ds(n, 1), at], (SUBS, LANES))

        rates = [wide(rates_ref, n) for n in range(states)]
        start = tuple(dx_ref[n, :, at] * wide(entry_ref, n) + ex_ref[n, :, at] for n in range(states))

        def lap(t, h):
            rows = step_rows(t)
            d, u = dtm_s[rows, :], u_s[rows, :]
            new, y = [], [zero, zero]
            for n in range(states):
                now = jnp.exp2(d * rates[n]) * h[n] + u * table[rows, n * LANES : (n + 1) * LANES]
                y[n % 2] = y[n % 2] + now * table[rows, (states + n) * LANES : (states + n + 1) * LANES]
                new.append(now)
            y_s[rows, :] = y[0] + y[1]
            return tuple(new)

        lax.fori_loop(0, steps, lap, start, unroll=UNROLL)
        scanned = y_s[...] + vec_ref[pl.ds(taps + 2, 1), at] * x
        gate = gate_ref[:, at]
        sig = jax.nn.sigmoid(gate)
        gated_ref[:, at] = (scanned * gate * sig).astype(bf16)
        ggate = (ggated_ref[:, at] * scanned * (sig * (1.0 + gate * (1.0 - sig)))).astype(bf16)
        ggate_ref[:, at] = ggate
        if chips:
            chip, spot = chip_spot(tile, chips, tiles)
            held[chip, :, tile_at(spot * LANES)] = ggate
        return 0

    lax.fori_loop(0, tiles, scan, 0)
    for n in range(chips):
        blocks[n][...] = held[here[2] ^ n]
    thin = cot_ref.shape[1] // rows_size
    for n in range(rows_size):
        lines[n][:, :width] = gated_ref[...]
        lines[n][:, width:] = cot_ref[:, tile_at((here[1] ^ n) * thin, thin)]


def forward(masks, cot, vec, rates, entry, table, dt, inner, gate, ggated, dx, ex, taps, chips, rows_size):
    length, width = inner.shape
    states = rates.shape[0]
    shape = jax.ShapeDtypeStruct
    return plain_call(
        functools.partial(forward_kernel, states, taps, chips, rows_size),
        "forward",
        [shape((length, width), bf16)] * 2
        + [shape((length, width + cot.shape[1] // rows_size), bf16)] * rows_size
        + [shape((length, width // max(chips, 1)), bf16)] * chips,
        (masks, cot, vec, rates, entry, table, dt, inner, gate, ggated, dx, ex),
        8,
        [pltpu.VMEM((length, LANES), f32)] * 3 + [pltpu.VMEM((max(chips, 1), length, width // max(chips, 1)), bf16)],
        8,
    )


def backward_kernel(
    states, rank, taps, chips,
    here, win_hbm, dtw_hbm, wx_hbm, masks, proj_ref, tok_ref, gain_ref, vec_ref, rates_ref, entry_ref, arrive_ref,
    table, dt_ref, inner_ref, gs_ref, dx_ref, ex_ref, db_ref, fx_ref, ggate_ref, ext_ref,
    ngrad, *rest,
):
    blocks, rest = rest[: max(chips, 1)], rest[max(chips, 1) :]
    (acc, hs, decays, dtm_s, u_s, s1_s, s2_s, isg, raw_s, sent_s, low_acc, pg, small, held, win_ref, dtw_ref, wx_ref, sems) = rest[-18:]
    length, width = inner_ref.shape
    model = tok_ref.shape[1]
    steps, tiles = length // SUBS, width // LANES
    rim = taps - 1
    maps = rank + 2 * states
    row_dtw = maps
    row_rate = row_dtw + rank
    row_taps = row_rate + states
    row_dtb, row_skip, row_cb, row_gain = (row_taps + taps + k for k in range(4))
    zero = jnp.zeros((SUBS, LANES), f32)
    half = states // 2
    block = min(512, width)
    pairs = ((dtw_hbm, dtw_ref), (wx_hbm, wx_ref), (win_hbm, win_ref))
    loads = [pltpu.make_async_copy(a, b, sems.at[n]) for n, (a, b) in enumerate(pairs)]
    for load in loads:
        load.start()
    low_acc[...] = jnp.zeros_like(low_acc)
    small[pl.ds(small.shape[0] - EDGE, EDGE), :] = jnp.zeros((EDGE, width), f32)
    low = proj_ref[:, :rank].astype(bf16)

    def clear(t, _):
        acc[step_rows(t), :] = jnp.zeros((SUBS, acc.shape[1]), f32)
        return 0

    lax.fori_loop(0, steps, clear, 0)
    loads[0].wait()

    def scan(tile, _):
        at = tile_at(tile * LANES)
        dt = dt_ref[:, at]
        x = inner_ref[:, at].astype(f32)
        dtm_s[...] = jnp.where(masks[0] > 0.0, FAR, dt)
        u_s[...] = dt * x

        def wide(ref, n):
            return jnp.broadcast_to(ref[pl.ds(n, 1), at], (SUBS, LANES))

        rates = [wide(rates_ref, n) for n in range(states)]
        start = []
        for n in range(states):
            h0 = dx_ref[n, :, at] * wide(entry_ref, n) + ex_ref[n, :, at]
            hs[0, n] = h0
            start.append(h0)

        def lap(t, h):
            rows = step_rows(t)
            d, u = dtm_s[rows, :], u_s[rows, :]
            new = []
            for n in range(states):
                a = jnp.exp2(d * rates[n])
                decays[t, n] = a
                now = a * h[n] + u * table[rows, n * LANES : (n + 1) * LANES]
                hs[t + 1, n] = now
                new.append(now)
            return tuple(new)

        lax.fori_loop(0, steps, lap, tuple(start), unroll=UNROLL)
        for first in range(0, states, half):
            some = rates[first : first + half]

            def back(k, carry):
                f, r = carry
                t = steps - 1 - k
                rows = step_rows(t)
                dtt, g, u = dt_ref[rows, at], gs_ref[rows, at], u_s[rows, :]
                fn, rn, s1, s2 = [], [], zero, zero
                for k in range(half):
                    n = first + k
                    into, out = (slice(m * LANES, (m + 1) * LANES) for m in (n, states + n))
                    adj = g * table[rows, out] + f[k]
                    acc[rows, into] += adj * u
                    acc[rows, out] += g * hs[t + 1, n]
                    s1 = s1 + adj * table[rows, into]
                    flow = decays[t, n] * adj
                    fn.append(flow)
                    flow = flow * hs[t, n]
                    s2 = s2 + flow * some[k]
                    rn.append(r[k] + flow * dtt)
                if first == 0:
                    s1_s[rows, :] = s1
                    s2_s[rows, :] = s2
                else:
                    s1_s[rows, :] += s1
                    s2_s[rows, :] += s2
                return tuple(fn), tuple(rn)

            f0 = tuple(
                db_ref[first + k, :, at] * wide(arrive_ref, first + k) + fx_ref[first + k, :, at] for k in range(half)
            )
            _, r = lax.fori_loop(0, steps, back, (f0, (zero,) * half), unroll=UNROLL)
            for k in range(half):
                small[pl.ds(row_rate + first + k, 1), at] = jnp.sum(r[k], axis=0, keepdims=True)
        s1, gs = s1_s[...], gs_ref[:, at]
        step_grad = s1 * x + LN2 * s2_s[...]
        isg[:, at] = s1 * dt + gs * vec_ref[pl.ds(taps + 2, 1), at]
        raw = nn(low, dtw_ref[:, at]) + vec_ref[pl.ds(taps + 1, 1), at]
        raw_grad = step_grad * jax.nn.sigmoid(raw)
        raw_s[:, at] = raw_grad.astype(bf16)
        small[pl.ds(row_dtb, 1), at] = jnp.sum(raw_grad, axis=0, keepdims=True)
        small[pl.ds(row_skip, 1), at] = jnp.sum(gs * x, axis=0, keepdims=True)
        return 0

    lax.fori_loop(0, tiles, scan, 0)

    def low_part(j, _):
        wide = tile_at(j * block, block)
        small[pl.ds(row_dtw, rank), wide] = tn(low, raw_s[:, wide])
        low_acc[:, :rank] += nt(raw_s[:, wide], dtw_ref[:, wide])
        return 0

    lax.fori_loop(0, width // block, low_part, 0)
    wide_row = lax.broadcasted_iota(jnp.int32, (2 * states * LANES, LANES), 0)
    wide_lane = lax.broadcasted_iota(jnp.int32, (2 * states * LANES, LANES), 1)
    ones = jnp.where(wide_lane == rank + wide_row // LANES, 1.0, 0.0).astype(bf16)
    high = acc[...].astype(bf16)
    low_acc[...] += nn(high, ones) + nn((acc[...] - high.astype(f32)).astype(bf16), ones)
    pg[...] = low_acc[...].astype(bf16)
    for load in loads[1:]:
        load.wait()
    ngrad[...] = jnp.zeros_like(ngrad)

    def close(j, _):
        wide = tile_at(j * block, block)
        ngrad[pl.ds(0, length), :] += nt(ggate_ref[:, wide], win_ref[:, tile_at(width + j * block, block)])
        small[pl.ds(0, maps), wide] = tn(pg[...], inner_ref[:, wide])[:maps]
        inner_grad = isg[:, wide] + nn(pg[:, :maps], wx_ref[:, wide])
        mask = [masks[k] for k in range(taps)]
        row = lax.broadcasted_iota(jnp.int32, (SUBS, LANES), 0)
        for tile in range(block // LANES):
            far = tile_at(j * block + tile * LANES)
            ext = ext_ref[:, far].astype(f32)[2 * EDGE - rim * SUBS :]
            windows = conv_windows(ext, taps, length)
            pre = conv_sum(windows, mask, vec_ref, far, taps)
            sig = jax.nn.sigmoid(pre)
            grad = inner_grad[:, tile * LANES : (tile + 1) * LANES] * (sig * (1.0 + pre * (1.0 - sig)))
            small[pl.ds(row_cb, 1), far] = jnp.sum(grad, axis=0, keepdims=True)
            small[pl.ds(row_taps + rim, 1), far] = jnp.sum(grad * windows[0], axis=0, keepdims=True)
            near = [grad[step * SUBS : (step + 1) * SUBS] * vec_ref[pl.ds(rim, 1), far] for step in range(steps)]
            head = [zero] * rim
            for k in range(1, taps):
                masked = grad * mask[k]
                small[pl.ds(row_taps + rim - k, 1), far] = jnp.sum(masked * windows[k], axis=0, keepdims=True)
                masked = masked * vec_ref[pl.ds(rim - k, 1), far]
                for step in range(steps):
                    piece = masked[step * SUBS : (step + 1) * SUBS]
                    if step >= k:
                        near[step - k] = near[step - k] + piece
                    else:
                        head[rim + step - k] = head[rim + step - k] + piece
            edge = zero
            for b in range(rim):
                moved = jnp.where(row == SUBS - 1, 0.0, pltpu.roll(head[b], SUBS - 1, 0))
                near[steps - rim + b] = near[steps - rim + b] + moved
                edge = jnp.where(row == b, jnp.broadcast_to(head[b][:1], (SUBS, LANES)), edge)
            sent = jnp.concatenate(near + [edge, zero], axis=0)
            sent_s[:, tile * LANES : (tile + 1) * LANES] = sent.astype(bf16)
            if chips:
                chip, spot = chip_spot(j * (block // LANES) + tile, chips, tiles)
                held[chip, :, tile_at(spot * LANES)] = sent.astype(bf16)
            else:
                blocks[0][:, far] = sent.astype(bf16)
        ngrad[...] += nt(sent_s[...], win_ref[:, wide])
        return 0

    lax.fori_loop(0, width // block, close, 0)
    x = tok_ref[...].astype(f32)
    inv = lax.rsqrt(jnp.mean(x * x, axis=-1, keepdims=True) + epsilon)
    small[pl.ds(row_gain, 1), pl.ds(0, model)] = jnp.sum(ngrad[...] * (x * inv), axis=0, keepdims=True)
    if chips:
        part = width // chips
        row = lax.broadcasted_iota(jnp.int32, (EDGE, part), 0)
        extra = jnp.zeros((EDGE, part), f32)
        normed = x[length:] * inv[length:] * gain_ref[...]
        count = model // part
        for b in range(rim):
            for c in range(count):
                piece = jnp.broadcast_to(normed[b : b + 1, c * part : (c + 1) * part], (EDGE, part))
                extra = jnp.where(row == rim + b * count + c, piece, extra)
        edge_rows = pl.ds(length, EDGE)
        for n in range(chips):
            held[n, edge_rows, :] = (held[n, edge_rows, :].astype(f32) + extra).astype(bf16)
        for n in range(chips):
            blocks[n][...] = held[here[2] ^ n]
    mine_ref, theirs_ref = rest[:2]
    chunk = mine_ref.shape[2]
    for c in range(2):

        @pl.when(here[0] == c)
        def _():
            for n in range(mine_ref.shape[0]):
                at, other = (2 * n + c) * chunk, (2 * n + 1 - c) * chunk
                mine_ref[n] = small[:, at : at + chunk]
                theirs_ref[n] = small[:, other : other + chunk].astype(bf16)


def backward(masks, in_weight, dtw, wx, proj, tok, gain, vec, rates, entry, arrive, table, dt, inner, gs, deep4,
             ggate, ext, taps, chips, chunks):
    length, width = inner.shape
    model = tok.shape[1]
    states = rates.shape[0]
    rank = dtw.shape[0]
    block = min(512, width)
    steps = length // SUBS
    rows = 2 * rank + 3 * states + taps + 4
    rows = -(-rows // EDGE) * EDGE
    shape = jax.ShapeDtypeStruct
    parts = max(chips, 1)
    chunk = (chunks, rows, width // (2 * chunks))
    return plain_call(
        functools.partial(backward_kernel, states, rank, taps, chips),
        "backward",
        [shape((length + EDGE, model), f32)]
        + [shape((length + EDGE, width // parts), bf16)] * parts
        + [shape(chunk, f32), shape(chunk, bf16)],
        (in_weight, dtw, wx, masks, proj, tok, gain, vec, rates, entry, arrive, table, dt, inner, gs, *deep4, ggate, ext),
        24,
        [
            pltpu.VMEM((length, 2 * states * LANES), f32),
            pltpu.VMEM((steps + 1, states, SUBS, LANES), f32),
            pltpu.VMEM((steps, states, SUBS, LANES), f32),
        ]
        + [pltpu.VMEM((length, LANES), f32)] * 4
        + [
            pltpu.VMEM((length, width), f32),
            pltpu.VMEM((length, width), bf16),
            pltpu.VMEM((length + EDGE, block), bf16),
            pltpu.VMEM((length, LANES), f32),
            pltpu.VMEM((length, LANES), bf16),
            pltpu.VMEM((rows, width), f32),
            pltpu.VMEM((parts, length + EDGE, width // parts), bf16),
        ]
        + [pltpu.VMEM(x.shape, x.dtype) for x in (in_weight, dtw, wx)]
        + [pltpu.SemaphoreType.DMA((3,))],
        24,
        [ANY_SPEC] * 3,
    )


def finish_kernel(rim, here, ngrad_ref, back_ref, tok_ref, cot_ref, gain_ref, gated_ref, wo_ref, grad_ref, mixed_ref):
    length = cot_ref.shape[0]
    x = tok_ref[pl.ds(0, length), :].astype(f32)
    mixed_ref[...] = turned((x + nn(gated_ref[...], wo_ref[...])).astype(bf16), True)
    inv = lax.rsqrt(jnp.mean(x * x, axis=-1, keepdims=True) + epsilon)
    scaled = x * inv
    row = lax.broadcasted_iota(jnp.int32, (SUBS, x.shape[1]), 0)
    pieces = [ngrad_ref[pl.ds(0, length - rim * SUBS), :]]
    for b in range(rim):
        late = jnp.where(row == SUBS - 1, back_ref[pl.ds(b, 1), :], 0.0)
        pieces.append(ngrad_ref[pl.ds(length - (rim - b) * SUBS, SUBS), :] + late)
    hat = jnp.concatenate(pieces, axis=0) * gain_ref[...]
    grad = cot_ref[...].astype(f32) + inv * (hat - scaled * jnp.mean(hat * scaled, axis=-1, keepdims=True))
    grad_ref[...] = turned(grad.astype(bf16), True)


def span_of(x, states):
    return x[2 * states : 2 * states + 1] + x[2 * states + 1 : 2 * states + 2] + x[2 * states + 2 : 2 * states + 3]


def span_rows(d):
    high = d.astype(bf16).astype(f32)
    middle = (d - high).astype(bf16).astype(f32)
    row = lax.broadcasted_iota(jnp.int32, (EDGE, d.shape[1]), 0)
    return jnp.where(row == 0, high, jnp.where(row == 1, middle, jnp.where(row == 2, d - high - middle, 0.0)))


def pair_parts(here, mine, other, rates, states):
    first = here[0] == 0
    near, far = jnp.where(first, mine, other), jnp.where(first, other, mine)
    d0, d1 = span_of(near, states), span_of(far, states)
    state = jnp.exp2(rates * d1) * near[:states] + far[:states]
    flow = near[states : 2 * states] + jnp.exp2(rates * d0) * far[states : 2 * states]
    return state, flow, span_rows(d0 + d1)


def pair_kernel(states, here, mine_ref, other_ref, rates_ref, out_ref):
    state, flow, spans = pair_parts(
        here, mine_ref[...].astype(f32), other_ref[...].astype(f32), rates_ref[...], states
    )
    out_ref[...] = jnp.concatenate([state, flow, spans], axis=0).astype(bf16)


def pair_half_kernel(states, here, mine_ref, other_ref, rates_ref, out_ref):
    half = rates_ref.shape[1] // 2
    at = tile_at(here[0] * half, half)
    parts = pair_parts(here, mine_ref[:, at].astype(f32), other_ref[:, at].astype(f32), rates_ref[:, at], states)
    out_ref[...] = jnp.concatenate(parts, axis=0).astype(bf16)


def quad_kernel(states, here, mine_ref, got_ref, rates_ref, near_ref, out_ref):
    half = rates_ref.shape[1] // 2
    rates = rates_ref[:, tile_at(here[0] * half, half)]
    mine, got = mine_ref[...].astype(f32), got_ref[...].astype(f32)
    first = here[2] % 2 == 0
    low, high = jnp.where(first, mine, got), jnp.where(first, got, mine)
    d0, d1 = span_of(low, states), span_of(high, states)
    w0, w1 = jnp.exp2(rates * d0), jnp.exp2(rates * d1)
    near_ref[pl.ds(0, states), :] = jnp.where(first, 0.0, low[:states])
    near_ref[pl.ds(states, states), :] = jnp.where(first, high[states : 2 * states], 0.0)
    near_ref[pl.ds(2 * states, states), :] = jnp.where(first, 1.0, w0)
    near_ref[pl.ds(3 * states, states), :] = jnp.where(first, w1, 1.0)
    state = w1 * low[:states] + high[:states]
    flow = low[states : 2 * states] + w0 * high[states : 2 * states]
    out_ref[...] = jnp.where(here[2] < 2, state, flow).astype(bf16)


def enter_half_kernel(states, here, near_ref, got_ref, out_ref):
    got = got_ref[...].astype(f32)
    low = here[2] < 2
    entry = near_ref[pl.ds(0, states), :] + jnp.where(low, 0.0, near_ref[pl.ds(2 * states, states), :] * got)
    arrive = near_ref[pl.ds(states, states), :] + jnp.where(low, near_ref[pl.ds(3 * states, states), :] * got, 0.0)
    out_ref[...] = jnp.concatenate([entry, arrive], axis=0)


def enter_both_kernel(states, here, other_ref, rates_ref, here_ref, there_ref, entry_ref, arrive_ref):
    core = here[0]
    half = rates_ref.shape[1] // 2
    for part, side in ((here_ref, core), (there_ref, 1 - core)):
        at = tile_at(side * half, half)
        other = other_ref[:, at].astype(f32)
        whole = jnp.exp2(rates_ref[:, at] * span_of(other, states))
        entry, arrive = part[pl.ds(0, states), :], part[pl.ds(states, states), :]
        entry_ref[:, at] = jnp.where(core == 1, whole * entry + other[:states], entry)
        arrive_ref[:, at] = jnp.where(core == 0, whole * arrive + other[states : 2 * states], arrive)


def enter_kernel(states, count, here, other_ref, rates_ref, chips_ref, entry_ref, arrive_ref):
    core, place = here[0], here[2]
    rates = rates_ref[...]

    def split(x):
        return x[:states], x[states : 2 * states], jnp.exp2(rates * span_of(x, states))

    def lap(k, carry):
        entry, arrive = carry
        s, _, whole = split(chips_ref[k].astype(f32))
        entry = jnp.where(k < place, whole * entry + s, entry)
        back = count - 1 - k
        _, f, whole = split(chips_ref[back].astype(f32))
        arrive = jnp.where(back > place, whole * arrive + f, arrive)
        return entry, arrive

    entry, arrive = lax.fori_loop(0, count, lap, (jnp.zeros_like(rates), jnp.zeros_like(rates)))
    s, f, whole = split(other_ref[...].astype(f32))
    entry_ref[...] = jnp.where(core == 1, whole * entry + s, entry)
    arrive_ref[...] = jnp.where(core == 0, whole * arrive + f, arrive)


def out_kernel(size, chips, thin, here, *rest):
    parts, (mine_ref, theirs_ref) = rest[:size], rest[size:]
    model = mine_ref.shape[2]
    width = parts[0].shape[1] - 2 * chips * thin
    left = jnp.concatenate([x[:, width:] for x in parts], axis=0)
    out = tn(left, jnp.concatenate([x[:, :width] for x in parts], axis=0))
    for c in range(2):

        @pl.when(here[0] == c)
        def _():
            for q in range(chips):
                for ref, side in ((mine_ref, c), (theirs_ref, 1 - c)):
                    at = (2 * q + side) * thin
                    for n in range(width // model):
                        piece = out[at : at + thin, n * model : (n + 1) * model]
                        ref[q, pl.ds(n * thin, thin), :] = piece.astype(ref.dtype)


def split_cores(here, x, mine_ref, theirs_ref):
    count, rows = mine_ref.shape[:2]
    for c in range(2):

        @pl.when(here[0] == c)
        def _():
            for n in range(count):
                mine_ref[n] = x[(c * count + n) * rows : (c * count + n + 1) * rows]
                theirs_ref[n] = x[((1 - c) * count + n) * rows : ((1 - c) * count + n + 1) * rows].astype(bf16)


def gate_kernel(size, here, gain_ref, *rest):
    toks, gots, (normed_ref, mine_ref, theirs_ref) = rest[:size], rest[size:-3], rest[-3:]
    length = toks[0].shape[0]
    for k, x in enumerate(toks):
        normed_ref[pl.ds(k * length, length), :] = normalise(turned(x[...], False), gain_ref[...])
    got = jnp.concatenate([x[...] for x in gots], axis=0)
    split_cores(here, tn(got, normed_ref[...]), mine_ref, theirs_ref)


def flat(x, pieces):
    rows = x.shape[0] // pieces
    return jnp.concatenate([x[n * rows : (n + 1) * rows] for n in range(pieces)], axis=1)


def tall(x, pieces):
    lanes = x.shape[1] // pieces
    return jnp.concatenate([x[:, n * lanes : (n + 1) * lanes] for n in range(pieces)], axis=0)


def conv_kernel(length, rim, here, normed_ref, *rest):
    gots, (mine_ref, theirs_ref) = rest[:-2], rest[-2:]
    wide = gots[0].shape[1]
    model = normed_ref.shape[1]
    pieces = model // wide
    got = jnp.concatenate([got[pl.ds(0, length), :] for got in gots], axis=0)
    lefts, rights = [], []
    for k in range(len(gots)):
        edge = gots[k][pl.ds(length, EDGE), :].astype(f32)
        row = lax.broadcasted_iota(jnp.int32, (SUBS, model), 0)
        left = jnp.zeros((SUBS, model), f32)
        for b in range(rim):
            at = rim + b * pieces
            one = jnp.concatenate([edge[at + c : at + c + 1] for c in range(pieces)], axis=1)
            left = jnp.where(row == b, jnp.broadcast_to(one, left.shape), left)
        lefts.append(left)
        right = edge[:SUBS]
        rights.append(jnp.where(lax.broadcasted_iota(jnp.int32, right.shape, 0) < rim, right, 0.0))
    left, right = (jnp.concatenate(x, axis=0).astype(bf16) for x in (lefts, rights))
    conv = tn(got, normed_ref[...]) + tn(right, left)
    split_cores(here, conv, mine_ref, theirs_ref)


def halve_kernel(which, bit, here, mine_ref, got_ref, keep_ref, send_ref):
    place = (here[which] >> bit) & 1
    for n in range(mine_ref.shape[0] // 2):
        stay, leave = 2 * n + place, 2 * n + 1 - place
        keep_ref[n] = mine_ref[stay] + got_ref[stay].astype(f32)
        send_ref[n] = (mine_ref[leave] + got_ref[leave].astype(f32)).astype(bf16)


def small_last_kernel(here, mine_ref, got_ref, out_ref):
    small = mine_ref[0] + got_ref[0].astype(f32)
    out_ref[...] = flat(small, out_ref.shape[1] // small.shape[1]).astype(bf16)


def add_kernel(here, mine_ref, got_ref, out_ref):
    out_ref[...] = (mine_ref[...].astype(f32) + got_ref[...].astype(f32)).astype(bf16)


def in_merge_kernel(here, conv_mine, conv_got, gate_mine, gate_got, small_ref, own_ref, *parts):
    count, rows = conv_mine.shape[:2]
    for part in parts:
        part[pl.ds(rows, small_ref.shape[0]), :] = small_ref[...]
    for mine, got, first in ((conv_mine, conv_got, 0), (gate_mine, gate_got, count)):
        for n in range(count):
            both = mine[n] + got[n].astype(f32)
            for k in range(2 * count):

                @pl.when((here[1] ^ k) == first + n)
                def _():
                    if k == 0:
                        own_ref[...] = both
                    else:
                        parts[k - 1][pl.ds(0, rows), :] = both.astype(bf16)


def in_last_kernel(here, own_ref, small_ref, *rest):
    gots, (out_ref, small_out) = rest[:-2], rest[-2:]
    both, rows = own_ref[...], own_ref.shape[0]
    small_out[here[1]] = small_ref[...]
    for k, got in enumerate(gots):
        both = both + got[pl.ds(0, rows), :].astype(f32)
        small_out[here[1] ^ (k + 1)] = got[pl.ds(rows, small_ref.shape[0]), :]
    out_ref[...] = both.T


def out_last_kernel(here, mine_ref, got_ref, out_ref):
    thin, model = out_ref.shape[0], mine_ref.shape[2]
    both = mine_ref[0] + got_ref[0].astype(f32)
    for n in range(out_ref.shape[1] // model):
        out_ref[:, n * model : (n + 1) * model] = both[n * thin : (n + 1) * thin]


def unpack_kernel(edges, here, rates_ref, mine_ref, other_ref, *outs):
    size = mine_ref.shape[0]
    chunk = rates_ref.shape[1] // (2 * size)
    pieces = mine_ref.shape[2] // chunk
    for c, part in ((here[0], mine_ref), (1 - here[0], other_ref)):
        for k in range(size):
            at = tile_at((2 * k + c) * chunk, chunk)
            block = tall(part[k].astype(f32), pieces)
            for n, out in enumerate(outs):
                piece = block[edges[n] : edges[n + 1]]
                if (2 * k + 1) * chunk < out.shape[1]:
                    out[:, at] = piece * rates_ref[:, at] if n == 2 else piece


class Group:
    def __init__(self, axis, size, stride):
        self.axis, self.size, self.stride = axis, size, stride
        self.direct = size <= 4
        self.place = (lax.axis_index(axis) // stride) % size

    def lists(self):
        n = lax.axis_size(self.axis)
        span = self.stride * self.size
        return [
            [base + low + self.stride * k for k in range(self.size)]
            for base in range(0, n, span)
            for low in range(self.stride)
        ]

    def swap(self, x, k):
        n = lax.axis_size(self.axis)
        return lax.ppermute(x, self.axis, [(i, i ^ (k * self.stride)) for i in range(n)])

    def exchange(self, blocks):
        if not self.direct:
            got = lax.all_to_all(blocks, self.axis, 0, 0, axis_index_groups=self.lists(), tiled=True)
            return [got[k] for k in range(self.size)]
        pick = lambda k: lax.dynamic_index_in_dim(blocks, self.place ^ k, 0, keepdims=False)
        return [pick(0)] + [self.swap(pick(k), k) for k in range(1, self.size)]

    def trade(self, blocks):
        if not self.direct:
            return self.exchange(jnp.stack(blocks))
        return [blocks[0]] + [self.swap(blocks[k], k) for k in range(1, self.size)]

    def gather(self, x):
        if not self.direct:
            got = lax.all_gather(x, self.axis, axis_index_groups=self.lists())
            return [got[k] for k in range(self.size)]
        return [x] + [self.swap(x, k) for k in range(1, self.size)]

    def sender(self, k):
        return self.place ^ k if self.direct else k

    def in_order(self, parts):
        if not self.direct:
            return jnp.stack(parts)
        stacked = jnp.stack(parts)
        return jnp.stack(
            [lax.dynamic_index_in_dim(stacked, self.place ^ q, 0, keepdims=False) for q in range(self.size)]
        )


def total(parts):
    return functools.reduce(lambda a, b: a + b, [part.astype(f32) for part in parts])


def body(
    tokens,
    cotangent,
    doc_starts,
    in_weight,
    conv_weight,
    conv_bias,
    xproj_weight,
    dt_weight,
    dt_bias,
    a_log,
    skip_scale,
    out_weight,
    norm_gain,
):
    length, model = tokens.shape[1:]
    inner_width, states = a_log.shape
    low_rank = dt_weight.shape[0]
    taps = conv_weight.shape[1]
    rim = taps - 1
    dp_size, seq_size = lax.axis_size("dp"), lax.axis_size("seq")
    core, outer = Group("seq", 2, 1), Group("seq", seq_size // 2, 2)
    rows_group = Group("dp", dp_size, 1)
    width = in_weight.shape[1] // (dp_size * seq_size)
    half_rows = dp_size // 2
    thin = model // (dp_size * seq_size)
    part = inner_width // outer.size
    tiled = outer.size == 4 and dp_size == 4 and width == LANES and thin % EDGE == 0
    tiled = tiled and model % part == 0 and rim * (1 + model // part) <= EDGE
    chips = outer.size if tiled else 0
    shape = jax.ShapeDtypeStruct

    wx = xproj_weight.T
    decay_rates = -jnp.exp(a_log).T

    left = lax.ppermute(tokens[0, length - rim :], "seq", [(i, i + 1) for i in range(seq_size - 1)])
    tok, cot, ext, inner, gate, ggated, gs, dt, proj, table, mine, dx, ex, db, fx, vec, rates, gain, masks = front(
        doc_starts, tokens, cotangent, norm_gain, conv_weight.T, conv_bias, dt_bias, skip_scale, a_log.T, dt_weight, wx,
        in_weight, out_weight, left,
    )
    if tiled:
        after, _ = lax.optimization_barrier((tokens[0], left))
        tok_parts = outer.gather(after)
        mine, tok_parts = lax.optimization_barrier((mine, tok_parts))
    other = core.swap(mine, 1)
    entering = [shape(rates.shape, f32)] * 2
    if tiled:
        half = inner_width // 2
        (mine_half,) = plain_call(
            functools.partial(pair_half_kernel, states),
            "pair",
            [shape((2 * states + EDGE, half), bf16)],
            (mine, other, rates),
            1,
        )
        near, far = plain_call(
            functools.partial(quad_kernel, states),
            "quad",
            [shape((4 * states, half), f32), shape((states, half), bf16)],
            (mine_half, outer.swap(mine_half, 1), rates),
            1,
        )
        (here,) = plain_call(
            functools.partial(enter_half_kernel, states),
            "enter_half",
            [shape((2 * states, half), f32)],
            (near, outer.swap(far, 2)),
            1,
        )
        entry, arrive = plain_call(
            functools.partial(enter_both_kernel, states), "enter", entering, (other, rates, here, core.swap(here, 1)), 1
        )
    else:
        (chip,) = plain_call(
            functools.partial(pair_kernel, states), "pair", [shape(mine.shape, bf16)], (mine, other, rates), 2
        )
        got = outer.in_order(outer.gather(chip))
        entry, arrive = plain_call(
            functools.partial(enter_kernel, states, outer.size), "enter", entering, (other, rates, got), 2
        )
    gated, ggate, *late = forward(masks, cot, vec, rates, entry, table, dt, inner, gate, ggated, dx, ex, taps, chips, dp_size)
    lines_got = rows_group.trade(late[:dp_size])
    gate_got = outer.trade(late[dp_size:]) if tiled else None

    ngrad, *sent, small, small_theirs = backward(
        masks, in_weight, dt_weight, wx, proj, tok, gain, vec, rates, entry, arrive, table, dt, inner, gs,
        (dx, ex, db, fx), ggate, ext, taps, chips, dp_size,
    )
    rows, chunk = small.shape[1:]
    turn = [ngrad]

    def call(kernel, name, outs, args, us=2):
        args = tuple(args)
        got = plain_call(kernel, name, [shape(*x) for x in outs], args, us)
        turn[0] = got[0]
        return got

    def halve(group, bit, which, mine, got, name):
        count, *rest = mine.shape
        outs = [((count // 2, *rest), f32), ((count // 2, *rest), bf16)]
        keep, send = call(functools.partial(halve_kernel, which, bit), name, outs, (mine, got))
        return keep, group.swap(send, 1 << bit)

    lines = rows * chunk // model
    part = ((lines, model), bf16)
    back = lax.ppermute(ngrad[length:], "seq", [(i, i - 1) for i in range(1, seq_size)])

    def finished():
        return call(
            functools.partial(finish_kernel, rim),
            "finish",
            [((length, model), bf16)] * 2,
            (ngrad, back, tok, cot, gain, gated, out_weight),
        )

    if tiled:
        blocks = (half_rows, width, model)
        sent, small_theirs, *early_got = lax.optimization_barrier((sent, small_theirs, *lines_got, *gate_got[:-1]))
        lines_got, gate_got = early_got[:dp_size], early_got[dp_size:] + gate_got[-1:]
        small_got = core.swap(small_theirs, 1)
        conv_got = outer.trade(sent)
        small, small_got = halve(rows_group, 0, 1, small, small_got, "small_row0")
        block = (chips, LANES // 2, model)
        out, theirs = call(
            functools.partial(out_kernel, dp_size, chips, thin),
            "out_columns",
            [(block, f32), (block, bf16)],
            lines_got,
        )
        out_got = core.swap(theirs, 1)
        small, small_got = halve(rows_group, 1, 1, small, small_got, "small_row1")
        normed, gate, theirs = call(
            functools.partial(gate_kernel, chips),
            "gate_columns",
            [((chips * length, model), bf16), (blocks, f32), (blocks, bf16)],
            (gain, *tok_parts, *gate_got),
        )
        gate_got = core.swap(theirs, 1)
        (small,) = call(small_last_kernel, "small_last", [part], (small, small_got))
        small_got = outer.swap(small, 1)
        conv, theirs = call(
            functools.partial(conv_kernel, length, rim), "conv_columns", [(blocks, f32), (blocks, bf16)], (normed, *conv_got)
        )
        conv_got = core.swap(theirs, 1)
        (small,) = call(add_kernel, "small_chip0", [part], (small, small_got))
        small_got = outer.swap(small, 2)
        (small,) = call(add_kernel, "small_chip1", [part], (small, small_got))
        slab = (width, model)
        in_own, *sends = call(
            in_merge_kernel,
            "in_merge",
            [(slab, f32)] + [((width + lines, model), bf16)] * (dp_size - 1),
            (conv, conv_got, gate, gate_got, small),
        )
        in_own, *in_gots = rows_group.trade([in_own] + sends)
        out, out_got = halve(outer, 0, 2, out, out_got, "out_chip0")
        tokens_grad, mixed = finished()
        out, out_got = halve(outer, 1, 2, out, out_got, "out_chip1")
        outs = [((model, width), f32), ((dp_size, lines, model), bf16)]
        in_share, small = call(in_last_kernel, "in_last", outs, (in_own, small, *in_gots))
        small_other = core.swap(small, 1)
        (out_share,) = call(out_last_kernel, "out_last", [((thin, inner_width), f32)], (out, out_got))
    else:
        tokens_grad, mixed = finished()
        small = small + core.swap(small_theirs, 1).astype(f32)
        small = total(rows_group.exchange(small.astype(bf16)))
        small = total(outer.gather(small.astype(bf16))).astype(bf16)
        small = small.reshape(rows // lines, lines, -1).swapaxes(0, 1).reshape(lines, model)
        small = rows_group.in_order(rows_group.gather(small))
        small_other = core.swap(small, 1)
    sizes = [low_rank + 2 * states, low_rank, states, taps, 1, 1, 1, 1]
    edges = [sum(sizes[:k]) for k in range(len(sizes) + 1)]
    parts = call(
        functools.partial(unpack_kernel, edges),
        "unpack",
        [((size, inner_width), f32) for size in sizes[:-1]] + [((1, model), f32)],
        (decay_rates, small, small_other),
    )
    if not tiled:

        def normalised(x):
            wide = x.astype(f32)
            inv = lax.rsqrt(jnp.mean(wide * wide, axis=-1, keepdims=True) + epsilon)
            return (wide * inv * gain).astype(bf16)

        def summed(lefts, rights):
            return functools.reduce(lambda a, b: a + b, [tn(a, b) for a, b in zip(lefts, rights, strict=True)])

        def halved(x):
            return x.astype(bf16).reshape(model, 2, -1).swapaxes(0, 1)

        def by_chip(x):
            blocks = x.reshape(x.shape[0], half_rows, outer.size, 2, width)
            return outer.exchange(blocks.transpose(2, 0, 3, 1, 4).reshape(outer.size, x.shape[0], -1))

        normed_parts = [normalised(x) for x in outer.gather(tok)]
        gate_core = total(core.exchange(halved(summed([x[:length] for x in normed_parts], by_chip(ggate)))))
        conv_core = total(core.exchange(halved(summed(normed_parts, by_chip(sent[0])))))
        in_core = jnp.concatenate([conv_core, gate_core], axis=1).astype(bf16)
        in_share = total(rows_group.exchange(in_core.reshape(model, dp_size, width).swapaxes(0, 1)))
        out_sum = summed([x[:, inner_width:] for x in lines_got], [x[:, :inner_width] for x in lines_got]).astype(bf16)
        out_core = total(core.exchange(out_sum.reshape(outer.size, 2, thin, inner_width).swapaxes(0, 1)))
        out_share = total(outer.exchange(out_core.astype(bf16)))

    return (
        mixed[None],
        tokens_grad[None],
        in_share,
        parts[3].T,
        parts[6][0],
        parts[0].T,
        parts[1],
        parts[4][0],
        parts[2].T,
        parts[5][0],
        out_share.T,
        parts[7][0],
    )


def solution(mesh):
    whole = (P(),) * 10
    row = P("dp", "seq", None)
    columns = P(None, ("dp", "seq"))
    return jax.shard_map(
        body,
        mesh=mesh,
        in_specs=(row, row, P("dp", None)) + whole,
        out_specs=(row, row, columns) + (P(),) * 7 + (columns, P()),
        check_vma=False,
    )
```

```python
import functools

import jax
import jax.numpy as jnp
from jax import lax
from jax.experimental import pallas as pl
from jax.experimental.pallas import tpu as pltpu
from jax.sharding import PartitionSpec as P

epsilon = 1e-05
LANES = 128
SUBS = 8
FAR = 1e36
LEAST_RATE = 1e-33
LN2 = 0.6931471805599453
EDGE = 16
UNROLL = 16
bf16, f32 = jnp.bfloat16, jnp.float32


def nt(a, b):
    return lax.dot_general(a, b, (((1,), (1,)), ((), ())), preferred_element_type=f32)


def tn(a, b):
    return lax.dot_general(a, b, (((0,), (0,)), ((), ())), preferred_element_type=f32)


def nn(a, b):
    return jnp.dot(a, b, preferred_element_type=f32)


ANY_SPEC = pl.BlockSpec(memory_space=pltpu.HBM)


class Here:
    def __getitem__(self, which):
        if which == 1:
            return lax.axis_index("dp")
        seq = lax.axis_index("seq")
        return seq % 2 if which == 0 else seq // 2


def plain_call(kernel, name, out_shape, args, us, scratch=(), limit=12, specs=None):
    specs = specs or []
    full = lambda x: pl.BlockSpec(x.shape, lambda: (0,) * len(x.shape))
    stay = lambda n, x: pltpu.with_memory_space_constraint(x, pltpu.HBM) if specs[n : n + 1] == [ANY_SPEC] else x
    args = [stay(n, x) for n, x in enumerate(args)]
    return pl.pallas_call(
        lambda *refs: kernel(Here(), *refs),
        in_specs=list(specs) + [full(x) for x in args[len(specs) :]],
        out_specs=[full(x) for x in out_shape],
        out_shape=out_shape,
        scratch_shapes=list(scratch),
        compiler_params=pltpu.CompilerParams(vmem_limit_bytes=limit << 20),
        cost_estimate=pl.CostEstimate(flops=int(us * 1.1e9), bytes_accessed=0, transcendentals=0),
        name=name,
    )(*args)


def softplus(v):
    return jnp.maximum(v, 0.0) + jnp.log1p(jnp.exp(-jnp.abs(v)))


def tile_at(start, size=LANES):
    return pl.ds(pl.multiple_of(start, LANES), size)


def step_rows(t):
    return pl.ds(pl.multiple_of(t * SUBS, SUBS), SUBS)


def tap_masks(starts_ref, taps, length):
    row = lax.broadcasted_iota(jnp.int32, (length, LANES), 0)
    place = lax.axis_index("seq") * length + (row % SUBS) * (length // SUBS) + row // SUBS
    begin = jnp.zeros_like(place)
    reset = jnp.zeros((length, LANES), f32)
    for k in range(starts_ref.shape[1]):
        start = starts_ref[0, k]
        begin = jnp.maximum(begin, jnp.where(place >= start, start, 0))
        reset = jnp.where(place == start, 1.0, reset)
    return [reset] + [jnp.where(begin <= place - j, 1.0, 0.0) for j in range(1, taps)]


def turned(x, plain):
    length = x.shape[0]
    steps = length // SUBS
    a = lax.broadcasted_iota(jnp.int32, (length, length), 1 - plain)
    b = lax.broadcasted_iota(jnp.int32, (length, length), plain + 0)
    turn = jnp.where(b == (a % steps) * SUBS + a // steps, 1.0, 0.0).astype(bf16)
    return nn(turn, x).astype(bf16)


def spread(maps, table_ref, first, width):
    high = maps.astype(bf16)
    rest = maps - high.astype(f32)
    middle = rest.astype(bf16)
    low = (rest - middle.astype(f32)).astype(bf16)
    row = lax.broadcasted_iota(jnp.int32, (LANES, width * LANES), 0)
    lane = lax.broadcasted_iota(jnp.int32, (LANES, width * LANES), 1)
    ones = jnp.where(row == first + lane // LANES, 1.0, 0.0).astype(bf16)
    table_ref[...] = nn(high, ones) + nn(middle, ones) + nn(low, ones)


def sub_scan(decay, value, forward):
    row = lax.broadcasted_iota(jnp.int32, decay.shape, 0)
    if not forward:
        row = SUBS - 1 - row

    def moved(x, by, fill):
        return jnp.where(row < by, fill, pltpu.roll(x, by if forward else SUBS - by, 0))

    by = 1
    while by < SUBS:
        d, v = moved(decay, by, 1.0), moved(value, by, 0.0)
        value = decay * v + value
        decay = decay * d
        by *= 2
    return value, moved(decay, 1, 1.0), moved(value, 1, 0.0)


def conv_windows(ext, taps, length):
    return [ext[(taps - 1 - j) * SUBS : (taps - 1 - j) * SUBS + length] for j in range(taps)]


def conv_sum(windows, masks, vec_ref, at, taps):
    out = vec_ref[pl.ds(taps, 1), at] + vec_ref[pl.ds(taps - 1, 1), at] * windows[0]
    for j in range(1, taps):
        out = out + vec_ref[pl.ds(taps - 1 - j, 1), at] * windows[j] * masks[j]
    return out


def normalise(x, gain):
    wide = x.astype(f32)
    inv = lax.rsqrt(jnp.mean(wide * wide, axis=-1, keepdims=True) + epsilon)
    return (wide * inv * gain).astype(bf16)


def front_kernel(
    states, rank, taps,
    here, starts_hbm, tok_hbm, cot_hbm, gain_hbm, convw_hbm, convb_hbm, dtb_hbm, skip_hbm, alog_hbm, dtw_hbm, wx_hbm,
    win_hbm, wo_hbm, left_ref,
    tok_out, cot_out, ext_ref, inner_ref, gate_ref, ggated_ref, gs_ref, dt_ref, proj_ref, table, pack_ref,
    dx_ref, ex_ref, db_ref, fx_ref, vec_ref, rates_ref, gain_ref, masks, *rest,
):
    (normed, dtm_s, u_s, ends, starts_ref, tok_ref, cot_ref, gain_s, convw_s, convb_s, dtb_s, skip_s, alog_s, dtw_ref, wx_ref,
     win_ref, wo_ref, sems, wide_sems) = rest
    length, model = cot_ref.shape
    width = rates_ref.shape[1]
    steps = length // SUBS
    rim = taps - 1
    maps = rank + 2 * states
    block = min(512, width)
    pairs = (
        (tok_hbm.at[0], tok_ref), (gain_hbm, gain_s), (cot_hbm.at[0], cot_ref), (convw_hbm, convw_s),
        (convb_hbm, convb_s), (dtb_hbm, dtb_s), (skip_hbm, skip_s), (alog_hbm, alog_s), (wx_hbm, wx_ref),
        (dtw_hbm, dtw_ref), (starts_hbm, starts_ref),
    )
    loads = [pltpu.make_async_copy(a, b, sems.at[n]) for n, (a, b) in enumerate(pairs)]

    def weights(j):
        conv = tile_at(j * block, block)
        gate = tile_at(width + j * block, block)
        return [
            pltpu.make_async_copy(win_hbm.at[:, conv], win_ref.at[:, conv], wide_sems.at[0, j]),
            pltpu.make_async_copy(win_hbm.at[:, gate], win_ref.at[:, gate], wide_sems.at[1, j]),
            pltpu.make_async_copy(wo_hbm.at[conv, :], wo_ref.at[conv, :], wide_sems.at[2, j]),
        ]

    for load in loads:
        load.start()
    for j in range(min(2, width // block)):
        for load in weights(j):
            load.start()
    for load in loads[:2]:
        load.wait()
    gain_ref[...] = gain_s[...].astype(f32).reshape(1, model)
    tok_out[pl.ds(0, length), :] = turned(tok_ref[...], False)
    left = left_ref[...].astype(f32)
    tok_out[pl.ds(length, EDGE), :] = jnp.concatenate([left, jnp.zeros((EDGE - rim, model), f32)], axis=0).astype(bf16)
    for load in loads[2:]:
        load.wait()
    vec_ref[pl.ds(0, taps), :] = convw_s[...].astype(f32)
    for n, ref in enumerate((convb_s, dtb_s, skip_s)):
        vec_ref[pl.ds(taps + n, 1), :] = ref[...].astype(f32).reshape(1, width)
    rates_ref[...] = jnp.minimum(-jnp.exp(alog_s[...]), -LEAST_RATE) * (1.0 / LN2)
    cot = turned(cot_ref[...], False)
    cot_out[...] = cot
    normed[...] = normalise(tok_out[...], gain_ref[...])
    for k, mask in enumerate(tap_masks(starts_ref, taps, length)):
        masks[k] = mask
    proj_ref[...] = jnp.zeros_like(proj_ref)

    def project(j, _):
        wide = tile_at(j * block, block)
        for load in weights(j):
            load.wait()

        @pl.when(j + 2 < width // block)
        def _():
            for load in weights(j + 2):
                load.start()

        conv = nn(normed[...], win_ref[:, wide]).astype(bf16)
        gate = nn(normed[pl.ds(0, length), :], win_ref[:, tile_at(width + j * block, block)])
        ggated = nt(cot_out[...], wo_ref[wide, :])
        gate_ref[:, wide] = gate
        ggated_ref[:, wide] = ggated
        gs_ref[:, wide] = ggated * gate * jax.nn.sigmoid(gate)
        row = lax.broadcasted_iota(jnp.int32, (SUBS, LANES), 0)
        mask = [masks[k] for k in range(taps)]
        for tile in range(block // LANES):
            far = tile_at(j * block + tile * LANES)
            part = conv[:, tile * LANES : (tile + 1) * LANES].astype(f32)
            pieces = []
            for b in range(rim):
                first = length - (rim - b) * SUBS
                moved = pltpu.roll(part[first : first + SUBS], 1, 0)
                pieces.append(jnp.where(row == 0, part[length + b : length + b + 1], moved))
            ext = jnp.concatenate(pieces + [part[:length]], axis=0)
            pad = jnp.zeros((2 * EDGE - rim * SUBS, LANES), f32)
            ext_ref[:, far] = jnp.concatenate([pad, ext], axis=0).astype(bf16)
            pre = conv_sum(conv_windows(ext, taps, length), mask, vec_ref, far, taps)
            inner_ref[:, far] = (pre * jax.nn.sigmoid(pre)).astype(bf16)
        proj_ref[:, :maps] += nt(inner_ref[:, wide], wx_ref[:, wide])
        return 0

    lax.fori_loop(0, width // block, project, 0)
    spread(proj_ref[...], table, rank, 2 * states)
    ends[...] = jnp.zeros_like(ends)
    half = states // 2
    zero = jnp.zeros((SUBS, LANES), f32)
    one = jnp.ones((SUBS, LANES), f32)
    low = proj_ref[:, :rank].astype(bf16)

    def scan(tile, _):
        at = tile_at(tile * LANES)
        dt = softplus(nn(low, dtw_ref[:, at]) + vec_ref[pl.ds(taps + 1, 1), at])
        dt_ref[:, at] = dt
        u_s[...] = dt * inner_ref[:, at].astype(f32)
        dtm = jnp.where(masks[0] > 0.0, FAR, dt)
        dtm_s[...] = dtm
        span = jnp.sum(dtm, axis=0, keepdims=True)
        high = span.astype(bf16).astype(f32)
        middle = (span - high).astype(bf16).astype(f32)
        ends[pl.ds(2 * states, 1), at] = high
        ends[pl.ds(2 * states + 1, 1), at] = middle
        ends[pl.ds(2 * states + 2, 1), at] = span - high - middle
        for first in range(0, states, half):
            rates = [jnp.broadcast_to(rates_ref[pl.ds(first + k, 1), at], (SUBS, LANES)) for k in range(half)]

            def lap(t, carry):
                h, f, p = carry
                rows = step_rows(t)
                d, u, g = dtm_s[rows, :], u_s[rows, :], gs_ref[rows, at]
                hn, fn, pn = [], [], []
                for k in range(half):
                    n = first + k
                    a = jnp.exp2(d * rates[k])
                    hn.append(a * h[k] + u * table[rows, n * LANES : (n + 1) * LANES])
                    q = p[k] * a
                    pn.append(q)
                    n += states
                    fn.append(f[k] + q * (g * table[rows, n * LANES : (n + 1) * LANES]))
                return tuple(hn), tuple(fn), tuple(pn)

            start = ((zero,) * half, (zero,) * half, (one,) * half)
            h, f, p = lax.fori_loop(0, steps, lap, start, unroll=UNROLL)
            for k in range(half):
                n = first + k
                e_in, d_ex, e_ex = sub_scan(p[k], h[k], True)
                f_in, b_ex, f_ex = sub_scan(p[k], f[k], False)
                ends[pl.ds(n, 1), at] = e_in[SUBS - 1 :, :]
                ends[pl.ds(states + n, 1), at] = f_in[:1, :]
                dx_ref[n, :, at] = d_ex
                ex_ref[n, :, at] = e_ex
                db_ref[n, :, at] = b_ex
                fx_ref[n, :, at] = f_ex
        return 0

    lax.fori_loop(0, width // LANES, scan, 0)
    pack_ref[...] = ends[...].astype(bf16)


def front(starts, tok, cot, gain, convw, convb, dtb, skip, alog, dtw, wx, in_weight, out_weight, left):
    length, model = cot.shape[1:]
    states, width = alog.shape
    rank, taps = dtw.shape[0], convw.shape[0]
    pack_rows = 2 * states + EDGE
    shape = jax.ShapeDtypeStruct
    big = lambda dtype: shape((length, width), dtype)
    out = [
        shape((length + EDGE, model), bf16), shape((length, model), bf16), shape((length + 2 * EDGE, width), bf16),
        big(bf16), big(f32), big(f32), big(f32), big(f32),
        shape((length, LANES), f32), shape((length, 2 * states * LANES), f32), shape((pack_rows, width), bf16),
    ] + [shape((states, SUBS, width), f32)] * 4 + [
        shape((taps + 4, width), f32), shape((states, width), f32), shape((1, model), f32),
        shape((taps, length, LANES), f32),
    ]
    args = (starts, tok, cot, gain, convw, convb, dtb, skip, alog, dtw, wx, in_weight, out_weight, left)
    scratch = [
        pltpu.VMEM((length + EDGE, model), bf16),
        pltpu.VMEM((length, LANES), f32),
        pltpu.VMEM((length, LANES), f32),
        pltpu.VMEM((pack_rows, width), f32),
        pltpu.SMEM(starts.shape, jnp.int32),
        pltpu.VMEM((length, model), bf16),
        pltpu.VMEM((length, model), bf16),
    ] + [pltpu.VMEM(x.shape, x.dtype) for x in args[3:13]]
    scratch += [pltpu.SemaphoreType.DMA((11,)), pltpu.SemaphoreType.DMA((3, width // min(512, width)))]
    return plain_call(
        functools.partial(front_kernel, states, rank, taps), "front", out,
        args, 20, scratch, 24, [ANY_SPEC] * 13,
    )


def chip_spot(tile, chips, tiles):
    half, chip, core = tile // (2 * chips), (tile // 2) % chips, tile % 2
    return chip, core * (tiles // (2 * chips)) + half


def forward_kernel(
    states, taps, chips, rows_size,
    here, masks, cot_ref, tok_ref, far_ref, vec_ref, rates_ref, entry_ref, table, dt_ref, inner_ref, gate_ref, ggated_ref, dx_ref, ex_ref,
    gated_ref, ggate_ref, *rest,
):
    lines, blocks, (dtm_s, u_s, y_s, held) = rest[:rows_size], rest[rows_size:-4], rest[-4:]
    length, width = inner_ref.shape
    tiles, steps = width // LANES, length // SUBS
    zero = jnp.zeros((SUBS, LANES), f32)

    def scan(tile, _):
        at = tile_at(tile * LANES)
        dt = dt_ref[:, at]
        x = inner_ref[:, at].astype(f32)
        dtm_s[...] = jnp.where(masks[0] > 0.0, FAR, dt)
        u_s[...] = dt * x

        def wide(ref, n):
            return jnp.broadcast_to(ref[pl.ds(n, 1), at], (SUBS, LANES))

        rates = [wide(rates_ref, n) for n in range(states)]
        start = tuple(dx_ref[n, :, at] * wide(entry_ref, n) + ex_ref[n, :, at] for n in range(states))

        def lap(t, h):
            rows = step_rows(t)
            d, u = dtm_s[rows, :], u_s[rows, :]
            new, y = [], [zero, zero]
            for n in range(states):
                now = jnp.exp2(d * rates[n]) * h[n] + u * table[rows, n * LANES : (n + 1) * LANES]
                y[n % 2] = y[n % 2] + now * table[rows, (states + n) * LANES : (states + n + 1) * LANES]
                new.append(now)
            y_s[rows, :] = y[0] + y[1]
            return tuple(new)

        lax.fori_loop(0, steps, lap, start, unroll=UNROLL)
        scanned = y_s[...] + vec_ref[pl.ds(taps + 2, 1), at] * x
        gate = gate_ref[:, at]
        sig = jax.nn.sigmoid(gate)
        gated_ref[:, at] = (scanned * gate * sig).astype(bf16)
        ggate = (ggated_ref[:, at] * scanned * (sig * (1.0 + gate * (1.0 - sig)))).astype(bf16)
        ggate_ref[:, at] = ggate
        if chips:
            chip, spot = chip_spot(tile, chips, tiles)
            held[chip, :, tile_at(spot * LANES)] = ggate
        return 0

    lax.fori_loop(0, tiles, scan, 0)
    for n in range(chips):
        part = held.shape[2]
        blocks[n][:, :part] = held[here[2] ^ n]
        if n == 1:
            model = cot_ref.shape[1]
            blocks[n][:, part : part + model] = tok_ref[pl.ds(0, length), :]
            blocks[n][:, part + model :] = turned(far_ref[...], False)
    thin = cot_ref.shape[1] // rows_size
    for n in range(rows_size):
        lines[n][:, :width] = gated_ref[...]
        lines[n][:, width:] = cot_ref[:, tile_at((here[1] ^ n) * thin, thin)]


def forward(masks, cot, tok, far, vec, rates, entry, table, dt, inner, gate, ggated, dx, ex, taps, chips, rows_size):
    length, width = inner.shape
    states = rates.shape[0]
    shape = jax.ShapeDtypeStruct
    return plain_call(
        functools.partial(forward_kernel, states, taps, chips, rows_size),
        "forward",
        [shape((length, width), bf16)] * 2
        + [shape((length, width + cot.shape[1] // rows_size), bf16)] * rows_size
        + [shape((length, width // max(chips, 1) + 2 * cot.shape[1] * (n == 1)), bf16) for n in range(chips)],
        (masks, cot, tok, far, vec, rates, entry, table, dt, inner, gate, ggated, dx, ex),
        8,
        [pltpu.VMEM((length, LANES), f32)] * 3 + [pltpu.VMEM((max(chips, 1), length, width // max(chips, 1)), bf16)],
        8,
    )


def backward_kernel(
    states, rank, taps, chips,
    here, win_hbm, dtw_hbm, wx_hbm, masks, proj_ref, tok_ref, gain_ref, vec_ref, rates_ref, entry_ref, arrive_ref,
    table, dt_ref, inner_ref, gs_ref, dx_ref, ex_ref, db_ref, fx_ref, ggate_ref, ext_ref,
    ngrad, *rest,
):
    blocks, rest = rest[: max(chips, 1)], rest[max(chips, 1) :]
    (acc, hs, decays, dtm_s, u_s, s1_s, s2_s, isg, raw_s, sent_s, low_acc, pg, small, held, win_ref, dtw_ref, wx_ref, sems) = rest[-18:]
    length, width = inner_ref.shape
    model = tok_ref.shape[1]
    steps, tiles = length // SUBS, width // LANES
    rim = taps - 1
    maps = rank + 2 * states
    row_dtw = maps
    row_rate = row_dtw + rank
    row_taps = row_rate + states
    row_dtb, row_skip, row_cb, row_gain = (row_taps + taps + k for k in range(4))
    zero = jnp.zeros((SUBS, LANES), f32)
    half = states // 2
    block = min(512, width)
    pairs = ((dtw_hbm, dtw_ref), (wx_hbm, wx_ref), (win_hbm, win_ref))
    loads = [pltpu.make_async_copy(a, b, sems.at[n]) for n, (a, b) in enumerate(pairs)]
    for load in loads:
        load.start()
    low_acc[...] = jnp.zeros_like(low_acc)
    small[pl.ds(small.shape[0] - EDGE, EDGE), :] = jnp.zeros((EDGE, width), f32)
    low = proj_ref[:, :rank].astype(bf16)

    def clear(t, _):
        acc[step_rows(t), :] = jnp.zeros((SUBS, acc.shape[1]), f32)
        return 0

    lax.fori_loop(0, steps, clear, 0)
    loads[0].wait()

    def scan(tile, _):
        at = tile_at(tile * LANES)
        dt = dt_ref[:, at]
        x = inner_ref[:, at].astype(f32)
        dtm_s[...] = jnp.where(masks[0] > 0.0, FAR, dt)
        u_s[...] = dt * x

        def wide(ref, n):
            return jnp.broadcast_to(ref[pl.ds(n, 1), at], (SUBS, LANES))

        rates = [wide(rates_ref, n) for n in range(states)]
        start = []
        for n in range(states):
            h0 = dx_ref[n, :, at] * wide(entry_ref, n) + ex_ref[n, :, at]
            hs[0, n] = h0
            start.append(h0)

        def lap(t, h):
            rows = step_rows(t)
            d, u = dtm_s[rows, :], u_s[rows, :]
            new = []
            for n in range(states):
                a = jnp.exp2(d * rates[n])
                decays[t, n] = a
                now = a * h[n] + u * table[rows, n * LANES : (n + 1) * LANES]
                hs[t + 1, n] = now
                new.append(now)
            return tuple(new)

        lax.fori_loop(0, steps, lap, tuple(start), unroll=UNROLL)
        for first in range(0, states, half):
            some = rates[first : first + half]

            def back(k, carry):
                f, r = carry
                t = steps - 1 - k
                rows = step_rows(t)
                dtt, g, u = dt_ref[rows, at], gs_ref[rows, at], u_s[rows, :]
                fn, rn, s1, s2 = [], [], zero, zero
                for k in range(half):
                    n = first + k
                    into, out = (slice(m * LANES, (m + 1) * LANES) for m in (n, states + n))
                    adj = g * table[rows, out] + f[k]
                    acc[rows, into] += adj * u
                    acc[rows, out] += g * hs[t + 1, n]
                    s1 = s1 + adj * table[rows, into]
                    flow = decays[t, n] * adj
                    fn.append(flow)
                    flow = flow * hs[t, n]
                    s2 = s2 + flow * some[k]
                    rn.append(r[k] + flow * dtt)
                if first == 0:
                    s1_s[rows, :] = s1
                    s2_s[rows, :] = s2
                else:
                    s1_s[rows, :] += s1
                    s2_s[rows, :] += s2
                return tuple(fn), tuple(rn)

            f0 = tuple(
                db_ref[first + k, :, at] * wide(arrive_ref, first + k) + fx_ref[first + k, :, at] for k in range(half)
            )
            _, r = lax.fori_loop(0, steps, back, (f0, (zero,) * half), unroll=UNROLL)
            for k in range(half):
                small[pl.ds(row_rate + first + k, 1), at] = jnp.sum(r[k], axis=0, keepdims=True)
        s1, gs = s1_s[...], gs_ref[:, at]
        step_grad = s1 * x + LN2 * s2_s[...]
        isg[:, at] = s1 * dt + gs * vec_ref[pl.ds(taps + 2, 1), at]
        raw = nn(low, dtw_ref[:, at]) + vec_ref[pl.ds(taps + 1, 1), at]
        raw_grad = step_grad * jax.nn.sigmoid(raw)
        raw_s[:, at] = raw_grad.astype(bf16)
        small[pl.ds(row_dtb, 1), at] = jnp.sum(raw_grad, axis=0, keepdims=True)
        small[pl.ds(row_skip, 1), at] = jnp.sum(gs * x, axis=0, keepdims=True)
        return 0

    lax.fori_loop(0, tiles, scan, 0)

    def low_part(j, _):
        wide = tile_at(j * block, block)
        small[pl.ds(row_dtw, rank), wide] = tn(low, raw_s[:, wide])
        low_acc[:, :rank] += nt(raw_s[:, wide], dtw_ref[:, wide])
        return 0

    lax.fori_loop(0, width // block, low_part, 0)
    wide_row = lax.broadcasted_iota(jnp.int32, (2 * states * LANES, LANES), 0)
    wide_lane = lax.broadcasted_iota(jnp.int32, (2 * states * LANES, LANES), 1)
    ones = jnp.where(wide_lane == rank + wide_row // LANES, 1.0, 0.0).astype(bf16)
    high = acc[...].astype(bf16)
    low_acc[...] += nn(high, ones) + nn((acc[...] - high.astype(f32)).astype(bf16), ones)
    pg[...] = low_acc[...].astype(bf16)
    for load in loads[1:]:
        load.wait()
    ngrad[...] = jnp.zeros_like(ngrad)

    def close(j, _):
        wide = tile_at(j * block, block)
        ngrad[pl.ds(0, length), :] += nt(ggate_ref[:, wide], win_ref[:, tile_at(width + j * block, block)])
        small[pl.ds(0, maps), wide] = tn(pg[...], inner_ref[:, wide])[:maps]
        inner_grad = isg[:, wide] + nn(pg[:, :maps], wx_ref[:, wide])
        mask = [masks[k] for k in range(taps)]
        row = lax.broadcasted_iota(jnp.int32, (SUBS, LANES), 0)
        for tile in range(block // LANES):
            far = tile_at(j * block + tile * LANES)
            ext = ext_ref[:, far].astype(f32)[2 * EDGE - rim * SUBS :]
            windows = conv_windows(ext, taps, length)
            pre = conv_sum(windows, mask, vec_ref, far, taps)
            sig = jax.nn.sigmoid(pre)
            grad = inner_grad[:, tile * LANES : (tile + 1) * LANES] * (sig * (1.0 + pre * (1.0 - sig)))
            small[pl.ds(row_cb, 1), far] = jnp.sum(grad, axis=0, keepdims=True)
            small[pl.ds(row_taps + rim, 1), far] = jnp.sum(grad * windows[0], axis=0, keepdims=True)
            near = [grad[step * SUBS : (step + 1) * SUBS] * vec_ref[pl.ds(rim, 1), far] for step in range(steps)]
            head = [zero] * rim
            for k in range(1, taps):
                masked = grad * mask[k]
                small[pl.ds(row_taps + rim - k, 1), far] = jnp.sum(masked * windows[k], axis=0, keepdims=True)
                masked = masked * vec_ref[pl.ds(rim - k, 1), far]
                for step in range(steps):
                    piece = masked[step * SUBS : (step + 1) * SUBS]
                    if step >= k:
                        near[step - k] = near[step - k] + piece
                    else:
                        head[rim + step - k] = head[rim + step - k] + piece
            edge = zero
            for b in range(rim):
                moved = jnp.where(row == SUBS - 1, 0.0, pltpu.roll(head[b], SUBS - 1, 0))
                near[steps - rim + b] = near[steps - rim + b] + moved
                edge = jnp.where(row == b, jnp.broadcast_to(head[b][:1], (SUBS, LANES)), edge)
            sent = jnp.concatenate(near + [edge, zero], axis=0)
            sent_s[:, tile * LANES : (tile + 1) * LANES] = sent.astype(bf16)
            if chips:
                chip, spot = chip_spot(j * (block // LANES) + tile, chips, tiles)
                held[chip, :, tile_at(spot * LANES)] = sent.astype(bf16)
            else:
                blocks[0][:, far] = sent.astype(bf16)
        ngrad[...] += nt(sent_s[...], win_ref[:, wide])
        return 0

    lax.fori_loop(0, width // block, close, 0)
    x = tok_ref[...].astype(f32)
    inv = lax.rsqrt(jnp.mean(x * x, axis=-1, keepdims=True) + epsilon)
    small[pl.ds(row_gain, 1), pl.ds(0, model)] = jnp.sum(ngrad[...] * (x * inv), axis=0, keepdims=True)
    if chips:
        part = width // chips
        row = lax.broadcasted_iota(jnp.int32, (EDGE, part), 0)
        extra = jnp.zeros((EDGE, part), f32)
        normed = x[length:] * inv[length:] * gain_ref[...]
        count = model // part
        for b in range(rim):
            for c in range(count):
                piece = jnp.broadcast_to(normed[b : b + 1, c * part : (c + 1) * part], (EDGE, part))
                extra = jnp.where(row == rim + b * count + c, piece, extra)
        edge_rows = pl.ds(length, EDGE)
        for n in range(chips):
            held[n, edge_rows, :] = (held[n, edge_rows, :].astype(f32) + extra).astype(bf16)
        for n in range(chips):
            blocks[n][...] = held[here[2] ^ n]
    mine_ref, theirs_ref = rest[:2]
    chunk = mine_ref.shape[2]
    for c in range(2):

        @pl.when(here[0] == c)
        def _():
            for n in range(mine_ref.shape[0]):
                at, other = (2 * n + c) * chunk, (2 * n + 1 - c) * chunk
                mine_ref[n] = small[:, at : at + chunk]
                theirs_ref[n] = small[:, other : other + chunk].astype(bf16)


def backward(masks, in_weight, dtw, wx, proj, tok, gain, vec, rates, entry, arrive, table, dt, inner, gs, deep4,
             ggate, ext, taps, chips, chunks):
    length, width = inner.shape
    model = tok.shape[1]
    states = rates.shape[0]
    rank = dtw.shape[0]
    block = min(512, width)
    steps = length // SUBS
    rows = 2 * rank + 3 * states + taps + 4
    rows = -(-rows // EDGE) * EDGE
    shape = jax.ShapeDtypeStruct
    parts = max(chips, 1)
    chunk = (chunks, rows, width // (2 * chunks))
    return plain_call(
        functools.partial(backward_kernel, states, rank, taps, chips),
        "backward",
        [shape((length + EDGE, model), f32)]
        + [shape((length + EDGE, width // parts), bf16)] * parts
        + [shape(chunk, f32), shape(chunk, bf16)],
        (in_weight, dtw, wx, masks, proj, tok, gain, vec, rates, entry, arrive, table, dt, inner, gs, *deep4, ggate, ext),
        24,
        [
            pltpu.VMEM((length, 2 * states * LANES), f32),
            pltpu.VMEM((steps + 1, states, SUBS, LANES), f32),
            pltpu.VMEM((steps, states, SUBS, LANES), f32),
        ]
        + [pltpu.VMEM((length, LANES), f32)] * 4
        + [
            pltpu.VMEM((length, width), f32),
            pltpu.VMEM((length, width), bf16),
            pltpu.VMEM((length + EDGE, block), bf16),
            pltpu.VMEM((length, LANES), f32),
            pltpu.VMEM((length, LANES), bf16),
            pltpu.VMEM((rows, width), f32),
            pltpu.VMEM((parts, length + EDGE, width // parts), bf16),
        ]
        + [pltpu.VMEM(x.shape, x.dtype) for x in (in_weight, dtw, wx)]
        + [pltpu.SemaphoreType.DMA((3,))],
        24,
        [ANY_SPEC] * 3,
    )


def finish_kernel(rim, here, ngrad_ref, back_ref, tok_ref, cot_ref, gain_ref, gated_ref, wo_ref, grad_ref, mixed_ref):
    length = cot_ref.shape[0]
    x = tok_ref[pl.ds(0, length), :].astype(f32)
    mixed_ref[...] = turned((x + nn(gated_ref[...], wo_ref[...])).astype(bf16), True)
    inv = lax.rsqrt(jnp.mean(x * x, axis=-1, keepdims=True) + epsilon)
    scaled = x * inv
    row = lax.broadcasted_iota(jnp.int32, (SUBS, x.shape[1]), 0)
    pieces = [ngrad_ref[pl.ds(0, length - rim * SUBS), :]]
    for b in range(rim):
        late = jnp.where(row == SUBS - 1, back_ref[pl.ds(b, 1), :], 0.0)
        pieces.append(ngrad_ref[pl.ds(length - (rim - b) * SUBS, SUBS), :] + late)
    hat = jnp.concatenate(pieces, axis=0) * gain_ref[...]
    grad = cot_ref[...].astype(f32) + inv * (hat - scaled * jnp.mean(hat * scaled, axis=-1, keepdims=True))
    grad_ref[...] = turned(grad.astype(bf16), True)


def span_of(x, states):
    return x[2 * states : 2 * states + 1] + x[2 * states + 1 : 2 * states + 2] + x[2 * states + 2 : 2 * states + 3]


def span_rows(d):
    high = d.astype(bf16).astype(f32)
    middle = (d - high).astype(bf16).astype(f32)
    row = lax.broadcasted_iota(jnp.int32, (EDGE, d.shape[1]), 0)
    return jnp.where(row == 0, high, jnp.where(row == 1, middle, jnp.where(row == 2, d - high - middle, 0.0)))


def pair_parts(here, mine, other, rates, states):
    first = here[0] == 0
    near, far = jnp.where(first, mine, other), jnp.where(first, other, mine)
    d0, d1 = span_of(near, states), span_of(far, states)
    state = jnp.exp2(rates * d1) * near[:states] + far[:states]
    flow = near[states : 2 * states] + jnp.exp2(rates * d0) * far[states : 2 * states]
    return state, flow, span_rows(d0 + d1)


def pair_kernel(states, here, mine_ref, other_ref, rates_ref, out_ref):
    state, flow, spans = pair_parts(
        here, mine_ref[...].astype(f32), other_ref[...].astype(f32), rates_ref[...], states
    )
    out_ref[...] = jnp.concatenate([state, flow, spans], axis=0).astype(bf16)


def pair_half_kernel(states, here, mine_ref, other_ref, rates_ref, out_ref):
    half = rates_ref.shape[1] // 2
    at = tile_at(here[0] * half, half)
    parts = pair_parts(here, mine_ref[:, at].astype(f32), other_ref[:, at].astype(f32), rates_ref[:, at], states)
    out_ref[...] = jnp.concatenate(parts, axis=0).astype(bf16)


def quad_kernel(states, here, mine_ref, got_ref, rates_ref, near_ref, out_ref):
    half = rates_ref.shape[1] // 2
    rates = rates_ref[:, tile_at(here[0] * half, half)]
    mine, got = mine_ref[...].astype(f32), got_ref[...].astype(f32)
    first = here[2] % 2 == 0
    low, high = jnp.where(first, mine, got), jnp.where(first, got, mine)
    d0, d1 = span_of(low, states), span_of(high, states)
    w0, w1 = jnp.exp2(rates * d0), jnp.exp2(rates * d1)
    near_ref[pl.ds(0, states), :] = jnp.where(first, 0.0, low[:states])
    near_ref[pl.ds(states, states), :] = jnp.where(first, high[states : 2 * states], 0.0)
    near_ref[pl.ds(2 * states, states), :] = jnp.where(first, 1.0, w0)
    near_ref[pl.ds(3 * states, states), :] = jnp.where(first, w1, 1.0)
    state = w1 * low[:states] + high[:states]
    flow = low[states : 2 * states] + w0 * high[states : 2 * states]
    out_ref[...] = jnp.where(here[2] < 2, state, flow).astype(bf16)


def enter_half_kernel(states, here, near_ref, got_ref, out_ref):
    got = got_ref[...].astype(f32)
    low = here[2] < 2
    entry = near_ref[pl.ds(0, states), :] + jnp.where(low, 0.0, near_ref[pl.ds(2 * states, states), :] * got)
    arrive = near_ref[pl.ds(states, states), :] + jnp.where(low, near_ref[pl.ds(3 * states, states), :] * got, 0.0)
    out_ref[...] = jnp.concatenate([entry, arrive], axis=0)


def enter_both_kernel(states, here, other_ref, rates_ref, here_ref, there_ref, entry_ref, arrive_ref):
    core = here[0]
    half = rates_ref.shape[1] // 2
    for part, side in ((here_ref, core), (there_ref, 1 - core)):
        at = tile_at(side * half, half)
        other = other_ref[:, at].astype(f32)
        whole = jnp.exp2(rates_ref[:, at] * span_of(other, states))
        entry, arrive = part[pl.ds(0, states), :], part[pl.ds(states, states), :]
        entry_ref[:, at] = jnp.where(core == 1, whole * entry + other[:states], entry)
        arrive_ref[:, at] = jnp.where(core == 0, whole * arrive + other[states : 2 * states], arrive)


def enter_kernel(states, count, here, other_ref, rates_ref, chips_ref, entry_ref, arrive_ref):
    core, place = here[0], here[2]
    rates = rates_ref[...]

    def split(x):
        return x[:states], x[states : 2 * states], jnp.exp2(rates * span_of(x, states))

    def lap(k, carry):
        entry, arrive = carry
        s, _, whole = split(chips_ref[k].astype(f32))
        entry = jnp.where(k < place, whole * entry + s, entry)
        back = count - 1 - k
        _, f, whole = split(chips_ref[back].astype(f32))
        arrive = jnp.where(back > place, whole * arrive + f, arrive)
        return entry, arrive

    entry, arrive = lax.fori_loop(0, count, lap, (jnp.zeros_like(rates), jnp.zeros_like(rates)))
    s, f, whole = split(other_ref[...].astype(f32))
    entry_ref[...] = jnp.where(core == 1, whole * entry + s, entry)
    arrive_ref[...] = jnp.where(core == 0, whole * arrive + f, arrive)


def out_kernel(size, chips, thin, here, *rest):
    parts, (mine_ref, theirs_ref) = rest[:size], rest[size:]
    model = mine_ref.shape[2]
    width = parts[0].shape[1] - 2 * chips * thin
    left = jnp.concatenate([x[:, width:] for x in parts], axis=0)
    out = tn(left, jnp.concatenate([x[:, :width] for x in parts], axis=0))
    for c in range(2):

        @pl.when(here[0] == c)
        def _():
            for q in range(chips):
                for ref, side in ((mine_ref, c), (theirs_ref, 1 - c)):
                    at = (2 * q + side) * thin
                    for n in range(width // model):
                        piece = out[at : at + thin, n * model : (n + 1) * model]
                        ref[q, pl.ds(n * thin, thin), :] = piece.astype(ref.dtype)


def split_cores(here, x, mine_ref, theirs_ref):
    count, rows = mine_ref.shape[:2]
    for c in range(2):

        @pl.when(here[0] == c)
        def _():
            for n in range(count):
                mine_ref[n] = x[(c * count + n) * rows : (c * count + n + 1) * rows]
                theirs_ref[n] = x[((1 - c) * count + n) * rows : ((1 - c) * count + n + 1) * rows].astype(bf16)


def gate_kernel(here, gain_ref, tok_ref, far_ref, *rest):
    gots, (normed_ref, mine_ref, theirs_ref) = rest[:-3], rest[-3:]
    length, part = gots[0].shape
    model = gain_ref.shape[1]
    near = gots[1]
    toks = (
        tok_ref[pl.ds(0, length), :],
        near[:, part : part + model],
        turned(far_ref[...], False),
        near[:, part + model :],
    )
    for k, x in enumerate(toks):
        normed_ref[pl.ds(k * length, length), :] = normalise(x, gain_ref[...])
    got = jnp.concatenate([x[:, :part] for x in gots], axis=0)
    split_cores(here, tn(got, normed_ref[...]), mine_ref, theirs_ref)


def flat(x, pieces):
    rows = x.shape[0] // pieces
    return jnp.concatenate([x[n * rows : (n + 1) * rows] for n in range(pieces)], axis=1)


def tall(x, pieces):
    lanes = x.shape[1] // pieces
    return jnp.concatenate([x[:, n * lanes : (n + 1) * lanes] for n in range(pieces)], axis=0)


def conv_kernel(length, rim, here, normed_ref, *rest):
    gots, (mine_ref, theirs_ref) = rest[:-2], rest[-2:]
    wide = gots[0].shape[1]
    model = normed_ref.shape[1]
    pieces = model // wide
    got = jnp.concatenate([got[pl.ds(0, length), :] for got in gots], axis=0)
    lefts, rights = [], []
    for k in range(len(gots)):
        edge = gots[k][pl.ds(length, EDGE), :].astype(f32)
        row = lax.broadcasted_iota(jnp.int32, (SUBS, model), 0)
        left = jnp.zeros((SUBS, model), f32)
        for b in range(rim):
            at = rim + b * pieces
            one = jnp.concatenate([edge[at + c : at + c + 1] for c in range(pieces)], axis=1)
            left = jnp.where(row == b, jnp.broadcast_to(one, left.shape), left)
        lefts.append(left)
        right = edge[:SUBS]
        rights.append(jnp.where(lax.broadcasted_iota(jnp.int32, right.shape, 0) < rim, right, 0.0))
    left, right = (jnp.concatenate(x, axis=0).astype(bf16) for x in (lefts, rights))
    conv = tn(got, normed_ref[...]) + tn(right, left)
    split_cores(here, conv, mine_ref, theirs_ref)


def halve_kernel(which, bit, here, mine_ref, got_ref, keep_ref, send_ref):
    place = (here[which] >> bit) & 1
    for n in range(mine_ref.shape[0] // 2):
        stay, leave = 2 * n + place, 2 * n + 1 - place
        keep_ref[n] = mine_ref[stay] + got_ref[stay].astype(f32)
        send_ref[n] = (mine_ref[leave] + got_ref[leave].astype(f32)).astype(bf16)


def small_last_kernel(here, mine_ref, got_ref, out_ref):
    small = mine_ref[0] + got_ref[0].astype(f32)
    out_ref[...] = flat(small, out_ref.shape[1] // small.shape[1]).astype(bf16)


def add_kernel(here, mine_ref, got_ref, out_ref):
    out_ref[...] = (mine_ref[...].astype(f32) + got_ref[...].astype(f32)).astype(bf16)


def in_merge_kernel(here, conv_mine, conv_got, gate_mine, gate_got, small_ref, own_ref, *parts):
    count, rows = conv_mine.shape[:2]
    for part in parts:
        part[pl.ds(rows, small_ref.shape[0]), :] = small_ref[...]
    for mine, got, first in ((conv_mine, conv_got, 0), (gate_mine, gate_got, count)):
        for n in range(count):
            both = mine[n] + got[n].astype(f32)
            for k in range(2 * count):

                @pl.when((here[1] ^ k) == first + n)
                def _():
                    if k == 0:
                        own_ref[...] = both
                    else:
                        parts[k - 1][pl.ds(0, rows), :] = both.astype(bf16)


def in_last_kernel(here, own_ref, small_ref, *rest):
    gots, (out_ref, small_out) = rest[:-2], rest[-2:]
    both, rows = own_ref[...], own_ref.shape[0]
    small_out[here[1]] = small_ref[...]
    for k, got in enumerate(gots):
        both = both + got[pl.ds(0, rows), :].astype(f32)
        small_out[here[1] ^ (k + 1)] = got[pl.ds(rows, small_ref.shape[0]), :]
    out_ref[...] = both.T


def out_last_kernel(here, mine_ref, got_ref, out_ref):
    thin, model = out_ref.shape[0], mine_ref.shape[2]
    both = mine_ref[0] + got_ref[0].astype(f32)
    for n in range(out_ref.shape[1] // model):
        out_ref[:, n * model : (n + 1) * model] = both[n * thin : (n + 1) * thin]


def unpack_kernel(edges, here, rates_ref, mine_ref, other_ref, *outs):
    size = mine_ref.shape[0]
    chunk = rates_ref.shape[1] // (2 * size)
    pieces = mine_ref.shape[2] // chunk
    for c, part in ((here[0], mine_ref), (1 - here[0], other_ref)):
        for k in range(size):
            at = tile_at((2 * k + c) * chunk, chunk)
            block = tall(part[k].astype(f32), pieces)
            for n, out in enumerate(outs):
                piece = block[edges[n] : edges[n + 1]]
                if (2 * k + 1) * chunk < out.shape[1]:
                    out[:, at] = piece * rates_ref[:, at] if n == 2 else piece


class Group:
    def __init__(self, axis, size, stride):
        self.axis, self.size, self.stride = axis, size, stride
        self.direct = size <= 4
        self.place = (lax.axis_index(axis) // stride) % size

    def lists(self):
        n = lax.axis_size(self.axis)
        span = self.stride * self.size
        return [
            [base + low + self.stride * k for k in range(self.size)]
            for base in range(0, n, span)
            for low in range(self.stride)
        ]

    def swap(self, x, k):
        n = lax.axis_size(self.axis)
        return lax.ppermute(x, self.axis, [(i, i ^ (k * self.stride)) for i in range(n)])

    def exchange(self, blocks):
        if not self.direct:
            got = lax.all_to_all(blocks, self.axis, 0, 0, axis_index_groups=self.lists(), tiled=True)
            return [got[k] for k in range(self.size)]
        pick = lambda k: lax.dynamic_index_in_dim(blocks, self.place ^ k, 0, keepdims=False)
        return [pick(0)] + [self.swap(pick(k), k) for k in range(1, self.size)]

    def trade(self, blocks):
        if not self.direct:
            return self.exchange(jnp.stack(blocks))
        return [blocks[0]] + [self.swap(blocks[k], k) for k in range(1, self.size)]

    def gather(self, x):
        if not self.direct:
            got = lax.all_gather(x, self.axis, axis_index_groups=self.lists())
            return [got[k] for k in range(self.size)]
        return [x] + [self.swap(x, k) for k in range(1, self.size)]

    def sender(self, k):
        return self.place ^ k if self.direct else k

    def in_order(self, parts):
        if not self.direct:
            return jnp.stack(parts)
        stacked = jnp.stack(parts)
        return jnp.stack(
            [lax.dynamic_index_in_dim(stacked, self.place ^ q, 0, keepdims=False) for q in range(self.size)]
        )


def total(parts):
    return functools.reduce(lambda a, b: a + b, [part.astype(f32) for part in parts])


def body(
    tokens,
    cotangent,
    doc_starts,
    in_weight,
    conv_weight,
    conv_bias,
    xproj_weight,
    dt_weight,
    dt_bias,
    a_log,
    skip_scale,
    out_weight,
    norm_gain,
):
    length, model = tokens.shape[1:]
    inner_width, states = a_log.shape
    low_rank = dt_weight.shape[0]
    taps = conv_weight.shape[1]
    rim = taps - 1
    dp_size, seq_size = lax.axis_size("dp"), lax.axis_size("seq")
    core, outer = Group("seq", 2, 1), Group("seq", seq_size // 2, 2)
    rows_group = Group("dp", dp_size, 1)
    width = in_weight.shape[1] // (dp_size * seq_size)
    half_rows = dp_size // 2
    thin = model // (dp_size * seq_size)
    part = inner_width // outer.size
    tiled = outer.size == 4 and dp_size == 4 and width == LANES and thin % EDGE == 0
    tiled = tiled and model % part == 0 and rim * (1 + model // part) <= EDGE
    chips = outer.size if tiled else 0
    shape = jax.ShapeDtypeStruct

    wx = xproj_weight.T
    decay_rates = -jnp.exp(a_log).T

    edge = tokens[0, length - rim :]
    left = lax.ppermute(edge, "seq", [(i, i + 1) for i in range(seq_size - 1)])
    tok, cot, ext, inner, gate, ggated, gs, dt, proj, table, mine, dx, ex, db, fx, vec, rates, gain, masks = front(
        doc_starts, tokens, cotangent, norm_gain, conv_weight.T, conv_bias, dt_bias, skip_scale, a_log.T, dt_weight, wx,
        in_weight, out_weight, left,
    )
    beyond = cot
    if tiled:
        after, _ = lax.optimization_barrier((tokens[0], edge))
        beyond = outer.swap(after, 2)
        mine, beyond = lax.optimization_barrier((mine, beyond))
    other = core.swap(mine, 1)
    entering = [shape(rates.shape, f32)] * 2
    if tiled:
        half = inner_width // 2
        (mine_half,) = plain_call(
            functools.partial(pair_half_kernel, states),
            "pair",
            [shape((2 * states + EDGE, half), bf16)],
            (mine, other, rates),
            1,
        )
        near, far = plain_call(
            functools.partial(quad_kernel, states),
            "quad",
            [shape((4 * states, half), f32), shape((states, half), bf16)],
            (mine_half, outer.swap(mine_half, 1), rates),
            1,
        )
        (here,) = plain_call(
            functools.partial(enter_half_kernel, states),
            "enter_half",
            [shape((2 * states, half), f32)],
            (near, outer.swap(far, 2)),
            1,
        )
        entry, arrive = plain_call(
            functools.partial(enter_both_kernel, states), "enter", entering, (other, rates, here, core.swap(here, 1)), 1
        )
    else:
        (chip,) = plain_call(
            functools.partial(pair_kernel, states), "pair", [shape(mine.shape, bf16)], (mine, other, rates), 2
        )
        got = outer.in_order(outer.gather(chip))
        entry, arrive = plain_call(
            functools.partial(enter_kernel, states, outer.size), "enter", entering, (other, rates, got), 2
        )
    gated, ggate, *late = forward(masks, cot, tok, beyond, vec, rates, entry, table, dt, inner, gate, ggated, dx, ex, taps, chips, dp_size)
    lines_got = rows_group.trade(late[:dp_size])
    gate_got = outer.trade(late[dp_size:]) if tiled else None

    ngrad, *sent, small, small_theirs = backward(
        masks, in_weight, dt_weight, wx, proj, tok, gain, vec, rates, entry, arrive, table, dt, inner, gs,
        (dx, ex, db, fx), ggate, ext, taps, chips, dp_size,
    )
    rows, chunk = small.shape[1:]
    turn = [ngrad]

    def call(kernel, name, outs, args, us=2):
        args = tuple(args)
        got = plain_call(kernel, name, [shape(*x) for x in outs], args, us)
        turn[0] = got[0]
        return got

    def halve(group, bit, which, mine, got, name):
        count, *rest = mine.shape
        outs = [((count // 2, *rest), f32), ((count // 2, *rest), bf16)]
        keep, send = call(functools.partial(halve_kernel, which, bit), name, outs, (mine, got))
        return keep, group.swap(send, 1 << bit)

    lines = rows * chunk // model
    part = ((lines, model), bf16)
    back = lax.ppermute(ngrad[length:], "seq", [(i, i - 1) for i in range(1, seq_size)])

    def finished():
        return call(
            functools.partial(finish_kernel, rim),
            "finish",
            [((length, model), bf16)] * 2,
            (ngrad, back, tok, cot, gain, gated, out_weight),
        )

    if tiled:
        blocks = (half_rows, width, model)
        sent, small_theirs, *early_got = lax.optimization_barrier((sent, small_theirs, *lines_got, *gate_got[:-1]))
        lines_got, gate_got = early_got[:dp_size], early_got[dp_size:] + gate_got[-1:]
        small_got = core.swap(small_theirs, 1)
        conv_got = outer.trade(sent)
        small, small_got = halve(rows_group, 0, 1, small, small_got, "small_row0")
        block = (chips, LANES // 2, model)
        out, theirs = call(
            functools.partial(out_kernel, dp_size, chips, thin),
            "out_columns",
            [(block, f32), (block, bf16)],
            lines_got,
        )
        out_got = core.swap(theirs, 1)
        small, small_got = halve(rows_group, 1, 1, small, small_got, "small_row1")
        normed, gate, theirs = call(
            gate_kernel,
            "gate_columns",
            [((chips * length, model), bf16), (blocks, f32), (blocks, bf16)],
            (gain, tok, beyond, *gate_got),
        )
        gate_got = core.swap(theirs, 1)
        (small,) = call(small_last_kernel, "small_last", [part], (small, small_got))
        small_got = outer.swap(small, 1)
        conv, theirs = call(
            functools.partial(conv_kernel, length, rim), "conv_columns", [(blocks, f32), (blocks, bf16)], (normed, *conv_got)
        )
        conv_got = core.swap(theirs, 1)
        (small,) = call(add_kernel, "small_chip0", [part], (small, small_got))
        small_got = outer.swap(small, 2)
        (small,) = call(add_kernel, "small_chip1", [part], (small, small_got))
        slab = (width, model)
        in_own, *sends = call(
            in_merge_kernel,
            "in_merge",
            [(slab, f32)] + [((width + lines, model), bf16)] * (dp_size - 1),
            (conv, conv_got, gate, gate_got, small),
        )
        in_own, *in_gots = rows_group.trade([in_own] + sends)
        out, out_got = halve(outer, 0, 2, out, out_got, "out_chip0")
        tokens_grad, mixed = finished()
        out, out_got = halve(outer, 1, 2, out, out_got, "out_chip1")
        outs = [((model, width), f32), ((dp_size, lines, model), bf16)]
        in_share, small = call(in_last_kernel, "in_last", outs, (in_own, small, *in_gots))
        small_other = core.swap(small, 1)
        (out_share,) = call(out_last_kernel, "out_last", [((thin, inner_width), f32)], (out, out_got))
    else:
        tokens_grad, mixed = finished()
        small = small + core.swap(small_theirs, 1).astype(f32)
        small = total(rows_group.exchange(small.astype(bf16)))
        small = total(outer.gather(small.astype(bf16))).astype(bf16)
        small = small.reshape(rows // lines, lines, -1).swapaxes(0, 1).reshape(lines, model)
        small = rows_group.in_order(rows_group.gather(small))
        small_other = core.swap(small, 1)
    sizes = [low_rank + 2 * states, low_rank, states, taps, 1, 1, 1, 1]
    edges = [sum(sizes[:k]) for k in range(len(sizes) + 1)]
    parts = call(
        functools.partial(unpack_kernel, edges),
        "unpack",
        [((size, inner_width), f32) for size in sizes[:-1]] + [((1, model), f32)],
        (decay_rates, small, small_other),
    )
    if not tiled:

        def normalised(x):
            wide = x.astype(f32)
            inv = lax.rsqrt(jnp.mean(wide * wide, axis=-1, keepdims=True) + epsilon)
            return (wide * inv * gain).astype(bf16)

        def summed(lefts, rights):
            return functools.reduce(lambda a, b: a + b, [tn(a, b) for a, b in zip(lefts, rights, strict=True)])

        def halved(x):
            return x.astype(bf16).reshape(model, 2, -1).swapaxes(0, 1)

        def by_chip(x):
            blocks = x.reshape(x.shape[0], half_rows, outer.size, 2, width)
            return outer.exchange(blocks.transpose(2, 0, 3, 1, 4).reshape(outer.size, x.shape[0], -1))

        normed_parts = [normalised(x) for x in outer.gather(tok)]
        gate_core = total(core.exchange(halved(summed([x[:length] for x in normed_parts], by_chip(ggate)))))
        conv_core = total(core.exchange(halved(summed(normed_parts, by_chip(sent[0])))))
        in_core = jnp.concatenate([conv_core, gate_core], axis=1).astype(bf16)
        in_share = total(rows_group.exchange(in_core.reshape(model, dp_size, width).swapaxes(0, 1)))
        out_sum = summed([x[:, inner_width:] for x in lines_got], [x[:, :inner_width] for x in lines_got]).astype(bf16)
        out_core = total(core.exchange(out_sum.reshape(outer.size, 2, thin, inner_width).swapaxes(0, 1)))
        out_share = total(outer.exchange(out_core.astype(bf16)))

    return (
        mixed[None],
        tokens_grad[None],
        in_share,
        parts[3].T,
        parts[6][0],
        parts[0].T,
        parts[1],
        parts[4][0],
        parts[2].T,
        parts[5][0],
        out_share.T,
        parts[7][0],
    )


def solution(mesh):
    whole = (P(),) * 10
    row = P("dp", "seq", None)
    columns = P(None, ("dp", "seq"))
    return jax.shard_map(
        body,
        mesh=mesh,
        in_specs=(row, row, P("dp", None)) + whole,
        out_specs=(row, row, columns) + (P(),) * 7 + (columns, P()),
        check_vma=False,
    )
```

```python
import functools

import jax
import jax.numpy as jnp
from jax import lax
from jax.experimental import pallas as pl
from jax.experimental.pallas import tpu as pltpu
from jax.sharding import PartitionSpec as P

epsilon = 1e-05
LANES = 128
SUBS = 8
FAR = 1e36
LEAST_RATE = 1e-33
LN2 = 0.6931471805599453
EDGE = 16
UNROLL = 16
bf16, f32 = jnp.bfloat16, jnp.float32


def nt(a, b):
    return lax.dot_general(a, b, (((1,), (1,)), ((), ())), preferred_element_type=f32)


def tn(a, b):
    return lax.dot_general(a, b, (((0,), (0,)), ((), ())), preferred_element_type=f32)


def nn(a, b):
    return jnp.dot(a, b, preferred_element_type=f32)


ANY_SPEC = pl.BlockSpec(memory_space=pltpu.HBM)


class Here:
    def __getitem__(self, which):
        if which == 1:
            return lax.axis_index("dp")
        seq = lax.axis_index("seq")
        return seq % 2 if which == 0 else seq // 2


def plain_call(kernel, name, out_shape, args, us, scratch=(), limit=12, specs=None):
    specs = specs or []
    full = lambda x: pl.BlockSpec(x.shape, lambda: (0,) * len(x.shape))
    stay = lambda n, x: pltpu.with_memory_space_constraint(x, pltpu.HBM) if specs[n : n + 1] == [ANY_SPEC] else x
    args = [stay(n, x) for n, x in enumerate(args)]
    return pl.pallas_call(
        lambda *refs: kernel(Here(), *refs),
        in_specs=list(specs) + [full(x) for x in args[len(specs) :]],
        out_specs=[full(x) for x in out_shape],
        out_shape=out_shape,
        scratch_shapes=list(scratch),
        compiler_params=pltpu.CompilerParams(vmem_limit_bytes=limit << 20),
        cost_estimate=pl.CostEstimate(flops=int(us * 1.1e9), bytes_accessed=0, transcendentals=0),
        name=name,
    )(*args)


def softplus(v):
    return jnp.maximum(v, 0.0) + jnp.log1p(jnp.exp(-jnp.abs(v)))


def tile_at(start, size=LANES):
    return pl.ds(pl.multiple_of(start, LANES), size)


def step_rows(t):
    return pl.ds(pl.multiple_of(t * SUBS, SUBS), SUBS)


def tap_masks(starts_ref, taps, length):
    row = lax.broadcasted_iota(jnp.int32, (length, LANES), 0)
    place = lax.axis_index("seq") * length + (row % SUBS) * (length // SUBS) + row // SUBS
    begin = jnp.zeros_like(place)
    reset = jnp.zeros((length, LANES), f32)
    for k in range(starts_ref.shape[1]):
        start = starts_ref[0, k]
        begin = jnp.maximum(begin, jnp.where(place >= start, start, 0))
        reset = jnp.where(place == start, 1.0, reset)
    return [reset] + [jnp.where(begin <= place - j, 1.0, 0.0) for j in range(1, taps)]


def turned(x, plain):
    length = x.shape[0]
    steps = length // SUBS
    a = lax.broadcasted_iota(jnp.int32, (length, length), 1 - plain)
    b = lax.broadcasted_iota(jnp.int32, (length, length), plain + 0)
    turn = jnp.where(b == (a % steps) * SUBS + a // steps, 1.0, 0.0).astype(bf16)
    return nn(turn, x).astype(bf16)


def spread(maps, table_ref, first, width):
    high = maps.astype(bf16)
    rest = maps - high.astype(f32)
    middle = rest.astype(bf16)
    low = (rest - middle.astype(f32)).astype(bf16)
    row = lax.broadcasted_iota(jnp.int32, (LANES, width * LANES), 0)
    lane = lax.broadcasted_iota(jnp.int32, (LANES, width * LANES), 1)
    ones = jnp.where(row == first + lane // LANES, 1.0, 0.0).astype(bf16)
    table_ref[...] = nn(high, ones) + nn(middle, ones) + nn(low, ones)


def sub_scan(decay, value, forward):
    row = lax.broadcasted_iota(jnp.int32, decay.shape, 0)
    if not forward:
        row = SUBS - 1 - row

    def moved(x, by, fill):
        return jnp.where(row < by, fill, pltpu.roll(x, by if forward else SUBS - by, 0))

    by = 1
    while by < SUBS:
        d, v = moved(decay, by, 1.0), moved(value, by, 0.0)
        value = decay * v + value
        decay = decay * d
        by *= 2
    return value, moved(decay, 1, 1.0), moved(value, 1, 0.0)


def conv_windows(ext, taps, length):
    return [ext[(taps - 1 - j) * SUBS : (taps - 1 - j) * SUBS + length] for j in range(taps)]


def conv_sum(windows, masks, vec_ref, at, taps):
    out = vec_ref[pl.ds(taps, 1), at] + vec_ref[pl.ds(taps - 1, 1), at] * windows[0]
    for j in range(1, taps):
        out = out + vec_ref[pl.ds(taps - 1 - j, 1), at] * windows[j] * masks[j]
    return out


def normalise(x, gain):
    wide = x.astype(f32)
    inv = lax.rsqrt(jnp.mean(wide * wide, axis=-1, keepdims=True) + epsilon)
    return (wide * inv * gain).astype(bf16)


def front_kernel(
    states, rank, taps,
    here, starts_hbm, tok_hbm, cot_hbm, gain_hbm, convw_hbm, convb_hbm, dtb_hbm, skip_hbm, alog_hbm, dtw_hbm, wx_hbm,
    win_hbm, wo_hbm, left_ref,
    tok_out, cot_out, ext_ref, inner_ref, gate_ref, ggated_ref, gs_ref, dt_ref, proj_ref, table, pack_ref,
    dx_ref, ex_ref, db_ref, fx_ref, vec_ref, rates_ref, gain_ref, masks, *rest,
):
    (normed, dtm_s, u_s, ends, starts_ref, tok_ref, cot_ref, gain_s, convw_s, convb_s, dtb_s, skip_s, alog_s, dtw_ref, wx_ref,
     win_ref, wo_ref, sems, wide_sems) = rest
    length, model = cot_ref.shape
    width = rates_ref.shape[1]
    steps = length // SUBS
    rim = taps - 1
    maps = rank + 2 * states
    block = min(512, width)
    pairs = (
        (tok_hbm.at[0], tok_ref), (gain_hbm, gain_s), (cot_hbm.at[0], cot_ref), (convw_hbm, convw_s),
        (convb_hbm, convb_s), (dtb_hbm, dtb_s), (skip_hbm, skip_s), (alog_hbm, alog_s), (wx_hbm, wx_ref),
        (dtw_hbm, dtw_ref), (starts_hbm, starts_ref),
    )
    loads = [pltpu.make_async_copy(a, b, sems.at[n]) for n, (a, b) in enumerate(pairs)]

    def weights(j):
        conv = tile_at(j * block, block)
        gate = tile_at(width + j * block, block)
        return [
            pltpu.make_async_copy(win_hbm.at[:, conv], win_ref.at[:, conv], wide_sems.at[0, j]),
            pltpu.make_async_copy(win_hbm.at[:, gate], win_ref.at[:, gate], wide_sems.at[1, j]),
            pltpu.make_async_copy(wo_hbm.at[conv, :], wo_ref.at[conv, :], wide_sems.at[2, j]),
        ]

    for load in loads:
        load.start()
    for j in range(min(2, width // block)):
        for load in weights(j):
            load.start()
    for load in loads[:2]:
        load.wait()
    gain_ref[...] = gain_s[...].astype(f32).reshape(1, model)
    tok_out[pl.ds(0, length), :] = turned(tok_ref[...], False)
    left = left_ref[...].astype(f32)
    tok_out[pl.ds(length, EDGE), :] = jnp.concatenate([left, jnp.zeros((EDGE - rim, model), f32)], axis=0).astype(bf16)
    for load in loads[2:]:
        load.wait()
    vec_ref[pl.ds(0, taps), :] = convw_s[...].astype(f32)
    for n, ref in enumerate((convb_s, dtb_s, skip_s)):
        vec_ref[pl.ds(taps + n, 1), :] = ref[...].astype(f32).reshape(1, width)
    rates_ref[...] = jnp.minimum(-jnp.exp(alog_s[...]), -LEAST_RATE) * (1.0 / LN2)
    cot = turned(cot_ref[...], False)
    cot_out[...] = cot
    normed[...] = normalise(tok_out[...], gain_ref[...])
    for k, mask in enumerate(tap_masks(starts_ref, taps, length)):
        masks[k] = mask
    proj_ref[...] = jnp.zeros_like(proj_ref)

    def project(j, _):
        wide = tile_at(j * block, block)
        for load in weights(j):
            load.wait()

        @pl.when(j + 2 < width // block)
        def _():
            for load in weights(j + 2):
                load.start()

        conv = nn(normed[...], win_ref[:, wide]).astype(bf16)
        gate = nn(normed[pl.ds(0, length), :], win_ref[:, tile_at(width + j * block, block)])
        ggated = nt(cot_out[...], wo_ref[wide, :])
        gate_ref[:, wide] = gate
        ggated_ref[:, wide] = ggated
        gs_ref[:, wide] = ggated * gate * jax.nn.sigmoid(gate)
        row = lax.broadcasted_iota(jnp.int32, (SUBS, LANES), 0)
        mask = [masks[k] for k in range(taps)]
        for tile in range(block // LANES):
            far = tile_at(j * block + tile * LANES)
            part = conv[:, tile * LANES : (tile + 1) * LANES].astype(f32)
            pieces = []
            for b in range(rim):
                first = length - (rim - b) * SUBS
                moved = pltpu.roll(part[first : first + SUBS], 1, 0)
                pieces.append(jnp.where(row == 0, part[length + b : length + b + 1], moved))
            ext = jnp.concatenate(pieces + [part[:length]], axis=0)
            pad = jnp.zeros((2 * EDGE - rim * SUBS, LANES), f32)
            ext_ref[:, far] = jnp.concatenate([pad, ext], axis=0).astype(bf16)
            pre = conv_sum(conv_windows(ext, taps, length), mask, vec_ref, far, taps)
            inner_ref[:, far] = (pre * jax.nn.sigmoid(pre)).astype(bf16)
        proj_ref[:, :maps] += nt(inner_ref[:, wide], wx_ref[:, wide])
        return 0

    lax.fori_loop(0, width // block, project, 0)
    spread(proj_ref[...], table, rank, 2 * states)
    ends[...] = jnp.zeros_like(ends)
    half = states // 2
    zero = jnp.zeros((SUBS, LANES), f32)
    one = jnp.ones((SUBS, LANES), f32)
    low = proj_ref[:, :rank].astype(bf16)

    def scan(tile, _):
        at = tile_at(tile * LANES)
        dt = softplus(nn(low, dtw_ref[:, at]) + vec_ref[pl.ds(taps + 1, 1), at])
        dt_ref[:, at] = dt
        u_s[...] = dt * inner_ref[:, at].astype(f32)
        dtm = jnp.where(masks[0] > 0.0, FAR, dt)
        dtm_s[...] = dtm
        span = jnp.sum(dtm, axis=0, keepdims=True)
        high = span.astype(bf16).astype(f32)
        middle = (span - high).astype(bf16).astype(f32)
        ends[pl.ds(2 * states, 1), at] = high
        ends[pl.ds(2 * states + 1, 1), at] = middle
        ends[pl.ds(2 * states + 2, 1), at] = span - high - middle
        for first in range(0, states, half):
            rates = [jnp.broadcast_to(rates_ref[pl.ds(first + k, 1), at], (SUBS, LANES)) for k in range(half)]

            def lap(t, carry):
                h, f, p = carry
                rows = step_rows(t)
                d, u, g = dtm_s[rows, :], u_s[rows, :], gs_ref[rows, at]
                hn, fn, pn = [], [], []
                for k in range(half):
                    n = first + k
                    a = jnp.exp2(d * rates[k])
                    hn.append(a * h[k] + u * table[rows, n * LANES : (n + 1) * LANES])
                    q = p[k] * a
                    pn.append(q)
                    n += states
                    fn.append(f[k] + q * (g * table[rows, n * LANES : (n + 1) * LANES]))
                return tuple(hn), tuple(fn), tuple(pn)

            start = ((zero,) * half, (zero,) * half, (one,) * half)
            h, f, p = lax.fori_loop(0, steps, lap, start, unroll=UNROLL)
            for k in range(half):
                n = first + k
                e_in, d_ex, e_ex = sub_scan(p[k], h[k], True)
                f_in, b_ex, f_ex = sub_scan(p[k], f[k], False)
                ends[pl.ds(n, 1), at] = e_in[SUBS - 1 :, :]
                ends[pl.ds(states + n, 1), at] = f_in[:1, :]
                dx_ref[n, :, at] = d_ex
                ex_ref[n, :, at] = e_ex
                db_ref[n, :, at] = b_ex
                fx_ref[n, :, at] = f_ex
        return 0

    lax.fori_loop(0, width // LANES, scan, 0)
    pack_ref[...] = ends[...].astype(bf16)


def front(starts, tok, cot, gain, convw, convb, dtb, skip, alog, dtw, wx, in_weight, out_weight, left):
    length, model = cot.shape[1:]
    states, width = alog.shape
    rank, taps = dtw.shape[0], convw.shape[0]
    pack_rows = 2 * states + EDGE
    shape = jax.ShapeDtypeStruct
    big = lambda dtype: shape((length, width), dtype)
    out = [
        shape((length + EDGE, model), bf16), shape((length, model), bf16), shape((length + 2 * EDGE, width), bf16),
        big(bf16), big(f32), big(f32), big(f32), big(f32),
        shape((length, LANES), f32), shape((length, 2 * states * LANES), f32), shape((pack_rows, width), bf16),
    ] + [shape((states, SUBS, width), f32)] * 4 + [
        shape((taps + 4, width), f32), shape((states, width), f32), shape((1, model), f32),
        shape((taps, length, LANES), f32),
    ]
    args = (starts, tok, cot, gain, convw, convb, dtb, skip, alog, dtw, wx, in_weight, out_weight, left)
    scratch = [
        pltpu.VMEM((length + EDGE, model), bf16),
        pltpu.VMEM((length, LANES), f32),
        pltpu.VMEM((length, LANES), f32),
        pltpu.VMEM((pack_rows, width), f32),
        pltpu.SMEM(starts.shape, jnp.int32),
        pltpu.VMEM((length, model), bf16),
        pltpu.VMEM((length, model), bf16),
    ] + [pltpu.VMEM(x.shape, x.dtype) for x in args[3:13]]
    scratch += [pltpu.SemaphoreType.DMA((11,)), pltpu.SemaphoreType.DMA((3, width // min(512, width)))]
    return plain_call(
        functools.partial(front_kernel, states, rank, taps), "front", out,
        args, 20, scratch, 24, [ANY_SPEC] * 13,
    )


def chip_spot(tile, chips, tiles):
    half, chip, core = tile // (2 * chips), (tile // 2) % chips, tile % 2
    return chip, core * (tiles // (2 * chips)) + half


def forward_kernel(
    states, taps, chips, rows_size,
    here, masks, cot_ref, tok_ref, far_ref, vec_ref, rates_ref, entry_ref, table, dt_ref, inner_ref, gate_ref, ggated_ref, dx_ref, ex_ref,
    gated_ref, ggate_ref, *rest,
):
    hs_refs, rest = rest[:8], rest[8:]
    lines, blocks, (dtm_s, u_s, y_s, held) = rest[:rows_size], rest[rows_size:-4], rest[-4:]
    length, width = inner_ref.shape
    tiles, steps = width // LANES, length // SUBS
    zero = jnp.zeros((SUBS, LANES), f32)

    def scan(tile, _):
        at = tile_at(tile * LANES)
        dt = dt_ref[:, at]
        x = inner_ref[:, at].astype(f32)
        dtm_s[...] = jnp.where(masks[0] > 0.0, FAR, dt)
        u_s[...] = dt * x

        def wide(ref, n):
            return jnp.broadcast_to(ref[pl.ds(n, 1), at], (SUBS, LANES))

        rates = [wide(rates_ref, n) for n in range(states)]
        start = tuple(dx_ref[n, :, at] * wide(entry_ref, n) + ex_ref[n, :, at] for n in range(states))
        for n in range(states):
            hs_refs[n * 8 // states][tile, 0, n % (states // 8)] = start[n]

        def lap(t, h):
            rows = step_rows(t)
            d, u = dtm_s[rows, :], u_s[rows, :]
            new, y = [], [zero, zero]
            for n in range(states):
                now = jnp.exp2(d * rates[n]) * h[n] + u * table[rows, n * LANES : (n + 1) * LANES]
                hs_refs[n * 8 // states][tile, t + 1, n % (states // 8)] = now
                y[n % 2] = y[n % 2] + now * table[rows, (states + n) * LANES : (states + n + 1) * LANES]
                new.append(now)
            y_s[rows, :] = y[0] + y[1]
            return tuple(new)

        lax.fori_loop(0, steps, lap, start, unroll=UNROLL)
        scanned = y_s[...] + vec_ref[pl.ds(taps + 2, 1), at] * x
        gate = gate_ref[:, at]
        sig = jax.nn.sigmoid(gate)
        gated_ref[:, at] = (scanned * gate * sig).astype(bf16)
        ggate = (ggated_ref[:, at] * scanned * (sig * (1.0 + gate * (1.0 - sig)))).astype(bf16)
        ggate_ref[:, at] = ggate
        if chips:
            chip, spot = chip_spot(tile, chips, tiles)
            held[chip, :, tile_at(spot * LANES)] = ggate
        return 0

    lax.fori_loop(0, tiles, scan, 0)
    for n in range(chips):
        part = held.shape[2]
        blocks[n][:, :part] = held[here[2] ^ n]
        if n == 1:
            model = cot_ref.shape[1]
            blocks[n][:, part : part + model] = tok_ref[pl.ds(0, length), :]
            blocks[n][:, part + model :] = turned(far_ref[...], False)
    thin = cot_ref.shape[1] // rows_size
    for n in range(rows_size):
        lines[n][:, :width] = gated_ref[...]
        lines[n][:, width:] = cot_ref[:, tile_at((here[1] ^ n) * thin, thin)]


def forward(masks, cot, tok, far, vec, rates, entry, table, dt, inner, gate, ggated, dx, ex, taps, chips, rows_size):
    length, width = inner.shape
    states = rates.shape[0]
    shape = jax.ShapeDtypeStruct
    return plain_call(
        functools.partial(forward_kernel, states, taps, chips, rows_size),
        "forward",
        [shape((length, width), bf16)] * 2
        + [shape((width // LANES, length // SUBS + 1, states // 8, SUBS, LANES), f32)] * 8
        + [shape((length, width + cot.shape[1] // rows_size), bf16)] * rows_size
        + [shape((length, width // max(chips, 1) + 2 * cot.shape[1] * (n == 1)), bf16) for n in range(chips)],
        (masks, cot, tok, far, vec, rates, entry, table, dt, inner, gate, ggated, dx, ex),
        8,
        [pltpu.VMEM((length, LANES), f32)] * 3 + [pltpu.VMEM((max(chips, 1), length, width // max(chips, 1)), bf16)],
        4,
    )


def backward_kernel(
    states, rank, taps, chips,
    here, win_hbm, dtw_hbm, wx_hbm, masks, proj_ref, tok_ref, gain_ref, vec_ref, rates_ref, arrive_ref,
    table, dt_ref, inner_ref, gs_ref, hs0, hs1, hs2, hs3, hs4, hs5, hs6, hs7, db_ref, fx_ref, ggate_ref, ext_ref,
    ngrad, *rest,
):
    blocks, rest = rest[: max(chips, 1)], rest[max(chips, 1) :]
    (acc, dtm_s, u_s, s1_s, s2_s, isg, raw_s, sent_s, low_acc, pg, small, held, win_ref, dtw_ref, wx_ref, sems) = rest[-16:]
    length, width = inner_ref.shape
    model = tok_ref.shape[1]
    steps, tiles = length // SUBS, width // LANES
    rim = taps - 1
    maps = rank + 2 * states
    row_dtw = maps
    row_rate = row_dtw + rank
    row_taps = row_rate + states
    row_dtb, row_skip, row_cb, row_gain = (row_taps + taps + k for k in range(4))
    zero = jnp.zeros((SUBS, LANES), f32)
    half = states // 2
    hs_refs = (hs0, hs1, hs2, hs3, hs4, hs5, hs6, hs7)
    block = min(512, width)
    pairs = ((dtw_hbm, dtw_ref), (wx_hbm, wx_ref))
    loads = [pltpu.make_async_copy(a, b, sems.at[n]) for n, (a, b) in enumerate(pairs)]

    def weights(j):
        slot = j % 2
        return [
            pltpu.make_async_copy(
                win_hbm.at[:, tile_at(n * width + j * block, block)], win_ref.at[slot, n], sems.at[2 + 2 * slot + n]
            )
            for n in range(2)
        ]

    for load in loads:
        load.start()
    for j in range(min(2, width // block)):
        for load in weights(j):
            load.start()
    low_acc[...] = jnp.zeros_like(low_acc)
    small[pl.ds(small.shape[0] - EDGE, EDGE), :] = jnp.zeros((EDGE, width), f32)
    low = proj_ref[:, :rank].astype(bf16)

    def clear(t, _):
        acc[step_rows(t), :] = jnp.zeros((SUBS, acc.shape[1]), f32)
        return 0

    lax.fori_loop(0, steps, clear, 0)
    loads[0].wait()

    def scan(tile, _):
        at = tile_at(tile * LANES)
        dt = dt_ref[:, at]
        x = inner_ref[:, at].astype(f32)
        dtm_s[...] = jnp.where(masks[0] > 0.0, FAR, dt)
        u_s[...] = dt * x

        def wide(ref, n):
            return jnp.broadcast_to(ref[pl.ds(n, 1), at], (SUBS, LANES))

        rates = [wide(rates_ref, n) for n in range(states)]
        for first in range(0, states, half):
            some = rates[first : first + half]

            def back(k, carry):
                f, r = carry
                t = steps - 1 - k
                rows = step_rows(t)
                dtt, g, u, d = dt_ref[rows, at], gs_ref[rows, at], u_s[rows, :], dtm_s[rows, :]
                fn, rn, s1, s2 = [], [], zero, zero
                for k in range(half):
                    n = first + k
                    into, out = (slice(m * LANES, (m + 1) * LANES) for m in (n, states + n))
                    adj = g * table[rows, out] + f[k]
                    acc[rows, into] += adj * u
                    acc[rows, out] += g * hs_refs[n * 8 // states][tile, t + 1, n % (states // 8)]
                    s1 = s1 + adj * table[rows, into]
                    flow = jnp.exp2(d * some[k]) * adj
                    fn.append(flow)
                    flow = flow * hs_refs[n * 8 // states][tile, t, n % (states // 8)]
                    s2 = s2 + flow * some[k]
                    rn.append(r[k] + flow * dtt)
                if first == 0:
                    s1_s[rows, :] = s1
                    s2_s[rows, :] = s2
                else:
                    s1_s[rows, :] += s1
                    s2_s[rows, :] += s2
                return tuple(fn), tuple(rn)

            f0 = tuple(
                db_ref[first + k, :, at] * wide(arrive_ref, first + k) + fx_ref[first + k, :, at] for k in range(half)
            )
            _, r = lax.fori_loop(0, steps, back, (f0, (zero,) * half), unroll=UNROLL)
            for k in range(half):
                small[pl.ds(row_rate + first + k, 1), at] = jnp.sum(r[k], axis=0, keepdims=True)
        s1, gs = s1_s[...], gs_ref[:, at]
        step_grad = s1 * x + LN2 * s2_s[...]
        isg[:, at] = s1 * dt + gs * vec_ref[pl.ds(taps + 2, 1), at]
        raw = nn(low, dtw_ref[:, at]) + vec_ref[pl.ds(taps + 1, 1), at]
        raw_grad = step_grad * jax.nn.sigmoid(raw)
        raw_s[:, at] = raw_grad.astype(bf16)
        small[pl.ds(row_dtb, 1), at] = jnp.sum(raw_grad, axis=0, keepdims=True)
        small[pl.ds(row_skip, 1), at] = jnp.sum(gs * x, axis=0, keepdims=True)
        return 0

    lax.fori_loop(0, tiles, scan, 0)

    def low_part(j, _):
        wide = tile_at(j * block, block)
        small[pl.ds(row_dtw, rank), wide] = tn(low, raw_s[:, wide])
        low_acc[:, :rank] += nt(raw_s[:, wide], dtw_ref[:, wide])
        return 0

    lax.fori_loop(0, width // block, low_part, 0)
    wide_row = lax.broadcasted_iota(jnp.int32, (2 * states * LANES, LANES), 0)
    wide_lane = lax.broadcasted_iota(jnp.int32, (2 * states * LANES, LANES), 1)
    ones = jnp.where(wide_lane == rank + wide_row // LANES, 1.0, 0.0).astype(bf16)
    high = acc[...].astype(bf16)
    low_acc[...] += nn(high, ones) + nn((acc[...] - high.astype(f32)).astype(bf16), ones)
    pg[...] = low_acc[...].astype(bf16)
    for load in loads[1:]:
        load.wait()
    ngrad[...] = jnp.zeros_like(ngrad)

    def close(j, _):
        wide = tile_at(j * block, block)
        for load in weights(j):
            load.wait()
        ngrad[pl.ds(0, length), :] += nt(ggate_ref[:, wide], win_ref[j % 2, 1])
        small[pl.ds(0, maps), wide] = tn(pg[...], inner_ref[:, wide])[:maps]
        inner_grad = isg[:, wide] + nn(pg[:, :maps], wx_ref[:, wide])
        mask = [masks[k] for k in range(taps)]
        row = lax.broadcasted_iota(jnp.int32, (SUBS, LANES), 0)
        for tile in range(block // LANES):
            far = tile_at(j * block + tile * LANES)
            ext = ext_ref[:, far].astype(f32)[2 * EDGE - rim * SUBS :]
            windows = conv_windows(ext, taps, length)
            pre = conv_sum(windows, mask, vec_ref, far, taps)
            sig = jax.nn.sigmoid(pre)
            grad = inner_grad[:, tile * LANES : (tile + 1) * LANES] * (sig * (1.0 + pre * (1.0 - sig)))
            small[pl.ds(row_cb, 1), far] = jnp.sum(grad, axis=0, keepdims=True)
            small[pl.ds(row_taps + rim, 1), far] = jnp.sum(grad * windows[0], axis=0, keepdims=True)
            near = [grad[step * SUBS : (step + 1) * SUBS] * vec_ref[pl.ds(rim, 1), far] for step in range(steps)]
            head = [zero] * rim
            for k in range(1, taps):
                masked = grad * mask[k]
                small[pl.ds(row_taps + rim - k, 1), far] = jnp.sum(masked * windows[k], axis=0, keepdims=True)
                masked = masked * vec_ref[pl.ds(rim - k, 1), far]
                for step in range(steps):
                    piece = masked[step * SUBS : (step + 1) * SUBS]
                    if step >= k:
                        near[step - k] = near[step - k] + piece
                    else:
                        head[rim + step - k] = head[rim + step - k] + piece
            edge = zero
            for b in range(rim):
                moved = jnp.where(row == SUBS - 1, 0.0, pltpu.roll(head[b], SUBS - 1, 0))
                near[steps - rim + b] = near[steps - rim + b] + moved
                edge = jnp.where(row == b, jnp.broadcast_to(head[b][:1], (SUBS, LANES)), edge)
            sent = jnp.concatenate(near + [edge, zero], axis=0)
            sent_s[:, tile * LANES : (tile + 1) * LANES] = sent.astype(bf16)
            if chips:
                chip, spot = chip_spot(j * (block // LANES) + tile, chips, tiles)
                held[chip, :, tile_at(spot * LANES)] = sent.astype(bf16)
            else:
                blocks[0][:, far] = sent.astype(bf16)
        ngrad[...] += nt(sent_s[...], win_ref[j % 2, 0])

        @pl.when(j + 2 < width // block)
        def _():
            for load in weights(j + 2):
                load.start()

        return 0

    lax.fori_loop(0, width // block, close, 0)
    x = tok_ref[...].astype(f32)
    inv = lax.rsqrt(jnp.mean(x * x, axis=-1, keepdims=True) + epsilon)
    small[pl.ds(row_gain, 1), pl.ds(0, model)] = jnp.sum(ngrad[...] * (x * inv), axis=0, keepdims=True)
    if chips:
        part = width // chips
        row = lax.broadcasted_iota(jnp.int32, (EDGE, part), 0)
        extra = jnp.zeros((EDGE, part), f32)
        normed = x[length:] * inv[length:] * gain_ref[...]
        count = model // part
        for b in range(rim):
            for c in range(count):
                piece = jnp.broadcast_to(normed[b : b + 1, c * part : (c + 1) * part], (EDGE, part))
                extra = jnp.where(row == rim + b * count + c, piece, extra)
        edge_rows = pl.ds(length, EDGE)
        for n in range(chips):
            held[n, edge_rows, :] = (held[n, edge_rows, :].astype(f32) + extra).astype(bf16)
        for n in range(chips):
            blocks[n][...] = held[here[2] ^ n]
    mine_ref, theirs_ref = rest[:2]
    chunk = mine_ref.shape[2]
    for c in range(2):

        @pl.when(here[0] == c)
        def _():
            for n in range(mine_ref.shape[0]):
                at, other = (2 * n + c) * chunk, (2 * n + 1 - c) * chunk
                mine_ref[n] = small[:, at : at + chunk]
                theirs_ref[n] = small[:, other : other + chunk].astype(bf16)


def backward(masks, in_weight, dtw, wx, proj, tok, gain, vec, rates, arrive, table, dt, inner, gs, deep3,
             ggate, ext, taps, chips, chunks):
    length, width = inner.shape
    model = tok.shape[1]
    states = rates.shape[0]
    rank = dtw.shape[0]
    block = min(512, width)
    steps = length // SUBS
    rows = 2 * rank + 3 * states + taps + 4
    rows = -(-rows // EDGE) * EDGE
    shape = jax.ShapeDtypeStruct
    parts = max(chips, 1)
    chunk = (chunks, rows, width // (2 * chunks))
    return plain_call(
        functools.partial(backward_kernel, states, rank, taps, chips),
        "backward",
        [shape((length + EDGE, model), f32)]
        + [shape((length + EDGE, width // parts), bf16)] * parts
        + [shape(chunk, f32), shape(chunk, bf16)],
        (in_weight, dtw, wx, masks, proj, tok, gain, vec, rates, arrive, table, dt, inner, gs, *deep3, ggate, ext),
        24,
        [
            pltpu.VMEM((length, 2 * states * LANES), f32),
        ]
        + [pltpu.VMEM((length, LANES), f32)] * 4
        + [
            pltpu.VMEM((length, width), f32),
            pltpu.VMEM((length, width), bf16),
            pltpu.VMEM((length + EDGE, block), bf16),
            pltpu.VMEM((length, LANES), f32),
            pltpu.VMEM((length, LANES), bf16),
            pltpu.VMEM((rows, width), f32),
            pltpu.VMEM((parts, length + EDGE, width // parts), bf16),
        ]
        + [pltpu.VMEM((2, 2, model, block), bf16)]
        + [pltpu.VMEM(x.shape, x.dtype) for x in (dtw, wx)]
        + [pltpu.SemaphoreType.DMA((6,))],
        16,
        [ANY_SPEC] * 3,
    )


def finish_kernel(rim, here, ngrad_ref, back_ref, tok_ref, cot_ref, gain_ref, gated_ref, wo_ref, grad_ref, mixed_ref):
    length = cot_ref.shape[0]
    x = tok_ref[pl.ds(0, length), :].astype(f32)
    mixed_ref[...] = turned((x + nn(gated_ref[...], wo_ref[...])).astype(bf16), True)
    inv = lax.rsqrt(jnp.mean(x * x, axis=-1, keepdims=True) + epsilon)
    scaled = x * inv
    row = lax.broadcasted_iota(jnp.int32, (SUBS, x.shape[1]), 0)
    pieces = [ngrad_ref[pl.ds(0, length - rim * SUBS), :]]
    for b in range(rim):
        late = jnp.where(row == SUBS - 1, back_ref[pl.ds(b, 1), :], 0.0)
        pieces.append(ngrad_ref[pl.ds(length - (rim - b) * SUBS, SUBS), :] + late)
    hat = jnp.concatenate(pieces, axis=0) * gain_ref[...]
    grad = cot_ref[...].astype(f32) + inv * (hat - scaled * jnp.mean(hat * scaled, axis=-1, keepdims=True))
    grad_ref[...] = turned(grad.astype(bf16), True)


def span_of(x, states):
    return x[2 * states : 2 * states + 1] + x[2 * states + 1 : 2 * states + 2] + x[2 * states + 2 : 2 * states + 3]


def span_rows(d):
    high = d.astype(bf16).astype(f32)
    middle = (d - high).astype(bf16).astype(f32)
    row = lax.broadcasted_iota(jnp.int32, (EDGE, d.shape[1]), 0)
    return jnp.where(row == 0, high, jnp.where(row == 1, middle, jnp.where(row == 2, d - high - middle, 0.0)))


def pair_parts(here, mine, other, rates, states):
    first = here[0] == 0
    near, far = jnp.where(first, mine, other), jnp.where(first, other, mine)
    d0, d1 = span_of(near, states), span_of(far, states)
    state = jnp.exp2(rates * d1) * near[:states] + far[:states]
    flow = near[states : 2 * states] + jnp.exp2(rates * d0) * far[states : 2 * states]
    return state, flow, span_rows(d0 + d1)


def pair_kernel(states, here, mine_ref, other_ref, rates_ref, out_ref):
    state, flow, spans = pair_parts(
        here, mine_ref[...].astype(f32), other_ref[...].astype(f32), rates_ref[...], states
    )
    out_ref[...] = jnp.concatenate([state, flow, spans], axis=0).astype(bf16)


def pair_half_kernel(states, here, mine_ref, other_ref, rates_ref, out_ref):
    half = rates_ref.shape[1] // 2
    at = tile_at(here[0] * half, half)
    parts = pair_parts(here, mine_ref[:, at].astype(f32), other_ref[:, at].astype(f32), rates_ref[:, at], states)
    out_ref[...] = jnp.concatenate(parts, axis=0).astype(bf16)


def quad_kernel(states, here, mine_ref, got_ref, rates_ref, near_ref, out_ref):
    half = rates_ref.shape[1] // 2
    rates = rates_ref[:, tile_at(here[0] * half, half)]
    mine, got = mine_ref[...].astype(f32), got_ref[...].astype(f32)
    first = here[2] % 2 == 0
    low, high = jnp.where(first, mine, got), jnp.where(first, got, mine)
    d0, d1 = span_of(low, states), span_of(high, states)
    w0, w1 = jnp.exp2(rates * d0), jnp.exp2(rates * d1)
    near_ref[pl.ds(0, states), :] = jnp.where(first, 0.0, low[:states])
    near_ref[pl.ds(states, states), :] = jnp.where(first, high[states : 2 * states], 0.0)
    near_ref[pl.ds(2 * states, states), :] = jnp.where(first, 1.0, w0)
    near_ref[pl.ds(3 * states, states), :] = jnp.where(first, w1, 1.0)
    state = w1 * low[:states] + high[:states]
    flow = low[states : 2 * states] + w0 * high[states : 2 * states]
    out_ref[...] = jnp.where(here[2] < 2, state, flow).astype(bf16)


def enter_half_kernel(states, here, near_ref, got_ref, out_ref):
    got = got_ref[...].astype(f32)
    low = here[2] < 2
    entry = near_ref[pl.ds(0, states), :] + jnp.where(low, 0.0, near_ref[pl.ds(2 * states, states), :] * got)
    arrive = near_ref[pl.ds(states, states), :] + jnp.where(low, near_ref[pl.ds(3 * states, states), :] * got, 0.0)
    out_ref[...] = jnp.concatenate([entry, arrive], axis=0)


def enter_both_kernel(states, here, other_ref, rates_ref, here_ref, there_ref, entry_ref, arrive_ref):
    core = here[0]
    half = rates_ref.shape[1] // 2
    for part, side in ((here_ref, core), (there_ref, 1 - core)):
        at = tile_at(side * half, half)
        other = other_ref[:, at].astype(f32)
        whole = jnp.exp2(rates_ref[:, at] * span_of(other, states))
        entry, arrive = part[pl.ds(0, states), :], part[pl.ds(states, states), :]
        entry_ref[:, at] = jnp.where(core == 1, whole * entry + other[:states], entry)
        arrive_ref[:, at] = jnp.where(core == 0, whole * arrive + other[states : 2 * states], arrive)


def enter_kernel(states, count, here, other_ref, rates_ref, chips_ref, entry_ref, arrive_ref):
    core, place = here[0], here[2]
    rates = rates_ref[...]

    def split(x):
        return x[:states], x[states : 2 * states], jnp.exp2(rates * span_of(x, states))

    def lap(k, carry):
        entry, arrive = carry
        s, _, whole = split(chips_ref[k].astype(f32))
        entry = jnp.where(k < place, whole * entry + s, entry)
        back = count - 1 - k
        _, f, whole = split(chips_ref[back].astype(f32))
        arrive = jnp.where(back > place, whole * arrive + f, arrive)
        return entry, arrive

    entry, arrive = lax.fori_loop(0, count, lap, (jnp.zeros_like(rates), jnp.zeros_like(rates)))
    s, f, whole = split(other_ref[...].astype(f32))
    entry_ref[...] = jnp.where(core == 1, whole * entry + s, entry)
    arrive_ref[...] = jnp.where(core == 0, whole * arrive + f, arrive)


def out_kernel(size, chips, thin, here, *rest):
    parts, (mine_ref, theirs_ref) = rest[:size], rest[size:]
    model = mine_ref.shape[2]
    width = parts[0].shape[1] - 2 * chips * thin
    left = jnp.concatenate([x[:, width:] for x in parts], axis=0)
    out = tn(left, jnp.concatenate([x[:, :width] for x in parts], axis=0))
    for c in range(2):

        @pl.when(here[0] == c)
        def _():
            for q in range(chips):
                for ref, side in ((mine_ref, c), (theirs_ref, 1 - c)):
                    at = (2 * q + side) * thin
                    for n in range(width // model):
                        piece = out[at : at + thin, n * model : (n + 1) * model]
                        ref[q, pl.ds(n * thin, thin), :] = piece.astype(ref.dtype)


def split_cores(here, x, mine_ref, theirs_ref):
    count, rows = mine_ref.shape[:2]
    for c in range(2):

        @pl.when(here[0] == c)
        def _():
            for n in range(count):
                mine_ref[n] = x[(c * count + n) * rows : (c * count + n + 1) * rows]
                theirs_ref[n] = x[((1 - c) * count + n) * rows : ((1 - c) * count + n + 1) * rows].astype(bf16)


def gate_kernel(here, gain_ref, tok_ref, far_ref, *rest):
    gots, (normed_ref, mine_ref, theirs_ref) = rest[:-3], rest[-3:]
    length, part = gots[0].shape
    model = gain_ref.shape[1]
    near = gots[1]
    toks = (
        tok_ref[pl.ds(0, length), :],
        near[:, part : part + model],
        turned(far_ref[...], False),
        near[:, part + model :],
    )
    for k, x in enumerate(toks):
        normed_ref[pl.ds(k * length, length), :] = normalise(x, gain_ref[...])
    got = jnp.concatenate([x[:, :part] for x in gots], axis=0)
    split_cores(here, tn(got, normed_ref[...]), mine_ref, theirs_ref)


def flat(x, pieces):
    rows = x.shape[0] // pieces
    return jnp.concatenate([x[n * rows : (n + 1) * rows] for n in range(pieces)], axis=1)


def tall(x, pieces):
    lanes = x.shape[1] // pieces
    return jnp.concatenate([x[:, n * lanes : (n + 1) * lanes] for n in range(pieces)], axis=0)


def conv_kernel(length, rim, here, normed_ref, *rest):
    gots, (mine_ref, theirs_ref) = rest[:-2], rest[-2:]
    wide = gots[0].shape[1]
    model = normed_ref.shape[1]
    pieces = model // wide
    got = jnp.concatenate([got[pl.ds(0, length), :] for got in gots], axis=0)
    lefts, rights = [], []
    for k in range(len(gots)):
        edge = gots[k][pl.ds(length, EDGE), :].astype(f32)
        row = lax.broadcasted_iota(jnp.int32, (SUBS, model), 0)
        left = jnp.zeros((SUBS, model), f32)
        for b in range(rim):
            at = rim + b * pieces
            one = jnp.concatenate([edge[at + c : at + c + 1] for c in range(pieces)], axis=1)
            left = jnp.where(row == b, jnp.broadcast_to(one, left.shape), left)
        lefts.append(left)
        right = edge[:SUBS]
        rights.append(jnp.where(lax.broadcasted_iota(jnp.int32, right.shape, 0) < rim, right, 0.0))
    left, right = (jnp.concatenate(x, axis=0).astype(bf16) for x in (lefts, rights))
    conv = tn(got, normed_ref[...]) + tn(right, left)
    split_cores(here, conv, mine_ref, theirs_ref)


def halve_kernel(which, bit, here, mine_ref, got_ref, keep_ref, send_ref):
    place = (here[which] >> bit) & 1
    for n in range(mine_ref.shape[0] // 2):
        stay, leave = 2 * n + place, 2 * n + 1 - place
        keep_ref[n] = mine_ref[stay] + got_ref[stay].astype(f32)
        send_ref[n] = (mine_ref[leave] + got_ref[leave].astype(f32)).astype(bf16)


def small_last_kernel(here, mine_ref, got_ref, out_ref):
    small = mine_ref[0] + got_ref[0].astype(f32)
    out_ref[...] = flat(small, out_ref.shape[1] // small.shape[1]).astype(bf16)


def add_kernel(here, mine_ref, got_ref, out_ref):
    out_ref[...] = (mine_ref[...].astype(f32) + got_ref[...].astype(f32)).astype(bf16)


def in_merge_kernel(here, conv_mine, conv_got, gate_mine, gate_got, small_ref, own_ref, *parts):
    count, rows = conv_mine.shape[:2]
    for part in parts:
        part[pl.ds(rows, small_ref.shape[0]), :] = small_ref[...]
    for mine, got, first in ((conv_mine, conv_got, 0), (gate_mine, gate_got, count)):
        for n in range(count):
            both = mine[n] + got[n].astype(f32)
            for k in range(2 * count):

                @pl.when((here[1] ^ k) == first + n)
                def _():
                    if k == 0:
                        own_ref[...] = both
                    else:
                        parts[k - 1][pl.ds(0, rows), :] = both.astype(bf16)


def in_last_kernel(here, own_ref, *rest):
    gots, out_ref = rest[:-1], rest[-1]
    both, rows = own_ref[...], own_ref.shape[0]
    for got in gots:
        both = both + got[pl.ds(0, rows), :].astype(f32)
    out_ref[...] = both.T


def join_kernel(here, small_ref, *rest):
    gots, small_out = rest[:-1], rest[-1]
    rows = small_ref.shape[0]
    small_out[here[1]] = small_ref[...]
    for k, got in enumerate(gots):
        small_out[here[1] ^ (k + 1)] = got[pl.ds(got.shape[0] - rows, rows), :]


def out_last_kernel(here, mine_ref, got_ref, out_ref):
    thin, model = out_ref.shape[0], mine_ref.shape[2]
    both = mine_ref[0] + got_ref[0].astype(f32)
    for n in range(out_ref.shape[1] // model):
        out_ref[:, n * model : (n + 1) * model] = both[n * thin : (n + 1) * thin]


def unpack_kernel(edges, here, rates_ref, mine_ref, other_ref, *outs):
    size = mine_ref.shape[0]
    chunk = rates_ref.shape[1] // (2 * size)
    pieces = mine_ref.shape[2] // chunk
    for c, part in ((here[0], mine_ref), (1 - here[0], other_ref)):
        for k in range(size):
            at = tile_at((2 * k + c) * chunk, chunk)
            block = tall(part[k].astype(f32), pieces)
            for n, out in enumerate(outs):
                piece = block[edges[n] : edges[n + 1]]
                if (2 * k + 1) * chunk < out.shape[1]:
                    out[:, at] = piece * rates_ref[:, at] if n == 2 else piece


class Group:
    def __init__(self, axis, size, stride):
        self.axis, self.size, self.stride = axis, size, stride
        self.direct = size <= 4
        self.place = (lax.axis_index(axis) // stride) % size

    def lists(self):
        n = lax.axis_size(self.axis)
        span = self.stride * self.size
        return [
            [base + low + self.stride * k for k in range(self.size)]
            for base in range(0, n, span)
            for low in range(self.stride)
        ]

    def swap(self, x, k):
        n = lax.axis_size(self.axis)
        return lax.ppermute(x, self.axis, [(i, i ^ (k * self.stride)) for i in range(n)])

    def exchange(self, blocks):
        if not self.direct:
            got = lax.all_to_all(blocks, self.axis, 0, 0, axis_index_groups=self.lists(), tiled=True)
            return [got[k] for k in range(self.size)]
        pick = lambda k: lax.dynamic_index_in_dim(blocks, self.place ^ k, 0, keepdims=False)
        return [pick(0)] + [self.swap(pick(k), k) for k in range(1, self.size)]

    def trade(self, blocks):
        if not self.direct:
            return self.exchange(jnp.stack(blocks))
        return [blocks[0]] + [self.swap(blocks[k], k) for k in range(1, self.size)]

    def gather(self, x):
        if not self.direct:
            got = lax.all_gather(x, self.axis, axis_index_groups=self.lists())
            return [got[k] for k in range(self.size)]
        return [x] + [self.swap(x, k) for k in range(1, self.size)]

    def sender(self, k):
        return self.place ^ k if self.direct else k

    def in_order(self, parts):
        if not self.direct:
            return jnp.stack(parts)
        stacked = jnp.stack(parts)
        return jnp.stack(
            [lax.dynamic_index_in_dim(stacked, self.place ^ q, 0, keepdims=False) for q in range(self.size)]
        )


def total(parts):
    return functools.reduce(lambda a, b: a + b, [part.astype(f32) for part in parts])


def body(
    tokens,
    cotangent,
    doc_starts,
    in_weight,
    conv_weight,
    conv_bias,
    xproj_weight,
    dt_weight,
    dt_bias,
    a_log,
    skip_scale,
    out_weight,
    norm_gain,
):
    length, model = tokens.shape[1:]
    inner_width, states = a_log.shape
    low_rank = dt_weight.shape[0]
    taps = conv_weight.shape[1]
    rim = taps - 1
    dp_size, seq_size = lax.axis_size("dp"), lax.axis_size("seq")
    core, outer = Group("seq", 2, 1), Group("seq", seq_size // 2, 2)
    rows_group = Group("dp", dp_size, 1)
    width = in_weight.shape[1] // (dp_size * seq_size)
    half_rows = dp_size // 2
    thin = model // (dp_size * seq_size)
    part = inner_width // outer.size
    tiled = outer.size == 4 and dp_size == 4 and width == LANES and thin % EDGE == 0
    tiled = tiled and model % part == 0 and rim * (1 + model // part) <= EDGE
    chips = outer.size if tiled else 0
    shape = jax.ShapeDtypeStruct

    wx = xproj_weight.T
    decay_rates = -jnp.exp(a_log).T

    edge = tokens[0, length - rim :]
    left = lax.ppermute(edge, "seq", [(i, i + 1) for i in range(seq_size - 1)])
    tok, cot, ext, inner, gate, ggated, gs, dt, proj, table, mine, dx, ex, db, fx, vec, rates, gain, masks = front(
        doc_starts, tokens, cotangent, norm_gain, conv_weight.T, conv_bias, dt_bias, skip_scale, a_log.T, dt_weight, wx,
        in_weight, out_weight, left,
    )
    beyond = cot
    if tiled:
        after, _ = lax.optimization_barrier((tokens[0], edge))
        beyond = outer.swap(after, 2)
        mine, beyond = lax.optimization_barrier((mine, beyond))
    other = core.swap(mine, 1)
    entering = [shape(rates.shape, f32)] * 2
    if tiled:
        half = inner_width // 2
        (mine_half,) = plain_call(
            functools.partial(pair_half_kernel, states),
            "pair",
            [shape((2 * states + EDGE, half), bf16)],
            (mine, other, rates),
            1,
        )
        near, far = plain_call(
            functools.partial(quad_kernel, states),
            "quad",
            [shape((4 * states, half), f32), shape((states, half), bf16)],
            (mine_half, outer.swap(mine_half, 1), rates),
            1,
        )
        (here,) = plain_call(
            functools.partial(enter_half_kernel, states),
            "enter_half",
            [shape((2 * states, half), f32)],
            (near, outer.swap(far, 2)),
            1,
        )
        entry, arrive = plain_call(
            functools.partial(enter_both_kernel, states), "enter", entering, (other, rates, here, core.swap(here, 1)), 1
        )
    else:
        (chip,) = plain_call(
            functools.partial(pair_kernel, states), "pair", [shape(mine.shape, bf16)], (mine, other, rates), 2
        )
        got = outer.in_order(outer.gather(chip))
        entry, arrive = plain_call(
            functools.partial(enter_kernel, states, outer.size), "enter", entering, (other, rates, got), 2
        )
    gated, ggate, *late = forward(masks, cot, tok, beyond, vec, rates, entry, table, dt, inner, gate, ggated, dx, ex, taps, chips, dp_size)
    hs, late = late[:8], late[8:]
    lines_got = rows_group.trade(late[:dp_size])
    gate_got = outer.trade(late[dp_size:]) if tiled else None

    ngrad, *sent, small, small_theirs = backward(
        masks, in_weight, dt_weight, wx, proj, tok, gain, vec, rates, arrive, table, dt, inner, gs,
        (*hs, db, fx), ggate, ext, taps, chips, dp_size,
    )
    rows, chunk = small.shape[1:]
    turn = [ngrad]

    def call(kernel, name, outs, args, us=2):
        args = tuple(args)
        got = plain_call(kernel, name, [shape(*x) for x in outs], args, us)
        turn[0] = got[0]
        return got

    def halve(group, bit, which, mine, got, name):
        count, *rest = mine.shape
        outs = [((count // 2, *rest), f32), ((count // 2, *rest), bf16)]
        keep, send = call(functools.partial(halve_kernel, which, bit), name, outs, (mine, got))
        return keep, group.swap(send, 1 << bit)

    lines = rows * chunk // model
    part = ((lines, model), bf16)
    back = lax.ppermute(ngrad[length:], "seq", [(i, i - 1) for i in range(1, seq_size)])

    def finished():
        return call(
            functools.partial(finish_kernel, rim),
            "finish",
            [((length, model), bf16)] * 2,
            (ngrad, back, tok, cot, gain, gated, out_weight),
        )

    if tiled:
        blocks = (half_rows, width, model)
        sent, small_theirs, *early_got = lax.optimization_barrier((sent, small_theirs, *lines_got, *gate_got[:-1]))
        lines_got, gate_got = early_got[:dp_size], early_got[dp_size:] + gate_got[-1:]
        small_got = core.swap(small_theirs, 1)
        conv_got = outer.trade(sent)
        small, small_got = halve(rows_group, 0, 1, small, small_got, "small_row0")
        block = (chips, LANES // 2, model)
        out, theirs = call(
            functools.partial(out_kernel, dp_size, chips, thin),
            "out_columns",
            [(block, f32), (block, bf16)],
            lines_got,
        )
        out_got = core.swap(theirs, 1)
        small, small_got = halve(rows_group, 1, 1, small, small_got, "small_row1")
        normed, gate, theirs = call(
            gate_kernel,
            "gate_columns",
            [((chips * length, model), bf16), (blocks, f32), (blocks, bf16)],
            (gain, tok, beyond, *gate_got),
        )
        gate_got = core.swap(theirs, 1)
        (small,) = call(small_last_kernel, "small_last", [part], (small, small_got))
        small_got = outer.swap(small, 1)
        conv, theirs = call(
            functools.partial(conv_kernel, length, rim), "conv_columns", [(blocks, f32), (blocks, bf16)], (normed, *conv_got)
        )
        conv_got = core.swap(theirs, 1)
        (small,) = call(add_kernel, "small_chip0", [part], (small, small_got))
        small_got = outer.swap(small, 2)
        (small,) = call(add_kernel, "small_chip1", [part], (small, small_got))
        slab = (width, model)
        in_own, *sends = call(
            in_merge_kernel,
            "in_merge",
            [(slab, f32)] + [((width + lines, model), bf16)] * (dp_size - 1),
            (conv, conv_got, gate, gate_got, small),
        )
        in_own, *in_gots = rows_group.trade([in_own] + sends)
        out, out_got = halve(outer, 0, 2, out, out_got, "out_chip0")
        tokens_grad, mixed = finished()
        out, out_got = halve(outer, 1, 2, out, out_got, "out_chip1")
        (small,) = call(join_kernel, "join", [((dp_size, lines, model), bf16)], (small, *in_gots))
        small_other = core.swap(small, 1)
        tied, _ = lax.optimization_barrier(((in_own, *in_gots), small))
        (in_share,) = call(in_last_kernel, "in_last", [((model, width), f32)], tied)
        (out_share,) = call(out_last_kernel, "out_last", [((thin, inner_width), f32)], (out, out_got))
    else:
        tokens_grad, mixed = finished()
        small = small + core.swap(small_theirs, 1).astype(f32)
        small = total(rows_group.exchange(small.astype(bf16)))
        small = total(outer.gather(small.astype(bf16))).astype(bf16)
        small = small.reshape(rows // lines, lines, -1).swapaxes(0, 1).reshape(lines, model)
        small = rows_group.in_order(rows_group.gather(small))
        small_other = core.swap(small, 1)
    sizes = [low_rank + 2 * states, low_rank, states, taps, 1, 1, 1, 1]
    edges = [sum(sizes[:k]) for k in range(len(sizes) + 1)]
    parts = call(
        functools.partial(unpack_kernel, edges),
        "unpack",
        [((size, inner_width), f32) for size in sizes[:-1]] + [((1, model), f32)],
        (decay_rates, small, small_other),
    )
    if not tiled:

        def normalised(x):
            wide = x.astype(f32)
            inv = lax.rsqrt(jnp.mean(wide * wide, axis=-1, keepdims=True) + epsilon)
            return (wide * inv * gain).astype(bf16)

        def summed(lefts, rights):
            return functools.reduce(lambda a, b: a + b, [tn(a, b) for a, b in zip(lefts, rights, strict=True)])

        def halved(x):
            return x.astype(bf16).reshape(model, 2, -1).swapaxes(0, 1)

        def by_chip(x):
            blocks = x.reshape(x.shape[0], half_rows, outer.size, 2, width)
            return outer.exchange(blocks.transpose(2, 0, 3, 1, 4).reshape(outer.size, x.shape[0], -1))

        normed_parts = [normalised(x) for x in outer.gather(tok)]
        gate_core = total(core.exchange(halved(summed([x[:length] for x in normed_parts], by_chip(ggate)))))
        conv_core = total(core.exchange(halved(summed(normed_parts, by_chip(sent[0])))))
        in_core = jnp.concatenate([conv_core, gate_core], axis=1).astype(bf16)
        in_share = total(rows_group.exchange(in_core.reshape(model, dp_size, width).swapaxes(0, 1)))
        out_sum = summed([x[:, inner_width:] for x in lines_got], [x[:, :inner_width] for x in lines_got]).astype(bf16)
        out_core = total(core.exchange(out_sum.reshape(outer.size, 2, thin, inner_width).swapaxes(0, 1)))
        out_share = total(outer.exchange(out_core.astype(bf16)))

    return (
        mixed[None],
        tokens_grad[None],
        in_share,
        parts[3].T,
        parts[6][0],
        parts[0].T,
        parts[1],
        parts[4][0],
        parts[2].T,
        parts[5][0],
        out_share.T,
        parts[7][0],
    )


def solution(mesh):
    whole = (P(),) * 10
    row = P("dp", "seq", None)
    columns = P(None, ("dp", "seq"))
    return jax.shard_map(
        body,
        mesh=mesh,
        in_specs=(row, row, P("dp", None)) + whole,
        out_specs=(row, row, columns) + (P(),) * 7 + (columns, P()),
        check_vma=False,
    )
```

```python
import functools

import jax
import jax.numpy as jnp
from jax import lax
from jax.experimental import pallas as pl
from jax.experimental.pallas import tpu as pltpu
from jax.sharding import PartitionSpec as P

epsilon = 1e-05
LANES = 128
SUBS = 8
FAR = 1e36
LEAST_RATE = 1e-33
LN2 = 0.6931471805599453
EDGE = 16
UNROLL = 16
bf16, f32 = jnp.bfloat16, jnp.float32


def nt(a, b):
    return lax.dot_general(a, b, (((1,), (1,)), ((), ())), preferred_element_type=f32)


def tn(a, b):
    return lax.dot_general(a, b, (((0,), (0,)), ((), ())), preferred_element_type=f32)


def nn(a, b):
    return jnp.dot(a, b, preferred_element_type=f32)


ANY_SPEC = pl.BlockSpec(memory_space=pltpu.HBM)


class Here:
    def __getitem__(self, which):
        if which == 1:
            return lax.axis_index("dp")
        seq = lax.axis_index("seq")
        return seq % 2 if which == 0 else seq // 2


def plain_call(kernel, name, out_shape, args, us, scratch=(), limit=12, specs=None):
    specs = specs or []
    full = lambda x: pl.BlockSpec(x.shape, lambda: (0,) * len(x.shape))
    stay = lambda n, x: pltpu.with_memory_space_constraint(x, pltpu.HBM) if specs[n : n + 1] == [ANY_SPEC] else x
    args = [stay(n, x) for n, x in enumerate(args)]
    return pl.pallas_call(
        lambda *refs: kernel(Here(), *refs),
        in_specs=list(specs) + [full(x) for x in args[len(specs) :]],
        out_specs=[full(x) for x in out_shape],
        out_shape=out_shape,
        scratch_shapes=list(scratch),
        compiler_params=pltpu.CompilerParams(vmem_limit_bytes=limit << 20),
        cost_estimate=pl.CostEstimate(flops=int(us * 1.1e9), bytes_accessed=0, transcendentals=0),
        name=name,
    )(*args)


def softplus(v):
    return jnp.maximum(v, 0.0) + jnp.log1p(jnp.exp(-jnp.abs(v)))


def tile_at(start, size=LANES):
    return pl.ds(pl.multiple_of(start, LANES), size)


def step_rows(t):
    return pl.ds(pl.multiple_of(t * SUBS, SUBS), SUBS)


def tap_masks(starts_ref, taps, length):
    row = lax.broadcasted_iota(jnp.int32, (length, LANES), 0)
    place = lax.axis_index("seq") * length + (row % SUBS) * (length // SUBS) + row // SUBS
    begin = jnp.zeros_like(place)
    reset = jnp.zeros((length, LANES), f32)
    for k in range(starts_ref.shape[1]):
        start = starts_ref[0, k]
        begin = jnp.maximum(begin, jnp.where(place >= start, start, 0))
        reset = jnp.where(place == start, 1.0, reset)
    return [reset] + [jnp.where(begin <= place - j, 1.0, 0.0) for j in range(1, taps)]


def turned(x, plain):
    length = x.shape[0]
    steps = length // SUBS
    a = lax.broadcasted_iota(jnp.int32, (length, length), 1 - plain)
    b = lax.broadcasted_iota(jnp.int32, (length, length), plain + 0)
    turn = jnp.where(b == (a % steps) * SUBS + a // steps, 1.0, 0.0).astype(bf16)
    return nn(turn, x).astype(bf16)


def spread(maps, table_ref, first, width):
    high = maps.astype(bf16)
    rest = maps - high.astype(f32)
    middle = rest.astype(bf16)
    low = (rest - middle.astype(f32)).astype(bf16)
    row = lax.broadcasted_iota(jnp.int32, (LANES, width * LANES), 0)
    lane = lax.broadcasted_iota(jnp.int32, (LANES, width * LANES), 1)
    ones = jnp.where(row == first + lane // LANES, 1.0, 0.0).astype(bf16)
    table_ref[...] = nn(high, ones) + nn(middle, ones) + nn(low, ones)


def sub_scan(decay, value, forward):
    row = lax.broadcasted_iota(jnp.int32, decay.shape, 0)
    if not forward:
        row = SUBS - 1 - row

    def moved(x, by, fill):
        return jnp.where(row < by, fill, pltpu.roll(x, by if forward else SUBS - by, 0))

    by = 1
    while by < SUBS:
        d, v = moved(decay, by, 1.0), moved(value, by, 0.0)
        value = decay * v + value
        decay = decay * d
        by *= 2
    return value, moved(decay, 1, 1.0), moved(value, 1, 0.0)


def conv_windows(ext, taps, length):
    return [ext[(taps - 1 - j) * SUBS : (taps - 1 - j) * SUBS + length] for j in range(taps)]


def conv_sum(windows, masks, vec_ref, at, taps):
    out = vec_ref[pl.ds(taps, 1), at] + vec_ref[pl.ds(taps - 1, 1), at] * windows[0]
    for j in range(1, taps):
        out = out + vec_ref[pl.ds(taps - 1 - j, 1), at] * windows[j] * masks[j]
    return out


def normalise(x, gain):
    wide = x.astype(f32)
    inv = lax.rsqrt(jnp.mean(wide * wide, axis=-1, keepdims=True) + epsilon)
    return (wide * inv * gain).astype(bf16)


def front_kernel(
    states, rank, taps,
    here, starts_hbm, tok_hbm, cot_hbm, gain_hbm, convw_hbm, convb_hbm, dtb_hbm, skip_hbm, alog_hbm, dtw_hbm, wx_hbm,
    win_hbm, wo_hbm, left_ref,
    tok_out, cot_out, ext_ref, inner_ref, gate_ref, ggated_ref, gs_ref, dt_ref, proj_ref, table, pack_ref,
    dx_ref, ex_ref, db_ref, fx_ref, vec_ref, rates_ref, gain_ref, masks, *rest,
):
    (normed, dtm_s, u_s, ends, starts_ref, tok_ref, cot_ref, gain_s, convw_s, convb_s, dtb_s, skip_s, alog_s, dtw_ref, wx_ref,
     win_ref, wo_ref, sems, wide_sems) = rest
    length, model = cot_ref.shape
    width = rates_ref.shape[1]
    steps = length // SUBS
    rim = taps - 1
    maps = rank + 2 * states
    block = min(512, width)
    pairs = (
        (tok_hbm.at[0], tok_ref), (gain_hbm, gain_s), (cot_hbm.at[0], cot_ref), (convw_hbm, convw_s),
        (convb_hbm, convb_s), (dtb_hbm, dtb_s), (skip_hbm, skip_s), (alog_hbm, alog_s), (wx_hbm, wx_ref),
        (dtw_hbm, dtw_ref), (starts_hbm, starts_ref),
    )
    loads = [pltpu.make_async_copy(a, b, sems.at[n]) for n, (a, b) in enumerate(pairs)]

    def weights(j):
        conv = tile_at(j * block, block)
        gate = tile_at(width + j * block, block)
        return [
            pltpu.make_async_copy(win_hbm.at[:, conv], win_ref.at[:, conv], wide_sems.at[0, j]),
            pltpu.make_async_copy(win_hbm.at[:, gate], win_ref.at[:, gate], wide_sems.at[1, j]),
            pltpu.make_async_copy(wo_hbm.at[conv, :], wo_ref.at[conv, :], wide_sems.at[2, j]),
        ]

    for load in loads:
        load.start()
    for j in range(min(2, width // block)):
        for load in weights(j):
            load.start()
    for load in loads[:2]:
        load.wait()
    gain_ref[...] = gain_s[...].astype(f32).reshape(1, model)
    tok_out[pl.ds(0, length), :] = turned(tok_ref[...], False)
    left = left_ref[...].astype(f32)
    tok_out[pl.ds(length, EDGE), :] = jnp.concatenate([left, jnp.zeros((EDGE - rim, model), f32)], axis=0).astype(bf16)
    for load in loads[2:]:
        load.wait()
    vec_ref[pl.ds(0, taps), :] = convw_s[...].astype(f32)
    for n, ref in enumerate((convb_s, dtb_s, skip_s)):
        vec_ref[pl.ds(taps + n, 1), :] = ref[...].astype(f32).reshape(1, width)
    rates_ref[...] = jnp.minimum(-jnp.exp(alog_s[...]), -LEAST_RATE) * (1.0 / LN2)
    cot = turned(cot_ref[...], False)
    cot_out[...] = cot
    normed[...] = normalise(tok_out[...], gain_ref[...])
    for k, mask in enumerate(tap_masks(starts_ref, taps, length)):
        masks[k] = mask
    proj_ref[...] = jnp.zeros_like(proj_ref)

    def project(j, _):
        wide = tile_at(j * block, block)
        for load in weights(j):
            load.wait()

        @pl.when(j + 2 < width // block)
        def _():
            for load in weights(j + 2):
                load.start()

        conv = nn(normed[...], win_ref[:, wide]).astype(bf16)
        gate = nn(normed[pl.ds(0, length), :], win_ref[:, tile_at(width + j * block, block)])
        ggated = nt(cot_out[...], wo_ref[wide, :])
        gate_ref[:, wide] = gate
        ggated_ref[:, wide] = ggated
        gs_ref[:, wide] = ggated * gate * jax.nn.sigmoid(gate)
        row = lax.broadcasted_iota(jnp.int32, (SUBS, LANES), 0)
        mask = [masks[k] for k in range(taps)]
        for tile in range(block // LANES):
            far = tile_at(j * block + tile * LANES)
            part = conv[:, tile * LANES : (tile + 1) * LANES].astype(f32)
            pieces = []
            for b in range(rim):
                first = length - (rim - b) * SUBS
                moved = pltpu.roll(part[first : first + SUBS], 1, 0)
                pieces.append(jnp.where(row == 0, part[length + b : length + b + 1], moved))
            ext = jnp.concatenate(pieces + [part[:length]], axis=0)
            pad = jnp.zeros((2 * EDGE - rim * SUBS, LANES), f32)
            ext_ref[:, far] = jnp.concatenate([pad, ext], axis=0).astype(bf16)
            pre = conv_sum(conv_windows(ext, taps, length), mask, vec_ref, far, taps)
            inner_ref[:, far] = (pre * jax.nn.sigmoid(pre)).astype(bf16)
        proj_ref[:, :maps] += nt(inner_ref[:, wide], wx_ref[:, wide])
        return 0

    lax.fori_loop(0, width // block, project, 0)
    spread(proj_ref[...], table, rank, 2 * states)
    ends[...] = jnp.zeros_like(ends)
    half = states // 2
    zero = jnp.zeros((SUBS, LANES), f32)
    one = jnp.ones((SUBS, LANES), f32)
    low = proj_ref[:, :rank].astype(bf16)

    def scan(tile, _):
        at = tile_at(tile * LANES)
        dt = softplus(nn(low, dtw_ref[:, at]) + vec_ref[pl.ds(taps + 1, 1), at])
        dt_ref[:, at] = dt
        u_s[...] = dt * inner_ref[:, at].astype(f32)
        dtm = jnp.where(masks[0] > 0.0, FAR, dt)
        dtm_s[...] = dtm
        span = jnp.sum(dtm, axis=0, keepdims=True)
        high = span.astype(bf16).astype(f32)
        middle = (span - high).astype(bf16).astype(f32)
        ends[pl.ds(2 * states, 1), at] = high
        ends[pl.ds(2 * states + 1, 1), at] = middle
        ends[pl.ds(2 * states + 2, 1), at] = span - high - middle
        for first in range(0, states, half):
            rates = [jnp.broadcast_to(rates_ref[pl.ds(first + k, 1), at], (SUBS, LANES)) for k in range(half)]

            def lap(t, carry):
                h, f, p = carry
                rows = step_rows(t)
                d, u, g = dtm_s[rows, :], u_s[rows, :], gs_ref[rows, at]
                hn, fn, pn = [], [], []
                for k in range(half):
                    n = first + k
                    a = jnp.exp2(d * rates[k])
                    hn.append(a * h[k] + u * table[rows, n * LANES : (n + 1) * LANES])
                    q = p[k] * a
                    pn.append(q)
                    n += states
                    fn.append(f[k] + q * (g * table[rows, n * LANES : (n + 1) * LANES]))
                return tuple(hn), tuple(fn), tuple(pn)

            start = ((zero,) * half, (zero,) * half, (one,) * half)
            h, f, p = lax.fori_loop(0, steps, lap, start, unroll=UNROLL)
            for k in range(half):
                n = first + k
                e_in, d_ex, e_ex = sub_scan(p[k], h[k], True)
                f_in, b_ex, f_ex = sub_scan(p[k], f[k], False)
                ends[pl.ds(n, 1), at] = e_in[SUBS - 1 :, :]
                ends[pl.ds(states + n, 1), at] = f_in[:1, :]
                dx_ref[n, :, at] = d_ex
                ex_ref[n, :, at] = e_ex
                db_ref[n, :, at] = b_ex
                fx_ref[n, :, at] = f_ex
        return 0

    lax.fori_loop(0, width // LANES, scan, 0)
    pack_ref[...] = ends[...].astype(bf16)


def front(starts, tok, cot, gain, convw, convb, dtb, skip, alog, dtw, wx, in_weight, out_weight, left):
    length, model = cot.shape[1:]
    states, width = alog.shape
    rank, taps = dtw.shape[0], convw.shape[0]
    pack_rows = 2 * states + EDGE
    shape = jax.ShapeDtypeStruct
    big = lambda dtype: shape((length, width), dtype)
    out = [
        shape((length + EDGE, model), bf16), shape((length, model), bf16), shape((length + 2 * EDGE, width), bf16),
        big(bf16), big(f32), big(f32), big(f32), big(f32),
        shape((length, LANES), f32), shape((length, 2 * states * LANES), f32), shape((pack_rows, width), bf16),
    ] + [shape((states, SUBS, width), f32)] * 4 + [
        shape((taps + 4, width), f32), shape((states, width), f32), shape((1, model), f32),
        shape((taps, length, LANES), f32),
    ]
    args = (starts, tok, cot, gain, convw, convb, dtb, skip, alog, dtw, wx, in_weight, out_weight, left)
    scratch = [
        pltpu.VMEM((length + EDGE, model), bf16),
        pltpu.VMEM((length, LANES), f32),
        pltpu.VMEM((length, LANES), f32),
        pltpu.VMEM((pack_rows, width), f32),
        pltpu.SMEM(starts.shape, jnp.int32),
        pltpu.VMEM((length, model), bf16),
        pltpu.VMEM((length, model), bf16),
    ] + [pltpu.VMEM(x.shape, x.dtype) for x in args[3:13]]
    scratch += [pltpu.SemaphoreType.DMA((11,)), pltpu.SemaphoreType.DMA((3, width // min(512, width)))]
    return plain_call(
        functools.partial(front_kernel, states, rank, taps), "front", out,
        args, 20, scratch, 24, [ANY_SPEC] * 13,
    )


def chip_spot(tile, chips, tiles):
    half, chip, core = tile // (2 * chips), (tile // 2) % chips, tile % 2
    return chip, core * (tiles // (2 * chips)) + half


def forward_kernel(
    states, taps, chips, rows_size,
    here, masks, cot_ref, tok_ref, far_ref, vec_ref, rates_ref, entry_ref, table, dt_ref, inner_ref, gate_ref, ggated_ref, dx_ref, ex_ref,
    gated_ref, ggate_ref, *rest,
):
    hs_refs, rest = rest[:8], rest[8:]
    lines, blocks, (dtm_s, u_s, y_s, held) = rest[:rows_size], rest[rows_size:-4], rest[-4:]
    length, width = inner_ref.shape
    tiles, steps = width // LANES, length // SUBS
    zero = jnp.zeros((SUBS, LANES), f32)

    def scan(tile, _):
        at = tile_at(tile * LANES)
        dt = dt_ref[:, at]
        x = inner_ref[:, at].astype(f32)
        dtm_s[...] = jnp.where(masks[0] > 0.0, FAR, dt)
        u_s[...] = dt * x

        def wide(ref, n):
            return jnp.broadcast_to(ref[pl.ds(n, 1), at], (SUBS, LANES))

        rates = [wide(rates_ref, n) for n in range(states)]
        start = tuple(dx_ref[n, :, at] * wide(entry_ref, n) + ex_ref[n, :, at] for n in range(states))
        for n in range(states):
            hs_refs[n * 8 // states][tile, 0, n % (states // 8)] = start[n]

        def lap(t, h):
            rows = step_rows(t)
            d, u = dtm_s[rows, :], u_s[rows, :]
            new, y = [], [zero, zero]
            for n in range(states):
                now = jnp.exp2(d * rates[n]) * h[n] + u * table[rows, n * LANES : (n + 1) * LANES]
                hs_refs[n * 8 // states][tile, t + 1, n % (states // 8)] = now
                y[n % 2] = y[n % 2] + now * table[rows, (states + n) * LANES : (states + n + 1) * LANES]
                new.append(now)
            y_s[rows, :] = y[0] + y[1]
            return tuple(new)

        lax.fori_loop(0, steps, lap, start, unroll=UNROLL)
        scanned = y_s[...] + vec_ref[pl.ds(taps + 2, 1), at] * x
        gate = gate_ref[:, at]
        sig = jax.nn.sigmoid(gate)
        gated_ref[:, at] = (scanned * gate * sig).astype(bf16)
        ggate = (ggated_ref[:, at] * scanned * (sig * (1.0 + gate * (1.0 - sig)))).astype(bf16)
        ggate_ref[:, at] = ggate
        if chips:
            chip, spot = chip_spot(tile, chips, tiles)
            held[chip, :, tile_at(spot * LANES)] = ggate
        return 0

    lax.fori_loop(0, tiles, scan, 0)
    for n in range(chips):
        part = held.shape[2]
        blocks[n][:, :part] = held[here[2] ^ n]
        if n == 1:
            model = cot_ref.shape[1]
            blocks[n][:, part : part + model] = tok_ref[pl.ds(0, length), :]
            blocks[n][:, part + model :] = turned(far_ref[...], False)
    thin = cot_ref.shape[1] // rows_size
    for n in range(rows_size):
        lines[n][:, :width] = gated_ref[...]
        lines[n][:, width:] = cot_ref[:, tile_at((here[1] ^ n) * thin, thin)]


def forward(masks, cot, tok, far, vec, rates, entry, table, dt, inner, gate, ggated, dx, ex, taps, chips, rows_size):
    length, width = inner.shape
    states = rates.shape[0]
    shape = jax.ShapeDtypeStruct
    return plain_call(
        functools.partial(forward_kernel, states, taps, chips, rows_size),
        "forward",
        [shape((length, width), bf16)] * 2
        + [shape((width // LANES, length // SUBS + 1, states // 8, SUBS, LANES), f32)] * 8
        + [shape((length, width + cot.shape[1] // rows_size), bf16)] * rows_size
        + [shape((length, width // max(chips, 1) + 2 * cot.shape[1] * (n == 1)), bf16) for n in range(chips)],
        (masks, cot, tok, far, vec, rates, entry, table, dt, inner, gate, ggated, dx, ex),
        8,
        [pltpu.VMEM((length, LANES), f32)] * 3 + [pltpu.VMEM((max(chips, 1), length, width // max(chips, 1)), bf16)],
        4,
    )


def backward_kernel(
    states, rank, taps, chips,
    here, win_hbm, dtw_hbm, wx_hbm, masks, proj_ref, tok_ref, gain_ref, vec_ref, rates_ref, arrive_ref,
    table, dt_ref, inner_ref, gs_ref, hs0, hs1, hs2, hs3, hs4, hs5, hs6, hs7, db_ref, fx_ref, ggate_ref, ext_ref,
    ngrad, *rest,
):
    blocks, rest = rest[: max(chips, 1)], rest[max(chips, 1) :]
    (acc, dtm_s, u_s, s1_s, s2_s, isg, raw_s, sent_s, low_acc, pg, small, held, win_ref, dtw_ref, wx_ref, sems) = rest[-16:]
    length, width = inner_ref.shape
    model = tok_ref.shape[1]
    steps, tiles = length // SUBS, width // LANES
    rim = taps - 1
    maps = rank + 2 * states
    row_dtw = maps
    row_rate = row_dtw + rank
    row_taps = row_rate + states
    row_dtb, row_skip, row_cb, row_gain = (row_taps + taps + k for k in range(4))
    zero = jnp.zeros((SUBS, LANES), f32)
    half = states // 2
    hs_refs = (hs0, hs1, hs2, hs3, hs4, hs5, hs6, hs7)
    block = min(512, width)
    pairs = ((dtw_hbm, dtw_ref), (wx_hbm, wx_ref))
    loads = [pltpu.make_async_copy(a, b, sems.at[n]) for n, (a, b) in enumerate(pairs)]

    def weights(j):
        slot = j % 2
        return [
            pltpu.make_async_copy(
                win_hbm.at[:, tile_at(n * width + j * block, block)], win_ref.at[slot, n], sems.at[2 + 2 * slot + n]
            )
            for n in range(2)
        ]

    for load in loads:
        load.start()
    for j in range(min(2, width // block)):
        for load in weights(j):
            load.start()
    low_acc[...] = jnp.zeros_like(low_acc)
    small[pl.ds(small.shape[0] - EDGE, EDGE), :] = jnp.zeros((EDGE, width), f32)
    low = proj_ref[:, :rank].astype(bf16)

    def clear(t, _):
        acc[step_rows(t), :] = jnp.zeros((SUBS, acc.shape[1]), f32)
        return 0

    lax.fori_loop(0, steps, clear, 0)
    loads[0].wait()

    def scan(tile, _):
        at = tile_at(tile * LANES)
        dt = dt_ref[:, at]
        x = inner_ref[:, at].astype(f32)
        dtm_s[...] = jnp.where(masks[0] > 0.0, FAR, dt)
        u_s[...] = dt * x

        def wide(ref, n):
            return jnp.broadcast_to(ref[pl.ds(n, 1), at], (SUBS, LANES))

        rates = [wide(rates_ref, n) for n in range(states)]
        for first in range(0, states, half):
            some = rates[first : first + half]

            def back(k, carry):
                f, r = carry
                t = steps - 1 - k
                rows = step_rows(t)
                dtt, g, u, d = dt_ref[rows, at], gs_ref[rows, at], u_s[rows, :], dtm_s[rows, :]
                fn, rn, s1, s2 = [], [], zero, zero
                for k in range(half):
                    n = first + k
                    into, out = (slice(m * LANES, (m + 1) * LANES) for m in (n, states + n))
                    adj = g * table[rows, out] + f[k]
                    acc[rows, into] += adj * u
                    acc[rows, out] += g * hs_refs[n * 8 // states][tile, t + 1, n % (states // 8)]
                    s1 = s1 + adj * table[rows, into]
                    flow = jnp.exp2(d * some[k]) * adj
                    fn.append(flow)
                    flow = flow * hs_refs[n * 8 // states][tile, t, n % (states // 8)]
                    s2 = s2 + flow * some[k]
                    rn.append(r[k] + flow * dtt)
                if first == 0:
                    s1_s[rows, :] = s1
                    s2_s[rows, :] = s2
                else:
                    s1_s[rows, :] += s1
                    s2_s[rows, :] += s2
                return tuple(fn), tuple(rn)

            f0 = tuple(
                db_ref[first + k, :, at] * wide(arrive_ref, first + k) + fx_ref[first + k, :, at] for k in range(half)
            )
            _, r = lax.fori_loop(0, steps, back, (f0, (zero,) * half), unroll=UNROLL)
            for k in range(half):
                small[pl.ds(row_rate + first + k, 1), at] = jnp.sum(r[k], axis=0, keepdims=True)
        s1, gs = s1_s[...], gs_ref[:, at]
        step_grad = s1 * x + LN2 * s2_s[...]
        isg[:, at] = s1 * dt + gs * vec_ref[pl.ds(taps + 2, 1), at]
        raw = nn(low, dtw_ref[:, at]) + vec_ref[pl.ds(taps + 1, 1), at]
        raw_grad = step_grad * jax.nn.sigmoid(raw)
        raw_s[:, at] = raw_grad.astype(bf16)
        small[pl.ds(row_dtb, 1), at] = jnp.sum(raw_grad, axis=0, keepdims=True)
        small[pl.ds(row_skip, 1), at] = jnp.sum(gs * x, axis=0, keepdims=True)
        return 0

    lax.fori_loop(0, tiles, scan, 0)

    def low_part(j, _):
        wide = tile_at(j * block, block)
        small[pl.ds(row_dtw, rank), wide] = tn(low, raw_s[:, wide])
        low_acc[:, :rank] += nt(raw_s[:, wide], dtw_ref[:, wide])
        return 0

    lax.fori_loop(0, width // block, low_part, 0)
    wide_row = lax.broadcasted_iota(jnp.int32, (2 * states * LANES, LANES), 0)
    wide_lane = lax.broadcasted_iota(jnp.int32, (2 * states * LANES, LANES), 1)
    ones = jnp.where(wide_lane == rank + wide_row // LANES, 1.0, 0.0).astype(bf16)
    high = acc[...].astype(bf16)
    low_acc[...] += nn(high, ones) + nn((acc[...] - high.astype(f32)).astype(bf16), ones)
    pg[...] = low_acc[...].astype(bf16)
    for load in loads[1:]:
        load.wait()
    ngrad[...] = jnp.zeros_like(ngrad)

    def close(j, _):
        wide = tile_at(j * block, block)
        for load in weights(j):
            load.wait()
        small[pl.ds(0, maps), wide] = tn(pg[...], inner_ref[:, wide])[:maps]
        inner_grad = isg[:, wide] + nn(pg[:, :maps], wx_ref[:, wide])
        mask = [masks[k] for k in range(taps)]
        row = lax.broadcasted_iota(jnp.int32, (SUBS, LANES), 0)
        for tile in range(block // LANES):
            far = tile_at(j * block + tile * LANES)
            ext = ext_ref[:, far].astype(f32)[2 * EDGE - rim * SUBS :]
            windows = conv_windows(ext, taps, length)
            pre = conv_sum(windows, mask, vec_ref, far, taps)
            sig = jax.nn.sigmoid(pre)
            grad = inner_grad[:, tile * LANES : (tile + 1) * LANES] * (sig * (1.0 + pre * (1.0 - sig)))
            small[pl.ds(row_cb, 1), far] = jnp.sum(grad, axis=0, keepdims=True)
            small[pl.ds(row_taps + rim, 1), far] = jnp.sum(grad * windows[0], axis=0, keepdims=True)
            near = [grad[step * SUBS : (step + 1) * SUBS] * vec_ref[pl.ds(rim, 1), far] for step in range(steps)]
            head = [zero] * rim
            for k in range(1, taps):
                masked = grad * mask[k]
                small[pl.ds(row_taps + rim - k, 1), far] = jnp.sum(masked * windows[k], axis=0, keepdims=True)
                masked = masked * vec_ref[pl.ds(rim - k, 1), far]
                for step in range(steps):
                    piece = masked[step * SUBS : (step + 1) * SUBS]
                    if step >= k:
                        near[step - k] = near[step - k] + piece
                    else:
                        head[rim + step - k] = head[rim + step - k] + piece
            edge = zero
            for b in range(rim):
                moved = jnp.where(row == SUBS - 1, 0.0, pltpu.roll(head[b], SUBS - 1, 0))
                near[steps - rim + b] = near[steps - rim + b] + moved
                edge = jnp.where(row == b, jnp.broadcast_to(head[b][:1], (SUBS, LANES)), edge)
            sent = jnp.concatenate(near + [edge, zero], axis=0)
            sent_s[:, tile * LANES : (tile + 1) * LANES] = sent.astype(bf16)
            if chips:
                chip, spot = chip_spot(j * (block // LANES) + tile, chips, tiles)
                held[chip, :, tile_at(spot * LANES)] = sent.astype(bf16)
            else:
                blocks[0][:, far] = sent.astype(bf16)
        part = nt(sent_s[...], win_ref[j % 2, 0])
        ngrad[pl.ds(0, length), :] += part[:length] + nt(ggate_ref[:, wide], win_ref[j % 2, 1])
        ngrad[pl.ds(length, EDGE), :] += part[length:]

        @pl.when(j + 2 < width // block)
        def _():
            for load in weights(j + 2):
                load.start()

        return 0

    lax.fori_loop(0, width // block, close, 0)
    x = tok_ref[...].astype(f32)
    inv = lax.rsqrt(jnp.mean(x * x, axis=-1, keepdims=True) + epsilon)
    small[pl.ds(row_gain, 1), pl.ds(0, model)] = jnp.sum(ngrad[...] * (x * inv), axis=0, keepdims=True)
    if chips:
        part = width // chips
        row = lax.broadcasted_iota(jnp.int32, (EDGE, part), 0)
        extra = jnp.zeros((EDGE, part), f32)
        normed = x[length:] * inv[length:] * gain_ref[...]
        count = model // part
        for b in range(rim):
            for c in range(count):
                piece = jnp.broadcast_to(normed[b : b + 1, c * part : (c + 1) * part], (EDGE, part))
                extra = jnp.where(row == rim + b * count + c, piece, extra)
        edge_rows = pl.ds(length, EDGE)
        for n in range(chips):
            held[n, edge_rows, :] = (held[n, edge_rows, :].astype(f32) + extra).astype(bf16)
        for n in range(chips):
            blocks[n][...] = held[here[2] ^ n]
    mine_ref, theirs_ref = rest[:2]
    chunk = mine_ref.shape[2]
    for c in range(2):

        @pl.when(here[0] == c)
        def _():
            for n in range(mine_ref.shape[0]):
                at, other = (2 * n + c) * chunk, (2 * n + 1 - c) * chunk
                mine_ref[n] = small[:, at : at + chunk]
                theirs_ref[n] = small[:, other : other + chunk].astype(bf16)


def backward(masks, in_weight, dtw, wx, proj, tok, gain, vec, rates, arrive, table, dt, inner, gs, deep3,
             ggate, ext, taps, chips, chunks):
    length, width = inner.shape
    model = tok.shape[1]
    states = rates.shape[0]
    rank = dtw.shape[0]
    block = min(512, width)
    steps = length // SUBS
    rows = 2 * rank + 3 * states + taps + 4
    rows = -(-rows // EDGE) * EDGE
    shape = jax.ShapeDtypeStruct
    parts = max(chips, 1)
    chunk = (chunks, rows, width // (2 * chunks))
    return plain_call(
        functools.partial(backward_kernel, states, rank, taps, chips),
        "backward",
        [shape((length + EDGE, model), f32)]
        + [shape((length + EDGE, width // parts), bf16)] * parts
        + [shape(chunk, f32), shape(chunk, bf16)],
        (in_weight, dtw, wx, masks, proj, tok, gain, vec, rates, arrive, table, dt, inner, gs, *deep3, ggate, ext),
        24,
        [
            pltpu.VMEM((length, 2 * states * LANES), f32),
        ]
        + [pltpu.VMEM((length, LANES), f32)] * 4
        + [
            pltpu.VMEM((length, width), f32),
            pltpu.VMEM((length, width), bf16),
            pltpu.VMEM((length + EDGE, block), bf16),
            pltpu.VMEM((length, LANES), f32),
            pltpu.VMEM((length, LANES), bf16),
            pltpu.VMEM((rows, width), f32),
            pltpu.VMEM((parts, length + EDGE, width // parts), bf16),
        ]
        + [pltpu.VMEM((2, 2, model, block), bf16)]
        + [pltpu.VMEM(x.shape, x.dtype) for x in (dtw, wx)]
        + [pltpu.SemaphoreType.DMA((6,))],
        16,
        [ANY_SPEC] * 3,
    )


def finish_kernel(rim, here, ngrad_ref, back_ref, tok_ref, cot_ref, gain_ref, gated_ref, wo_ref, grad_ref, mixed_ref):
    length = cot_ref.shape[0]
    x = tok_ref[pl.ds(0, length), :].astype(f32)
    mixed_ref[...] = turned((x + nn(gated_ref[...], wo_ref[...])).astype(bf16), True)
    inv = lax.rsqrt(jnp.mean(x * x, axis=-1, keepdims=True) + epsilon)
    scaled = x * inv
    row = lax.broadcasted_iota(jnp.int32, (SUBS, x.shape[1]), 0)
    pieces = [ngrad_ref[pl.ds(0, length - rim * SUBS), :]]
    for b in range(rim):
        late = jnp.where(row == SUBS - 1, back_ref[pl.ds(b, 1), :], 0.0)
        pieces.append(ngrad_ref[pl.ds(length - (rim - b) * SUBS, SUBS), :] + late)
    hat = jnp.concatenate(pieces, axis=0) * gain_ref[...]
    grad = cot_ref[...].astype(f32) + inv * (hat - scaled * jnp.mean(hat * scaled, axis=-1, keepdims=True))
    grad_ref[...] = turned(grad.astype(bf16), True)


def span_of(x, states):
    return x[2 * states : 2 * states + 1] + x[2 * states + 1 : 2 * states + 2] + x[2 * states + 2 : 2 * states + 3]


def span_rows(d):
    high = d.astype(bf16).astype(f32)
    middle = (d - high).astype(bf16).astype(f32)
    row = lax.broadcasted_iota(jnp.int32, (EDGE, d.shape[1]), 0)
    return jnp.where(row == 0, high, jnp.where(row == 1, middle, jnp.where(row == 2, d - high - middle, 0.0)))


def pair_parts(here, mine, other, rates, states):
    first = here[0] == 0
    near, far = jnp.where(first, mine, other), jnp.where(first, other, mine)
    d0, d1 = span_of(near, states), span_of(far, states)
    state = jnp.exp2(rates * d1) * near[:states] + far[:states]
    flow = near[states : 2 * states] + jnp.exp2(rates * d0) * far[states : 2 * states]
    return state, flow, span_rows(d0 + d1)


def pair_kernel(states, here, mine_ref, other_ref, rates_ref, out_ref):
    state, flow, spans = pair_parts(
        here, mine_ref[...].astype(f32), other_ref[...].astype(f32), rates_ref[...], states
    )
    out_ref[...] = jnp.concatenate([state, flow, spans], axis=0).astype(bf16)


def pair_half_kernel(states, here, mine_ref, other_ref, rates_ref, out_ref):
    half = rates_ref.shape[1] // 2
    at = tile_at(here[0] * half, half)
    parts = pair_parts(here, mine_ref[:, at].astype(f32), other_ref[:, at].astype(f32), rates_ref[:, at], states)
    out_ref[...] = jnp.concatenate(parts, axis=0).astype(bf16)


def quad_kernel(states, here, mine_ref, got_ref, rates_ref, near_ref, out_ref):
    half = rates_ref.shape[1] // 2
    rates = rates_ref[:, tile_at(here[0] * half, half)]
    mine, got = mine_ref[...].astype(f32), got_ref[...].astype(f32)
    first = here[2] % 2 == 0
    low, high = jnp.where(first, mine, got), jnp.where(first, got, mine)
    d0, d1 = span_of(low, states), span_of(high, states)
    w0, w1 = jnp.exp2(rates * d0), jnp.exp2(rates * d1)
    near_ref[pl.ds(0, states), :] = jnp.where(first, 0.0, low[:states])
    near_ref[pl.ds(states, states), :] = jnp.where(first, high[states : 2 * states], 0.0)
    near_ref[pl.ds(2 * states, states), :] = jnp.where(first, 1.0, w0)
    near_ref[pl.ds(3 * states, states), :] = jnp.where(first, w1, 1.0)
    state = w1 * low[:states] + high[:states]
    flow = low[states : 2 * states] + w0 * high[states : 2 * states]
    out_ref[...] = jnp.where(here[2] < 2, state, flow).astype(bf16)


def enter_half_kernel(states, here, near_ref, got_ref, out_ref):
    got = got_ref[...].astype(f32)
    low = here[2] < 2
    entry = near_ref[pl.ds(0, states), :] + jnp.where(low, 0.0, near_ref[pl.ds(2 * states, states), :] * got)
    arrive = near_ref[pl.ds(states, states), :] + jnp.where(low, near_ref[pl.ds(3 * states, states), :] * got, 0.0)
    out_ref[...] = jnp.concatenate([entry, arrive], axis=0)


def enter_both_kernel(states, here, other_ref, rates_ref, here_ref, there_ref, entry_ref, arrive_ref):
    core = here[0]
    half = rates_ref.shape[1] // 2
    for part, side in ((here_ref, core), (there_ref, 1 - core)):
        at = tile_at(side * half, half)
        other = other_ref[:, at].astype(f32)
        whole = jnp.exp2(rates_ref[:, at] * span_of(other, states))
        entry, arrive = part[pl.ds(0, states), :], part[pl.ds(states, states), :]
        entry_ref[:, at] = jnp.where(core == 1, whole * entry + other[:states], entry)
        arrive_ref[:, at] = jnp.where(core == 0, whole * arrive + other[states : 2 * states], arrive)


def enter_kernel(states, count, here, other_ref, rates_ref, chips_ref, entry_ref, arrive_ref):
    core, place = here[0], here[2]
    rates = rates_ref[...]

    def split(x):
        return x[:states], x[states : 2 * states], jnp.exp2(rates * span_of(x, states))

    def lap(k, carry):
        entry, arrive = carry
        s, _, whole = split(chips_ref[k].astype(f32))
        entry = jnp.where(k < place, whole * entry + s, entry)
        back = count - 1 - k
        _, f, whole = split(chips_ref[back].astype(f32))
        arrive = jnp.where(back > place, whole * arrive + f, arrive)
        return entry, arrive

    entry, arrive = lax.fori_loop(0, count, lap, (jnp.zeros_like(rates), jnp.zeros_like(rates)))
    s, f, whole = split(other_ref[...].astype(f32))
    entry_ref[...] = jnp.where(core == 1, whole * entry + s, entry)
    arrive_ref[...] = jnp.where(core == 0, whole * arrive + f, arrive)


def out_kernel(size, chips, thin, here, *rest):
    parts, (mine_ref, theirs_ref) = rest[:size], rest[size:]
    model = mine_ref.shape[2]
    width = parts[0].shape[1] - 2 * chips * thin
    left = jnp.concatenate([x[:, width:] for x in parts], axis=0)
    out = tn(left, jnp.concatenate([x[:, :width] for x in parts], axis=0))
    for c in range(2):

        @pl.when(here[0] == c)
        def _():
            for q in range(chips):
                for ref, side in ((mine_ref, c), (theirs_ref, 1 - c)):
                    at = (2 * q + side) * thin
                    for n in range(width // model):
                        piece = out[at : at + thin, n * model : (n + 1) * model]
                        ref[q, pl.ds(n * thin, thin), :] = piece.astype(ref.dtype)


def split_cores(here, x, mine_ref, theirs_ref):
    count, rows = mine_ref.shape[:2]
    for c in range(2):

        @pl.when(here[0] == c)
        def _():
            for n in range(count):
                mine_ref[n] = x[(c * count + n) * rows : (c * count + n + 1) * rows]
                theirs_ref[n] = x[((1 - c) * count + n) * rows : ((1 - c) * count + n + 1) * rows].astype(bf16)


def gate_kernel(here, gain_ref, tok_ref, far_ref, *rest):
    gots, (normed_ref, mine_ref, theirs_ref) = rest[:-3], rest[-3:]
    length, part = gots[0].shape
    model = gain_ref.shape[1]
    near = gots[1]
    toks = (
        tok_ref[pl.ds(0, length), :],
        near[:, part : part + model],
        turned(far_ref[...], False),
        near[:, part + model :],
    )
    for k, x in enumerate(toks):
        normed_ref[pl.ds(k * length, length), :] = normalise(x, gain_ref[...])
    got = jnp.concatenate([x[:, :part] for x in gots], axis=0)
    split_cores(here, tn(got, normed_ref[...]), mine_ref, theirs_ref)


def flat(x, pieces):
    rows = x.shape[0] // pieces
    return jnp.concatenate([x[n * rows : (n + 1) * rows] for n in range(pieces)], axis=1)


def tall(x, pieces):
    lanes = x.shape[1] // pieces
    return jnp.concatenate([x[:, n * lanes : (n + 1) * lanes] for n in range(pieces)], axis=0)


def conv_kernel(length, rim, here, normed_ref, *rest):
    gots, (mine_ref, theirs_ref) = rest[:-2], rest[-2:]
    wide = gots[0].shape[1]
    model = normed_ref.shape[1]
    pieces = model // wide
    got = jnp.concatenate([got[pl.ds(0, length), :] for got in gots], axis=0)
    lefts, rights = [], []
    for k in range(len(gots)):
        edge = gots[k][pl.ds(length, EDGE), :].astype(f32)
        row = lax.broadcasted_iota(jnp.int32, (SUBS, model), 0)
        left = jnp.zeros((SUBS, model), f32)
        for b in range(rim):
            at = rim + b * pieces
            one = jnp.concatenate([edge[at + c : at + c + 1] for c in range(pieces)], axis=1)
            left = jnp.where(row == b, jnp.broadcast_to(one, left.shape), left)
        lefts.append(left)
        right = edge[:SUBS]
        rights.append(jnp.where(lax.broadcasted_iota(jnp.int32, right.shape, 0) < rim, right, 0.0))
    left, right = (jnp.concatenate(x, axis=0).astype(bf16) for x in (lefts, rights))
    conv = tn(got, normed_ref[...]) + tn(right, left)
    split_cores(here, conv, mine_ref, theirs_ref)


def halve_kernel(which, bit, here, mine_ref, got_ref, keep_ref, send_ref):
    place = (here[which] >> bit) & 1
    for n in range(mine_ref.shape[0] // 2):
        stay, leave = 2 * n + place, 2 * n + 1 - place
        keep_ref[n] = mine_ref[stay] + got_ref[stay].astype(f32)
        send_ref[n] = (mine_ref[leave] + got_ref[leave].astype(f32)).astype(bf16)


def small_last_kernel(here, mine_ref, got_ref, out_ref):
    small = mine_ref[0] + got_ref[0].astype(f32)
    out_ref[...] = flat(small, out_ref.shape[1] // small.shape[1]).astype(bf16)


def add_kernel(here, mine_ref, got_ref, out_ref):
    out_ref[...] = (mine_ref[...].astype(f32) + got_ref[...].astype(f32)).astype(bf16)


def in_merge_kernel(here, conv_mine, conv_got, gate_mine, gate_got, small_ref, own_ref, *parts):
    count, rows = conv_mine.shape[:2]
    for part in parts:
        part[pl.ds(rows, small_ref.shape[0]), :] = small_ref[...]
    for mine, got, first in ((conv_mine, conv_got, 0), (gate_mine, gate_got, count)):
        for n in range(count):
            both = mine[n] + got[n].astype(f32)
            for k in range(2 * count):

                @pl.when((here[1] ^ k) == first + n)
                def _():
                    if k == 0:
                        own_ref[...] = both
                    else:
                        parts[k - 1][pl.ds(0, rows), :] = both.astype(bf16)


def in_last_kernel(here, own_ref, *rest):
    gots, out_ref = rest[:-1], rest[-1]
    both, rows = own_ref[...], own_ref.shape[0]
    for got in gots:
        both = both + got[pl.ds(0, rows), :].astype(f32)
    out_ref[...] = both.T


def join_kernel(here, small_ref, *rest):
    gots, small_out = rest[:-1], rest[-1]
    rows = small_ref.shape[0]
    small_out[here[1]] = small_ref[...]
    for k, got in enumerate(gots):
        small_out[here[1] ^ (k + 1)] = got[pl.ds(got.shape[0] - rows, rows), :]


def out_last_kernel(here, mine_ref, got_ref, out_ref):
    thin, model = out_ref.shape[0], mine_ref.shape[2]
    both = mine_ref[0] + got_ref[0].astype(f32)
    for n in range(out_ref.shape[1] // model):
        out_ref[:, n * model : (n + 1) * model] = both[n * thin : (n + 1) * thin]


def unpack_kernel(edges, here, rates_ref, mine_ref, other_ref, *outs):
    size = mine_ref.shape[0]
    chunk = rates_ref.shape[1] // (2 * size)
    pieces = mine_ref.shape[2] // chunk
    for c, part in ((here[0], mine_ref), (1 - here[0], other_ref)):
        for k in range(size):
            at = tile_at((2 * k + c) * chunk, chunk)
            block = tall(part[k].astype(f32), pieces)
            for n, out in enumerate(outs):
                piece = block[edges[n] : edges[n + 1]]
                if (2 * k + 1) * chunk < out.shape[1]:
                    out[:, at] = piece * rates_ref[:, at] if n == 2 else piece


class Group:
    def __init__(self, axis, size, stride):
        self.axis, self.size, self.stride = axis, size, stride
        self.direct = size <= 4
        self.place = (lax.axis_index(axis) // stride) % size

    def lists(self):
        n = lax.axis_size(self.axis)
        span = self.stride * self.size
        return [
            [base + low + self.stride * k for k in range(self.size)]
            for base in range(0, n, span)
            for low in range(self.stride)
        ]

    def swap(self, x, k):
        n = lax.axis_size(self.axis)
        return lax.ppermute(x, self.axis, [(i, i ^ (k * self.stride)) for i in range(n)])

    def exchange(self, blocks):
        if not self.direct:
            got = lax.all_to_all(blocks, self.axis, 0, 0, axis_index_groups=self.lists(), tiled=True)
            return [got[k] for k in range(self.size)]
        pick = lambda k: lax.dynamic_index_in_dim(blocks, self.place ^ k, 0, keepdims=False)
        return [pick(0)] + [self.swap(pick(k), k) for k in range(1, self.size)]

    def trade(self, blocks):
        if not self.direct:
            return self.exchange(jnp.stack(blocks))
        return [blocks[0]] + [self.swap(blocks[k], k) for k in range(1, self.size)]

    def gather(self, x):
        if not self.direct:
            got = lax.all_gather(x, self.axis, axis_index_groups=self.lists())
            return [got[k] for k in range(self.size)]
        return [x] + [self.swap(x, k) for k in range(1, self.size)]

    def sender(self, k):
        return self.place ^ k if self.direct else k

    def in_order(self, parts):
        if not self.direct:
            return jnp.stack(parts)
        stacked = jnp.stack(parts)
        return jnp.stack(
            [lax.dynamic_index_in_dim(stacked, self.place ^ q, 0, keepdims=False) for q in range(self.size)]
        )


def total(parts):
    return functools.reduce(lambda a, b: a + b, [part.astype(f32) for part in parts])


def body(
    tokens,
    cotangent,
    doc_starts,
    in_weight,
    conv_weight,
    conv_bias,
    xproj_weight,
    dt_weight,
    dt_bias,
    a_log,
    skip_scale,
    out_weight,
    norm_gain,
):
    length, model = tokens.shape[1:]
    inner_width, states = a_log.shape
    low_rank = dt_weight.shape[0]
    taps = conv_weight.shape[1]
    rim = taps - 1
    dp_size, seq_size = lax.axis_size("dp"), lax.axis_size("seq")
    core, outer = Group("seq", 2, 1), Group("seq", seq_size // 2, 2)
    rows_group = Group("dp", dp_size, 1)
    width = in_weight.shape[1] // (dp_size * seq_size)
    half_rows = dp_size // 2
    thin = model // (dp_size * seq_size)
    part = inner_width // outer.size
    tiled = outer.size == 4 and dp_size == 4 and width == LANES and thin % EDGE == 0
    tiled = tiled and model % part == 0 and rim * (1 + model // part) <= EDGE
    chips = outer.size if tiled else 0
    shape = jax.ShapeDtypeStruct

    wx = xproj_weight.T
    decay_rates = -jnp.exp(a_log).T

    edge = tokens[0, length - rim :]
    left = lax.ppermute(edge, "seq", [(i, i + 1) for i in range(seq_size - 1)])
    tok, cot, ext, inner, gate, ggated, gs, dt, proj, table, mine, dx, ex, db, fx, vec, rates, gain, masks = front(
        doc_starts, tokens, cotangent, norm_gain, conv_weight.T, conv_bias, dt_bias, skip_scale, a_log.T, dt_weight, wx,
        in_weight, out_weight, left,
    )
    beyond = cot
    if tiled:
        after, _ = lax.optimization_barrier((tokens[0], edge))
        beyond = outer.swap(after, 2)
        mine, beyond = lax.optimization_barrier((mine, beyond))
    other = core.swap(mine, 1)
    entering = [shape(rates.shape, f32)] * 2
    if tiled:
        half = inner_width // 2
        (mine_half,) = plain_call(
            functools.partial(pair_half_kernel, states),
            "pair",
            [shape((2 * states + EDGE, half), bf16)],
            (mine, other, rates),
            1,
        )
        near, far = plain_call(
            functools.partial(quad_kernel, states),
            "quad",
            [shape((4 * states, half), f32), shape((states, half), bf16)],
            (mine_half, outer.swap(mine_half, 1), rates),
            1,
        )
        (here,) = plain_call(
            functools.partial(enter_half_kernel, states),
            "enter_half",
            [shape((2 * states, half), f32)],
            (near, outer.swap(far, 2)),
            1,
        )
        entry, arrive = plain_call(
            functools.partial(enter_both_kernel, states), "enter", entering, (other, rates, here, core.swap(here, 1)), 1
        )
    else:
        (chip,) = plain_call(
            functools.partial(pair_kernel, states), "pair", [shape(mine.shape, bf16)], (mine, other, rates), 2
        )
        got = outer.in_order(outer.gather(chip))
        entry, arrive = plain_call(
            functools.partial(enter_kernel, states, outer.size), "enter", entering, (other, rates, got), 2
        )
    gated, ggate, *late = forward(masks, cot, tok, beyond, vec, rates, entry, table, dt, inner, gate, ggated, dx, ex, taps, chips, dp_size)
    hs, late = late[:8], late[8:]
    lines_got = rows_group.trade(late[:dp_size])
    gate_got = outer.trade(late[dp_size:]) if tiled else None

    ngrad, *sent, small, small_theirs = backward(
        masks, in_weight, dt_weight, wx, proj, tok, gain, vec, rates, arrive, table, dt, inner, gs,
        (*hs, db, fx), ggate, ext, taps, chips, dp_size,
    )
    rows, chunk = small.shape[1:]
    turn = [ngrad]

    def call(kernel, name, outs, args, us=2):
        args = tuple(args)
        got = plain_call(kernel, name, [shape(*x) for x in outs], args, us)
        turn[0] = got[0]
        return got

    def halve(group, bit, which, mine, got, name):
        count, *rest = mine.shape
        outs = [((count // 2, *rest), f32), ((count // 2, *rest), bf16)]
        keep, send = call(functools.partial(halve_kernel, which, bit), name, outs, (mine, got))
        return keep, group.swap(send, 1 << bit)

    lines = rows * chunk // model
    part = ((lines, model), bf16)
    back = lax.ppermute(ngrad[length:], "seq", [(i, i - 1) for i in range(1, seq_size)])

    def finished():
        return call(
            functools.partial(finish_kernel, rim),
            "finish",
            [((length, model), bf16)] * 2,
            (ngrad, back, tok, cot, gain, gated, out_weight),
        )

    if tiled:
        blocks = (half_rows, width, model)
        sent, small_theirs, *early_got = lax.optimization_barrier((sent, small_theirs, *lines_got, *gate_got[:-1]))
        lines_got, gate_got = early_got[:dp_size], early_got[dp_size:] + gate_got[-1:]
        small_got = core.swap(small_theirs, 1)
        conv_got = outer.trade(sent)
        small, small_got = halve(rows_group, 0, 1, small, small_got, "small_row0")
        block = (chips, LANES // 2, model)
        out, theirs = call(
            functools.partial(out_kernel, dp_size, chips, thin),
            "out_columns",
            [(block, f32), (block, bf16)],
            lines_got,
        )
        out_got = core.swap(theirs, 1)
        small, small_got = halve(rows_group, 1, 1, small, small_got, "small_row1")
        normed, gate, theirs = call(
            gate_kernel,
            "gate_columns",
            [((chips * length, model), bf16), (blocks, f32), (blocks, bf16)],
            (gain, tok, beyond, *gate_got),
        )
        gate_got = core.swap(theirs, 1)
        (small,) = call(small_last_kernel, "small_last", [part], (small, small_got))
        small_got = outer.swap(small, 1)
        conv, theirs = call(
            functools.partial(conv_kernel, length, rim), "conv_columns", [(blocks, f32), (blocks, bf16)], (normed, *conv_got)
        )
        conv_got = core.swap(theirs, 1)
        (small,) = call(add_kernel, "small_chip0", [part], (small, small_got))
        small_got = outer.swap(small, 2)
        (small,) = call(add_kernel, "small_chip1", [part], (small, small_got))
        slab = (width, model)
        in_own, *sends = call(
            in_merge_kernel,
            "in_merge",
            [(slab, f32)] + [((width + lines, model), bf16)] * (dp_size - 1),
            (conv, conv_got, gate, gate_got, small),
        )
        in_own, *in_gots = rows_group.trade([in_own] + sends)
        out, out_got = halve(outer, 0, 2, out, out_got, "out_chip0")
        tokens_grad, mixed = finished()
        out, out_got = halve(outer, 1, 2, out, out_got, "out_chip1")
        (small,) = call(join_kernel, "join", [((dp_size, lines, model), bf16)], (small, *in_gots))
        small_other = core.swap(small, 1)
        tied, _ = lax.optimization_barrier(((in_own, *in_gots), small))
        (in_share,) = call(in_last_kernel, "in_last", [((model, width), f32)], tied)
        (out_share,) = call(out_last_kernel, "out_last", [((thin, inner_width), f32)], (out, out_got))
    else:
        tokens_grad, mixed = finished()
        small = small + core.swap(small_theirs, 1).astype(f32)
        small = total(rows_group.exchange(small.astype(bf16)))
        small = total(outer.gather(small.astype(bf16))).astype(bf16)
        small = small.reshape(rows // lines, lines, -1).swapaxes(0, 1).reshape(lines, model)
        small = rows_group.in_order(rows_group.gather(small))
        small_other = core.swap(small, 1)
    sizes = [low_rank + 2 * states, low_rank, states, taps, 1, 1, 1, 1]
    edges = [sum(sizes[:k]) for k in range(len(sizes) + 1)]
    parts = call(
        functools.partial(unpack_kernel, edges),
        "unpack",
        [((size, inner_width), f32) for size in sizes[:-1]] + [((1, model), f32)],
        (decay_rates, small, small_other),
    )
    if not tiled:

        def normalised(x):
            wide = x.astype(f32)
            inv = lax.rsqrt(jnp.mean(wide * wide, axis=-1, keepdims=True) + epsilon)
            return (wide * inv * gain).astype(bf16)

        def summed(lefts, rights):
            return functools.reduce(lambda a, b: a + b, [tn(a, b) for a, b in zip(lefts, rights, strict=True)])

        def halved(x):
            return x.astype(bf16).reshape(model, 2, -1).swapaxes(0, 1)

        def by_chip(x):
            blocks = x.reshape(x.shape[0], half_rows, outer.size, 2, width)
            return outer.exchange(blocks.transpose(2, 0, 3, 1, 4).reshape(outer.size, x.shape[0], -1))

        normed_parts = [normalised(x) for x in outer.gather(tok)]
        gate_core = total(core.exchange(halved(summed([x[:length] for x in normed_parts], by_chip(ggate)))))
        conv_core = total(core.exchange(halved(summed(normed_parts, by_chip(sent[0])))))
        in_core = jnp.concatenate([conv_core, gate_core], axis=1).astype(bf16)
        in_share = total(rows_group.exchange(in_core.reshape(model, dp_size, width).swapaxes(0, 1)))
        out_sum = summed([x[:, inner_width:] for x in lines_got], [x[:, :inner_width] for x in lines_got]).astype(bf16)
        out_core = total(core.exchange(out_sum.reshape(outer.size, 2, thin, inner_width).swapaxes(0, 1)))
        out_share = total(outer.exchange(out_core.astype(bf16)))

    return (
        mixed[None],
        tokens_grad[None],
        in_share,
        parts[3].T,
        parts[6][0],
        parts[0].T,
        parts[1],
        parts[4][0],
        parts[2].T,
        parts[5][0],
        out_share.T,
        parts[7][0],
    )


def solution(mesh):
    whole = (P(),) * 10
    row = P("dp", "seq", None)
    columns = P(None, ("dp", "seq"))
    return jax.shard_map(
        body,
        mesh=mesh,
        in_specs=(row, row, P("dp", None)) + whole,
        out_specs=(row, row, columns) + (P(),) * 7 + (columns, P()),
        check_vma=False,
    )
```
